32 devices in a mesh: dp: 4 (over x, core), expert: 8 (over z, y).
Axes of the slice: x: 2, y: 2, z: 4, core: 2. Of those that a mesh axis runs over, the one named last changes fastest.
Arguments:
- points: float32 [16384], P(('dp', 'expert')), may hold values from -6 to 6
- experts: int32 [16384, 2], P(('dp', 'expert')), may hold values from 0 to 7, all different within a row; in each aligned block of 512 rows (0 to 511, 512 to 1023, ...) at most 256 rows name the same one
- lengths: int32 [32, 3], P(('dp', 'expert')), may hold values from 1 to 320, 512 in all within a row
- domains: int32 [32, 3], P(('dp', 'expert')), may hold values from 0 to 8, as said below
- domain_weights: float32 [9], replicated, may hold values from 0.5 to 2
- vectors: float32 [5, 384], P(None, 'expert'), may hold values from -4 to 4, as said below
- attend_input: float32 [384, 1152], P('expert'), may hold values from -0.3125 to 0.3125
- attend_output: float32 [384, 384], P('expert'), may hold values from -0.875 to 0.875
- router: float32 [384, 9], P('expert'), may hold values from -0.3125 to 0.3125
- shared_input: float32 [384, 3072], P('expert'), may hold values from -0.3125 to 0.3125
- shared_output: float32 [1536, 384], P('expert'), may hold values from -0.3125 to 0.3125
- horizon: float32 [384, 105], P('expert'), may hold values from -0.3125 to 0.3125
- expert_input: float32 [2, 384, 6144], P(None, None, 'expert'), may hold values from -0.3125 to 0.3125
- expert_output: float32 [6144, 384], P('expert'), may hold values from -0.625 to 0.625
- mean_vectors: float32 [5, 384], P(None, 'expert'), may hold values from -5.340576e-05 to 5.340576e-05
- mean_attend_input: float32 [384, 1152], P('expert'), may hold values from -4.7683716e-06 to 4.7683716e-06
- mean_attend_output: float32 [384, 384], P('expert'), may hold values from -4.7683716e-06 to 4.7683716e-06
- mean_router: float32 [384, 9], P('expert'), may hold values from -4.7683716e-06 to 4.7683716e-06
- mean_shared_input: float32 [384, 3072], P('expert'), may hold values from -4.7683716e-06 to 4.7683716e-06
- mean_shared_output: float32 [1536, 384], P('expert'), may hold values from -4.7683716e-06 to 4.7683716e-06
- mean_horizon: float32 [384, 105], P('expert'), may hold values from -4.7683716e-06 to 4.7683716e-06
- mean_expert_input: float32 [2, 384, 6144], P(None, None, 'expert'), may hold values from -4.7683716e-06 to 4.7683716e-06
- mean_expert_output: float32 [6144, 384], P('expert'), may hold values from -4.7683716e-06 to 4.7683716e-06
- square_vectors: float32 [5, 384], P(None, 'expert'), may hold values from 1.0650773e-11 to 4.260309e-11
- square_attend_input: float32 [384, 1152], P('expert'), may hold values from 1.06507725e-13 to 4.260309e-13
- square_attend_output: float32 [384, 384], P('expert'), may hold values from 1.06507725e-13 to 4.260309e-13
- square_router: float32 [384, 9], P('expert'), may hold values from 1.06507725e-13 to 4.260309e-13
- square_shared_input: float32 [384, 3072], P('expert'), may hold values from 1.06507725e-13 to 4.260309e-13
- square_shared_output: float32 [1536, 384], P('expert'), may hold values from 1.06507725e-13 to 4.260309e-13
- square_horizon: float32 [384, 105], P('expert'), may hold values from 1.06507725e-13 to 4.260309e-13
- square_expert_input: float32 [2, 384, 6144], P(None, None, 'expert'), may hold values from 1.06507725e-13 to 4.260309e-13
- square_expert_output: float32 [6144, 384], P('expert'), may hold values from 1.06507725e-13 to 4.260309e-13
Outputs:
- vectors_next: float32 [5, 384], P(None, 'expert')
- vectors_mean: float32 [5, 384], P(None, 'expert')
- vectors_square: float32 [5, 384], P(None, 'expert')
- attend_input_next: float32 [384, 1152], P('expert')
- attend_input_mean: float32 [384, 1152], P('expert')
- attend_input_square: float32 [384, 1152], P('expert')
- attend_output_next: float32 [384, 384], P('expert')
- attend_output_mean: float32 [384, 384], P('expert')
- attend_output_square: float32 [384, 384], P('expert')
- router_next: float32 [384, 9], P('expert')
- router_mean: float32 [384, 9], P('expert')
- router_square: float32 [384, 9], P('expert')
- shared_input_next: float32 [384, 3072], P('expert')
- shared_input_mean: float32 [384, 3072], P('expert')
- shared_input_square: float32 [384, 3072], P('expert')
- shared_output_next: float32 [1536, 384], P('expert')
- shared_output_mean: float32 [1536, 384], P('expert')
- shared_output_square: float32 [1536, 384], P('expert')
- horizon_next: float32 [384, 105], P('expert')
- horizon_mean: float32 [384, 105], P('expert')
- horizon_square: float32 [384, 105], P('expert')
- expert_input_next: float32 [2, 384, 6144], P(None, None, 'expert')
- expert_input_mean: float32 [2, 384, 6144], P(None, None, 'expert')
- expert_input_square: float32 [2, 384, 6144], P(None, None, 'expert')
- expert_output_next: float32 [6144, 384], P('expert')
- expert_output_mean: float32 [6144, 384], P('expert')
- expert_output_square: float32 [6144, 384], P('expert')
- domain_totals: float32 [2, 9], replicated
- grad_norm: float32 [1], replicated
- trust_norms: float32 [9, 2], replicated
The draws below stay inside these ranges and needn't reach their ends.
Inputs may be any that keep to these rules, and one draw needn't show every extreme that they name: Each point names two different experts. Among the points of one device no expert is named more than 256 times, and in every draw some expert is named exactly 256 times by the points of some device. Each row lists the lengths of one device's series in order; it sums to 512 and its largest entry is exactly 320. `domains`: in every draw one domain, neither the first nor the last, names no series. The first two rows are the embedding vectors, the last three are norm gains, all positive.
All inputs are finite; a program needn't handle non-finite values.
Results may differ from the reference program's by a relative error of at most 0.0006.
The reference program's roundings to bfloat16 on the way count: a program that leaves them out, or rounds other values in their place, can miss the bound.
Values may be sent and summed in bfloat16 or wider, within the bound.
No kernel may reach another device: no remote copies, remote signals or barrier semaphores. Data moves between devices by JAX's collectives and lax.ppermute only.
A program may use at most 192 MiB of HBM per device.

```python
import math
import jax
import jax.numpy as jnp
import numpy as np
from jax import lax

D = 384
HEADS = 12
HD = 32
FF = 768
FFS = 1536
EXPERTS = 8
HOR = 105
DOMAINS = 9
SERIES = 3
STEP = 10
TOK_DEV = 512
LONGEST = 320
CAP = 256
TOKENS = 16384
PARAMS = 9482880
DEVICES = 32


def draw_vectors(key, part):
    key = jax.random.fold_in(key, 11)
    key_gain, key_embed = jax.random.split(key)
    ramp = jnp.linspace(0.5, 1.5, D, dtype=jnp.float32)
    rough = jnp.exp(0.15 * jax.random.normal(key_gain, (3, D), jnp.float32))
    embed_rows = jnp.clip(jax.random.normal(key_embed, (2, D), jnp.float32), -4.0, 4.0)
    return jnp.concatenate([embed_rows, ramp[None, :] * rough], 0)


def draw_domains(key, part):
    key = jax.random.fold_in(key, 23)
    key_absent, key_rows = jax.random.split(key)
    absent = jax.random.randint(key_absent, (), 1, DOMAINS - 1, jnp.int32)
    raw_rows = jax.random.randint(key_rows, (DEVICES, SERIES), 0, DOMAINS - 1, jnp.int32)
    return (raw_rows + (raw_rows >= absent).astype(jnp.int32)).astype(jnp.int32)


def steps_of(stream_key, shape, cuts, smallest, top_value):
    factor_of, own = 1.0, jax.random.fold_in(stream_key, 6)
    for dim, blocks in cuts:
        heights = jnp.exp(jax.random.uniform(jax.random.fold_in(own, dim), (blocks,), jnp.float32, smallest / len(cuts), top_value / len(cuts)))
        factor_of = factor_of * jnp.repeat(heights, shape[dim] // blocks).reshape([-1 if axis == dim else 1 for axis in range(len(shape))])
    return factor_of


def split_up(count, total, limit, slope):
    loads = [(1 << 20) // math.isqrt(standing ** slope) + 1 for standing in range(2, count + 1)]
    rest, given = total - limit - (count - 1), [1] * (count - 1)
    while rest > 0:
        movable = [i for i in range(count - 1) if given[i] < limit]
        mass, budget = sum([loads[i] for i in movable]), rest
        for i in movable:
            addition = min(limit - given[i], max(1, budget * loads[i] // mass), rest)
            given[i] = given[i] + addition
            rest = rest - addition
    return np.array([limit] + given)


def ragged_sizes(stream_key, number_of, total, most, slope):
    if number_of == 2:
        one = jax.random.randint(stream_key, (), max(1, total - most), min(most, total - 1) + 1)
        return jnp.stack([one, total - one])
    sizes = jnp.asarray(split_up(number_of, total, most, slope), jnp.int32)
    pairs = (number_of - 1) // 2
    donor, receiver = sizes[1:1 + 2 * pairs:2], sizes[2:2 + 2 * pairs:2]
    room = jnp.minimum(donor - 1, most - receiver)
    shifted = jax.random.randint(jax.random.fold_in(stream_key, 1), (pairs,), 0, 1 << 20) % (room + 1)
    sizes = sizes.at[1:1 + 2 * pairs:2].set(donor - shifted).at[2:2 + 2 * pairs:2].set(receiver + shifted)
    return sizes[jax.random.permutation(jax.random.fold_in(stream_key, 2), number_of)]


def shared_out(key, own, number, rows, count, top, bound, lean):
    order = jax.random.permutation(key, count)
    packed, usual = shares(count, rows * top, bound, lean, True), shares(count, rows * top, bound, lean, False)
    places = jnp.arange(count)

    def named(sizes, rotation):
        used = int((sizes > 0).sum())
        fixed = max(1, used // 4)
        shifted = fixed + (places - fixed + rotation * (used - fixed)) % max(1, count - fixed)
        return jnp.zeros((count,), jnp.int32).at[order[jnp.where(places < fixed, places, shifted)]].set(jnp.asarray(sizes, jnp.int32))

    sizes = jnp.where(number % 4 == 0, named(packed, number // 4), named(usual, number - number // 4 - 1))
    mixed = jax.random.permutation(jax.random.fold_in(own, 3), count)
    source_of, receiver = mixed[0:count // 2 * 2:2], mixed[1:count // 2 * 2:2]
    margin = jnp.minimum(sizes[source_of] - 1, bound - sizes[receiver]) // 2
    margin = jnp.where((source_of == order[0]) | (receiver == order[0]) | (sizes[receiver] == 0), 0, jnp.maximum(margin, 0))
    shifted = jax.random.randint(jax.random.fold_in(own, 4), (count // 2,), 0, 1 << 20) % (margin + 1)
    sizes = sizes.at[source_of].add(-shifted).at[receiver].add(shifted)
    members = jnp.searchsorted(jnp.cumsum(sizes), jnp.arange(rows * top), side="right").astype(jnp.int32)
    listing = members.reshape(top, rows).T
    listing = listing[jax.random.permutation(jax.random.fold_in(own, 1), rows)]
    rotation = jax.random.randint(jax.random.fold_in(own, 2), (rows, 1), 0, top)
    return jnp.take_along_axis(listing, (jnp.arange(top)[None, :] + rotation) % top, axis=1)


def shares(count, total, reach, slope, full):
    portions = [(1 << 20) // math.isqrt(rank ** slope) + 1 for rank in range(1, count + 1)]
    largest = reach if full else min(reach, max(-(-total // count), total * portions[0] // sum(portions)))
    least = 1 if total - largest >= count - 1 else 0
    given, spare = [largest] + [least] * (count - 1), total - largest - least * (count - 1)
    while spare > 0:
        movable = [i for i in range(1, count) if given[i] < largest] or [i for i in range(1, count) if given[i] < reach]
        whole, budget = sum([portions[i] for i in movable]), spare
        for i in movable:
            extra = min(reach - given[i], max(1, budget * portions[i] // whole), spare)
            given[i] = given[i] + extra
            spare = spare - extra
    return np.array(given)


def gaussian(key, shape, width, most, shards=(), held_as=jnp.bfloat16):
    array = width * jax.random.normal(key, shape, jnp.float32)
    if shards:
        array = array * steps_of(key, shape, shards, -0.22, 0.18)
    return jnp.clip(array, -most, most).astype(held_as)


def setup_inputs(seed: int = 0) -> dict:
    streams_of = jax.random.split(jax.random.key(seed), 33)
    points = gaussian(streams_of[0], (TOKENS,), 1.0, 6.0, ((0, 32),), jnp.float32)
    experts_keys = jax.random.split(jax.random.fold_in(streams_of[1], 1), TOKENS // TOK_DEV)
    experts_turns = jax.random.permutation(jax.random.fold_in(streams_of[1], 3), TOKENS // TOK_DEV)
    experts = jax.vmap(lambda own, number: shared_out(jax.random.fold_in(streams_of[1], 2), own, number, TOK_DEV, EXPERTS, 2, CAP, 2))(experts_keys, experts_turns).reshape((TOKENS, 2))
    lengths = jax.vmap(lambda own: ragged_sizes(own, SERIES, TOK_DEV, LONGEST, 1))(jax.random.split(streams_of[2], DEVICES)).reshape((DEVICES, SERIES)).astype(jnp.int32)
    domains = draw_domains(jax.random.fold_in(streams_of[32], 71), 0)
    domain_weights = jnp.clip(jnp.exp(jax.random.uniform(streams_of[4], (DOMAINS,), jnp.float32, math.log(0.5), math.log(2.0))), 0.5, 2.0)
    vectors = draw_vectors(jax.random.fold_in(streams_of[32], 71), 0)
    attend_input = gaussian(streams_of[6], (D, 3 * D), D ** -0.5, 0.3125, ((0, 8),), jnp.float32)
    attend_output = gaussian(streams_of[7], (D, D), (D // 8) ** -0.5, 0.875, ((0, 8),), jnp.float32)
    router = gaussian(streams_of[8], (D, EXPERTS + 1), D ** -0.5, 0.3125, ((0, 8),), jnp.float32)
    shared_input = gaussian(streams_of[9], (D, 2 * FFS), D ** -0.5, 0.3125, ((0, 8),), jnp.float32)
    shared_output = gaussian(streams_of[10], (FFS, D), (FFS // 4) ** -0.5, 0.3125, ((0, 8),), jnp.float32)
    horizon = gaussian(streams_of[11], (D, HOR), D ** -0.5, 0.3125, ((0, 8),), jnp.float32)
    expert_input = gaussian(streams_of[12], (2, D, EXPERTS * FF), D ** -0.5, 0.3125, ((2, 8),), jnp.float32)
    expert_output = gaussian(streams_of[13], (EXPERTS * FF, D), (FF // 8) ** -0.5, 0.625, ((0, 8),), jnp.float32)
    mean_vectors = gaussian(streams_of[14], (5, D), (0.011 * PARAMS ** -0.5), 5.340576171875e-05, ((1, 8),), jnp.float32)
    mean_attend_input = gaussian(streams_of[15], (D, 3 * D), (0.0011 * PARAMS ** -0.5), 4.76837158203125e-06, ((0, 8),), jnp.float32)
    mean_attend_output = gaussian(streams_of[16], (D, D), (0.0011 * PARAMS ** -0.5), 4.76837158203125e-06, ((0, 8),), jnp.float32)
    mean_router = gaussian(streams_of[17], (D, EXPERTS + 1), (0.0011 * PARAMS ** -0.5), 4.76837158203125e-06, ((0, 8),), jnp.float32)
    mean_shared_input = gaussian(streams_of[18], (D, 2 * FFS), (0.0011 * PARAMS ** -0.5), 4.76837158203125e-06, ((0, 8),), jnp.float32)
    mean_shared_output = gaussian(streams_of[19], (FFS, D), (0.0011 * PARAMS ** -0.5), 4.76837158203125e-06, ((0, 8),), jnp.float32)
    mean_horizon = gaussian(streams_of[20], (D, HOR), (0.0011 * PARAMS ** -0.5), 4.76837158203125e-06, ((0, 8),), jnp.float32)
    mean_expert_input = gaussian(streams_of[21], (2, D, EXPERTS * FF), (0.0011 * PARAMS ** -0.5), 4.76837158203125e-06, ((2, 8),), jnp.float32)
    mean_expert_output = gaussian(streams_of[22], (EXPERTS * FF, D), (0.0011 * PARAMS ** -0.5), 4.76837158203125e-06, ((0, 8),), jnp.float32)
    square_vectors = jnp.clip(jnp.exp(math.log(4.2603091193749165e-11) - 1.3862944 * jax.random.uniform(streams_of[23], (5, D), jnp.float32) ** steps_of(streams_of[23], (5, D), ((1, 8),), -0.2, 0.2)), 1.0650772798437291e-11, 4.2603091193749165e-11)
    square_attend_input = jnp.clip(jnp.exp(math.log(4.2603090109546993e-13) - 1.3862944 * jax.random.uniform(streams_of[24], (D, 3 * D), jnp.float32) ** steps_of(streams_of[24], (D, 3 * D), ((0, 8),), -0.2, 0.2)), 1.0650772527386748e-13, 4.2603090109546993e-13)
    square_attend_output = jnp.clip(jnp.exp(math.log(4.2603090109546993e-13) - 1.3862944 * jax.random.uniform(streams_of[25], (D, D), jnp.float32) ** steps_of(streams_of[25], (D, D), ((0, 8),), -0.2, 0.2)), 1.0650772527386748e-13, 4.2603090109546993e-13)
    square_router = jnp.clip(jnp.exp(math.log(4.2603090109546993e-13) - 1.3862944 * jax.random.uniform(streams_of[26], (D, EXPERTS + 1), jnp.float32) ** steps_of(streams_of[26], (D, EXPERTS + 1), ((0, 8),), -0.2, 0.2)), 1.0650772527386748e-13, 4.2603090109546993e-13)
    square_shared_input = jnp.clip(jnp.exp(math.log(4.2603090109546993e-13) - 1.3862944 * jax.random.uniform(streams_of[27], (D, 2 * FFS), jnp.float32) ** steps_of(streams_of[27], (D, 2 * FFS), ((0, 8),), -0.2, 0.2)), 1.0650772527386748e-13, 4.2603090109546993e-13)
    square_shared_output = jnp.clip(jnp.exp(math.log(4.2603090109546993e-13) - 1.3862944 * jax.random.uniform(streams_of[28], (FFS, D), jnp.float32) ** steps_of(streams_of[28], (FFS, D), ((0, 8),), -0.2, 0.2)), 1.0650772527386748e-13, 4.2603090109546993e-13)
    square_horizon = jnp.clip(jnp.exp(math.log(4.2603090109546993e-13) - 1.3862944 * jax.random.uniform(streams_of[29], (D, HOR), jnp.float32) ** steps_of(streams_of[29], (D, HOR), ((0, 8),), -0.2, 0.2)), 1.0650772527386748e-13, 4.2603090109546993e-13)
    square_expert_input = jnp.clip(jnp.exp(math.log(4.2603090109546993e-13) - 1.3862944 * jax.random.uniform(streams_of[30], (2, D, EXPERTS * FF), jnp.float32) ** steps_of(streams_of[30], (2, D, EXPERTS * FF), ((2, 8),), -0.2, 0.2)), 1.0650772527386748e-13, 4.2603090109546993e-13)
    square_expert_output = jnp.clip(jnp.exp(math.log(4.2603090109546993e-13) - 1.3862944 * jax.random.uniform(streams_of[31], (EXPERTS * FF, D), jnp.float32) ** steps_of(streams_of[31], (EXPERTS * FF, D), ((0, 8),), -0.2, 0.2)), 1.0650772527386748e-13, 4.2603090109546993e-13)
    return {"points": points, "experts": experts, "lengths": lengths, "domains": domains, "domain_weights": domain_weights, "vectors": vectors, "attend_input": attend_input, "attend_output": attend_output, "router": router, "shared_input": shared_input, "shared_output": shared_output, "horizon": horizon, "expert_input": expert_input, "expert_output": expert_output, "mean_vectors": mean_vectors, "mean_attend_input": mean_attend_input, "mean_attend_output": mean_attend_output, "mean_router": mean_router, "mean_shared_input": mean_shared_input, "mean_shared_output": mean_shared_output, "mean_horizon": mean_horizon, "mean_expert_input": mean_expert_input, "mean_expert_output": mean_expert_output, "square_vectors": square_vectors, "square_attend_input": square_attend_input, "square_attend_output": square_attend_output, "square_router": square_router, "square_shared_input": square_shared_input, "square_shared_output": square_shared_output, "square_horizon": square_horizon, "square_expert_input": square_expert_input, "square_expert_output": square_expert_output}


HORIZONS = (1, 8, 32, 64)
REACH = 64
KINK_THRESHOLD = 2.0
EPS_NORM = 1e-06
CLIP = 0.01
BETA_ONE = 0.9
BETA_TWO = 0.99
EPS_ADAM = 1e-08
DECAY = 0.01
RATE = 0.3
HIGHEST = lax.Precision.HIGHEST

@jax.custom_vjp
def low(v):
    return lax.optimization_barrier(v.astype(jnp.bfloat16)).astype(jnp.float32)

@jax.custom_vjp
def bfloat_backward(v):
    return v

def low_keep(v):
    return (low(v), None)

def low_pass(kept, grad):
    return (grad,)

def back_keep(v):
    return (v, None)

def back_low(kept, grad):
    return (low(grad),)
low.defvjp(low_keep, low_pass)
bfloat_backward.defvjp(back_keep, back_low)

def ahead_table():
    return np.concatenate([np.arange(horizon_len) for horizon_len in HORIZONS]).astype(np.int32)

def bilinear_contract(left, right):
    return jnp.dot(left, right, precision=HIGHEST)

def sigmoid_linear(inputs):
    return inputs * jax.nn.sigmoid(inputs)

def rms_norm(inputs, weight_gain):
    return inputs * lax.rsqrt(lax.optimization_barrier(jnp.mean(inputs * inputs, axis=-1, keepdims=True)) + EPS_NORM) * weight_gain

def rope_tables(position):
    half_width = HD // 2
    frequency = jnp.exp(-jnp.log(10000.0) * jnp.arange(half_width, dtype=jnp.float32) / half_width)
    angles = position.astype(jnp.float32)[:, None] * frequency[None, :]
    return (jnp.cos(angles)[:, None, :], jnp.sin(angles)[:, None, :])

def rotate(inputs, cosine, sine):
    half_width = inputs.shape[-1] // 2
    first_half = inputs[..., :half_width]
    second_half = inputs[..., half_width:]
    return jnp.concatenate([first_half * cosine - second_half * sine, second_half * cosine + first_half * sine], -1)

def layout(samples, series_lengths, series_domains):
    amount = samples.shape[0]
    places = jnp.arange(amount, dtype=jnp.int32)
    finish = jnp.cumsum(series_lengths).astype(jnp.int32)
    anchor = (finish - series_lengths).astype(jnp.int32)
    series = lax.optimization_barrier(jnp.sum((places[:, None] >= finish[None, :]).astype(jnp.int32), 1)).astype(jnp.int32)
    member = series[:, None] == jnp.arange(series_lengths.shape[0], dtype=jnp.int32)[None, :]
    begin_at = lax.optimization_barrier(jnp.sum(jnp.where(member, anchor[None, :], 0), 1)).astype(jnp.int32)
    finish_at = lax.optimization_barrier(jnp.sum(jnp.where(member, finish[None, :], 0), 1)).astype(jnp.int32)
    domain_of = lax.optimization_barrier(jnp.sum(jnp.where(member, series_domains[None, :], 0), 1)).astype(jnp.int32)
    ahead_steps = jnp.asarray(ahead_table())
    reached = places[:, None] + 1 + ahead_steps[None, :]
    valid_mask = (reached < finish_at[:, None]).astype(jnp.float32)
    padded = jnp.concatenate([samples, jnp.zeros((REACH + 1,), samples.dtype)])
    future = jnp.stack([padded[1 + offset:1 + offset + amount] for offset in range(REACH)], 1)
    observed_future = future[:, ahead_table()]
    return (series, places - begin_at, domain_of, valid_mask, observed_future)

def domain_count(series_lengths, series_domains):
    series, position, domain_of, valid_mask, observed_future = layout(jnp.zeros((TOK_DEV,), jnp.float32), series_lengths, series_domains)
    domain_onehot_rows = (domain_of[:, None] == jnp.arange(DOMAINS)[None, :]).astype(jnp.float32)
    return lax.optimization_barrier(jnp.sum(domain_onehot_rows * lax.optimization_barrier(jnp.sum(valid_mask, -1))[:, None], 0))

def block_loss(masters, samples, routes, series_lengths, series_domains, domain_weighting):
    gain_rows, input_w, output_w, router_w, shin_w, shout_w, readout_coefficients, exin_w, exout_w = [low(master) for master in masters]
    amount = samples.shape[0]
    series, position, domain_of, valid_mask, observed_future = layout(samples, series_lengths, series_domains)
    embedded = sigmoid_linear(samples[:, None] * gain_rows[0]) * (samples[:, None] * gain_rows[1])
    first_norm = low(rms_norm(embedded, gain_rows[2]))
    projected = bfloat_backward(bilinear_contract(first_norm, input_w)).reshape(amount, 3, HEADS, HD)
    cosine, sine = rope_tables(position)
    queries = low(rotate(projected[:, 0], cosine, sine))
    key_rows = low(rotate(projected[:, 1], cosine, sine))
    value_rows = low(projected[:, 2])
    scores = bfloat_backward(jnp.einsum('qhd,khd->hqk', queries, key_rows, precision=HIGHEST) * HD ** (-0.5))
    places = jnp.arange(amount)
    allowed = (series[:, None] == series[None, :]) & (places[None, :] <= places[:, None])
    scores = jnp.where(allowed[None], scores, -1e+30)
    exponent = jnp.exp(scores - lax.optimization_barrier(jnp.max(scores, -1, keepdims=True)))
    attention = low(exponent / lax.optimization_barrier(jnp.sum(exponent, -1, keepdims=True)))
    mixed = low(bfloat_backward(jnp.einsum('hqk,khd->qhd', attention, value_rows, precision=HIGHEST))).reshape(amount, D)
    after_attend = embedded + bfloat_backward(bilinear_contract(mixed, output_w))
    second_norm = low(rms_norm(after_attend, gain_rows[3]))
    logits = bfloat_backward(bilinear_contract(second_norm, router_w))
    expert_logits = logits[:, :EXPERTS]
    expert_exp = jnp.exp(expert_logits - lax.optimization_barrier(jnp.max(expert_logits, -1, keepdims=True)))
    probs_all = expert_exp / lax.optimization_barrier(jnp.sum(expert_exp, -1, keepdims=True))
    chosen = (routes[:, :, None] == jnp.arange(EXPERTS)[None, None, :]).astype(jnp.float32)
    gate_values = lax.optimization_barrier(jnp.sum(chosen * probs_all[:, None, :], -1))
    shared_gate = jax.nn.sigmoid(logits[:, EXPERTS:])
    shared_both = bfloat_backward(bilinear_contract(second_norm, shin_w))
    shared_hidden = low(sigmoid_linear(shared_both[:, :FFS]) * shared_both[:, FFS:])
    shared = bfloat_backward(bilinear_contract(shared_hidden, shout_w))
    flat_routes = routes.reshape(-1)
    expert_hot = (flat_routes[:, None] == jnp.arange(EXPERTS)[None, :]).astype(jnp.int32)
    ranked = lax.optimization_barrier(jnp.sum((jnp.cumsum(expert_hot, 0) - expert_hot) * expert_hot, 1)).astype(jnp.int32)
    slot_index = (flat_routes * CAP + ranked).astype(jnp.int32)
    slot_rows = jnp.zeros((EXPERTS * CAP, D), jnp.float32).at[slot_index].set(jnp.repeat(second_norm, 2, 0))
    slot_rows = slot_rows.reshape(EXPERTS, CAP, D)
    expert_both = bfloat_backward(jnp.einsum('ecd,gdef->gecf', slot_rows, exin_w.reshape(2, D, EXPERTS, FF), precision=HIGHEST))
    expert_hidden = low(sigmoid_linear(expert_both[0]) * expert_both[1])
    expert_rows = jnp.einsum('ecf,efd->ecd', expert_hidden, exout_w.reshape(EXPERTS, FF, D), precision=HIGHEST)
    picked = bfloat_backward(expert_rows.reshape(EXPERTS * CAP, D)[slot_index].reshape(amount, 2, D))
    after_mixer = after_attend + shared_gate * shared + lax.optimization_barrier(jnp.sum(gate_values[:, :, None] * picked, 1))
    final_layer_scaling = low(rms_norm(after_mixer, gain_rows[4]))
    predicted_series = bfloat_backward(bilinear_contract(final_layer_scaling, readout_coefficients))
    prediction_residual = predicted_series - observed_future
    absolute_size = jnp.abs(prediction_residual)
    smooth_absolute_cost = jnp.where(absolute_size <= KINK_THRESHOLD, 0.5 * prediction_residual * prediction_residual, KINK_THRESHOLD * (absolute_size - 0.5 * KINK_THRESHOLD)) * valid_mask
    domain_onehot_rows = (domain_of[:, None] == jnp.arange(DOMAINS)[None, :]).astype(jnp.float32)
    domain_sums = lax.optimization_barrier(jnp.sum(domain_onehot_rows * lax.optimization_barrier(jnp.sum(smooth_absolute_cost, -1))[:, None], 0))
    return (jnp.sum(domain_sums * domain_weighting), domain_sums)

def reference(points, experts, lengths, domains, domain_weights, vectors, attend_input, attend_output, router, shared_input, shared_output, horizon, expert_input, expert_output, mean_vectors, mean_attend_input, mean_attend_output, mean_router, mean_shared_input, mean_shared_output, mean_horizon, mean_expert_input, mean_expert_output, square_vectors, square_attend_input, square_attend_output, square_router, square_shared_input, square_shared_output, square_horizon, square_expert_input, square_expert_output):
    masters = [vectors, attend_input, attend_output, router, shared_input, shared_output, horizon, expert_input, expert_output]
    first_moments = [mean_vectors, mean_attend_input, mean_attend_output, mean_router, mean_shared_input, mean_shared_output, mean_horizon, mean_expert_input, mean_expert_output]
    second_moments = [square_vectors, square_attend_input, square_attend_output, square_router, square_shared_input, square_shared_output, square_horizon, square_expert_input, square_expert_output]
    blocks = (points.reshape(-1, TOK_DEV), experts.reshape(-1, TOK_DEV, 2), lengths, domains)

    def count_block(portion):
        return domain_count(portion[0], portion[1])
    counts = lax.optimization_barrier(jnp.sum(lax.map(count_block, (lengths, domains)), 0))
    domain_weighting = domain_weights / jnp.maximum(counts, 1.0)

    def total(weights):

        def accumulate(running, portion):
            loss_value, domain_sums = jax.checkpoint(block_loss)(weights, portion[0], portion[1], portion[2], portion[3], domain_weighting)
            return ((running[0] + loss_value, running[1] + domain_sums), None)
        initial = (jnp.zeros((), jnp.float32), jnp.zeros((DOMAINS,), jnp.float32))
        (loss_value, domain_sums), unused = lax.scan(accumulate, initial, blocks)
        return (loss_value, domain_sums)
    loss_value, pullback, domain_sums = jax.vjp(total, masters, has_aux=True)
    gradients = pullback(jnp.ones((), jnp.float32))[0]
    grad_norm = jnp.sqrt(sum((jnp.sum(gradient * gradient) for gradient in gradients)))
    factor = jnp.minimum(1.0, CLIP / grad_norm)
    results = []
    trust_pairs = []
    for master, gradient, moment_one, moment_two in zip(masters, gradients, first_moments, second_moments):
        clipped = gradient * factor
        moment_new = BETA_ONE * moment_one + (1.0 - BETA_ONE) * clipped
        square_new = BETA_TWO * moment_two + (1.0 - BETA_TWO) * clipped * clipped
        direction = moment_new / (1.0 - BETA_ONE ** STEP) / (jnp.sqrt(square_new / (1.0 - BETA_TWO ** STEP)) + EPS_ADAM) + DECAY * master
        weight_norm = jnp.sqrt(jnp.sum(master * master))
        update_norm = jnp.sqrt(jnp.sum(direction * direction))
        results.append(master - RATE * (weight_norm / update_norm) * direction)
        results.append(moment_new)
        results.append(square_new)
        trust_pairs.append(jnp.stack([weight_norm, update_norm]))
    domain_totals = jnp.stack([domain_sums, counts])
    trust_norms = jnp.stack(trust_pairs)
    return (results[0], results[1], results[2], results[3], results[4], results[5], results[6], results[7], results[8], results[9], results[10], results[11], results[12], results[13], results[14], results[15], results[16], results[17], results[18], results[19], results[20], results[21], results[22], results[23], results[24], results[25], results[26], domain_totals, grad_norm.reshape(1), trust_norms)
```

```python
import jax
import jax.numpy as jnp
import numpy as np
from jax import lax
from jax.sharding import PartitionSpec as P

D = 384
HEADS = 12
HD = 32
FFS = 1536
EXPERTS = 8
DOMAINS = 9
STEP = 10
CAP = 256


HORIZONS = (1, 8, 32, 64)
REACH = 64
KINK_THRESHOLD = 2.0
EPS_NORM = 1e-06
CLIP = 0.01
BETA_ONE = 0.9
BETA_TWO = 0.99
EPS_ADAM = 1e-08
DECAY = 0.01
RATE = 0.3


def ahead_table():
    return np.concatenate([np.arange(horizon_len) for horizon_len in HORIZONS]).astype(np.int32)


def sigmoid_linear(inputs):
    return inputs * jax.nn.sigmoid(inputs)


def gated_unit(gate_in, lift_in):
    return sigmoid_linear(gate_in) * lift_in


def rms_norm(inputs, weight_gain):
    return (
        inputs
        * lax.rsqrt(jnp.mean(inputs * inputs, axis=-1, keepdims=True) + EPS_NORM)
        * weight_gain
    )


def rope_tables(position):
    half_width = HD // 2
    frequency = jnp.exp(-jnp.log(10000.0) * jnp.arange(half_width, dtype=jnp.float32) / half_width)
    angles = position.astype(jnp.float32)[:, None] * frequency[None, :]
    return (jnp.cos(angles)[:, None, :], jnp.sin(angles)[:, None, :])


def rotate(inputs, cosine, sine):
    half_width = inputs.shape[-1] // 2
    first_half = inputs[..., :half_width]
    second_half = inputs[..., half_width:]
    return jnp.concatenate(
        [first_half * cosine - second_half * sine, second_half * cosine + first_half * sine], -1
    )


def layout(samples, series_lengths, series_domains):
    amount = samples.shape[0]
    places = jnp.arange(amount, dtype=jnp.int32)
    finish = jnp.cumsum(series_lengths)
    anchor = finish - series_lengths
    series = jnp.sum((places[:, None] >= finish[None, :]).astype(jnp.int32), 1)
    member = series[:, None] == jnp.arange(series_lengths.shape[0], dtype=jnp.int32)[None, :]
    begin_at = jnp.sum(jnp.where(member, anchor[None, :], 0), 1)
    finish_at = jnp.sum(jnp.where(member, finish[None, :], 0), 1)
    domain_of = jnp.sum(jnp.where(member, series_domains[None, :], 0), 1)
    ahead_steps = jnp.asarray(ahead_table())
    reached = places[:, None] + 1 + ahead_steps[None, :]
    valid_mask = (reached < finish_at[:, None]).astype(jnp.float32)
    padded = jnp.concatenate([samples, jnp.zeros((REACH + 1,), samples.dtype)])
    future = jnp.stack([padded[1 + offset : 1 + offset + amount] for offset in range(REACH)], 1)
    observed_future = future[:, ahead_table()]
    return (series, places - begin_at, domain_of, valid_mask, observed_future)


def flip(value, axis_name, bit):
    count = lax.axis_size(axis_name)
    return lax.ppermute(value, axis_name, [(i, i ^ bit) for i in range(count)])


def bits_of(axis_name):
    count = lax.axis_size(axis_name)
    return [1 << i for i in range(count.bit_length() - 1)]


def sum_small(value, axes):
    for axis_name in axes:
        for bit in bits_of(axis_name):
            value = value + flip(value, axis_name, bit)
    return value


def halves(value, axis, take_high):
    size = value.shape[axis] // 2
    low = lax.slice_in_dim(value, 0, size, axis=axis)
    high = lax.slice_in_dim(value, size, 2 * size, axis=axis)
    return (jnp.where(take_high, high, low), jnp.where(take_high, low, high))


def scatter_sum(value, axis, bits):
    for bit in bits:
        side = (lax.axis_index("dp") & bit) != 0
        keep, give = halves(value, axis, side)
        value = keep + flip(give, "dp", bit)
    return value


def join(value, axis, bits):
    for bit in reversed(bits):
        side = (lax.axis_index("dp") & bit) != 0
        other = flip(value, "dp", bit)
        value = jnp.concatenate(
            [jnp.where(side, other, value), jnp.where(side, value, other)], axis
        )
    return value


def spread(value):
    count = lax.axis_size("expert")
    return lax.all_to_all(
        jnp.broadcast_to(value[None], (count, *value.shape)),
        "expert",
        split_axis=0,
        concat_axis=0,
        tiled=True,
    )


def gather_packed(value):
    core = (lax.axis_index("dp") & 1) != 0
    mine, unused = halves(value, 1, core)
    return join(spread(mine), 2, [1])


def expert_scatter(value):
    return jnp.sum(
        lax.all_to_all(value, "expert", split_axis=0, concat_axis=0, tiled=True), 0
    )


def shards(
    points,
    experts,
    lengths,
    domains,
    domain_weights,
    vectors,
    attend_input,
    attend_output,
    router,
    shared_input,
    shared_output,
    horizon,
    expert_input,
    expert_output,
    mean_vectors,
    mean_attend_input,
    mean_attend_output,
    mean_router,
    mean_shared_input,
    mean_shared_output,
    mean_horizon,
    mean_expert_input,
    mean_expert_output,
    square_vectors,
    square_attend_input,
    square_attend_output,
    square_router,
    square_shared_input,
    square_shared_output,
    square_horizon,
    square_expert_input,
    square_expert_output,
):
    coarse_float_kind = jnp.bfloat16
    fine_float_kind = jnp.float32
    expert_count = lax.axis_size("expert")
    dp_bits = bits_of("dp")
    local_rows = attend_input.shape[0]
    head_columns = horizon.shape[1]
    small = jnp.concatenate([router, horizon, vectors.T], 1).astype(coarse_float_kind)
    small_columns = small.shape[1]
    small = jnp.pad(small, ((0, 0), (0, 128 - small_columns)))
    first_pack = gather_packed(
        jnp.concatenate(
            [
                attend_input.astype(coarse_float_kind),
                small,
                attend_output.astype(coarse_float_kind),
            ],
            1,
        )
    ).reshape(D, -1)
    input_low = first_pack[:, : 3 * D]
    router_low = first_pack[:, 3 * D : 3 * D + EXPERTS + 1]
    readout_bfloat = first_pack[:, 3 * D + EXPERTS + 1 : 3 * D + EXPERTS + 1 + head_columns]
    vec_low = first_pack[:, 3 * D + small_columns - 5 : 3 * D + small_columns].T
    output_low = first_pack[:, 3 * D + 128 :]
    shin_low = gather_packed(shared_input.astype(coarse_float_kind)).reshape(D, -1)
    shout_low = gather_packed(shared_output.astype(coarse_float_kind)).reshape(FFS, D)
    gain_rows = vec_low.astype(fine_float_kind)
    amount = points.shape[0]
    series, position, domain_of, valid_mask, observed_future = layout(
        points, lengths[0], domains[0]
    )
    cosine, sine = rope_tables(position)

    def front(gain_gate, gain_value, gain_norm):
        embedded = sigmoid_linear(points[:, None] * gain_gate) * (points[:, None] * gain_value)
        return (embedded, rms_norm(embedded, gain_norm))

    (embedded, first_norm), front_back = jax.vjp(front, gain_rows[0], gain_rows[1], gain_rows[2])
    first_low = first_norm.astype(coarse_float_kind)
    projected = jnp.dot(first_low, input_low, preferred_element_type=fine_float_kind)

    def turn(flat_rows):
        pieces = flat_rows.reshape(amount, 3, HEADS, HD)
        return (
            rotate(pieces[:, 0], cosine, sine),
            rotate(pieces[:, 1], cosine, sine),
            pieces[:, 2],
        )

    (queries, key_rows, value_rows), turn_back = jax.vjp(turn, projected)
    queries = queries.astype(coarse_float_kind)
    key_rows = key_rows.astype(coarse_float_kind)
    value_rows = value_rows.astype(coarse_float_kind)
    places = jnp.arange(amount)
    allowed = ((series[:, None] == series[None, :]) & (places[None, :] <= places[:, None]))[None]

    def score_block():
        raw_scores = jnp.einsum(
            "qhd,khd->hqk", queries, key_rows, preferred_element_type=fine_float_kind
        ) * HD ** (-0.5)
        return jnp.where(allowed, raw_scores, -1e30)

    scores = score_block()
    row_top = jnp.max(scores, -1, keepdims=True)
    exponent = jnp.exp(scores - row_top)
    row_total = jnp.sum(exponent, -1, keepdims=True)
    log_total = row_top + jnp.log(row_total)
    attention = (exponent / row_total).astype(coarse_float_kind)
    mixed = (
        jnp.einsum("hqk,khd->qhd", attention, value_rows, preferred_element_type=fine_float_kind)
        .reshape(amount, D)
        .astype(coarse_float_kind)
    )
    after_attend = embedded + jnp.dot(mixed, output_low, preferred_element_type=fine_float_kind)
    second_norm, second_back = jax.vjp(rms_norm, after_attend, gain_rows[3])
    second_low = second_norm.astype(coarse_float_kind)
    logits = jnp.dot(second_low, router_low, preferred_element_type=fine_float_kind)
    chosen = (experts[:, :, None] == jnp.arange(EXPERTS)[None, None, :]).astype(fine_float_kind)

    def gating(logit_rows):
        expert_logits = logit_rows[:, :EXPERTS]
        expert_exp = jnp.exp(expert_logits - jnp.max(expert_logits, -1, keepdims=True))
        probs_all = expert_exp / jnp.sum(expert_exp, -1, keepdims=True)
        return (
            jnp.sum(chosen * probs_all[:, None, :], -1),
            jax.nn.sigmoid(logit_rows[:, EXPERTS:]),
        )

    (gate_values, shared_gate), gating_back = jax.vjp(gating, logits)
    shared_both = jnp.dot(second_low, shin_low, preferred_element_type=fine_float_kind)
    shared_hidden, shared_back = jax.vjp(gated_unit, shared_both[:, :FFS], shared_both[:, FFS:])
    shared_low = shared_hidden.astype(coarse_float_kind)
    shared = jnp.dot(shared_low, shout_low, preferred_element_type=fine_float_kind)
    expert_devices = lax.axis_size("expert")
    group_size = expert_devices // EXPERTS
    flat_routes = experts.reshape(-1)
    expert_hot = (flat_routes[:, None] == jnp.arange(EXPERTS)[None, :]).astype(jnp.int32)
    ranked = jnp.sum((jnp.cumsum(expert_hot, 0) - expert_hot) * expert_hot, 1)
    slot_index = flat_routes * CAP + ranked

    slots = jnp.arange(EXPERTS * CAP)
    slot_pairs = slot_index.reshape(amount, 2)
    slot_hot = [
        (slots[:, None] == slot_pairs[None, :, k]).astype(coarse_float_kind) for k in range(2)
    ]

    def to_slots(first_rows, second_rows):
        if second_rows is None:
            buffer = jnp.dot(
                slot_hot[0] + slot_hot[1], first_rows, preferred_element_type=fine_float_kind
            )
        else:
            buffer = jnp.dot(
                slot_hot[0], first_rows, preferred_element_type=fine_float_kind
            ) + jnp.dot(slot_hot[1], second_rows, preferred_element_type=fine_float_kind)
        buffer = buffer.astype(coarse_float_kind).reshape(EXPERTS, CAP, -1)
        return jnp.repeat(buffer, group_size, 0)

    def bring_back(returned):
        summed = jnp.sum(returned.reshape(EXPERTS, group_size, CAP, returned.shape[-1]), 1)
        return summed.reshape(EXPERTS * CAP, -1)[slot_index].reshape(amount, 2, -1)

    gate_up_low = expert_input.astype(coarse_float_kind)
    down_low = expert_output.astype(coarse_float_kind)
    arrived = lax.all_to_all(
        to_slots(second_low, None), "expert", split_axis=0, concat_axis=0, tiled=True
    ).reshape(-1, D)
    expert_gate = jnp.dot(arrived, gate_up_low[0], preferred_element_type=fine_float_kind)
    expert_lift = jnp.dot(arrived, gate_up_low[1], preferred_element_type=fine_float_kind)
    expert_hidden = gated_unit(expert_gate, expert_lift).astype(coarse_float_kind)
    expert_rows = jnp.dot(expert_hidden, down_low, preferred_element_type=fine_float_kind)
    picked = bring_back(
        lax.all_to_all(
            expert_rows.reshape(expert_devices, -1, D),
            "expert",
            split_axis=0,
            concat_axis=0,
            tiled=True,
        )
    )
    after_mixer = after_attend + shared_gate * shared + jnp.sum(gate_values[:, :, None] * picked, 1)
    final_layer_scaling, third_back = jax.vjp(rms_norm, after_mixer, gain_rows[4])
    final_layer_bfloat = final_layer_scaling.astype(coarse_float_kind)
    predicted_series = jnp.dot(
        final_layer_bfloat, readout_bfloat, preferred_element_type=fine_float_kind
    )
    domain_onehot_rows = (domain_of[:, None] == jnp.arange(DOMAINS)[None, :]).astype(
        fine_float_kind
    )

    def smooth_absolute_sample_costs(prediction_source):
        prediction_residual = prediction_source - observed_future
        absolute_size = jnp.abs(prediction_residual)
        return jnp.sum(
            jnp.where(
                absolute_size <= KINK_THRESHOLD,
                0.5 * prediction_residual * prediction_residual,
                KINK_THRESHOLD * (absolute_size - 0.5 * KINK_THRESHOLD),
            )
            * valid_mask,
            -1,
        )

    sample_penalty, smooth_absolute_backward = jax.vjp(
        smooth_absolute_sample_costs, predicted_series
    )
    local_counts = jnp.sum(domain_onehot_rows * jnp.sum(valid_mask, -1)[:, None], 0)
    local_sums = jnp.sum(domain_onehot_rows * sample_penalty[:, None], 0)
    counts = sum_small(local_counts, ("dp", "expert"))
    domain_sums = sum_small(local_sums, ("dp", "expert"))
    domain_weighting = domain_weights / jnp.maximum(counts, 1.0)
    (prediction_slope,) = smooth_absolute_backward(
        jnp.sum(domain_onehot_rows * domain_weighting[None, :], 1)
    )
    prediction_bfloat = prediction_slope.astype(coarse_float_kind)
    head_gradient = jnp.dot(
        final_layer_bfloat.T, prediction_bfloat, preferred_element_type=fine_float_kind
    )
    grad_mixer, grad_gain_three = third_back(
        jnp.dot(prediction_bfloat, readout_bfloat.T, preferred_element_type=fine_float_kind)
    )
    grad_shared_low = (shared_gate * grad_mixer).astype(coarse_float_kind)
    grad_shared_gate = jnp.sum(grad_mixer * shared, -1, keepdims=True)
    grad_gates = jnp.sum(grad_mixer[:, None, :] * picked, -1)
    grad_picked = (gate_values[:, :, None] * grad_mixer[:, None, :]).astype(coarse_float_kind)
    received = lax.all_to_all(
        to_slots(grad_picked[:, 0], grad_picked[:, 1]), "expert", split_axis=0, concat_axis=0, tiled=True
    ).reshape(-1, D)
    grad_hidden = jnp.dot(received, down_low.T, preferred_element_type=fine_float_kind)
    grad_expert_out = jnp.dot(expert_hidden.T, received, preferred_element_type=fine_float_kind)
    gate_again, lift_again = (expert_gate, expert_lift)
    unused_hidden, expert_back = jax.vjp(gated_unit, gate_again, lift_again)
    grad_gate, grad_lift = expert_back(grad_hidden)
    grad_gate = grad_gate.astype(coarse_float_kind)
    grad_lift = grad_lift.astype(coarse_float_kind)
    grad_expert_in = jnp.stack(
        [
            jnp.dot(arrived.T, grad_gate, preferred_element_type=fine_float_kind),
            jnp.dot(arrived.T, grad_lift, preferred_element_type=fine_float_kind),
        ]
    )
    grad_rows = jnp.dot(
        grad_gate, gate_up_low[0].T, preferred_element_type=fine_float_kind
    ) + jnp.dot(grad_lift, gate_up_low[1].T, preferred_element_type=fine_float_kind)
    routed_back = lax.all_to_all(
        grad_rows.reshape(expert_devices, -1, D).astype(jnp.bfloat16),
        "expert",
        split_axis=0,
        concat_axis=0,
        tiled=True,
    )
    if group_size > 1:
        routed_back = jnp.sum(
            routed_back.reshape(EXPERTS, group_size, CAP, D).astype(fine_float_kind), 1
        )
        grad_second = jnp.dot(
            (slot_hot[0] + slot_hot[1]).T.astype(fine_float_kind),
            routed_back.reshape(-1, D),
            precision=lax.Precision.HIGHEST,
        )
    else:
        grad_second = jnp.dot(
            (slot_hot[0] + slot_hot[1]).T,
            routed_back.reshape(-1, D),
            preferred_element_type=fine_float_kind,
        )
    grad_shared_hidden = jnp.dot(
        grad_shared_low, shout_low.T, preferred_element_type=fine_float_kind
    )
    grad_shout = jnp.dot(shared_low.T, grad_shared_low, preferred_element_type=fine_float_kind)
    grad_shared_gatein, grad_shared_lift = shared_back(grad_shared_hidden)
    grad_shared_both = jnp.concatenate([grad_shared_gatein, grad_shared_lift], 1).astype(
        coarse_float_kind
    )
    grad_shin = jnp.dot(second_low.T, grad_shared_both, preferred_element_type=fine_float_kind)
    grad_second = grad_second + jnp.dot(
        grad_shared_both, shin_low.T, preferred_element_type=fine_float_kind
    )
    (grad_logits,) = gating_back((grad_gates, grad_shared_gate))
    grad_logits = grad_logits.astype(coarse_float_kind)
    grad_router = jnp.dot(second_low.T, grad_logits, preferred_element_type=fine_float_kind)
    grad_second = grad_second + jnp.dot(
        grad_logits, router_low.T, preferred_element_type=fine_float_kind
    )
    grad_attend_norm, grad_gain_two = second_back(grad_second)
    grad_attend = grad_mixer + grad_attend_norm
    grad_attend_low = grad_attend.astype(coarse_float_kind)
    grad_output = jnp.dot(mixed.T, grad_attend_low, preferred_element_type=fine_float_kind)
    grad_mixed = (
        jnp.dot(grad_attend_low, output_low.T, preferred_element_type=fine_float_kind)
        .astype(coarse_float_kind)
        .reshape(amount, HEADS, HD)
    )
    attention_again = jnp.exp(score_block() - log_total)
    grad_values = jnp.einsum(
        "hqk,qhd->khd",
        attention_again.astype(coarse_float_kind),
        grad_mixed,
        preferred_element_type=fine_float_kind,
    )
    grad_probs = jnp.einsum(
        "qhd,khd->hqk", grad_mixed, value_rows, preferred_element_type=fine_float_kind
    )
    grad_scores = (
        attention_again * (grad_probs - jnp.sum(grad_probs * attention_again, -1, keepdims=True))
    ).astype(coarse_float_kind)
    grad_queries = jnp.einsum(
        "hqk,khd->qhd", grad_scores, key_rows, preferred_element_type=fine_float_kind
    ) * HD ** (-0.5)
    grad_keys = jnp.einsum(
        "hqk,qhd->khd", grad_scores, queries, preferred_element_type=fine_float_kind
    ) * HD ** (-0.5)
    (grad_projected,) = turn_back((grad_queries, grad_keys, grad_values))
    grad_projected = grad_projected.astype(coarse_float_kind)
    grad_input = jnp.dot(first_low.T, grad_projected, preferred_element_type=fine_float_kind)
    grad_first = jnp.dot(grad_projected, input_low.T, preferred_element_type=fine_float_kind)
    grad_gain_gate, grad_gain_value, grad_gain_one = front_back((grad_attend, grad_first))
    grad_vectors = jnp.stack(
        [grad_gain_gate, grad_gain_value, grad_gain_one, grad_gain_two, grad_gain_three]
    )
    parts = scatter_sum(grad_expert_in.reshape(-1, grad_expert_in.shape[-1]), 0, dp_bits)
    expert_in_total = join(parts, 0, dp_bits).reshape(grad_expert_in.shape)
    expert_out_total = join(scatter_sum(grad_expert_out, 0, dp_bits), 0, dp_bits)
    shin_total = join(
        expert_scatter(scatter_sum(grad_shin.reshape(expert_count, local_rows, -1), 2, dp_bits)),
        1,
        dp_bits,
    )
    shout_total = join(
        expert_scatter(scatter_sum(grad_shout.reshape(expert_count, -1, D), 1, dp_bits)),
        0,
        dp_bits,
    )
    small_gradient = jnp.concatenate([grad_router, head_gradient, grad_vectors.T], 1)
    small_gradient = jnp.pad(small_gradient, ((0, 0), (0, 128 - small_columns)))
    last_pack = jnp.concatenate([grad_input, small_gradient, grad_output], 1)
    last_part = expert_scatter(
        scatter_sum(last_pack.reshape(expert_count, local_rows, -1), 2, [1])
    )
    for bit in dp_bits[1:]:
        last_part = last_part + flip(last_part, "dp", bit)
    last_total = join(last_part, 1, [1])
    edge = 3 * D + EXPERTS + 1
    gradients = (
        last_total[:, edge + head_columns : edge + head_columns + 5].T,
        last_total[:, : 3 * D],
        last_total[:, 3 * D + 128 :],
        last_total[:, 3 * D : edge],
        shin_total,
        shout_total,
        last_total[:, edge : edge + head_columns],
        expert_in_total,
        expert_out_total,
    )
    masters = (
        vectors,
        attend_input,
        attend_output,
        router,
        shared_input,
        shared_output,
        horizon,
        expert_input,
        expert_output,
    )
    first_moments = (
        mean_vectors,
        mean_attend_input,
        mean_attend_output,
        mean_router,
        mean_shared_input,
        mean_shared_output,
        mean_horizon,
        mean_expert_input,
        mean_expert_output,
    )
    second_moments = (
        square_vectors,
        square_attend_input,
        square_attend_output,
        square_router,
        square_shared_input,
        square_shared_output,
        square_horizon,
        square_expert_input,
        square_expert_output,
    )
    local_square = jnp.sum(jnp.stack([jnp.sum(gradient * gradient) for gradient in gradients]))
    grad_norm = jnp.sqrt(sum_small(local_square.reshape(1), ("expert",))[0])
    factor = jnp.minimum(1.0, CLIP / grad_norm)
    moments_new = []
    directions = []
    for master, gradient, moment_one, moment_two in zip(
        masters, gradients, first_moments, second_moments
    ):
        clipped = gradient * factor
        moment_new = BETA_ONE * moment_one + (1.0 - BETA_ONE) * clipped
        square_new = BETA_TWO * moment_two + (1.0 - BETA_TWO) * clipped * clipped
        directions.append(
            moment_new
            / (1.0 - BETA_ONE**STEP)
            / (jnp.sqrt(square_new / (1.0 - BETA_TWO**STEP)) + EPS_ADAM)
            + DECAY * master
        )
        moments_new.append((moment_new, square_new))
    weight_square = jnp.stack([jnp.sum(master * master) for master in masters])
    update_square = jnp.stack([jnp.sum(direction * direction) for direction in directions])
    weight_square = sum_small(weight_square, ("expert",))
    update_square = sum_small(update_square, ("expert",))
    weight_norm = jnp.sqrt(weight_square)
    update_norm = jnp.sqrt(update_square)
    results = []
    for position_index in range(9):
        ratio = weight_norm[position_index] / update_norm[position_index]
        results.append(masters[position_index] - RATE * ratio * directions[position_index])
        results.append(moments_new[position_index][0])
        results.append(moments_new[position_index][1])
    results.append(jnp.stack([domain_sums, counts]))
    results.append(grad_norm.reshape(1))
    results.append(jnp.stack([weight_norm, update_norm], 1))
    return tuple(results)


def solution(mesh):
    placed = (
        P(("dp", "expert")),
        P(("dp", "expert"), None),
        P(("dp", "expert"), None),
        P(("dp", "expert"), None),
        P(),
        P(None, "expert"),
        P("expert", None),
        P("expert", None),
        P("expert", None),
        P("expert", None),
        P("expert", None),
        P("expert", None),
        P(None, None, "expert"),
        P("expert", None),
        P(None, "expert"),
        P("expert", None),
        P("expert", None),
        P("expert", None),
        P("expert", None),
        P("expert", None),
        P("expert", None),
        P(None, None, "expert"),
        P("expert", None),
        P(None, "expert"),
        P("expert", None),
        P("expert", None),
        P("expert", None),
        P("expert", None),
        P("expert", None),
        P("expert", None),
        P(None, None, "expert"),
        P("expert", None),
    )
    return jax.shard_map(
        shards,
        mesh=mesh,
        in_specs=placed,
        out_specs=(
            P(None, "expert"),
            P(None, "expert"),
            P(None, "expert"),
            P("expert", None),
            P("expert", None),
            P("expert", None),
            P("expert", None),
            P("expert", None),
            P("expert", None),
            P("expert", None),
            P("expert", None),
            P("expert", None),
            P("expert", None),
            P("expert", None),
            P("expert", None),
            P("expert", None),
            P("expert", None),
            P("expert", None),
            P("expert", None),
            P("expert", None),
            P("expert", None),
            P(None, None, "expert"),
            P(None, None, "expert"),
            P(None, None, "expert"),
            P("expert", None),
            P("expert", None),
            P("expert", None),
            P(),
            P(),
            P(),
        ),
        check_vma=False,
    )
```

```python
import functools

import jax
import jax.numpy as jnp
import numpy as np
from jax import lax
from jax.experimental import pallas as pl
from jax.experimental.pallas import tpu as pltpu
from jax.sharding import PartitionSpec as P

D = 384
HEADS = 12
HD = 32
FFS = 1536
EXPERTS = 8
DOMAINS = 9
STEP = 10
CAP = 256


HORIZONS = (1, 8, 32, 64)
REACH = 64
KINK_THRESHOLD = 2.0
EPS_NORM = 1e-06
CLIP = 0.01
BETA_ONE = 0.9
BETA_TWO = 0.99
EPS_ADAM = 1e-08
DECAY = 0.01
RATE = 0.3


def ahead_table():
    return np.concatenate([np.arange(horizon_len) for horizon_len in HORIZONS]).astype(np.int32)


def target_columns(samples):
    amount = samples.shape[0]
    padded = jnp.concatenate([samples, jnp.zeros((REACH + 1,), samples.dtype)])
    future = jnp.stack([padded[1 + offset : 1 + offset + amount] for offset in range(REACH)], 1)
    return future[:, ahead_table()]


ROW_BLOCK = 256
SMALL = 128
HORIZON_AT = EXPERTS + 1
VECTORS_AT = 120
SMALL_AT = 4 * D
COUNTS_AT = 125
CODE_ROWS = 16
VMEM = 56 * 1024 * 1024
F32 = jnp.float32
BF16 = jnp.bfloat16


def mm(left, right):
    return jnp.dot(left, right, preferred_element_type=F32)


def mm_nt(left, right):
    return lax.dot_general(left, right, (((1,), (1,)), ((), ())), preferred_element_type=F32)


def mm_tn(left, right):
    return lax.dot_general(left, right, (((0,), (0,)), ((), ())), preferred_element_type=F32)


def inverse_rms(rows):
    return lax.rsqrt(jnp.mean(rows * rows, axis=-1, keepdims=True) + EPS_NORM)


def rms_back(rows, inverse, gain, slope):
    gain_slope = jnp.sum(slope * rows * inverse, 0, keepdims=True)
    scaled = slope * gain
    return (
        inverse * scaled
        - rows * (inverse * inverse * inverse) * jnp.mean(rows * scaled, -1, keepdims=True),
        gain_slope,
    )


def lanes_of(shape):
    return lax.broadcasted_iota(jnp.int32, shape, len(shape) - 1)


def half_swap(rows):
    half_width = HD // 2
    lane = lanes_of(rows.shape)
    return jnp.where(
        lane % HD < half_width,
        pltpu.roll(rows, rows.shape[1] - half_width, 1),
        pltpu.roll(rows, half_width, 1),
    )


SLOT, SERIES_OF, FINISH, DOMAIN, CHOICE, VALUE, PLACE = 0, 2, 3, 4, 5, 7, 8


def tables_kernel(
    lengths, domains, frequency, points_row, experts_row, cosine, sine, columns_out, rows_out
):
    amount = points_row.shape[1]
    place = lax.broadcasted_iota(jnp.int32, (1, amount), 1)
    series = jnp.zeros((1, amount), jnp.int32)
    begin = jnp.zeros((1, amount), jnp.int32)
    finish = jnp.zeros((1, amount), jnp.int32)
    domain = jnp.zeros((1, amount), jnp.int32)
    start = jnp.int32(0)
    for index in range(lengths.shape[1]):
        stop = start + lengths[0, index]
        inside = (place >= start) & (place < stop)
        series = jnp.where(inside, index, series)
        begin = jnp.where(inside, start, begin)
        finish = jnp.where(inside, stop, finish)
        domain = jnp.where(inside, domains[0, index], domain)
        start = stop
    name = lax.broadcasted_iota(jnp.int32, (16, amount), 0)
    choices = [experts_row[k : k + 1, :] for k in range(2)]
    named = [(name == choice).astype(F32) for choice in choices]
    earlier = (
        lax.broadcasted_iota(jnp.int32, (amount, amount), 0)
        < lax.broadcasted_iota(jnp.int32, (amount, amount), 1)
    )
    before = mm((named[0] + named[1]).astype(BF16), earlier.astype(F32).astype(BF16))
    entries = []
    for k in range(2):
        rank = jnp.sum(named[k] * before, 0, keepdims=True)
        entries.append(choices[k].astype(F32) * CAP + rank)
    entries += [series, finish, domain, *choices, points_row[...], place - begin]
    row = lax.broadcasted_iota(jnp.int32, (128, amount), 0)
    table = jnp.zeros((128, amount), F32)
    for index, entry in enumerate(entries):
        table = jnp.where(row == index, entry.astype(F32), table)
    rows_out[...] = table[:8]
    columns = table.T
    columns_out[...] = columns
    angles = columns[:, PLACE : PLACE + 1] * frequency[...]
    cosine[...] = jnp.cos(angles)
    turned = jnp.sin(angles)
    sine[...] = jnp.where(lanes_of((amount, 128)) % HD < HD // 2, -turned, turned)


def allowed_block(table, rows_table, start, rows, keys):
    query = start + lax.broadcasted_iota(jnp.int32, (rows, keys), 0)
    key = lax.broadcasted_iota(jnp.int32, (rows, keys), 1)
    series_col = table[start : start + rows, SERIES_OF : SERIES_OF + 1]
    return (series_col == rows_table[SERIES_OF : SERIES_OF + 1, :keys]) & (key <= query)


def slot_rows_hot(slot_row, expert):
    slot = expert * CAP + lax.broadcasted_iota(jnp.int32, (CAP, slot_row.shape[1]), 0)
    return (slot_row.astype(jnp.int32) == slot).astype(F32).astype(BF16)


def slot_cols_hot(slot_col, expert):
    slot = expert * CAP + lax.broadcasted_iota(jnp.int32, (slot_col.shape[0], CAP), 1)
    return (slot_col.astype(jnp.int32) == slot).astype(F32).astype(BF16)


def pack_kernel(small_end, core, lengths, domains, ahead, input_w, output_w, router, horizon, vectors, out):
    rows = input_w.shape[0]

    def placed(count, at):
        row = lax.broadcasted_iota(jnp.int32, (count, SMALL), 0)
        return (row + at == lanes_of((count, SMALL))).astype(F32).astype(BF16)

    small = (
        mm_tn(router[...].astype(BF16), placed(HORIZON_AT, 0))
        + mm(horizon[...].astype(BF16), placed(small_end - HORIZON_AT, HORIZON_AT))
        + mm_tn(vectors[...].astype(BF16), placed(vectors.shape[0], VECTORS_AT))
    )
    row = lax.broadcasted_iota(jnp.int32, (rows, SMALL), 0)
    lane = lanes_of((rows, SMALL))
    counts = jnp.zeros((rows, SMALL), F32)
    for series in range(lengths.shape[1]):
        left = jnp.maximum(lengths[0, series] - 1 - ahead[...], 0).astype(F32)
        entries = jnp.sum(left, -1, keepdims=True)
        counts = counts + jnp.where(row == domains[0, series], entries, 0.0)
    high = jnp.floor(counts * (1.0 / 256.0))
    small = jnp.where(lane == COUNTS_AT, high, small)
    small = jnp.where(lane == COUNTS_AT + 1, counts - 256.0 * high, small)
    flat = jnp.concatenate([input_w[...], output_w[...]], 1)
    half = 2 * D
    mine = jnp.where(core[0] == 0, flat[:, :half], flat[:, half:]).astype(BF16)
    for target in range(out.shape[0]):
        out[target, :, :half] = mine
        out[target, :, half:] = small.astype(BF16)


def front_kernel(
    local_rows, core, mine, other, cosine, sine, known, slot_row,
    embedded_out, first_out, qkv_out, log_out, mixed_out, after_out, second_out, logits_out,
    slots_out, gains_out, pack, counts_out,
):
    amount = known.shape[0]
    half = 2 * D
    low = core[0] == 0
    pack[:, :half] = jnp.where(low, mine[:, :half], other[:, :half])
    pack[:, half:SMALL_AT] = jnp.where(low, other[:, :half], mine[:, :half])
    pack[:, SMALL_AT:] = mine[:, half:]
    table = mine[:, half:].astype(F32).T
    gains = table[VECTORS_AT : VECTORS_AT + 8]
    gains_out[...] = gains
    other_table = other[:, half:].astype(F32).T
    row = lax.broadcasted_iota(jnp.int32, (D, SMALL), 0)
    fold = (row % local_rows == lanes_of((D, SMALL))).astype(F32).astype(BF16)
    digits = mm(table[VECTORS_AT : VECTORS_AT + 8].astype(BF16), fold) + mm(
        other_table[VECTORS_AT : VECTORS_AT + 8].astype(BF16), fold
    )
    at = COUNTS_AT - VECTORS_AT
    counts_out[...] = digits[at : at + 1] * 256.0 + digits[at + 1 : at + 2]
    value = known[:, VALUE : VALUE + 1]
    gate = value * gains[0:1]
    embedded = gate * jax.nn.sigmoid(gate) * (value * gains[1:2])
    embedded_out[...] = embedded
    first = (embedded * inverse_rms(embedded) * gains[2:3]).astype(BF16)
    first_out[...] = first
    projected = mm(first, pack[:, : 3 * D])
    cos_rows, sin_rows = cosine[...], sine[...]
    for block in range(6):
        part = projected[:, block * 128 : (block + 1) * 128]
        part = part * cos_rows + half_swap(part) * sin_rows
        qkv_out[:, block * 128 : (block + 1) * 128] = part.astype(BF16)
    qkv_out[:, 2 * D :] = projected[:, 2 * D :].astype(BF16)
    lane = lanes_of((ROW_BLOCK, 128))
    for start in range(0, amount, ROW_BLOCK):
        keys = start + ROW_BLOCK
        allowed = allowed_block(known[...], slot_row[...], start, ROW_BLOCK, keys)
        log_rows = jnp.zeros((ROW_BLOCK, 128), F32)
        for group in range(D // 128):
            query = qkv_out[start : start + ROW_BLOCK, group * 128 : (group + 1) * 128]
            key = qkv_out[:keys, D + group * 128 : D + (group + 1) * 128]
            held = qkv_out[:keys, 2 * D + group * 128 : 2 * D + (group + 1) * 128]
            gathered = jnp.zeros((ROW_BLOCK, 128), F32)
            for head in range(128 // HD):
                own = lane // HD == head
                raw = mm_nt(jnp.where(own, query, jnp.zeros_like(query)), key) * HD ** (-0.5)
                raw = jnp.where(allowed, raw, -1e30)
                top = jnp.max(raw, -1, keepdims=True)
                exponent = jnp.exp(raw - top)
                total = jnp.sum(exponent, -1, keepdims=True)
                attention = (exponent * (1.0 / total)).astype(BF16)
                gathered = jnp.where(own, mm(attention, held), gathered)
                log_rows = jnp.where(
                    lane == group * (128 // HD) + head, top + jnp.log(total), log_rows
                )
            mixed_out[start : start + ROW_BLOCK, group * 128 : (group + 1) * 128] = (
                gathered.astype(BF16)
            )
        log_out[start : start + ROW_BLOCK, :] = log_rows
    after = embedded + mm(mixed_out[...], pack[:, 3 * D : 4 * D])
    after_out[...] = after
    second = (after * inverse_rms(after) * gains[3:4]).astype(BF16)
    second_out[...] = second
    logits_out[...] = mm(second, pack[:, SMALL_AT:])
    for expert in range(EXPERTS):
        hot = slot_rows_hot(slot_row[0:1, :], expert) + slot_rows_hot(slot_row[1:2, :], expert)
        slots_out[expert * CAP : (expert + 1) * CAP, :] = mm(hot, second).astype(BF16)


def shared_kernel(second, gate_w, lift_w, down_w, shared_out):
    gate = mm(second[...], gate_w[...])
    lift = mm(second[...], lift_w[...])
    hidden = (gate * jax.nn.sigmoid(gate) * lift).astype(BF16)
    part = mm(hidden, down_w[...])

    @pl.when(pl.program_id(0) == 0)
    def _():
        shared_out[...] = part

    @pl.when(pl.program_id(0) != 0)
    def _():
        shared_out[...] += part


def expert_kernel(rows, gate_up, down, rows_out):
    gate = mm(rows[...], gate_up[0])
    lift = mm(rows[...], gate_up[1])
    hidden = (gate * jax.nn.sigmoid(gate) * lift).astype(BF16)
    result = mm(hidden, down[...])
    if len(rows_out.shape) == 2:
        rows_out[...] = result
        return
    for source in range(rows_out.shape[0]):
        part = result[source * CAP : (source + 1) * CAP]
        top = jnp.max(jnp.abs(part), -1, keepdims=True)
        power = jnp.ceil(jnp.log2(jnp.maximum(top, 1e-30)))
        code = jnp.clip(jnp.round(part * jnp.exp2(15.0 - power)), -32767.0, 32767.0)
        rows_out[source, :CAP, :] = code.astype(jnp.int32).astype(jnp.int16)
        row = lax.broadcasted_iota(jnp.int32, (CAP, CAP), 0)
        column = lax.broadcasted_iota(jnp.int32, (CAP, CAP), 1)
        powers = jnp.sum(jnp.where(row == column, power, 0.0), 0, keepdims=True)
        powers = jnp.concatenate([powers, jnp.zeros((1, D - CAP), F32)], 1)
        rows_out[source, CAP:, :] = (
            jnp.broadcast_to(powers, (CODE_ROWS, D)).astype(jnp.int32).astype(jnp.int16)
        )


def unit_back(rows, slope, gate_w, lift_w, down_w):
    gate = mm(rows, gate_w)
    lift = mm(rows, lift_w)
    bent = jax.nn.sigmoid(gate)
    smooth = gate * bent
    hidden = (smooth * lift).astype(BF16)
    hidden_slope = mm_nt(slope, down_w)
    gate_slope = (hidden_slope * lift * (bent * (1.0 + gate * (1.0 - bent)))).astype(BF16)
    lift_slope = (hidden_slope * smooth).astype(BF16)
    return hidden, gate_slope, lift_slope


def expert_back_kernel(rows, slope, gate_up, down, rows_out, in_out, out_out):
    hidden, gate_slope, lift_slope = unit_back(
        rows[...], slope[...], gate_up[0], gate_up[1], down[...]
    )
    rows_out[...] = (mm_nt(gate_slope, gate_up[0]) + mm_nt(lift_slope, gate_up[1])).astype(BF16)

    @pl.when(pl.program_id(0) == 0)
    def _():
        in_out[...] = jnp.zeros_like(in_out)
        out_out[...] = jnp.zeros_like(out_out)

    in_out[0] += mm_tn(rows[...], gate_slope)
    in_out[1] += mm_tn(rows[...], lift_slope)
    out_out[...] += mm_tn(hidden, slope[...])


def shared_back_kernel(second, slope, gate_w, lift_w, down_w, second_out, in_out, out_out):
    hidden, gate_slope, lift_slope = unit_back(
        second[...], slope[...], gate_w[...], lift_w[...], down_w[...]
    )
    part = mm_nt(gate_slope, gate_w[...]) + mm_nt(lift_slope, lift_w[...])

    @pl.when(pl.program_id(0) == 0)
    def _():
        second_out[...] = part

    @pl.when(pl.program_id(0) != 0)
    def _():
        second_out[...] += part

    in_out[0] = mm_tn(second[...], gate_slope)
    in_out[1] = mm_tn(second[...], lift_slope)
    out_out[...] = mm_tn(hidden, slope[...])


def expert_back_split_kernel(
    core, rows, slope, gate_up, down, rows_out, in_keep, in_give, out_keep, out_give
):
    hidden, gate_slope, lift_slope = unit_back(
        rows[...], slope[...], gate_up[0], gate_up[1], down[...]
    )
    rows_out[...] = (mm_nt(gate_slope, gate_up[0]) + mm_nt(lift_slope, gate_up[1])).astype(BF16)

    @pl.when(pl.program_id(0) == 0)
    def _():
        for ref in (in_keep, in_give, out_keep, out_give):
            ref[...] = jnp.zeros_like(ref)

    half = hidden.shape[1] // 2
    low = core[0] == 0
    gate = mm_tn(rows[...], gate_slope)
    lift = mm_tn(rows[...], lift_slope)
    in_keep[...] += jnp.where(low, gate, lift)
    in_give[...] += jnp.where(low, lift, gate)
    first = mm_tn(hidden[:, :half], slope[...])
    last = mm_tn(hidden[:, half:], slope[...])
    out_keep[...] += jnp.where(low, first, last)
    out_give[...] += jnp.where(low, last, first)


def shared_back_split_kernel(
    sides, second, slope, gate_w, lift_w, down_w,
    second_out, in_keep, in_give, out_keep, out_give, out_ref,
):
    hidden, gate_slope, lift_slope = unit_back(
        second[...], slope[...], gate_w[...], lift_w[...], down_w[...]
    )
    part = mm_nt(gate_slope, gate_w[...]) + mm_nt(lift_slope, lift_w[...])

    @pl.when(pl.program_id(0) == 0)
    def _():
        second_out[...] = part

    @pl.when(pl.program_id(0) != 0)
    def _():
        second_out[...] += part

    core, cross = sides[0], sides[1]
    low = core == 0
    gate = mm_tn(second[...], gate_slope)
    lift = mm_tn(second[...], lift_slope)
    in_keep[0] = jnp.where(low, gate, lift)
    in_give[0] = jnp.where(low, lift, gate)
    out_ref[...] = mm_tn(hidden, slope[...])
    quarter = out_keep.shape[1] // 2
    for shard in range(2):
        for side in range(2):
            for ref, half in ((out_keep, core), (out_give, 1 - core)):
                piece = half * 2 + jnp.bitwise_xor(cross, side)
                start = pl.multiple_of(shard * 4 * quarter + piece * quarter, 8)
                ref[side, shard * quarter : (shard + 1) * quarter, :] = out_ref[
                    pl.ds(start, quarter), :
                ]


def fold_kernel(in_keep, in_other, out_keep, out_other, keep, give):
    wide = in_keep.shape[2]
    for side, ref in enumerate((keep, give)):
        ref[:, :wide] = in_keep[side] + in_other[side]
        ref[:, wide:] = out_keep[side] + out_other[side]


def middle_kernel(
    returned, known, slot_row, after, shared, logits, small, gains, target, ahead, weighting,
    mixer_out, shared_slope_out, slots_out, logits_slope_out, small_out, gain_out, sums_out,
):
    amount = after.shape[0]
    lane = lanes_of((amount, SMALL))
    table = known[...]
    integers = table[:, :8].astype(jnp.int32)
    chosen = [
        (lane == integers[:, CHOICE + k : CHOICE + k + 1]).astype(F32) for k in range(2)
    ]
    place = lax.broadcasted_iota(jnp.int32, (amount, SMALL), 0)
    usable = (place + 1 + ahead[...] < integers[:, FINISH : FINISH + 1]).astype(F32)
    logit = logits[...]
    routed = lane < EXPERTS
    top = jnp.max(jnp.where(routed, logit, -1e30), -1, keepdims=True)
    exponent = jnp.where(routed, jnp.exp(jnp.where(routed, logit - top, 0.0)), 0.0)
    probs = exponent / jnp.sum(exponent, -1, keepdims=True)
    gates = [jnp.sum(chosen[k] * probs, -1, keepdims=True) for k in range(2)]
    shared_gate = jax.nn.sigmoid(
        jnp.sum(jnp.where(lane == EXPERTS, logit, 0.0), -1, keepdims=True)
    )
    picked = [jnp.zeros((amount, D), F32), jnp.zeros((amount, D), F32)]
    for expert in range(EXPERTS):
        if len(returned.shape) == 2:
            rows = returned[expert * CAP : (expert + 1) * CAP, :]
            scale = 1.0
        else:
            rows = returned[expert, :CAP, :].astype(jnp.int32).astype(F32)
            powers = returned[expert, CAP:, :].astype(jnp.int32).astype(F32)
            scale = jnp.exp2(powers[0:1, :CAP] - 15.0)
        high = rows.astype(BF16)
        rest = (rows - high.astype(F32)).astype(BF16)
        for k in range(2):
            slot = expert * CAP + lax.broadcasted_iota(jnp.int32, (amount, CAP), 1)
            hot = jnp.where(integers[:, SLOT + k : SLOT + k + 1] == slot, scale, 0.0).astype(BF16)
            picked[k] = picked[k] + (mm(hot, high) + mm(hot, rest))
    mixer = (
        after[...] + shared_gate * shared[...] + (gates[0] * picked[0] + gates[1] * picked[1])
    )
    inverse = inverse_rms(mixer)
    gain = gains[4:5]
    third = (mixer * inverse * gain).astype(BF16)
    residue = mm(third, small[...]) - target[...]
    size = jnp.abs(residue)
    cost = (
        jnp.where(
            size <= KINK_THRESHOLD,
            0.5 * residue * residue,
            KINK_THRESHOLD * (size - 0.5 * KINK_THRESHOLD),
        )
        * usable
    )
    domain_hot = (lane == integers[:, DOMAIN : DOMAIN + 1]).astype(F32)
    sums_out[...] = jnp.sum(domain_hot * jnp.sum(cost, -1, keepdims=True), 0, keepdims=True)
    weight = jnp.sum(domain_hot * weighting[...], -1, keepdims=True)
    slope = (
        jnp.clip(residue, -KINK_THRESHOLD, KINK_THRESHOLD) * usable * weight
    ).astype(BF16)
    small_out[...] = mm_tn(third, slope)
    mixer_slope, gain_slope = rms_back(mixer, inverse, gain, mm_nt(slope, small[...]))
    gain_out[...] = gain_slope
    mixer_out[...] = mixer_slope
    shared_slope_out[...] = (shared_gate * mixer_slope).astype(BF16)
    gate_slope = jnp.sum(mixer_slope * shared[...], -1, keepdims=True)
    probs_slope = chosen[0] * jnp.sum(mixer_slope * picked[0], -1, keepdims=True) + chosen[
        1
    ] * jnp.sum(mixer_slope * picked[1], -1, keepdims=True)
    inner = jnp.sum(probs * probs_slope, -1, keepdims=True)
    logits_slope_out[...] = jnp.where(
        routed,
        probs * (probs_slope - inner),
        jnp.where(lane == EXPERTS, gate_slope * (shared_gate * (1.0 - shared_gate)), 0.0),
    ).astype(BF16)
    slopes = [(gates[k] * mixer_slope).astype(BF16) for k in range(2)]
    for expert in range(EXPERTS):
        slots_out[expert * CAP : (expert + 1) * CAP, :] = (
            mm(slot_rows_hot(slot_row[0:1, :], expert), slopes[0])
            + mm(slot_rows_hot(slot_row[1:2, :], expert), slopes[1])
        ).astype(BF16)


def attend_back_kernel(
    returned, known, second_slope, logits_slope, small, after, mixer_slope, gains, mixed, second,
    output_w, small_before,
    attend_out, mixed_out, output_out, gain_out, small_out,
):
    slope = second_slope[...] + mm_nt(logits_slope[...], small[...])
    for expert in range(EXPERTS):
        hot = slot_cols_hot(known[:, 0:1], expert) + slot_cols_hot(known[:, 1:2], expert)
        slope = slope + mm(hot, returned[expert * CAP : (expert + 1) * CAP, :])
    after_rows = after[...]
    part, gain_slope = rms_back(after_rows, inverse_rms(after_rows), gains[3:4], slope)
    gain_out[...] = gain_slope
    attend = mixer_slope[...] + part
    attend_out[...] = attend
    low = attend.astype(BF16)
    output_out[...] = mm_tn(mixed[...], low)
    mixed_out[...] = mm_nt(low, output_w[...]).astype(BF16)
    small_out[...] = small_before[...] + mm_tn(second[...], logits_slope[...])


def front_back_kernel(
    fast, core, mixed_slope, qkv, log_total, known, rows_table, cosine, sine, first, embedded,
    gains, input_w, attend_slope, small_before, gain_two, gain_three, output_before,
    keep_out, give_out,
    pack_out, query_acc, key_acc, held_acc, slope_ref,
):
    amount = first.shape[0]
    key_acc[...] = jnp.zeros_like(key_acc)
    held_acc[...] = jnp.zeros_like(held_acc)
    lane = lanes_of((ROW_BLOCK, 128))
    lane_all = lanes_of((amount, 128))
    for start in range(0, amount, ROW_BLOCK):
        keys = start + ROW_BLOCK
        here = slice(start, start + ROW_BLOCK)
        allowed = allowed_block(known[...], rows_table[...], start, ROW_BLOCK, keys)
        for group in range(D // 128):
            wide = slice(group * 128, (group + 1) * 128)
            query = qkv[here, group * 128 : (group + 1) * 128]
            key = qkv[:keys, D + group * 128 : D + (group + 1) * 128]
            held = qkv[:keys, 2 * D + group * 128 : 2 * D + (group + 1) * 128]
            out_slope = mixed_slope[here, wide]
            query_sum = jnp.zeros((ROW_BLOCK, 128), F32)
            key_sum = jnp.zeros((keys, 128), F32)
            held_sum = jnp.zeros((keys, 128), F32)
            for head in range(128 // HD):
                own = lane // HD == head
                own_query = jnp.where(own, query, jnp.zeros_like(query))
                own_slope = jnp.where(own, out_slope, jnp.zeros_like(out_slope))
                own_key = jnp.where(lane_all[:keys] // HD == head, key, jnp.zeros_like(key))
                at = group * (128 // HD) + head
                raw = mm_nt(own_query, key) * HD ** (-0.5)
                probs = jnp.exp(jnp.where(allowed, raw - log_total[here, at : at + 1], -1e30))
                held_sum = held_sum + mm_tn(probs.astype(BF16), own_slope)
                probs_slope = mm_nt(own_slope, held)
                inner = jnp.sum(probs_slope * probs, -1, keepdims=True)
                raw_slope = (probs * (probs_slope - inner)).astype(BF16)
                query_sum = query_sum + mm(raw_slope, own_key)
                key_sum = key_sum + mm_tn(raw_slope, own_query)
            query_acc[here, wide] = query_sum
            key_acc[:keys, wide] += key_sum
            held_acc[:keys, wide] += held_sum
    cos_rows, sin_rows = cosine[...], sine[...]
    for block in range(3):
        wide = slice(block * 128, (block + 1) * 128)
        for base, acc in ((0, query_acc), (D, key_acc)):
            part = acc[:, wide] * HD ** (-0.5)
            part = part * cos_rows + half_swap(part * sin_rows)
            slope_ref[:, base + block * 128 : base + (block + 1) * 128] = part.astype(BF16)
    slope_ref[:, 2 * D :] = held_acc[...].astype(BF16)
    projected_slope = slope_ref[...]
    pack_out[:, : 3 * D] = mm_tn(first[...], projected_slope)
    pack_out[:, 3 * D : SMALL_AT] = output_before[...]
    first_slope = mm_nt(projected_slope, input_w[...])
    rows = embedded[...]
    part, gain_one = rms_back(rows, inverse_rms(rows), gains[2:3], first_slope)
    slope = attend_slope[...] + part
    value = known[:, VALUE : VALUE + 1]
    gate = value * gains[0:1]
    bent = jax.nn.sigmoid(gate)
    gate_gradient = jnp.sum(
        slope * (value * gains[1:2]) * (bent * (1.0 + gate * (1.0 - bent))) * value,
        0,
        keepdims=True,
    )
    lift_gradient = jnp.sum(slope * (gate * bent) * value, 0, keepdims=True)
    row = lax.broadcasted_iota(jnp.int32, (128, D), 0)
    table = jnp.zeros((128, D), F32)
    for offset, piece in enumerate(
        (gate_gradient, lift_gradient, gain_one, gain_two[...], gain_three[...])
    ):
        table = jnp.where(row == VECTORS_AT + offset, piece, table)
    pack_out[:, SMALL_AT:] = small_before[...] + table.T
    if not fast:
        keep_out[...] = pack_out[...]
        give_out[...] = jnp.zeros_like(give_out)
        return
    shard = keep_out.shape[0] // EXPERTS
    for index in range(EXPERTS):
        here = slice(index * shard, (index + 1) * shard)
        base = 2 * shard * index
        keep_out[here, :] = pack_out[pl.ds(pl.multiple_of(base + core[0] * shard, 8), shard), :]
        give_out[here, :] = pack_out[
            pl.ds(pl.multiple_of(base + (1 - core[0]) * shard, 8), shard), :
        ]


def lamb_direction(master, gradient, mean, square, factor):
    clipped = gradient * factor
    mean_next = BETA_ONE * mean + (1.0 - BETA_ONE) * clipped
    square_next = BETA_TWO * square + (1.0 - BETA_TWO) * clipped * clipped
    direction = (
        mean_next
        / (1.0 - BETA_ONE**STEP)
        / (jnp.sqrt(square_next / (1.0 - BETA_TWO**STEP)) + EPS_ADAM)
        + DECAY * master
    )
    return mean_next, square_next, direction


def whole(array):
    shape = array.shape
    return pl.BlockSpec(shape, lambda *unused: (0,) * len(shape))


def params(**extra):
    return pltpu.CompilerParams(vmem_limit_bytes=VMEM, **extra)


def cost(flops, size):
    return pl.CostEstimate(
        flops=int(flops / 1000), bytes_accessed=int(size / 1000), transcendentals=0
    )


def columns(array, width, at):
    return (array, pl.BlockSpec((array.shape[0], width), lambda *unused: (0, at)))


def simple_call(kernel, outs, args, flops, scratch=()):
    pairs = [a if isinstance(a, tuple) else (a, whole(a)) for a in args]
    args = [a for a, spec in pairs]
    size = sum(a.size * a.dtype.itemsize for a in list(args) + list(outs))
    return pl.pallas_call(
        kernel,
        out_shape=outs,
        in_specs=[spec for a, spec in pairs],
        out_specs=[whole(a) for a in outs],
        scratch_shapes=list(scratch),
        grid=(1,),
        compiler_params=params(),
        cost_estimate=cost(flops, size),
    )(*args)


def out(shape, dtype=F32):
    return jax.ShapeDtypeStruct(shape, dtype)


def flip(value, axis_name, bit):
    count = lax.axis_size(axis_name)
    return lax.ppermute(value, axis_name, [(i, i ^ bit) for i in range(count)])


def bits_of(axis_name):
    count = lax.axis_size(axis_name)
    return [1 << i for i in range(count.bit_length() - 1)]


def sum_small(value, axes):
    for axis_name in axes:
        for bit in bits_of(axis_name):
            value = value + flip(value, axis_name, bit)
    return value


def halves(value, axis, take_high):
    size = value.shape[axis] // 2
    side = take_high.astype(jnp.int32)
    return (
        lax.dynamic_slice_in_dim(value, side * size, size, axis),
        lax.dynamic_slice_in_dim(value, (1 - side) * size, size, axis),
    )


def scatter_sum(value, axis, bits):
    for bit in bits:
        side = (lax.axis_index("dp") & bit) != 0
        keep, give = halves(value, axis, side)
        value = keep + flip(give, "dp", bit)
    return value


def join(value, axis, bits):
    for bit in reversed(bits):
        side = (lax.axis_index("dp") & bit) != 0
        other = flip(value, "dp", bit)
        value = jnp.concatenate(
            [jnp.where(side, other, value), jnp.where(side, value, other)], axis
        )
    return value


def ready(value, *others):
    return lax.optimization_barrier((value, *others))[0]


def exchange(value):
    return lax.all_to_all(value, "expert", split_axis=0, concat_axis=0, tiled=True)


def spread(value):
    count = lax.axis_size("expert")
    return exchange(jnp.broadcast_to(value[None], (count, *value.shape)))


def expert_scatter(value):
    return jnp.sum(exchange(value), 0)


def squares_kernel(weights, sums, *refs):
    total = jnp.zeros((1, 1), F32)
    for weight, ref in zip(weights, refs[:-1]):
        piece = ref[...]
        part = jnp.sum(jnp.sum(piece * piece, -1, keepdims=True), 0, keepdims=True)
        total = total + part * weight
    refs[-1][0:1, :] = jnp.broadcast_to(total, (1, 128))
    refs[-1][1:2, :] = sums[...]


def sum_all(value):
    while value.ndim > 2:
        value = jnp.sum(value, 0)
    return jnp.sum(jnp.sum(value, 0, keepdims=True), -1, keepdims=True)


TILED = (4, 7, 8)


def tile_spec(index, shape, steps):
    if index == 7:
        return pl.BlockSpec((2, D // steps, shape[2]), lambda i: (0, i, 0))
    if index == 8:
        return pl.BlockSpec((shape[0] // steps, D), lambda i: (i, 0))
    if index == 4 and len(shape) == 3:
        half = steps // 2
        return pl.BlockSpec((1, shape[1], shape[2] // half), lambda i: (i // half, 0, i % half))
    if index == 4:
        return pl.BlockSpec((shape[0], shape[1] // steps), lambda i: (0, i))
    return pl.BlockSpec(shape, lambda i: (0,) * len(shape))


def tile_specs(arrays, steps):
    return [tile_spec(index, array.shape, steps) for index, array in enumerate(arrays)]


def prepare_kernel(count, *refs):
    masters = refs[:count]
    gate_up_low, down_low, totals = refs[count:]
    step = pl.program_id(0)
    gate_up_low[...] = masters[7][...].astype(BF16)
    down_low[...] = masters[8][...].astype(BF16)

    @pl.when(step == 0)
    def _():
        totals[...] = jnp.zeros_like(totals)

    def add(index):
        master = masters[index][...]
        totals[index : index + 1, :] += jnp.broadcast_to(sum_all(master * master), (1, 128))

    for index in TILED:
        add(index)

    @pl.when(step == 0)
    def _():
        for index in range(count):
            if index not in TILED:
                add(index)


def picked_piece(pieces, index, part):
    value = part(pieces[0])
    for other in range(1, len(pieces)):
        value = jnp.where(index == other, part(pieces[other]), value)
    return value


def moments_kernel(fast, count, small_end, sides, square_ref, *refs):
    masters, means, squares = (refs[k * count : (k + 1) * count] for k in range(3))
    results = refs[-3 * count - 1 :]
    pieces = refs[3 * count : -3 * count - 1]
    totals = results[-1]
    factor = jnp.minimum(1.0, CLIP / jnp.sqrt(square_ref[0:1, 0:1]))
    step = pl.program_id(0)

    @pl.when(step == 0)
    def _():
        totals[...] = jnp.zeros_like(totals)

    def last_rows(start, stop):
        if not fast:
            return pieces[0][:, start:stop]
        mine, other = pieces[0][:, start:stop], pieces[1][:, start:stop]
        low = sides[0] == 0
        return jnp.concatenate([jnp.where(low, mine, other), jnp.where(low, other, mine)], 0)

    def gradient_of(index):
        if index in (0, 3):
            table = last_rows(SMALL_AT, SMALL_AT + SMALL).T
            return table[VECTORS_AT : VECTORS_AT + 5] if index == 0 else table[:HORIZON_AT]
        if index == 6:
            return last_rows(SMALL_AT, SMALL_AT + SMALL)[:, HORIZON_AT:small_end]
        if index == 1:
            return last_rows(0, 3 * D)
        if index == 2:
            return last_rows(3 * D, SMALL_AT)
        if not fast:
            return pieces[{4: 1, 5: 2, 7: 3, 8: 4}[index]][...]
        low = sides[0] == 0
        me = sides[0] * 2 + sides[1]
        shared = pieces[2:6]
        wide = 2 * FFS // 4
        if index == 4:
            at = pl.multiple_of((step % 2) * (wide // 2), 128)
            return picked_piece(
                shared,
                jnp.bitwise_xor(step // 2, me),
                lambda ref: ref[:, pl.ds(at, wide // 2)],
            )
        if index == 5:
            return jnp.concatenate(
                [
                    picked_piece(shared, jnp.bitwise_xor(piece, me), lambda ref: ref[:, wide:])
                    for piece in range(4)
                ],
                0,
            )
        if index == 7:
            mine, other = pieces[6][...], pieces[7][...]
            return jnp.stack([jnp.where(low, mine, other), jnp.where(low, other, mine)])
        return jnp.where(step // 4 == sides[0], pieces[8][...], pieces[9][...])

    def update(index):
        gradient = gradient_of(index)
        if index == 4 and gradient.ndim == 3:
            gradient = gradient[0]
        scale = factor.reshape(1, 1, 1) if gradient.ndim == 3 else factor
        mean_next, square_next, direction = lamb_direction(
            masters[index][...], gradient, means[index][...], squares[index][...], scale
        )
        results[index][...] = direction
        results[count + index][...] = mean_next
        results[2 * count + index][...] = square_next
        totals[index : index + 1, :] += jnp.broadcast_to(sum_all(direction * direction), (1, 128))

    for index in TILED:
        update(index)
    for index in range(count):
        if index not in TILED:
            pl.when(step == min(index, 7))(functools.partial(update, index))


def step_kernel(count, totals, master_totals, *refs):
    masters, directions = refs[:count], refs[count : 2 * count]
    results = refs[2 * count :]
    step = pl.program_id(0)

    def update(index):
        ratio = jnp.sqrt(master_totals[index : index + 1, 0:1]) / jnp.sqrt(
            totals[index : index + 1, 0:1]
        )
        ratio = RATE * ratio
        if len(masters[index].shape) == 3:
            ratio = ratio.reshape(1, 1, 1)
        results[index][...] = masters[index][...] - ratio * directions[index][...]

    for index in TILED:
        update(index)
    for index in range(count):
        if index not in TILED:
            pl.when(step == min(index, 7))(functools.partial(update, index))


def shards(
    points,
    experts,
    lengths,
    domains,
    domain_weights,
    vectors,
    attend_input,
    attend_output,
    router,
    shared_input,
    shared_output,
    horizon,
    expert_input,
    expert_output,
    mean_vectors,
    mean_attend_input,
    mean_attend_output,
    mean_router,
    mean_shared_input,
    mean_shared_output,
    mean_horizon,
    mean_expert_input,
    mean_expert_output,
    square_vectors,
    square_attend_input,
    square_attend_output,
    square_router,
    square_shared_input,
    square_shared_output,
    square_horizon,
    square_expert_input,
    square_expert_output,
):
    expert_count = lax.axis_size("expert")
    group_size = expert_count // EXPERTS
    dp_count = lax.axis_size("dp")
    dp_bits = bits_of("dp")
    amount = points.shape[0]
    local_rows = attend_input.shape[0]
    head_columns = horizon.shape[1]
    hidden_local = expert_output.shape[0]
    small_end = HORIZON_AT + head_columns
    fast = group_size == 1 and dp_count == 4 and local_rows % 16 == 0
    core = lax.axis_index("dp") & 1
    sides = jnp.stack([core, lax.axis_index("dp") >> 1]).astype(jnp.int32)
    in_smem = pl.BlockSpec(memory_space=pltpu.SMEM)
    in_vmem = pl.BlockSpec(memory_space=pltpu.VMEM)
    ahead_row = jnp.pad(
        jnp.asarray(ahead_table())[None], ((0, 0), (0, SMALL - head_columns)), constant_values=1 << 20
    )
    packed = pl.pallas_call(
        functools.partial(pack_kernel, small_end),
        out_shape=out((expert_count, local_rows, 2 * D + SMALL), BF16),
        in_specs=[*[in_smem] * 3, *[in_vmem] * 6],
        out_specs=in_vmem,
        compiler_params=params(),
        cost_estimate=cost(1e6, 1e6),
    )(sides, lengths, domains, ahead_row, attend_input, attend_output, router.T, horizon, vectors)
    gathered = exchange(packed)

    def state(group):
        return tuple(a.T if index == 3 else a for index, a in enumerate(group))

    masters = state(
        (
            vectors, attend_input, attend_output, router, shared_input, shared_output, horizon,
            expert_input, expert_output,
        )
    )
    first_moments = state(
        (
            mean_vectors, mean_attend_input, mean_attend_output, mean_router, mean_shared_input,
            mean_shared_output, mean_horizon, mean_expert_input, mean_expert_output,
        )
    )
    second_moments = state(
        (
            square_vectors, square_attend_input, square_attend_output, square_router,
            square_shared_input, square_shared_output, square_horizon, square_expert_input,
            square_expert_output,
        )
    )
    count = len(masters)
    steps = 8
    gate_up_low, down_low, master_squares = pl.pallas_call(
        functools.partial(prepare_kernel, count),
        out_shape=[
            out(expert_input.shape, BF16), out(expert_output.shape, BF16), out((16, 128)),
        ],
        grid=(steps,),
        in_specs=tile_specs(masters, steps),
        out_specs=[
            tile_spec(7, expert_input.shape, steps),
            tile_spec(8, expert_output.shape, steps),
            whole(out((16, 128))),
        ],
        compiler_params=params(),
        cost_estimate=cost(3e6, 7e6),
    )(*masters)
    frequency = jnp.exp(-jnp.log(10000.0) * jnp.arange(HD // 2, dtype=F32) / (HD // 2))
    cosine, sine, known, rows_table = pl.pallas_call(
        tables_kernel,
        out_shape=[out((amount, 128)), out((amount, 128)), out((amount, 128)), out((8, amount))],
        in_specs=[*[in_smem] * 2, *[in_vmem] * 3],
        out_specs=[in_vmem] * 4,
        compiler_params=params(),
        cost_estimate=cost(1e6, 1e6),
    )(
        lengths,
        domains,
        jnp.tile(frequency, 128 // (HD // 2))[None],
        points.reshape(1, amount),
        experts.T,
    )
    folds = FFS // D
    shared_piece = jnp.concatenate(
        [
            shared_input,
            shared_output.reshape(folds, local_rows, D).swapaxes(0, 1).reshape(local_rows, -1),
        ],
        1,
    ).astype(BF16)
    for bit in dp_bits:
        shared_piece, unused = halves(shared_piece, 1, (lax.axis_index("dp") & bit) != 0)
    gathered = ready(
        gathered, known, gate_up_low, down_low, master_squares, shared_piece
    ).reshape(D, -1)
    gathered_other = flip(gathered, "dp", 1)
    shared_pieces = spread(ready(shared_piece, gathered))
    (
        embedded, first, qkv, log_total, mixed, after, second, logits, slots, gains, pack,
        counts_half,
    ) = simple_call(
        functools.partial(front_kernel, local_rows),
        [
            out((amount, D)), out((amount, D), BF16), out((amount, 3 * D), BF16),
            out((amount, 128)), out((amount, D), BF16), out((amount, D)),
            out((amount, D), BF16), out((amount, SMALL)), out((EXPERTS * CAP, D), BF16),
            out((8, D)), out((D, SMALL_AT + SMALL), BF16), out((1, SMALL)),
        ],
        [(sides, in_smem), gathered, gathered_other, cosine, sine, known, rows_table],
        8e9,
    )

    def to_devices(rows):
        rows = rows.reshape(EXPERTS, CAP, D)
        return exchange(jnp.repeat(rows, group_size, 0)).reshape(-1, D)

    def to_points(rows):
        rows = exchange(rows.reshape(expert_count, CAP, D))
        if group_size > 1:
            kind = rows.dtype
            rows = rows.reshape(EXPERTS, group_size, CAP, D).astype(F32)
            rows = jnp.sum(rows, 1).astype(kind)
        return rows.reshape(-1, D)

    arrived = to_devices(ready(slots, shared_pieces))
    first_bit = dp_bits[-1]
    shared_pieces = ready(shared_pieces, slots)
    shared_other = flip(shared_pieces, "dp", first_bit)
    arrived = ready(arrived, shared_other)
    block = 512
    total_rows = arrived.shape[0]
    coded = group_size == 1
    sources = block // CAP
    expert_rows = pl.pallas_call(
        expert_kernel,
        out_shape=(
            out((EXPERTS, CAP + CODE_ROWS, D), jnp.int16) if coded else out((total_rows, D))
        ),
        grid=(total_rows // block,),
        in_specs=[
            pl.BlockSpec((block, D), lambda i: (i, 0)), whole(gate_up_low), whole(down_low),
        ],
        out_specs=(
            pl.BlockSpec((sources, CAP + CODE_ROWS, D), lambda i: (i, 0, 0))
            if coded
            else pl.BlockSpec((block, D), lambda i: (i, 0))
        ),
        compiler_params=params(),
        cost_estimate=cost(total_rows * D * 3 * hidden_local * 2, 7e6),
    )(arrived, gate_up_low, down_low)
    returned = exchange(expert_rows) if coded else to_points(expert_rows)
    shared_pieces = ready(shared_pieces, expert_rows)
    side = (lax.axis_index("dp") & first_bit) != 0
    shared_pack = jnp.concatenate(
        [
            jnp.where(side, shared_other, shared_pieces),
            jnp.where(side, shared_pieces, shared_other),
        ],
        2,
    )
    shared_pack = join(shared_pack, 2, dp_bits[:-1])
    shin_low = shared_pack[:, :, : 2 * FFS].reshape(D, -1)
    shout_low = (
        shared_pack[:, :, 2 * FFS :]
        .reshape(expert_count, local_rows, folds, D)
        .swapaxes(1, 2)
        .reshape(FFS, D)
    )
    chunk = 512
    chunks = FFS // chunk
    shared = pl.pallas_call(
        shared_kernel,
        out_shape=out((amount, D)),
        grid=(chunks,),
        in_specs=[
            whole(second),
            pl.BlockSpec((D, chunk), lambda i: (0, i)),
            pl.BlockSpec((D, chunk), lambda i: (0, i + chunks)),
            pl.BlockSpec((chunk, D), lambda i: (i, 0)),
        ],
        out_specs=pl.BlockSpec((amount, D), lambda i: (0, 0)),
        compiler_params=params(),
        cost_estimate=cost(amount * D * 3 * FFS * 2, 5e6),
    )(second, shin_low, shin_low, shout_low)
    counts = ready(counts_half, expert_rows)
    for bit in dp_bits[1:]:
        counts = counts + flip(counts, "dp", bit)
    weighting = jnp.pad(domain_weights, (0, SMALL - DOMAINS))[None] / jnp.maximum(counts, 1.0)
    side_pad = ((0, 0), (HORIZON_AT, SMALL - small_end))
    target = jnp.pad(target_columns(points), side_pad)
    ahead_small = jnp.pad(
        jnp.asarray(ahead_table())[None], ((0, 0), side_pad[1]), constant_values=1 << 20
    )
    small_low = columns(pack, SMALL, SMALL_AT // SMALL)
    (
        mixer_slope, shared_slope, slope_slots, logits_slope, small_head, gain_three, local_sums,
    ) = simple_call(
        middle_kernel,
        [
            out((amount, D)), out((amount, D), BF16), out((EXPERTS * CAP, D), BF16),
            out((amount, SMALL), BF16), out((D, SMALL)), out((1, D)), out((1, SMALL)),
        ],
        [
            returned, known, rows_table, after, shared, logits, small_low, gains, target,
            ahead_small, weighting,
        ],
        7e9,
    )
    received = to_devices(slope_slots)
    chunk = D
    chunks = FFS // chunk
    back_in = [
        pl.BlockSpec((amount, D), lambda i, *unused: (0, 0)),
        pl.BlockSpec((amount, D), lambda i, *unused: (0, 0)),
        pl.BlockSpec((D, chunk), lambda i, *unused: (0, i)),
        pl.BlockSpec((D, chunk), lambda i, *unused: (0, i + chunks)),
        pl.BlockSpec((chunk, D), lambda i, *unused: (i, 0)),
    ]
    second_spec = pl.BlockSpec((amount, D), lambda i, *unused: (0, 0))
    back_args = (second, shared_slope, shin_low, shin_low, shout_low)
    back_cost = cost(amount * D * 8 * FFS * 2, 14e6)
    if fast:
        in_spec = pl.BlockSpec(
            (1, D, chunk), lambda i, sides: (jnp.bitwise_xor(i // 2, sides[1]), 0, i % 2)
        )
        out_spec = pl.BlockSpec((2, D // chunks, D), lambda i, sides: (0, i, 0))
        shared_second_slope, in_keep, in_give, out_keep, out_give = pl.pallas_call(
            shared_back_split_kernel,
            out_shape=[
                out((amount, D)), out((2, D, FFS // 2)), out((2, D, FFS // 2)), out((2, D, D)),
                out((2, D, D)),
            ],
            grid_spec=pltpu.PrefetchScalarGridSpec(
                num_scalar_prefetch=1,
                grid=(chunks,),
                in_specs=back_in,
                out_specs=[second_spec, in_spec, in_spec, out_spec, out_spec],
                scratch_shapes=[pltpu.VMEM((chunk, D), F32)],
            ),
            compiler_params=params(),
            cost_estimate=back_cost,
        )(sides, *back_args)
    else:
        shared_second_slope, grad_shin, grad_shout = pl.pallas_call(
            shared_back_kernel,
            out_shape=[out((amount, D)), out((2, D, FFS)), out((FFS, D))],
            grid=(chunks,),
            in_specs=back_in,
            out_specs=[
                second_spec,
                pl.BlockSpec((2, D, chunk), lambda i: (0, 0, i)),
                pl.BlockSpec((chunk, D), lambda i: (i, 0)),
            ],
            compiler_params=params(),
            cost_estimate=back_cost,
        )(*back_args)
    received = ready(received, shared_second_slope)
    row_spec = pl.BlockSpec((block, D), lambda i: (i, 0))
    expert_cost = cost(total_rows * D * 8 * hidden_local * 2, 10e6)
    weight_specs = [whole(gate_up_low), whole(down_low)]
    if fast:
        half_shapes = [out((D, hidden_local))] * 2 + [out((hidden_local // 2, D))] * 2
        grad_rows, expert_in, expert_in_give, expert_out, expert_out_give = pl.pallas_call(
            expert_back_split_kernel,
            out_shape=[out((total_rows, D), BF16), *half_shapes],
            grid=(total_rows // block,),
            in_specs=[in_smem, row_spec, row_spec, *weight_specs],
            out_specs=[row_spec, *[whole(a) for a in half_shapes]],
            compiler_params=params(),
            cost_estimate=expert_cost,
        )(sides, arrived, received, gate_up_low, down_low)
    else:
        grad_rows, grad_expert_in, grad_expert_out = pl.pallas_call(
            expert_back_kernel,
            out_shape=[
                out((total_rows, D), BF16), out((2, D, hidden_local)), out((hidden_local, D)),
            ],
            grid=(total_rows // block,),
            in_specs=[row_spec, row_spec, *weight_specs],
            out_specs=[
                row_spec,
                pl.BlockSpec((2, D, hidden_local), lambda i: (0, 0, 0)),
                pl.BlockSpec((hidden_local, D), lambda i: (0, 0)),
            ],
            compiler_params=params(),
            cost_estimate=expert_cost,
        )(arrived, received, gate_up_low, down_low)
    routed_back = to_points(grad_rows)
    if fast:
        in_other, out_other = flip(in_give, "dp", 1), flip(out_give, "dp", 1)
        fold_in = pl.BlockSpec((2, D // 4, FFS // 2), lambda i: (0, i, 0))
        fold_out = pl.BlockSpec((2, D // 4, D), lambda i: (0, i, 0))
        wide = FFS // 2 + D
        fold_to = pl.BlockSpec((D // 4, wide), lambda i: (i, 0))
        shared_keep, shared_give = pl.pallas_call(
            fold_kernel,
            out_shape=[out((D, wide)), out((D, wide))],
            grid=(4,),
            in_specs=[fold_in, fold_in, fold_out, fold_out],
            out_specs=[fold_to, fold_to],
            compiler_params=params(),
            cost_estimate=cost(2e6, 10e6),
        )(in_keep, in_other, out_keep, out_other)
        shared_other = flip(shared_give, "dp", 2)
        expert_in = expert_in + flip(expert_in_give, "dp", 1)
        expert_out = expert_out + flip(expert_out_give, "dp", 1)
        sums = local_sums + flip(local_sums, "dp", 2)
        routed_back = ready(routed_back, shared_other, expert_in, expert_out, sums)
    attend_slope, mixed_slope, grad_output, gain_two, small_routed = simple_call(
        attend_back_kernel,
        [
            out((amount, D)), out((amount, D), BF16), out((D, D)), out((1, D)), out((D, SMALL)),
        ],
        [
            routed_back, known, shared_second_slope, logits_slope, small_low, after,
            mixer_slope, gains, mixed, second, columns(pack, D, 3), small_head,
        ],
        2e9,
    )
    shard_rows = D // 2 if fast else D
    pack_columns = SMALL_AT + SMALL
    last_keep, last_give = simple_call(
        functools.partial(front_back_kernel, fast),
        [out((shard_rows, pack_columns)), out((shard_rows if fast else 8, pack_columns))],
        [
            (sides, in_smem), mixed_slope, qkv, log_total, known, rows_table, cosine, sine, first,
            embedded, gains, columns(pack, 3 * D, 0), attend_slope, small_routed, gain_two,
            gain_three, grad_output,
        ],
        16e9,
        [
            pltpu.VMEM((D, pack_columns), F32),
            pltpu.VMEM((amount, D), F32),
            pltpu.VMEM((amount, D), F32),
            pltpu.VMEM((amount, D), F32),
            pltpu.VMEM((amount, 3 * D), BF16),
        ],
    )

    if fast:
        shared_sum = (shared_keep + shared_other).reshape(expert_count, local_rows, wide)
        shared_sum = expert_scatter(ready(shared_sum, mixed_slope))
        expert_in = ready(expert_in, mixed_slope)
        expert_out = ready(expert_out, mixed_slope)
        expert_in_other = flip(expert_in, "dp", 2)
        expert_out_other = flip(expert_out, "dp", 2)
        last_part = last_keep + flip(last_give, "dp", 1)
        last_part = ready(last_part, shared_sum, expert_in_other, expert_out_other)
        last_part = expert_scatter(last_part.reshape(expert_count, local_rows // 2, -1))
        last_part = last_part + flip(last_part, "dp", 2)
        expert_in = expert_in + expert_in_other
        expert_out = expert_out + expert_out_other
        shared_cross = flip(shared_sum, "dp", 2)
        square_pieces = [expert_in, expert_out, shared_sum, shared_cross, last_part]
        weights = (1.0,) * 5
        square_bits = [1]
        pieces = [
            last_part, flip(last_part, "dp", 1), shared_sum, shared_cross,
            flip(shared_sum, "dp", 1), flip(shared_cross, "dp", 1), expert_in,
            flip(expert_in, "dp", 1), expert_out, flip(expert_out, "dp", 1),
        ]
        tile_in = pl.BlockSpec((D // steps, hidden_local), lambda i: (i, 0))
        half_steps = steps // 2
        tile_out = pl.BlockSpec((hidden_local // steps, D), lambda i: (i % half_steps, 0))
        piece_specs = [*[whole(a) for a in pieces[:6]], tile_in, tile_in, tile_out, tile_out]
    else:
        sums = local_sums
        shin_part = scatter_sum(grad_shin, 0, [1])[0].reshape(expert_count, local_rows, FFS)
        shin_part = expert_scatter(scatter_sum(shin_part, 2, dp_bits[1:]))
        shout_part = scatter_sum(grad_shout.reshape(expert_count, -1, D), 1, dp_bits)
        shout_part = expert_scatter(shout_part)
        expert_in_part = scatter_sum(grad_expert_in.reshape(-1, hidden_local), 0, dp_bits)
        expert_out_part = scatter_sum(grad_expert_out, 0, dp_bits)
        last_part = expert_scatter(last_keep.reshape(expert_count, local_rows, -1))
        for bit in dp_bits:
            last_part = last_part + flip(last_part, "dp", bit)
        square_pieces = [expert_in_part, expert_out_part, shin_part, shout_part, last_part]
        weights = (1.0, 1.0, 1.0, 1.0, 1.0 / dp_count)
        square_bits = dp_bits
        pieces = [
            last_part,
            join(join(shin_part, 1, dp_bits[1:])[None], 0, [1]),
            join(shout_part, 0, dp_bits),
            join(expert_in_part, 0, dp_bits).reshape(expert_input.shape),
            join(expert_out_part, 0, dp_bits),
        ]
        piece_specs = [
            whole(last_part),
            *[tile_spec(i, a.shape, steps) for i, a in zip((4, 5, 7, 8), pieces[1:])],
        ]
    (both_sums,) = simple_call(
        functools.partial(squares_kernel, weights), [out((2, 128))], [sums, *square_pieces], 3e6
    )
    for bit in square_bits:
        both_sums = both_sums + flip(both_sums, "dp", bit)
    both_sums = sum_small(both_sums, ("expert",))
    domain_sums = both_sums[1, :DOMAINS]
    grad_norm = jnp.sqrt(both_sums[0, 0:1])
    shapes = [out(a.shape) for a in masters]
    state_specs = tile_specs(masters, steps)
    updates = pl.pallas_call(
        functools.partial(moments_kernel, fast, count, small_end),
        out_shape=[*shapes, *shapes, *shapes, out((16, 128))],
        grid=(steps,),
        in_specs=[
            in_smem, whole(both_sums), *state_specs, *state_specs, *state_specs, *piece_specs,
        ],
        out_specs=[*state_specs, *state_specs, *state_specs, whole(out((16, 128)))],
        compiler_params=params(),
        cost_estimate=cost(3e7, 34e6),
    )(sides, both_sums, *masters, *first_moments, *second_moments, *pieces)
    directions = updates[:count]
    all_totals = sum_small(
        jnp.concatenate([updates[-1][:count], master_squares[:count]], 0), ("expert",)
    )
    totals, master_totals = all_totals[:count], all_totals[count:]
    next_masters = pl.pallas_call(
        functools.partial(step_kernel, count),
        out_shape=shapes,
        grid=(steps,),
        in_specs=[whole(totals), whole(master_totals), *state_specs, *state_specs],
        out_specs=state_specs,
        compiler_params=params(),
        cost_estimate=cost(3e6, 15e6),
    )(totals, master_totals, *masters, *directions)
    results = []
    for index in range(count):
        for group in (next_masters, updates[count : 2 * count], updates[2 * count : 3 * count]):
            results.append(group[index].T if index == 3 else group[index])
    norms = jnp.sqrt(all_totals[:, 0])
    results.append(jnp.stack([domain_sums, counts[0, :DOMAINS]]))
    results.append(grad_norm)
    results.append(jnp.stack([norms[count:], norms[:count]], 1))
    return tuple(results)


def solution(mesh):
    placed = (
        P(("dp", "expert")),
        P(("dp", "expert"), None),
        P(("dp", "expert"), None),
        P(("dp", "expert"), None),
        P(),
        P(None, "expert"),
        P("expert", None),
        P("expert", None),
        P("expert", None),
        P("expert", None),
        P("expert", None),
        P("expert", None),
        P(None, None, "expert"),
        P("expert", None),
        P(None, "expert"),
        P("expert", None),
        P("expert", None),
        P("expert", None),
        P("expert", None),
        P("expert", None),
        P("expert", None),
        P(None, None, "expert"),
        P("expert", None),
        P(None, "expert"),
        P("expert", None),
        P("expert", None),
        P("expert", None),
        P("expert", None),
        P("expert", None),
        P("expert", None),
        P(None, None, "expert"),
        P("expert", None),
    )
    return jax.shard_map(
        shards,
        mesh=mesh,
        in_specs=placed,
        out_specs=(
            P(None, "expert"),
            P(None, "expert"),
            P(None, "expert"),
            P("expert", None),
            P("expert", None),
            P("expert", None),
            P("expert", None),
            P("expert", None),
            P("expert", None),
            P("expert", None),
            P("expert", None),
            P("expert", None),
            P("expert", None),
            P("expert", None),
            P("expert", None),
            P("expert", None),
            P("expert", None),
            P("expert", None),
            P("expert", None),
            P("expert", None),
            P("expert", None),
            P(None, None, "expert"),
            P(None, None, "expert"),
            P(None, None, "expert"),
            P("expert", None),
            P("expert", None),
            P("expert", None),
            P(),
            P(),
            P(),
        ),
        check_vma=False,
    )
```

```python
import functools

import jax
import jax.numpy as jnp
import numpy as np
from jax import lax
from jax.experimental import pallas as pl
from jax.experimental.pallas import tpu as pltpu
from jax.sharding import PartitionSpec as P

D = 384
HEADS = 12
HD = 32
FFS = 1536
EXPERTS = 8
DOMAINS = 9
STEP = 10
CAP = 256


HORIZONS = (1, 8, 32, 64)
REACH = 64
KINK_THRESHOLD = 2.0
EPS_NORM = 1e-06
CLIP = 0.01
BETA_ONE = 0.9
BETA_TWO = 0.99
EPS_ADAM = 1e-08
DECAY = 0.01
RATE = 0.3


def ahead_table():
    return np.concatenate([np.arange(horizon_len) for horizon_len in HORIZONS]).astype(np.int32)


def target_columns(samples):
    amount = samples.shape[0]
    padded = jnp.concatenate([samples, jnp.zeros((REACH + 1,), samples.dtype)])
    future = jnp.stack([padded[1 + offset : 1 + offset + amount] for offset in range(REACH)], 1)
    return future[:, ahead_table()]


ROW_BLOCK = 256
SMALL = 128
HORIZON_AT = EXPERTS + 1
VECTORS_AT = 120
SMALL_AT = 4 * D
COUNTS_AT = 125
CODE_ROWS = 16
VMEM = 56 * 1024 * 1024
F32 = jnp.float32
BF16 = jnp.bfloat16


def mm(left, right):
    return jnp.dot(left, right, preferred_element_type=F32)


def mm_nt(left, right):
    return lax.dot_general(left, right, (((1,), (1,)), ((), ())), preferred_element_type=F32)


def mm_tn(left, right):
    return lax.dot_general(left, right, (((0,), (0,)), ((), ())), preferred_element_type=F32)


def inverse_rms(rows):
    return lax.rsqrt(jnp.mean(rows * rows, axis=-1, keepdims=True) + EPS_NORM)


def rms_back(rows, inverse, gain, slope):
    gain_slope = jnp.sum(slope * rows * inverse, 0, keepdims=True)
    scaled = slope * gain
    return (
        inverse * scaled
        - rows * (inverse * inverse * inverse) * jnp.mean(rows * scaled, -1, keepdims=True),
        gain_slope,
    )


def lanes_of(shape):
    return lax.broadcasted_iota(jnp.int32, shape, len(shape) - 1)


def half_swap(rows):
    half_width = HD // 2
    lane = lanes_of(rows.shape)
    return jnp.where(
        lane % HD < half_width,
        pltpu.roll(rows, rows.shape[1] - half_width, 1),
        pltpu.roll(rows, half_width, 1),
    )


SLOT, SERIES_OF, FINISH, DOMAIN, CHOICE, VALUE, PLACE = 0, 2, 3, 4, 5, 7, 8


def tables_kernel(
    lengths, domains, frequency, points_row, experts_row, cosine, sine, columns_out, rows_out
):
    amount = points_row.shape[1]
    place = lax.broadcasted_iota(jnp.int32, (1, amount), 1)
    series = jnp.zeros((1, amount), jnp.int32)
    begin = jnp.zeros((1, amount), jnp.int32)
    finish = jnp.zeros((1, amount), jnp.int32)
    domain = jnp.zeros((1, amount), jnp.int32)
    start = jnp.int32(0)
    for index in range(lengths.shape[1]):
        stop = start + lengths[0, index]
        inside = (place >= start) & (place < stop)
        series = jnp.where(inside, index, series)
        begin = jnp.where(inside, start, begin)
        finish = jnp.where(inside, stop, finish)
        domain = jnp.where(inside, domains[0, index], domain)
        start = stop
    name = lax.broadcasted_iota(jnp.int32, (16, amount), 0)
    choices = [experts_row[k : k + 1, :] for k in range(2)]
    named = [(name == choice).astype(F32) for choice in choices]
    earlier = (
        lax.broadcasted_iota(jnp.int32, (amount, amount), 0)
        < lax.broadcasted_iota(jnp.int32, (amount, amount), 1)
    )
    before = mm((named[0] + named[1]).astype(BF16), earlier.astype(F32).astype(BF16))
    entries = []
    for k in range(2):
        rank = jnp.sum(named[k] * before, 0, keepdims=True)
        entries.append(choices[k].astype(F32) * CAP + rank)
    entries += [series, finish, domain, *choices, points_row[...], place - begin]
    row = lax.broadcasted_iota(jnp.int32, (128, amount), 0)
    table = jnp.zeros((128, amount), F32)
    for index, entry in enumerate(entries):
        table = jnp.where(row == index, entry.astype(F32), table)
    rows_out[...] = table[:8]
    columns = table.T
    columns_out[...] = columns
    angles = columns[:, PLACE : PLACE + 1] * frequency[...]
    cosine[...] = jnp.cos(angles)
    turned = jnp.sin(angles)
    sine[...] = jnp.where(lanes_of((amount, 128)) % HD < HD // 2, -turned, turned)


def allowed_block(table, rows_table, start, rows, keys):
    query = start + lax.broadcasted_iota(jnp.int32, (rows, keys), 0)
    key = lax.broadcasted_iota(jnp.int32, (rows, keys), 1)
    series_col = table[start : start + rows, SERIES_OF : SERIES_OF + 1]
    return (series_col == rows_table[SERIES_OF : SERIES_OF + 1, :keys]) & (key <= query)


def slot_rows_hot(slot_row, expert):
    slot = expert * CAP + lax.broadcasted_iota(jnp.int32, (CAP, slot_row.shape[1]), 0)
    return (slot_row.astype(jnp.int32) == slot).astype(F32).astype(BF16)


def slot_cols_hot(slot_col, expert):
    slot = expert * CAP + lax.broadcasted_iota(jnp.int32, (slot_col.shape[0], CAP), 1)
    return (slot_col.astype(jnp.int32) == slot).astype(F32).astype(BF16)


def pack_kernel(small_end, core, lengths, domains, ahead, input_w, output_w, router, horizon, vectors, out):
    rows = input_w.shape[0]

    def placed(count, at):
        row = lax.broadcasted_iota(jnp.int32, (count, SMALL), 0)
        return (row + at == lanes_of((count, SMALL))).astype(F32).astype(BF16)

    small = (
        mm_tn(router[...].astype(BF16), placed(HORIZON_AT, 0))
        + mm(horizon[...].astype(BF16), placed(small_end - HORIZON_AT, HORIZON_AT))
        + mm_tn(vectors[...].astype(BF16), placed(vectors.shape[0], VECTORS_AT))
    )
    row = lax.broadcasted_iota(jnp.int32, (rows, SMALL), 0)
    lane = lanes_of((rows, SMALL))
    counts = jnp.zeros((rows, SMALL), F32)
    for series in range(lengths.shape[1]):
        left = jnp.maximum(lengths[0, series] - 1 - ahead[...], 0).astype(F32)
        entries = jnp.sum(left, -1, keepdims=True)
        counts = counts + jnp.where(row == domains[0, series], entries, 0.0)
    high = jnp.floor(counts * (1.0 / 256.0))
    small = jnp.where(lane == COUNTS_AT, high, small)
    small = jnp.where(lane == COUNTS_AT + 1, counts - 256.0 * high, small)
    flat = jnp.concatenate([input_w[...], output_w[...]], 1)
    half = 2 * D
    mine = jnp.where(core[0] == 0, flat[:, :half], flat[:, half:]).astype(BF16)
    for target in range(out.shape[0]):
        out[target, :, :half] = mine
        out[target, :, half:] = small.astype(BF16)


def front_kernel(
    local_rows, core, mine, other, cosine, sine, known, slot_row,
    embedded_out, first_out, qkv_out, log_out, mixed_out, after_out, second_out, logits_out,
    slots_out, gains_out, pack, counts_out,
):
    amount = known.shape[0]
    half = 2 * D
    low = core[0] == 0
    pack[:, :half] = jnp.where(low, mine[:, :half], other[:, :half])
    pack[:, half:SMALL_AT] = jnp.where(low, other[:, :half], mine[:, :half])
    pack[:, SMALL_AT:] = mine[:, half:]
    table = mine[:, half:].astype(F32).T
    gains = table[VECTORS_AT : VECTORS_AT + 8]
    gains_out[...] = gains
    other_table = other[:, half:].astype(F32).T
    row = lax.broadcasted_iota(jnp.int32, (D, SMALL), 0)
    fold = (row % local_rows == lanes_of((D, SMALL))).astype(F32).astype(BF16)
    digits = mm(table[VECTORS_AT : VECTORS_AT + 8].astype(BF16), fold) + mm(
        other_table[VECTORS_AT : VECTORS_AT + 8].astype(BF16), fold
    )
    at = COUNTS_AT - VECTORS_AT
    counts_out[...] = digits[at : at + 1] * 256.0 + digits[at + 1 : at + 2]
    value = known[:, VALUE : VALUE + 1]
    gate = value * gains[0:1]
    embedded = gate * jax.nn.sigmoid(gate) * (value * gains[1:2])
    embedded_out[...] = embedded
    first = (embedded * inverse_rms(embedded) * gains[2:3]).astype(BF16)
    first_out[...] = first
    projected = mm(first, pack[:, : 3 * D])
    cos_rows, sin_rows = cosine[...], sine[...]
    for block in range(6):
        part = projected[:, block * 128 : (block + 1) * 128]
        part = part * cos_rows + half_swap(part) * sin_rows
        qkv_out[:, block * 128 : (block + 1) * 128] = part.astype(BF16)
    qkv_out[:, 2 * D :] = projected[:, 2 * D :].astype(BF16)
    lane = lanes_of((ROW_BLOCK, 128))
    for start in range(0, amount, ROW_BLOCK):
        keys = start + ROW_BLOCK
        allowed = allowed_block(known[...], slot_row[...], start, ROW_BLOCK, keys)
        log_rows = jnp.zeros((ROW_BLOCK, 128), F32)
        for group in range(D // 128):
            query = qkv_out[start : start + ROW_BLOCK, group * 128 : (group + 1) * 128]
            key = qkv_out[:keys, D + group * 128 : D + (group + 1) * 128]
            held = qkv_out[:keys, 2 * D + group * 128 : 2 * D + (group + 1) * 128]
            gathered = jnp.zeros((ROW_BLOCK, 128), F32)
            for head in range(128 // HD):
                own = lane // HD == head
                raw = mm_nt(jnp.where(own, query, jnp.zeros_like(query)), key) * HD ** (-0.5)
                raw = jnp.where(allowed, raw, -1e30)
                top = jnp.max(raw, -1, keepdims=True)
                exponent = jnp.exp(raw - top)
                total = jnp.sum(exponent, -1, keepdims=True)
                attention = (exponent * (1.0 / total)).astype(BF16)
                gathered = jnp.where(own, mm(attention, held), gathered)
                log_rows = jnp.where(
                    lane == group * (128 // HD) + head, top + jnp.log(total), log_rows
                )
            mixed_out[start : start + ROW_BLOCK, group * 128 : (group + 1) * 128] = (
                gathered.astype(BF16)
            )
        log_out[start : start + ROW_BLOCK, :] = log_rows
    after = embedded + mm(mixed_out[...], pack[:, 3 * D : 4 * D])
    after_out[...] = after
    second = (after * inverse_rms(after) * gains[3:4]).astype(BF16)
    second_out[...] = second
    logits_out[...] = mm(second, pack[:, SMALL_AT:])
    for expert in range(EXPERTS):
        hot = slot_rows_hot(slot_row[0:1, :], expert) + slot_rows_hot(slot_row[1:2, :], expert)
        slots_out[expert * CAP : (expert + 1) * CAP, :] = mm(hot, second).astype(BF16)


def shared_kernel(second, gate_w, lift_w, down_w, shared_out):
    gate = mm(second[...], gate_w[...])
    lift = mm(second[...], lift_w[...])
    hidden = (gate * jax.nn.sigmoid(gate) * lift).astype(BF16)
    part = mm(hidden, down_w[...])

    @pl.when(pl.program_id(0) == 0)
    def _():
        shared_out[...] = part

    @pl.when(pl.program_id(0) != 0)
    def _():
        shared_out[...] += part


def expert_kernel(rows, gate_up, down, rows_out):
    gate = mm(rows[...], gate_up[0])
    lift = mm(rows[...], gate_up[1])
    hidden = (gate * jax.nn.sigmoid(gate) * lift).astype(BF16)
    result = mm(hidden, down[...])
    if len(rows_out.shape) == 2:
        rows_out[...] = result
        return
    for source in range(rows_out.shape[0]):
        part = result[source * CAP : (source + 1) * CAP]
        top = jnp.max(jnp.abs(part), -1, keepdims=True)
        power = jnp.ceil(jnp.log2(jnp.maximum(top, 1e-30)))
        code = jnp.clip(jnp.round(part * jnp.exp2(15.0 - power)), -32767.0, 32767.0)
        rows_out[source, :CAP, :] = code.astype(jnp.int32).astype(jnp.int16)
        row = lax.broadcasted_iota(jnp.int32, (CAP, CAP), 0)
        column = lax.broadcasted_iota(jnp.int32, (CAP, CAP), 1)
        powers = jnp.sum(jnp.where(row == column, power, 0.0), 0, keepdims=True)
        powers = jnp.concatenate([powers, jnp.zeros((1, D - CAP), F32)], 1)
        rows_out[source, CAP:, :] = (
            jnp.broadcast_to(powers, (CODE_ROWS, D)).astype(jnp.int32).astype(jnp.int16)
        )


def unit_back(rows, slope, gate_w, lift_w, down_w):
    gate = mm(rows, gate_w)
    lift = mm(rows, lift_w)
    bent = jax.nn.sigmoid(gate)
    smooth = gate * bent
    hidden = (smooth * lift).astype(BF16)
    hidden_slope = mm_nt(slope, down_w)
    gate_slope = (hidden_slope * lift * (bent * (1.0 + gate * (1.0 - bent)))).astype(BF16)
    lift_slope = (hidden_slope * smooth).astype(BF16)
    return hidden, gate_slope, lift_slope


def expert_back_kernel(rows, slope, gate_up, down, rows_out, in_out, out_out):
    hidden, gate_slope, lift_slope = unit_back(
        rows[...], slope[...], gate_up[0], gate_up[1], down[...]
    )
    rows_out[...] = (mm_nt(gate_slope, gate_up[0]) + mm_nt(lift_slope, gate_up[1])).astype(BF16)

    @pl.when(pl.program_id(0) == 0)
    def _():
        in_out[...] = jnp.zeros_like(in_out)
        out_out[...] = jnp.zeros_like(out_out)

    in_out[0] += mm_tn(rows[...], gate_slope)
    in_out[1] += mm_tn(rows[...], lift_slope)
    out_out[...] += mm_tn(hidden, slope[...])


def shared_back_kernel(second, slope, gate_w, lift_w, down_w, second_out, in_out, out_out):
    hidden, gate_slope, lift_slope = unit_back(
        second[...], slope[...], gate_w[...], lift_w[...], down_w[...]
    )
    part = mm_nt(gate_slope, gate_w[...]) + mm_nt(lift_slope, lift_w[...])

    @pl.when(pl.program_id(0) == 0)
    def _():
        second_out[...] = part

    @pl.when(pl.program_id(0) != 0)
    def _():
        second_out[...] += part

    in_out[0] = mm_tn(second[...], gate_slope)
    in_out[1] = mm_tn(second[...], lift_slope)
    out_out[...] = mm_tn(hidden, slope[...])


def expert_back_split_kernel(
    core, rows, slope, gate_up, down, rows_out, in_keep, in_give, out_keep, out_give
):
    hidden, gate_slope, lift_slope = unit_back(
        rows[...], slope[...], gate_up[0], gate_up[1], down[...]
    )
    rows_out[...] = (mm_nt(gate_slope, gate_up[0]) + mm_nt(lift_slope, gate_up[1])).astype(BF16)

    @pl.when(pl.program_id(0) == 0)
    def _():
        for ref in (in_keep, in_give, out_keep, out_give):
            ref[...] = jnp.zeros_like(ref)

    half = hidden.shape[1] // 2
    low = core[0] == 0
    gate = mm_tn(rows[...], gate_slope)
    lift = mm_tn(rows[...], lift_slope)
    in_keep[...] += jnp.where(low, gate, lift)
    in_give[...] += jnp.where(low, lift, gate)
    first = mm_tn(hidden[:, :half], slope[...])
    last = mm_tn(hidden[:, half:], slope[...])
    out_keep[...] += jnp.where(low, first, last)
    out_give[...] += jnp.where(low, last, first)


def shared_back_split_kernel(
    sides, second, slope, gate_w, lift_w, down_w,
    second_out, in_keep, in_give, out_keep, out_give, out_ref,
):
    hidden, gate_slope, lift_slope = unit_back(
        second[...], slope[...], gate_w[...], lift_w[...], down_w[...]
    )
    part = mm_nt(gate_slope, gate_w[...]) + mm_nt(lift_slope, lift_w[...])

    @pl.when(pl.program_id(0) == 0)
    def _():
        second_out[...] = part

    @pl.when(pl.program_id(0) != 0)
    def _():
        second_out[...] += part

    core, cross = sides[0], sides[1]
    low = core == 0
    gate = mm_tn(second[...], gate_slope)
    lift = mm_tn(second[...], lift_slope)
    in_keep[0] = jnp.where(low, gate, lift)
    in_give[0] = jnp.where(low, lift, gate)
    out_ref[...] = mm_tn(hidden, slope[...])
    quarter = out_keep.shape[1] // 2
    for shard in range(2):
        for side in range(2):
            for ref, half in ((out_keep, core), (out_give, 1 - core)):
                piece = half * 2 + jnp.bitwise_xor(cross, side)
                start = pl.multiple_of(shard * 4 * quarter + piece * quarter, 8)
                ref[side, shard * quarter : (shard + 1) * quarter, :] = out_ref[
                    pl.ds(start, quarter), :
                ]


def coded_tile(value):
    top = jnp.max(jnp.abs(value), -1, keepdims=True)
    power = jnp.ceil(jnp.log2(jnp.maximum(top, 1e-30)))
    code = jnp.clip(jnp.round(value * jnp.exp2(15.0 - power)), -32767.0, 32767.0)
    return code, power


def encode(ref, tiles):
    lane = lanes_of(tiles[0].shape)
    powers = jnp.zeros(tiles[0].shape, F32)
    for index, tile in enumerate(tiles):
        code, power = coded_tile(tile)
        ref[:, index * 128 : (index + 1) * 128] = code.astype(jnp.int32).astype(jnp.int16)
        powers = jnp.where(lane == index, power, powers)
    ref[:, len(tiles) * 128 :] = powers.astype(jnp.int32).astype(jnp.int16)


def decode(ref):
    count = ref.shape[-1] // 128 - 1
    scale = jnp.exp2(ref[..., count * 128 :].astype(jnp.int32).astype(F32) - 15.0)
    return [
        ref[..., index * 128 : (index + 1) * 128].astype(jnp.int32).astype(F32)
        * scale[..., index : index + 1]
        for index in range(count)
    ]


def tiles_of(value):
    return [value[:, at : at + 128] for at in range(0, value.shape[1], 128)]


def fold_kernel(in_keep, in_other, out_keep, out_other, keep, give):
    wide = in_keep.shape[2]
    keep[:, :wide] = in_keep[0] + in_other[0]
    keep[:, wide:] = out_keep[0] + out_other[0]
    encode(give, tiles_of(in_keep[1] + in_other[1]) + tiles_of(out_keep[1] + out_other[1]))


def add_code_kernel(keep, other, code):
    encode(code, [mine + theirs for mine, theirs in zip(tiles_of(keep[...]), decode(other))])


def shard_sum_kernel(codes, total):
    for index, tile in enumerate(decode(codes)):
        total[:, index * 128 : (index + 1) * 128] = jnp.sum(tile, 0)


def expert_code_kernel(in_keep, in_other, out_keep, out_other, code):
    encode(code, tiles_of(in_keep[...] + in_other[...]) + tiles_of(out_keep[...] + out_other[...]))


def expert_sum_kernel(mine, other, in_total, out_total):
    split = in_total.shape[1] // 128
    for index, (left, right) in enumerate(zip(decode(mine), decode(other))):
        ref, at = (in_total, index) if index < split else (out_total, index - split)
        ref[:, at * 128 : (at + 1) * 128] = left + right


def last_code_kernel(core, keep, other, code):
    tiles = tiles_of(keep[...] + other[...])
    rough, power = coded_tile(tiles[5])
    tiles[6] = jnp.where(core[0] == 1, tiles[5] - rough * jnp.exp2(power - 15.0), tiles[6])
    encode(code, tiles)


def last_sum_kernel(core, codes, total):
    tiles = decode(codes)
    high = core[0] == 1
    fine = tiles[6]
    tiles[5] = jnp.where(high, tiles[5] + fine, tiles[5])
    tiles[6] = jnp.where(high, 0.0, fine)
    for index, tile in enumerate(tiles):
        total[:, index * 128 : (index + 1) * 128] = jnp.sum(tile, 0)


def middle_kernel(
    returned, known, slot_row, after, shared, logits, small, gains, target, ahead, weighting,
    mixer_out, shared_slope_out, slots_out, logits_slope_out, small_out, gain_out, sums_out,
):
    amount = after.shape[0]
    lane = lanes_of((amount, SMALL))
    table = known[...]
    integers = table[:, :8].astype(jnp.int32)
    chosen = [
        (lane == integers[:, CHOICE + k : CHOICE + k + 1]).astype(F32) for k in range(2)
    ]
    place = lax.broadcasted_iota(jnp.int32, (amount, SMALL), 0)
    usable = (place + 1 + ahead[...] < integers[:, FINISH : FINISH + 1]).astype(F32)
    logit = logits[...]
    routed = lane < EXPERTS
    top = jnp.max(jnp.where(routed, logit, -1e30), -1, keepdims=True)
    exponent = jnp.where(routed, jnp.exp(jnp.where(routed, logit - top, 0.0)), 0.0)
    probs = exponent / jnp.sum(exponent, -1, keepdims=True)
    gates = [jnp.sum(chosen[k] * probs, -1, keepdims=True) for k in range(2)]
    shared_gate = jax.nn.sigmoid(
        jnp.sum(jnp.where(lane == EXPERTS, logit, 0.0), -1, keepdims=True)
    )
    picked = [jnp.zeros((amount, D), F32), jnp.zeros((amount, D), F32)]
    for expert in range(EXPERTS):
        if len(returned.shape) == 2:
            rows = returned[expert * CAP : (expert + 1) * CAP, :]
            scale = 1.0
        else:
            rows = returned[expert, :CAP, :].astype(jnp.int32).astype(F32)
            powers = returned[expert, CAP:, :].astype(jnp.int32).astype(F32)
            scale = jnp.exp2(powers[0:1, :CAP] - 15.0)
        high = rows.astype(BF16)
        rest = (rows - high.astype(F32)).astype(BF16)
        for k in range(2):
            slot = expert * CAP + lax.broadcasted_iota(jnp.int32, (amount, CAP), 1)
            hot = jnp.where(integers[:, SLOT + k : SLOT + k + 1] == slot, scale, 0.0).astype(BF16)
            picked[k] = picked[k] + (mm(hot, high) + mm(hot, rest))
    mixer = (
        after[...] + shared_gate * shared[...] + (gates[0] * picked[0] + gates[1] * picked[1])
    )
    inverse = inverse_rms(mixer)
    gain = gains[4:5]
    third = (mixer * inverse * gain).astype(BF16)
    residue = mm(third, small[...]) - target[...]
    size = jnp.abs(residue)
    cost = (
        jnp.where(
            size <= KINK_THRESHOLD,
            0.5 * residue * residue,
            KINK_THRESHOLD * (size - 0.5 * KINK_THRESHOLD),
        )
        * usable
    )
    domain_hot = (lane == integers[:, DOMAIN : DOMAIN + 1]).astype(F32)
    sums_out[...] = jnp.sum(domain_hot * jnp.sum(cost, -1, keepdims=True), 0, keepdims=True)
    weight = jnp.sum(domain_hot * weighting[...], -1, keepdims=True)
    slope = (
        jnp.clip(residue, -KINK_THRESHOLD, KINK_THRESHOLD) * usable * weight
    ).astype(BF16)
    small_out[...] = mm_tn(third, slope)
    mixer_slope, gain_slope = rms_back(mixer, inverse, gain, mm_nt(slope, small[...]))
    gain_out[...] = gain_slope
    mixer_out[...] = mixer_slope
    shared_slope_out[...] = (shared_gate * mixer_slope).astype(BF16)
    gate_slope = jnp.sum(mixer_slope * shared[...], -1, keepdims=True)
    probs_slope = chosen[0] * jnp.sum(mixer_slope * picked[0], -1, keepdims=True) + chosen[
        1
    ] * jnp.sum(mixer_slope * picked[1], -1, keepdims=True)
    inner = jnp.sum(probs * probs_slope, -1, keepdims=True)
    logits_slope_out[...] = jnp.where(
        routed,
        probs * (probs_slope - inner),
        jnp.where(lane == EXPERTS, gate_slope * (shared_gate * (1.0 - shared_gate)), 0.0),
    ).astype(BF16)
    slopes = [(gates[k] * mixer_slope).astype(BF16) for k in range(2)]
    for expert in range(EXPERTS):
        slots_out[expert * CAP : (expert + 1) * CAP, :] = (
            mm(slot_rows_hot(slot_row[0:1, :], expert), slopes[0])
            + mm(slot_rows_hot(slot_row[1:2, :], expert), slopes[1])
        ).astype(BF16)


def attend_back_kernel(
    returned, known, second_slope, logits_slope, small, after, mixer_slope, gains, mixed, second,
    output_w, small_before,
    attend_out, mixed_out, output_out, gain_out, small_out,
):
    slope = second_slope[...] + mm_nt(logits_slope[...], small[...])
    for expert in range(EXPERTS):
        hot = slot_cols_hot(known[:, 0:1], expert) + slot_cols_hot(known[:, 1:2], expert)
        slope = slope + mm(hot, returned[expert * CAP : (expert + 1) * CAP, :])
    after_rows = after[...]
    part, gain_slope = rms_back(after_rows, inverse_rms(after_rows), gains[3:4], slope)
    gain_out[...] = gain_slope
    attend = mixer_slope[...] + part
    attend_out[...] = attend
    low = attend.astype(BF16)
    output_out[...] = mm_tn(mixed[...], low)
    mixed_out[...] = mm_nt(low, output_w[...]).astype(BF16)
    small_out[...] = small_before[...] + mm_tn(second[...], logits_slope[...])


def front_back_kernel(
    fast, core, mixed_slope, qkv, log_total, known, rows_table, cosine, sine, first, embedded,
    gains, input_w, attend_slope, small_before, gain_two, gain_three, output_before,
    keep_out, give_out,
    pack_out, query_acc, key_acc, held_acc, slope_ref,
):
    amount = first.shape[0]
    key_acc[...] = jnp.zeros_like(key_acc)
    held_acc[...] = jnp.zeros_like(held_acc)
    lane = lanes_of((ROW_BLOCK, 128))
    lane_all = lanes_of((amount, 128))
    for start in range(0, amount, ROW_BLOCK):
        keys = start + ROW_BLOCK
        here = slice(start, start + ROW_BLOCK)
        allowed = allowed_block(known[...], rows_table[...], start, ROW_BLOCK, keys)
        for group in range(D // 128):
            wide = slice(group * 128, (group + 1) * 128)
            query = qkv[here, group * 128 : (group + 1) * 128]
            key = qkv[:keys, D + group * 128 : D + (group + 1) * 128]
            held = qkv[:keys, 2 * D + group * 128 : 2 * D + (group + 1) * 128]
            out_slope = mixed_slope[here, wide]
            query_sum = jnp.zeros((ROW_BLOCK, 128), F32)
            key_sum = jnp.zeros((keys, 128), F32)
            held_sum = jnp.zeros((keys, 128), F32)
            for head in range(128 // HD):
                own = lane // HD == head
                own_query = jnp.where(own, query, jnp.zeros_like(query))
                own_slope = jnp.where(own, out_slope, jnp.zeros_like(out_slope))
                own_key = jnp.where(lane_all[:keys] // HD == head, key, jnp.zeros_like(key))
                at = group * (128 // HD) + head
                raw = mm_nt(own_query, key) * HD ** (-0.5)
                probs = jnp.exp(jnp.where(allowed, raw - log_total[here, at : at + 1], -1e30))
                held_sum = held_sum + mm_tn(probs.astype(BF16), own_slope)
                probs_slope = mm_nt(own_slope, held)
                inner = jnp.sum(probs_slope * probs, -1, keepdims=True)
                raw_slope = (probs * (probs_slope - inner)).astype(BF16)
                query_sum = query_sum + mm(raw_slope, own_key)
                key_sum = key_sum + mm_tn(raw_slope, own_query)
            query_acc[here, wide] = query_sum
            key_acc[:keys, wide] += key_sum
            held_acc[:keys, wide] += held_sum
    cos_rows, sin_rows = cosine[...], sine[...]
    for block in range(3):
        wide = slice(block * 128, (block + 1) * 128)
        for base, acc in ((0, query_acc), (D, key_acc)):
            part = acc[:, wide] * HD ** (-0.5)
            part = part * cos_rows + half_swap(part * sin_rows)
            slope_ref[:, base + block * 128 : base + (block + 1) * 128] = part.astype(BF16)
    slope_ref[:, 2 * D :] = held_acc[...].astype(BF16)
    projected_slope = slope_ref[...]
    pack_out[:, : 3 * D] = mm_tn(first[...], projected_slope)
    pack_out[:, 3 * D : SMALL_AT] = output_before[...]
    first_slope = mm_nt(projected_slope, input_w[...])
    rows = embedded[...]
    part, gain_one = rms_back(rows, inverse_rms(rows), gains[2:3], first_slope)
    slope = attend_slope[...] + part
    value = known[:, VALUE : VALUE + 1]
    gate = value * gains[0:1]
    bent = jax.nn.sigmoid(gate)
    gate_gradient = jnp.sum(
        slope * (value * gains[1:2]) * (bent * (1.0 + gate * (1.0 - bent))) * value,
        0,
        keepdims=True,
    )
    lift_gradient = jnp.sum(slope * (gate * bent) * value, 0, keepdims=True)
    row = lax.broadcasted_iota(jnp.int32, (128, D), 0)
    table = jnp.zeros((128, D), F32)
    for offset, piece in enumerate(
        (gate_gradient, lift_gradient, gain_one, gain_two[...], gain_three[...])
    ):
        table = jnp.where(row == VECTORS_AT + offset, piece, table)
    pack_out[:, SMALL_AT : SMALL_AT + SMALL] = small_before[...] + table.T
    if not fast:
        keep_out[...] = pack_out[:, : keep_out.shape[1]]
        give_out[...] = jnp.zeros_like(give_out)
        return
    pack_out[:, SMALL_AT + SMALL :] = jnp.zeros_like(pack_out[:, SMALL_AT + SMALL :])
    half = keep_out.shape[1]
    keep_out[...] = pack_out[:, pl.ds(pl.multiple_of(core[0] * half, 128), half)]
    give_out[...] = pack_out[:, pl.ds(pl.multiple_of((1 - core[0]) * half, 128), half)]


def lamb_direction(master, gradient, mean, square, factor):
    clipped = gradient * factor
    mean_next = BETA_ONE * mean + (1.0 - BETA_ONE) * clipped
    square_next = BETA_TWO * square + (1.0 - BETA_TWO) * clipped * clipped
    direction = (
        mean_next
        / (1.0 - BETA_ONE**STEP)
        / (jnp.sqrt(square_next / (1.0 - BETA_TWO**STEP)) + EPS_ADAM)
        + DECAY * master
    )
    return mean_next, square_next, direction


def whole(array):
    shape = array.shape
    return pl.BlockSpec(shape, lambda *unused: (0,) * len(shape))


def params(limit=VMEM):
    return pltpu.CompilerParams(vmem_limit_bytes=limit)


def cost(flops, size):
    return pl.CostEstimate(
        flops=int(flops / 1000), bytes_accessed=int(size / 1000), transcendentals=0
    )


def columns(array, width, at):
    return (array, pl.BlockSpec((array.shape[0], width), lambda *unused: (0, at)))


def simple_call(kernel, outs, args, flops, scratch=()):
    pairs = [a if isinstance(a, tuple) else (a, whole(a)) for a in args]
    args = [a for a, spec in pairs]
    size = sum(a.size * a.dtype.itemsize for a in list(args) + list(outs))
    return pl.pallas_call(
        kernel,
        out_shape=outs,
        in_specs=[spec for a, spec in pairs],
        out_specs=[whole(a) for a in outs],
        scratch_shapes=list(scratch),
        grid=(1,),
        compiler_params=params(),
        cost_estimate=cost(flops, size),
    )(*args)


def out(shape, dtype=F32):
    return jax.ShapeDtypeStruct(shape, dtype)


def flip(value, axis_name, bit):
    count = lax.axis_size(axis_name)
    return lax.ppermute(value, axis_name, [(i, i ^ bit) for i in range(count)])


def bits_of(axis_name):
    count = lax.axis_size(axis_name)
    return [1 << i for i in range(count.bit_length() - 1)]


def sum_small(value, axes):
    for axis_name in axes:
        for bit in bits_of(axis_name):
            value = value + flip(value, axis_name, bit)
    return value


def halves(value, axis, take_high):
    size = value.shape[axis] // 2
    side = take_high.astype(jnp.int32)
    return (
        lax.dynamic_slice_in_dim(value, side * size, size, axis),
        lax.dynamic_slice_in_dim(value, (1 - side) * size, size, axis),
    )


def scatter_sum(value, axis, bits):
    for bit in bits:
        side = (lax.axis_index("dp") & bit) != 0
        keep, give = halves(value, axis, side)
        value = keep + flip(give, "dp", bit)
    return value


def join(value, axis, bits):
    for bit in reversed(bits):
        side = (lax.axis_index("dp") & bit) != 0
        other = flip(value, "dp", bit)
        value = jnp.concatenate(
            [jnp.where(side, other, value), jnp.where(side, value, other)], axis
        )
    return value


def ready(value, *others):
    return lax.optimization_barrier((value, *others))[0]


def exchange(value):
    return lax.all_to_all(value, "expert", split_axis=0, concat_axis=0, tiled=True)


def spread(value):
    count = lax.axis_size("expert")
    return exchange(jnp.broadcast_to(value[None], (count, *value.shape)))


def expert_scatter(value):
    return jnp.sum(exchange(value), 0)


def squares_kernel(weights, sums, *refs):
    total = jnp.zeros((1, 1), F32)
    for weight, ref in zip(weights, refs[:-1]):
        piece = ref[...]
        part = jnp.sum(jnp.sum(piece * piece, -1, keepdims=True), 0, keepdims=True)
        total = total + part * weight
    refs[-1][0:1, :] = jnp.broadcast_to(total, (1, 128))
    refs[-1][1:2, :] = sums[...]


def sum_all(value):
    while value.ndim > 2:
        value = jnp.sum(value, 0)
    return jnp.sum(jnp.sum(value, 0, keepdims=True), -1, keepdims=True)


TILED = (4, 7, 8)


def tile_spec(index, shape, steps):
    if index == 7:
        return pl.BlockSpec((2, D // steps, shape[2]), lambda i: (0, i, 0))
    if index == 8:
        return pl.BlockSpec((shape[0] // steps, D), lambda i: (i, 0))
    if index == 4 and len(shape) == 3:
        half = steps // 2
        return pl.BlockSpec((1, shape[1], shape[2] // half), lambda i: (i // half, 0, i % half))
    if index == 4:
        return pl.BlockSpec((shape[0], shape[1] // steps), lambda i: (0, i))
    return pl.BlockSpec(shape, lambda i: (0,) * len(shape))


def tile_specs(arrays, steps):
    return [tile_spec(index, array.shape, steps) for index, array in enumerate(arrays)]


def prepare_kernel(count, *refs):
    masters = refs[:count]
    gate_up_low, down_low, totals = refs[count:]
    step = pl.program_id(0)
    gate_up_low[...] = masters[7][...].astype(BF16)
    down_low[...] = masters[8][...].astype(BF16)

    @pl.when(step == 0)
    def _():
        totals[...] = jnp.zeros_like(totals)

    def add(index):
        master = masters[index][...]
        totals[index : index + 1, :] += jnp.broadcast_to(sum_all(master * master), (1, 128))

    for index in TILED:
        add(index)

    @pl.when(step == 0)
    def _():
        for index in range(count):
            if index not in TILED:
                add(index)


def picked_piece(pieces, index, part):
    value = part(pieces[0])
    for other in range(1, len(pieces)):
        value = jnp.where(index == other, part(pieces[other]), value)
    return value


def moments_kernel(fast, count, small_end, sides, square_ref, *refs):
    masters, means, squares = (refs[k * count : (k + 1) * count] for k in range(3))
    results = refs[-3 * count - 1 :]
    pieces = refs[3 * count : -3 * count - 1]
    totals = results[-1]
    factor = jnp.minimum(1.0, CLIP / jnp.sqrt(square_ref[0:1, 0:1]))
    step = pl.program_id(0)

    @pl.when(step == 0)
    def _():
        totals[...] = jnp.zeros_like(totals)

    def last_rows(start, stop):
        if not fast:
            return pieces[0][:, start:stop]
        low = sides[0] == 0
        half = pieces[0].shape[1]
        parts = []
        for side in range(2):
            begin, end = max(start, side * half), min(stop, (side + 1) * half)
            if begin < end:
                begin, end = begin - side * half, end - side * half
                mine, other = pieces[0][:, begin:end], pieces[1][:, begin:end]
                parts.append(jnp.where(low == (side == 0), mine, other))
        return jnp.concatenate(parts, 1) if len(parts) > 1 else parts[0]

    def gradient_of(index):
        if index in (0, 3):
            table = last_rows(SMALL_AT, SMALL_AT + SMALL).T
            return table[VECTORS_AT : VECTORS_AT + 5] if index == 0 else table[:HORIZON_AT]
        if index == 6:
            return last_rows(SMALL_AT, SMALL_AT + SMALL)[:, HORIZON_AT:small_end]
        if index == 1:
            return last_rows(0, 3 * D)
        if index == 2:
            return last_rows(3 * D, SMALL_AT)
        if not fast:
            return pieces[{4: 1, 5: 2, 7: 3, 8: 4}[index]][...]
        low = sides[0] == 0
        me = sides[0] * 2 + sides[1]
        shared = pieces[2:6]
        wide = 2 * FFS // 4
        if index == 4:
            return picked_piece(
                shared, jnp.bitwise_xor(step, me), lambda ref: ref[:, :wide]
            )
        if index == 5:
            return jnp.concatenate(
                [
                    picked_piece(shared, jnp.bitwise_xor(piece, me), lambda ref: ref[:, wide:])
                    for piece in range(4)
                ],
                0,
            )
        if index == 7:
            mine, other = pieces[6][...], pieces[7][...]
            return jnp.stack([jnp.where(low, mine, other), jnp.where(low, other, mine)])
        return jnp.where(step // 2 == sides[0], pieces[8][...], pieces[9][...])

    def update(index):
        gradient = gradient_of(index)
        if index == 4 and gradient.ndim == 3:
            gradient = gradient[0]
        scale = factor.reshape(1, 1, 1) if gradient.ndim == 3 else factor
        mean_next, square_next, direction = lamb_direction(
            masters[index][...], gradient, means[index][...], squares[index][...], scale
        )
        results[index][...] = direction
        results[count + index][...] = mean_next
        results[2 * count + index][...] = square_next
        totals[index : index + 1, :] += jnp.broadcast_to(sum_all(direction * direction), (1, 128))

    for index in TILED:
        update(index)
    for index in range(count):
        if index not in TILED:
            pl.when(step == min(index, 3))(functools.partial(update, index))


def step_kernel(count, totals, master_totals, *refs):
    masters, directions = refs[:count], refs[count : 2 * count]
    results = refs[2 * count :]
    step = pl.program_id(0)

    def update(index):
        ratio = jnp.sqrt(master_totals[index : index + 1, 0:1]) / jnp.sqrt(
            totals[index : index + 1, 0:1]
        )
        ratio = RATE * ratio
        if len(masters[index].shape) == 3:
            ratio = ratio.reshape(1, 1, 1)
        results[index][...] = masters[index][...] - ratio * directions[index][...]

    for index in TILED:
        update(index)
    for index in range(count):
        if index not in TILED:
            pl.when(step == min(index, 3))(functools.partial(update, index))


def shards(
    points,
    experts,
    lengths,
    domains,
    domain_weights,
    vectors,
    attend_input,
    attend_output,
    router,
    shared_input,
    shared_output,
    horizon,
    expert_input,
    expert_output,
    mean_vectors,
    mean_attend_input,
    mean_attend_output,
    mean_router,
    mean_shared_input,
    mean_shared_output,
    mean_horizon,
    mean_expert_input,
    mean_expert_output,
    square_vectors,
    square_attend_input,
    square_attend_output,
    square_router,
    square_shared_input,
    square_shared_output,
    square_horizon,
    square_expert_input,
    square_expert_output,
):
    expert_count = lax.axis_size("expert")
    group_size = expert_count // EXPERTS
    dp_count = lax.axis_size("dp")
    dp_bits = bits_of("dp")
    amount = points.shape[0]
    local_rows = attend_input.shape[0]
    head_columns = horizon.shape[1]
    hidden_local = expert_output.shape[0]
    small_end = HORIZON_AT + head_columns
    fast = (
        group_size == 1 and dp_count == 4 and local_rows % 16 == 0 and hidden_local == 2 * D
    )
    core = lax.axis_index("dp") & 1
    sides = jnp.stack([core, lax.axis_index("dp") >> 1]).astype(jnp.int32)
    in_smem = pl.BlockSpec(memory_space=pltpu.SMEM)
    in_vmem = pl.BlockSpec(memory_space=pltpu.VMEM)
    ahead_row = jnp.pad(
        jnp.asarray(ahead_table())[None], ((0, 0), (0, SMALL - head_columns)), constant_values=1 << 20
    )
    packed = pl.pallas_call(
        functools.partial(pack_kernel, small_end),
        out_shape=out((expert_count, local_rows, 2 * D + SMALL), BF16),
        in_specs=[*[in_smem] * 3, *[in_vmem] * 6],
        out_specs=in_vmem,
        compiler_params=params(),
        cost_estimate=cost(1e6, 1e6),
    )(sides, lengths, domains, ahead_row, attend_input, attend_output, router.T, horizon, vectors)
    gathered = exchange(packed)

    def state(group):
        return tuple(a.T if index == 3 else a for index, a in enumerate(group))

    masters = state(
        (
            vectors, attend_input, attend_output, router, shared_input, shared_output, horizon,
            expert_input, expert_output,
        )
    )
    first_moments = state(
        (
            mean_vectors, mean_attend_input, mean_attend_output, mean_router, mean_shared_input,
            mean_shared_output, mean_horizon, mean_expert_input, mean_expert_output,
        )
    )
    second_moments = state(
        (
            square_vectors, square_attend_input, square_attend_output, square_router,
            square_shared_input, square_shared_output, square_horizon, square_expert_input,
            square_expert_output,
        )
    )
    count = len(masters)
    steps = 4
    gate_up_low, down_low, master_squares = pl.pallas_call(
        functools.partial(prepare_kernel, count),
        out_shape=[
            out(expert_input.shape, BF16), out(expert_output.shape, BF16), out((16, 128)),
        ],
        grid=(steps,),
        in_specs=tile_specs(masters, steps),
        out_specs=[
            tile_spec(7, expert_input.shape, steps),
            tile_spec(8, expert_output.shape, steps),
            whole(out((16, 128))),
        ],
        compiler_params=params(),
        cost_estimate=cost(3e6, 7e6),
    )(*masters)
    frequency = jnp.exp(-jnp.log(10000.0) * jnp.arange(HD // 2, dtype=F32) / (HD // 2))
    cosine, sine, known, rows_table = pl.pallas_call(
        tables_kernel,
        out_shape=[out((amount, 128)), out((amount, 128)), out((amount, 128)), out((8, amount))],
        in_specs=[*[in_smem] * 2, *[in_vmem] * 3],
        out_specs=[in_vmem] * 4,
        compiler_params=params(),
        cost_estimate=cost(1e6, 1e6),
    )(
        lengths,
        domains,
        jnp.tile(frequency, 128 // (HD // 2))[None],
        points.reshape(1, amount),
        experts.T,
    )
    folds = FFS // D
    shared_piece = jnp.concatenate(
        [
            shared_input,
            shared_output.reshape(folds, local_rows, D).swapaxes(0, 1).reshape(local_rows, -1),
        ],
        1,
    ).astype(BF16)
    for bit in dp_bits:
        shared_piece, unused = halves(shared_piece, 1, (lax.axis_index("dp") & bit) != 0)
    gathered = ready(
        gathered, known, gate_up_low, down_low, master_squares, shared_piece
    ).reshape(D, -1)
    gathered_other = flip(gathered, "dp", 1)
    shared_pieces = spread(ready(shared_piece, gathered))
    (
        embedded, first, qkv, log_total, mixed, after, second, logits, slots, gains, pack,
        counts_half,
    ) = simple_call(
        functools.partial(front_kernel, local_rows),
        [
            out((amount, D)), out((amount, D), BF16), out((amount, 3 * D), BF16),
            out((amount, 128)), out((amount, D), BF16), out((amount, D)),
            out((amount, D), BF16), out((amount, SMALL)), out((EXPERTS * CAP, D), BF16),
            out((8, D)), out((D, SMALL_AT + SMALL), BF16), out((1, SMALL)),
        ],
        [(sides, in_smem), gathered, gathered_other, cosine, sine, known, rows_table],
        8e9,
    )

    def to_devices(rows):
        rows = rows.reshape(EXPERTS, CAP, D)
        return exchange(jnp.repeat(rows, group_size, 0)).reshape(-1, D)

    def to_points(rows):
        rows = exchange(rows.reshape(expert_count, CAP, D))
        if group_size > 1:
            kind = rows.dtype
            rows = rows.reshape(EXPERTS, group_size, CAP, D).astype(F32)
            rows = jnp.sum(rows, 1).astype(kind)
        return rows.reshape(-1, D)

    arrived = to_devices(ready(slots, shared_pieces))
    first_bit = dp_bits[-1]
    shared_pieces = ready(shared_pieces, slots)
    shared_other = flip(shared_pieces, "dp", first_bit)
    arrived = ready(arrived, shared_other)
    block = 512
    total_rows = arrived.shape[0]
    coded = group_size == 1
    sources = block // CAP
    expert_rows = pl.pallas_call(
        expert_kernel,
        out_shape=(
            out((EXPERTS, CAP + CODE_ROWS, D), jnp.int16) if coded else out((total_rows, D))
        ),
        grid=(total_rows // block,),
        in_specs=[
            pl.BlockSpec((block, D), lambda i: (i, 0)), whole(gate_up_low), whole(down_low),
        ],
        out_specs=(
            pl.BlockSpec((sources, CAP + CODE_ROWS, D), lambda i: (i, 0, 0))
            if coded
            else pl.BlockSpec((block, D), lambda i: (i, 0))
        ),
        compiler_params=params(),
        cost_estimate=cost(total_rows * D * 3 * hidden_local * 2, 7e6),
    )(arrived, gate_up_low, down_low)
    returned = exchange(expert_rows) if coded else to_points(expert_rows)
    shared_pieces = ready(shared_pieces, expert_rows)
    side = (lax.axis_index("dp") & first_bit) != 0
    shared_pack = jnp.concatenate(
        [
            jnp.where(side, shared_other, shared_pieces),
            jnp.where(side, shared_pieces, shared_other),
        ],
        2,
    )
    shared_pack = join(shared_pack, 2, dp_bits[:-1])
    shin_low = shared_pack[:, :, : 2 * FFS].reshape(D, -1)
    shout_low = (
        shared_pack[:, :, 2 * FFS :]
        .reshape(expert_count, local_rows, folds, D)
        .swapaxes(1, 2)
        .reshape(FFS, D)
    )
    chunk = 512
    chunks = FFS // chunk
    shared = pl.pallas_call(
        shared_kernel,
        out_shape=out((amount, D)),
        grid=(chunks,),
        in_specs=[
            whole(second),
            pl.BlockSpec((D, chunk), lambda i: (0, i)),
            pl.BlockSpec((D, chunk), lambda i: (0, i + chunks)),
            pl.BlockSpec((chunk, D), lambda i: (i, 0)),
        ],
        out_specs=pl.BlockSpec((amount, D), lambda i: (0, 0)),
        compiler_params=params(),
        cost_estimate=cost(amount * D * 3 * FFS * 2, 5e6),
    )(second, shin_low, shin_low, shout_low)
    counts = ready(counts_half, expert_rows)
    for bit in dp_bits[1:]:
        counts = counts + flip(counts, "dp", bit)
    weighting = jnp.pad(domain_weights, (0, SMALL - DOMAINS))[None] / jnp.maximum(counts, 1.0)
    side_pad = ((0, 0), (HORIZON_AT, SMALL - small_end))
    target = jnp.pad(target_columns(points), side_pad)
    ahead_small = jnp.pad(
        jnp.asarray(ahead_table())[None], ((0, 0), side_pad[1]), constant_values=1 << 20
    )
    small_low = columns(pack, SMALL, SMALL_AT // SMALL)
    (
        mixer_slope, shared_slope, slope_slots, logits_slope, small_head, gain_three, local_sums,
    ) = simple_call(
        middle_kernel,
        [
            out((amount, D)), out((amount, D), BF16), out((EXPERTS * CAP, D), BF16),
            out((amount, SMALL), BF16), out((D, SMALL)), out((1, D)), out((1, SMALL)),
        ],
        [
            returned, known, rows_table, after, shared, logits, small_low, gains, target,
            ahead_small, weighting,
        ],
        7e9,
    )
    received = to_devices(slope_slots)
    chunk = D
    chunks = FFS // chunk
    back_in = [
        pl.BlockSpec((amount, D), lambda i, *unused: (0, 0)),
        pl.BlockSpec((amount, D), lambda i, *unused: (0, 0)),
        pl.BlockSpec((D, chunk), lambda i, *unused: (0, i)),
        pl.BlockSpec((D, chunk), lambda i, *unused: (0, i + chunks)),
        pl.BlockSpec((chunk, D), lambda i, *unused: (i, 0)),
    ]
    second_spec = pl.BlockSpec((amount, D), lambda i, *unused: (0, 0))
    back_args = (second, shared_slope, shin_low, shin_low, shout_low)
    back_cost = cost(amount * D * 8 * FFS * 2, 14e6)
    if fast:
        in_spec = pl.BlockSpec(
            (1, D, chunk), lambda i, sides: (jnp.bitwise_xor(i // 2, sides[1]), 0, i % 2)
        )
        out_spec = pl.BlockSpec((2, D // chunks, D), lambda i, sides: (0, i, 0))
        shared_second_slope, in_keep, in_give, out_keep, out_give = pl.pallas_call(
            shared_back_split_kernel,
            out_shape=[
                out((amount, D)), out((2, D, FFS // 2)), out((2, D, FFS // 2)), out((2, D, D)),
                out((2, D, D)),
            ],
            grid_spec=pltpu.PrefetchScalarGridSpec(
                num_scalar_prefetch=1,
                grid=(chunks,),
                in_specs=back_in,
                out_specs=[second_spec, in_spec, in_spec, out_spec, out_spec],
                scratch_shapes=[pltpu.VMEM((chunk, D), F32)],
            ),
            compiler_params=params(),
            cost_estimate=back_cost,
        )(sides, *back_args)
    else:
        shared_second_slope, grad_shin, grad_shout = pl.pallas_call(
            shared_back_kernel,
            out_shape=[out((amount, D)), out((2, D, FFS)), out((FFS, D))],
            grid=(chunks,),
            in_specs=back_in,
            out_specs=[
                second_spec,
                pl.BlockSpec((2, D, chunk), lambda i: (0, 0, i)),
                pl.BlockSpec((chunk, D), lambda i: (i, 0)),
            ],
            compiler_params=params(),
            cost_estimate=back_cost,
        )(*back_args)
    if fast:
        in_other, out_other = flip(in_give, "dp", 1), flip(out_give, "dp", 1)
        fold_in = pl.BlockSpec((2, D // 4, FFS // 2), lambda i: (0, i, 0))
        fold_out = pl.BlockSpec((2, D // 4, D), lambda i: (0, i, 0))
        wide = FFS // 2 + D
        fold_to = pl.BlockSpec((D // 4, wide), lambda i: (i, 0))
        code_to = pl.BlockSpec((D // 4, wide + 128), lambda i: (i, 0))
        shared_keep, shared_give = pl.pallas_call(
            fold_kernel,
            out_shape=[out((D, wide)), out((D, wide + 128), jnp.int16)],
            grid=(4,),
            in_specs=[fold_in, fold_in, fold_out, fold_out],
            out_specs=[fold_to, code_to],
            compiler_params=params(),
            cost_estimate=cost(2e6, 10e6),
        )(in_keep, in_other, out_keep, out_other)
        shared_other = flip(shared_give, "dp", 2)
        received = ready(received, shared_second_slope, shared_give)
    else:
        received = ready(received, shared_second_slope)
    row_spec = pl.BlockSpec((block, D), lambda i: (i, 0))
    expert_cost = cost(total_rows * D * 8 * hidden_local * 2, 10e6)
    weight_specs = [whole(gate_up_low), whole(down_low)]
    if fast:
        half_shapes = [out((D, hidden_local))] * 2 + [out((hidden_local // 2, D))] * 2
        grad_rows, expert_in, expert_in_give, expert_out, expert_out_give = pl.pallas_call(
            expert_back_split_kernel,
            out_shape=[out((total_rows, D), BF16), *half_shapes],
            grid=(total_rows // block,),
            in_specs=[in_smem, row_spec, row_spec, *weight_specs],
            out_specs=[row_spec, *[whole(a) for a in half_shapes]],
            compiler_params=params(),
            cost_estimate=expert_cost,
        )(sides, arrived, received, gate_up_low, down_low)
    else:
        grad_rows, grad_expert_in, grad_expert_out = pl.pallas_call(
            expert_back_kernel,
            out_shape=[
                out((total_rows, D), BF16), out((2, D, hidden_local)), out((hidden_local, D)),
            ],
            grid=(total_rows // block,),
            in_specs=[row_spec, row_spec, *weight_specs],
            out_specs=[
                row_spec,
                pl.BlockSpec((2, D, hidden_local), lambda i: (0, 0, 0)),
                pl.BlockSpec((hidden_local, D), lambda i: (0, 0)),
            ],
            compiler_params=params(),
            cost_estimate=expert_cost,
        )(arrived, received, gate_up_low, down_low)
    routed_back = to_points(grad_rows)
    if fast:
        shared_code = pl.pallas_call(
            add_code_kernel,
            out_shape=out((D, wide + 128), jnp.int16),
            grid=(4,),
            in_specs=[fold_to, code_to],
            out_specs=code_to,
            compiler_params=params(),
            cost_estimate=cost(2e6, 4e6),
        )(shared_keep, shared_other)
        expert_in_other = flip(expert_in_give, "dp", 1)
        expert_out_other = flip(expert_out_give, "dp", 1)
        sum_in = pl.BlockSpec((D // 4, hidden_local), lambda i: (i, 0))
        sum_out = pl.BlockSpec((D // 4, D), lambda i: (i, 0))
        expert_code = pl.pallas_call(
            expert_code_kernel,
            out_shape=out((D, wide + 128), jnp.int16),
            grid=(4,),
            in_specs=[sum_in, sum_in, sum_out, sum_out],
            out_specs=code_to,
            compiler_params=params(),
            cost_estimate=cost(2e6, 8e6),
        )(expert_in, expert_in_other, expert_out, expert_out_other)
        sums = local_sums + flip(local_sums, "dp", 2)
        routed_plain = routed_back
        routed_back = ready(routed_back, shared_code, expert_code, sums)
    attend_slope, mixed_slope, grad_output, gain_two, small_routed = simple_call(
        attend_back_kernel,
        [
            out((amount, D)), out((amount, D), BF16), out((D, D)), out((1, D)), out((D, SMALL)),
        ],
        [
            routed_back, known, shared_second_slope, logits_slope, small_low, after,
            mixer_slope, gains, mixed, second, columns(pack, D, 3), small_head,
        ],
        2e9,
    )
    pack_columns = SMALL_AT + SMALL
    half_columns = SMALL_AT // 2 + SMALL
    last_keep, last_give = simple_call(
        functools.partial(front_back_kernel, fast),
        [
            out((D, half_columns if fast else pack_columns)),
            out((D, half_columns) if fast else (8, 128)),
        ],
        [
            (sides, in_smem), mixed_slope, qkv, log_total, known, rows_table, cosine, sine, first,
            embedded, gains, columns(pack, 3 * D, 0), attend_slope, small_routed, gain_two,
            gain_three, grad_output,
        ],
        16e9,
        [
            pltpu.VMEM((D, 2 * half_columns), F32),
            pltpu.VMEM((amount, D), F32),
            pltpu.VMEM((amount, D), F32),
            pltpu.VMEM((amount, D), F32),
            pltpu.VMEM((amount, 3 * D), BF16),
        ],
    )

    if fast:
        shared_code = ready(shared_code, routed_plain).reshape(expert_count, local_rows, -1)
        (shared_sum,) = simple_call(
            shard_sum_kernel, [out((local_rows, wide))], [exchange(shared_code)], 4e6
        )
        expert_code_other = flip(ready(expert_code, mixed_slope), "dp", 2)
        last_give = ready(last_give, expert_code_other)
        (last_code,) = simple_call(
            last_code_kernel,
            [out((D, half_columns + 128), jnp.int16)],
            [(sides, in_smem), last_keep, flip(last_give, "dp", 1)],
            4e6,
        )
        last_code = ready(last_code, shared_sum).reshape(expert_count, local_rows, -1)
        (last_part,) = simple_call(
            last_sum_kernel,
            [out((local_rows, half_columns))],
            [(sides, in_smem), exchange(last_code)],
            4e6,
        )
        last_part = last_part + flip(last_part, "dp", 2)
        expert_in, expert_out = pl.pallas_call(
            expert_sum_kernel,
            out_shape=[out((D, hidden_local)), out((D, D))],
            grid=(4,),
            in_specs=[code_to, code_to],
            out_specs=[sum_in, sum_out],
            compiler_params=params(),
            cost_estimate=cost(2e6, 8e6),
        )(ready(expert_code, mixed_slope), expert_code_other)
        shared_cross = flip(shared_sum, "dp", 2)
        square_pieces = [expert_in, expert_out, shared_sum, shared_cross, last_part]
        weights = (1.0,) * 5
        square_bits = [1]
        pieces = [
            last_part, flip(last_part, "dp", 1), shared_sum, shared_cross,
            flip(shared_sum, "dp", 1), flip(shared_cross, "dp", 1), expert_in,
            flip(expert_in, "dp", 1), expert_out, flip(expert_out, "dp", 1),
        ]
        tile_in = pl.BlockSpec((D // steps, hidden_local), lambda i: (i, 0))
        half_steps = steps // 2
        tile_out = pl.BlockSpec((hidden_local // steps, D), lambda i: (i % half_steps, 0))
        piece_specs = [*[whole(a) for a in pieces[:6]], tile_in, tile_in, tile_out, tile_out]
    else:
        sums = local_sums
        shin_part = scatter_sum(grad_shin, 0, [1])[0].reshape(expert_count, local_rows, FFS)
        shin_part = expert_scatter(scatter_sum(shin_part, 2, dp_bits[1:]))
        shout_part = scatter_sum(grad_shout.reshape(expert_count, -1, D), 1, dp_bits)
        shout_part = expert_scatter(shout_part)
        expert_in_part = scatter_sum(grad_expert_in.reshape(-1, hidden_local), 0, dp_bits)
        expert_out_part = scatter_sum(grad_expert_out, 0, dp_bits)
        last_part = expert_scatter(last_keep.reshape(expert_count, local_rows, -1))
        for bit in dp_bits:
            last_part = last_part + flip(last_part, "dp", bit)
        square_pieces = [expert_in_part, expert_out_part, shin_part, shout_part, last_part]
        weights = (1.0, 1.0, 1.0, 1.0, 1.0 / dp_count)
        square_bits = dp_bits
        pieces = [
            last_part,
            join(join(shin_part, 1, dp_bits[1:])[None], 0, [1]),
            join(shout_part, 0, dp_bits),
            join(expert_in_part, 0, dp_bits).reshape(expert_input.shape),
            join(expert_out_part, 0, dp_bits),
        ]
        piece_specs = [
            whole(last_part),
            *[tile_spec(i, a.shape, steps) for i, a in zip((4, 5, 7, 8), pieces[1:])],
        ]
    (both_sums,) = simple_call(
        functools.partial(squares_kernel, weights), [out((2, 128))], [sums, *square_pieces], 3e6
    )
    for bit in square_bits:
        both_sums = both_sums + flip(both_sums, "dp", bit)
    both_sums = sum_small(both_sums, ("expert",))
    domain_sums = both_sums[1, :DOMAINS]
    grad_norm = jnp.sqrt(both_sums[0, 0:1])
    shapes = [out(a.shape) for a in masters]
    state_specs = tile_specs(masters, steps)
    updates = pl.pallas_call(
        functools.partial(moments_kernel, fast, count, small_end),
        out_shape=[*shapes, *shapes, *shapes, out((16, 128))],
        grid=(steps,),
        in_specs=[
            in_smem, whole(both_sums), *state_specs, *state_specs, *state_specs, *piece_specs,
        ],
        out_specs=[*state_specs, *state_specs, *state_specs, whole(out((16, 128)))],
        compiler_params=params(),
        cost_estimate=cost(3e7, 34e6),
    )(sides, both_sums, *masters, *first_moments, *second_moments, *pieces)
    directions = updates[:count]
    all_totals = sum_small(
        jnp.concatenate([updates[-1][:count], master_squares[:count]], 0), ("expert",)
    )
    totals, master_totals = all_totals[:count], all_totals[count:]
    next_masters = pl.pallas_call(
        functools.partial(step_kernel, count),
        out_shape=shapes,
        grid=(steps,),
        in_specs=[whole(totals), whole(master_totals), *state_specs, *state_specs],
        out_specs=state_specs,
        compiler_params=params(),
        cost_estimate=cost(3e6, 15e6),
    )(totals, master_totals, *masters, *directions)
    results = []
    for index in range(count):
        for group in (next_masters, updates[count : 2 * count], updates[2 * count : 3 * count]):
            results.append(group[index].T if index == 3 else group[index])
    norms = jnp.sqrt(all_totals[:, 0])
    results.append(jnp.stack([domain_sums, counts[0, :DOMAINS]]))
    results.append(grad_norm)
    results.append(jnp.stack([norms[count:], norms[:count]], 1))
    return tuple(results)


def solution(mesh):
    placed = (
        P(("dp", "expert")),
        P(("dp", "expert"), None),
        P(("dp", "expert"), None),
        P(("dp", "expert"), None),
        P(),
        P(None, "expert"),
        P("expert", None),
        P("expert", None),
        P("expert", None),
        P("expert", None),
        P("expert", None),
        P("expert", None),
        P(None, None, "expert"),
        P("expert", None),
        P(None, "expert"),
        P("expert", None),
        P("expert", None),
        P("expert", None),
        P("expert", None),
        P("expert", None),
        P("expert", None),
        P(None, None, "expert"),
        P("expert", None),
        P(None, "expert"),
        P("expert", None),
        P("expert", None),
        P("expert", None),
        P("expert", None),
        P("expert", None),
        P("expert", None),
        P(None, None, "expert"),
        P("expert", None),
    )
    return jax.shard_map(
        shards,
        mesh=mesh,
        in_specs=placed,
        out_specs=(
            P(None, "expert"),
            P(None, "expert"),
            P(None, "expert"),
            P("expert", None),
            P("expert", None),
            P("expert", None),
            P("expert", None),
            P("expert", None),
            P("expert", None),
            P("expert", None),
            P("expert", None),
            P("expert", None),
            P("expert", None),
            P("expert", None),
            P("expert", None),
            P("expert", None),
            P("expert", None),
            P("expert", None),
            P("expert", None),
            P("expert", None),
            P("expert", None),
            P(None, None, "expert"),
            P(None, None, "expert"),
            P(None, None, "expert"),
            P("expert", None),
            P("expert", None),
            P("expert", None),
            P(),
            P(),
            P(),
        ),
        check_vma=False,
    )
```

```python
import functools

import jax
import jax.numpy as jnp
import numpy as np
from jax import lax
from jax.experimental import pallas as pl
from jax.experimental.pallas import tpu as pltpu
from jax.sharding import PartitionSpec as P

D = 384
HEADS = 12
HD = 32
FFS = 1536
EXPERTS = 8
DOMAINS = 9
STEP = 10
CAP = 256


HORIZONS = (1, 8, 32, 64)
REACH = 64
KINK_THRESHOLD = 2.0
EPS_NORM = 1e-06
CLIP = 0.01
BETA_ONE = 0.9
BETA_TWO = 0.99
EPS_ADAM = 1e-08
DECAY = 0.01
RATE = 0.3


def ahead_table():
    return np.concatenate([np.arange(horizon_len) for horizon_len in HORIZONS]).astype(np.int32)


def target_columns(samples):
    amount = samples.shape[0]
    padded = jnp.concatenate([samples, jnp.zeros((REACH + 1,), samples.dtype)])
    future = jnp.stack([padded[1 + offset : 1 + offset + amount] for offset in range(REACH)], 1)
    return future[:, ahead_table()]


ROW_BLOCK = 256
SMALL = 128
HORIZON_AT = EXPERTS + 1
VECTORS_AT = 120
SMALL_AT = 4 * D
COUNTS_AT = 125
CODE_ROWS = 16
VMEM = 56 * 1024 * 1024
F32 = jnp.float32
BF16 = jnp.bfloat16


def mm(left, right):
    return jnp.dot(left, right, preferred_element_type=F32)


def mm_nt(left, right):
    return lax.dot_general(left, right, (((1,), (1,)), ((), ())), preferred_element_type=F32)


def mm_tn(left, right):
    return lax.dot_general(left, right, (((0,), (0,)), ((), ())), preferred_element_type=F32)


def inverse_rms(rows):
    return lax.rsqrt(jnp.mean(rows * rows, axis=-1, keepdims=True) + EPS_NORM)


def rms_back(rows, inverse, gain, slope):
    gain_slope = jnp.sum(slope * rows * inverse, 0, keepdims=True)
    scaled = slope * gain
    return (
        inverse * scaled
        - rows * (inverse * inverse * inverse) * jnp.mean(rows * scaled, -1, keepdims=True),
        gain_slope,
    )


def lanes_of(shape):
    return lax.broadcasted_iota(jnp.int32, shape, len(shape) - 1)


def half_swap(rows):
    half_width = HD // 2
    lane = lanes_of(rows.shape)
    return jnp.where(
        lane % HD < half_width,
        pltpu.roll(rows, rows.shape[1] - half_width, 1),
        pltpu.roll(rows, half_width, 1),
    )


SLOT, SERIES_OF, FINISH, DOMAIN, CHOICE, VALUE, PLACE = 0, 2, 3, 4, 5, 7, 8


def tables_kernel(
    lengths, domains, frequency, points_row, experts_row, cosine, sine, columns_out, rows_out
):
    amount = points_row.shape[1]
    place = lax.broadcasted_iota(jnp.int32, (1, amount), 1)
    series = jnp.zeros((1, amount), jnp.int32)
    begin = jnp.zeros((1, amount), jnp.int32)
    finish = jnp.zeros((1, amount), jnp.int32)
    domain = jnp.zeros((1, amount), jnp.int32)
    start = jnp.int32(0)
    for index in range(lengths.shape[1]):
        stop = start + lengths[0, index]
        inside = (place >= start) & (place < stop)
        series = jnp.where(inside, index, series)
        begin = jnp.where(inside, start, begin)
        finish = jnp.where(inside, stop, finish)
        domain = jnp.where(inside, domains[0, index], domain)
        start = stop
    name = lax.broadcasted_iota(jnp.int32, (16, amount), 0)
    choices = [experts_row[k : k + 1, :] for k in range(2)]
    named = [(name == choice).astype(F32) for choice in choices]
    earlier = (
        lax.broadcasted_iota(jnp.int32, (amount, amount), 0)
        < lax.broadcasted_iota(jnp.int32, (amount, amount), 1)
    )
    before = mm((named[0] + named[1]).astype(BF16), earlier.astype(F32).astype(BF16))
    entries = []
    for k in range(2):
        rank = jnp.sum(named[k] * before, 0, keepdims=True)
        entries.append(choices[k].astype(F32) * CAP + rank)
    entries += [series, finish, domain, *choices, points_row[...], place - begin]
    row = lax.broadcasted_iota(jnp.int32, (128, amount), 0)
    table = jnp.zeros((128, amount), F32)
    for index, entry in enumerate(entries):
        table = jnp.where(row == index, entry.astype(F32), table)
    rows_out[...] = table[:8]
    columns = table.T
    columns_out[...] = columns
    angles = columns[:, PLACE : PLACE + 1] * frequency[...]
    cosine[...] = jnp.cos(angles)
    turned = jnp.sin(angles)
    sine[...] = jnp.where(lanes_of((amount, 128)) % HD < HD // 2, -turned, turned)


def allowed_block(table, rows_table, start, rows, keys):
    query = start + lax.broadcasted_iota(jnp.int32, (rows, keys), 0)
    key = lax.broadcasted_iota(jnp.int32, (rows, keys), 1)
    series_col = table[start : start + rows, SERIES_OF : SERIES_OF + 1]
    return (series_col == rows_table[SERIES_OF : SERIES_OF + 1, :keys]) & (key <= query)


def slot_place(grouped, expert):
    return (expert % 4) * 2 + expert // 4 if grouped else expert


def slot_rows_hot(slot_row, expert):
    slot = expert * CAP + lax.broadcasted_iota(jnp.int32, (CAP, slot_row.shape[1]), 0)
    return (slot_row.astype(jnp.int32) == slot).astype(F32).astype(BF16)


def slot_cols_hot(slot_col, expert):
    slot = expert * CAP + lax.broadcasted_iota(jnp.int32, (slot_col.shape[0], CAP), 1)
    return (slot_col.astype(jnp.int32) == slot).astype(F32).astype(BF16)


def pack_kernel(small_end, core, lengths, domains, ahead, input_w, output_w, router, horizon, vectors, out):
    rows = input_w.shape[0]

    def placed(count, at):
        row = lax.broadcasted_iota(jnp.int32, (count, SMALL), 0)
        return (row + at == lanes_of((count, SMALL))).astype(F32).astype(BF16)

    small = (
        mm_tn(router[...].astype(BF16), placed(HORIZON_AT, 0))
        + mm(horizon[...].astype(BF16), placed(small_end - HORIZON_AT, HORIZON_AT))
        + mm_tn(vectors[...].astype(BF16), placed(vectors.shape[0], VECTORS_AT))
    )
    row = lax.broadcasted_iota(jnp.int32, (rows, SMALL), 0)
    lane = lanes_of((rows, SMALL))
    counts = jnp.zeros((rows, SMALL), F32)
    for series in range(lengths.shape[1]):
        left = jnp.maximum(lengths[0, series] - 1 - ahead[...], 0).astype(F32)
        entries = jnp.sum(left, -1, keepdims=True)
        counts = counts + jnp.where(row == domains[0, series], entries, 0.0)
    high = jnp.floor(counts * (1.0 / 256.0))
    small = jnp.where(lane == COUNTS_AT, high, small)
    small = jnp.where(lane == COUNTS_AT + 1, counts - 256.0 * high, small)
    flat = jnp.concatenate([input_w[...], output_w[...]], 1)
    half = 2 * D
    mine = jnp.where(core[0] == 0, flat[:, :half], flat[:, half:]).astype(BF16)
    for target in range(out.shape[0]):
        out[target, :, :half] = mine
        out[target, :, half:] = small.astype(BF16)


def pair_kernel(sides, own, far, out):
    low = sides[2] == 0
    first = jnp.where(low, own[...], far[...])
    second = jnp.where(low, far[...], own[...])
    for target in range(out.shape[0]):
        out[target, 0] = first
        out[target, 1] = second


def front_kernel(
    grouped, local_rows, core, mine, other, cosine, sine, known, slot_row,
    embedded_out, first_out, qkv_out, log_out, mixed_out, after_out, second_out, logits_out,
    slots_out, gains_out, pack, counts_out,
):
    amount = known.shape[0]
    half = 2 * D
    low = core[0] == 0
    for index in range(D // local_rows):
        place = slot_place(grouped, index)
        here = slice(index * local_rows, (index + 1) * local_rows)
        there = slice(place * local_rows, (place + 1) * local_rows)
        left, right = mine[there, :half], other[there, :half]
        pack[here, :half] = jnp.where(low, left, right)
        pack[here, half:SMALL_AT] = jnp.where(low, right, left)
        pack[here, SMALL_AT:] = mine[there, half:]
    table = pack[:, SMALL_AT:].astype(F32).T
    gains = table[VECTORS_AT : VECTORS_AT + 8]
    gains_out[...] = gains
    other_table = other[:, half:].astype(F32).T
    row = lax.broadcasted_iota(jnp.int32, (D, SMALL), 0)
    fold = (row % local_rows == lanes_of((D, SMALL))).astype(F32).astype(BF16)
    digits = mm(table[VECTORS_AT : VECTORS_AT + 8].astype(BF16), fold) + mm(
        other_table[VECTORS_AT : VECTORS_AT + 8].astype(BF16), fold
    )
    at = COUNTS_AT - VECTORS_AT
    counts_out[...] = digits[at : at + 1] * 256.0 + digits[at + 1 : at + 2]
    value = known[:, VALUE : VALUE + 1]
    gate = value * gains[0:1]
    embedded = gate * jax.nn.sigmoid(gate) * (value * gains[1:2])
    embedded_out[...] = embedded
    first = (embedded * inverse_rms(embedded) * gains[2:3]).astype(BF16)
    first_out[...] = first
    projected = mm(first, pack[:, : 3 * D])
    cos_rows, sin_rows = cosine[...], sine[...]
    for block in range(6):
        part = projected[:, block * 128 : (block + 1) * 128]
        part = part * cos_rows + half_swap(part) * sin_rows
        qkv_out[:, block * 128 : (block + 1) * 128] = part.astype(BF16)
    qkv_out[:, 2 * D :] = projected[:, 2 * D :].astype(BF16)
    lane = lanes_of((ROW_BLOCK, 128))
    for start in range(0, amount, ROW_BLOCK):
        keys = start + ROW_BLOCK
        allowed = allowed_block(known[...], slot_row[...], start, ROW_BLOCK, keys)
        log_rows = jnp.zeros((ROW_BLOCK, 128), F32)
        for group in range(D // 128):
            query = qkv_out[start : start + ROW_BLOCK, group * 128 : (group + 1) * 128]
            key = qkv_out[:keys, D + group * 128 : D + (group + 1) * 128]
            held = qkv_out[:keys, 2 * D + group * 128 : 2 * D + (group + 1) * 128]
            gathered = jnp.zeros((ROW_BLOCK, 128), F32)
            for head in range(128 // HD):
                own = lane // HD == head
                raw = mm_nt(jnp.where(own, query, jnp.zeros_like(query)), key) * HD ** (-0.5)
                raw = jnp.where(allowed, raw, -1e30)
                top = jnp.max(raw, -1, keepdims=True)
                exponent = jnp.exp(raw - top)
                total = jnp.sum(exponent, -1, keepdims=True)
                attention = (exponent * (1.0 / total)).astype(BF16)
                gathered = jnp.where(own, mm(attention, held), gathered)
                log_rows = jnp.where(
                    lane == group * (128 // HD) + head, top + jnp.log(total), log_rows
                )
            mixed_out[start : start + ROW_BLOCK, group * 128 : (group + 1) * 128] = (
                gathered.astype(BF16)
            )
        log_out[start : start + ROW_BLOCK, :] = log_rows
    after = embedded + mm(mixed_out[...], pack[:, 3 * D : 4 * D])
    after_out[...] = after
    second = (after * inverse_rms(after) * gains[3:4]).astype(BF16)
    second_out[...] = second
    logits_out[...] = mm(second, pack[:, SMALL_AT:])
    for expert in range(EXPERTS):
        hot = slot_rows_hot(slot_row[0:1, :], expert) + slot_rows_hot(slot_row[1:2, :], expert)
        place = slot_place(grouped, expert)
        slots_out[place * CAP : (place + 1) * CAP, :] = mm(hot, second).astype(BF16)


def shared_kernel(second, gate_w, lift_w, down_w, shared_out):
    gate = mm(second[...], gate_w[...])
    lift = mm(second[...], lift_w[...])
    hidden = (gate * jax.nn.sigmoid(gate) * lift).astype(BF16)
    part = mm(hidden, down_w[...])

    @pl.when(pl.program_id(0) == 0)
    def _():
        shared_out[...] = part

    @pl.when(pl.program_id(0) != 0)
    def _():
        shared_out[...] += part


def code_rows(part, ref):
    top = jnp.max(jnp.abs(part), -1, keepdims=True)
    power = jnp.ceil(jnp.log2(jnp.maximum(top, 1e-30)))
    code = jnp.clip(jnp.round(part * jnp.exp2(15.0 - power)), -32767.0, 32767.0)
    ref[:CAP, :] = code.astype(jnp.int32).astype(jnp.int16)
    row = lax.broadcasted_iota(jnp.int32, (CAP, CAP), 0)
    column = lax.broadcasted_iota(jnp.int32, (CAP, CAP), 1)
    powers = jnp.sum(jnp.where(row == column, power, 0.0), 0, keepdims=True)
    powers = jnp.concatenate([powers, jnp.zeros((1, D - CAP), F32)], 1)
    ref[CAP:, :] = jnp.broadcast_to(powers, (CODE_ROWS, D)).astype(jnp.int32).astype(jnp.int16)


def unit(rows, gate_up, down):
    gate = mm(rows, gate_up[0])
    lift = mm(rows, gate_up[1])
    hidden = (gate * jax.nn.sigmoid(gate) * lift).astype(BF16)
    return mm(hidden, down[...])


def expert_kernel(rows, gate_up, down, rows_out):
    rows_out[...] = unit(rows[...], gate_up, down)


def pair_expert_kernel(sides, rows, gate_up, down, gate_up_far, down_far, rows_out):
    sources = rows.shape[0]
    flat = rows[...].reshape(sources * CAP, D)

    def serve(weights):
        result = unit(flat, *weights)
        for source in range(sources):
            code_rows(result[source * CAP : (source + 1) * CAP], rows_out.at[source, 0])

    pl.when(pl.program_id(0) == 0)(lambda: serve((gate_up, down)))
    pl.when(pl.program_id(0) == 1)(lambda: serve((gate_up_far, down_far)))


def far_weights_kernel(sides, *refs):
    pieces, (gate_up, down) = refs[:4], refs[4:]
    me = sides[0] * 2 + sides[1]
    half, wide = pieces[0].shape[0], gate_up.shape[2]
    for piece in range(4):
        core, cross = piece // 2, piece % 2
        value = picked_piece(pieces, jnp.bitwise_xor(piece, me), lambda ref: ref[...])
        gate_up[core, cross * half : (cross + 1) * half, :] = value[:, :wide]
        down[piece * half : (piece + 1) * half, :] = value[:, wide:]


def shared_weights_kernel(local_rows, sides, *refs):
    pieces, (both, down) = refs[:4], refs[4:]
    me = sides[0] * 2 + sides[1]
    wide = pieces[0].shape[1]
    shard = down.shape[0] // (D // local_rows)
    for piece in range(4):
        value = picked_piece(pieces, jnp.bitwise_xor(piece, me), lambda ref: ref[...])
        for index in range(D // local_rows):
            place = slot_place(True, index)
            rows = value[place * local_rows : (place + 1) * local_rows]
            for at in range(0, wide, D):
                column = piece * wide + at
                part = rows[:, at : at + D]
                if column < 2 * FFS:
                    both[index * local_rows : (index + 1) * local_rows, column : column + D] = part
                else:
                    row = index * shard + (column - 2 * FFS) // D * local_rows
                    down[row : row + local_rows, :] = part


def unit_back(rows, slope, gate_w, lift_w, down_w):
    gate = mm(rows, gate_w)
    lift = mm(rows, lift_w)
    bent = jax.nn.sigmoid(gate)
    smooth = gate * bent
    hidden = (smooth * lift).astype(BF16)
    hidden_slope = mm_nt(slope, down_w)
    gate_slope = (hidden_slope * lift * (bent * (1.0 + gate * (1.0 - bent)))).astype(BF16)
    lift_slope = (hidden_slope * smooth).astype(BF16)
    return hidden, gate_slope, lift_slope


def expert_back_kernel(rows, slope, gate_up, down, rows_out, in_out, out_out):
    hidden, gate_slope, lift_slope = unit_back(
        rows[...], slope[...], gate_up[0], gate_up[1], down[...]
    )
    rows_out[...] = (mm_nt(gate_slope, gate_up[0]) + mm_nt(lift_slope, gate_up[1])).astype(BF16)

    @pl.when(pl.program_id(0) == 0)
    def _():
        in_out[...] = jnp.zeros_like(in_out)
        out_out[...] = jnp.zeros_like(out_out)

    in_out[0] += mm_tn(rows[...], gate_slope)
    in_out[1] += mm_tn(rows[...], lift_slope)
    out_out[...] += mm_tn(hidden, slope[...])


def shared_back_kernel(second, slope, gate_w, lift_w, down_w, second_out, in_out, out_out):
    hidden, gate_slope, lift_slope = unit_back(
        second[...], slope[...], gate_w[...], lift_w[...], down_w[...]
    )
    part = mm_nt(gate_slope, gate_w[...]) + mm_nt(lift_slope, lift_w[...])

    @pl.when(pl.program_id(0) == 0)
    def _():
        second_out[...] = part

    @pl.when(pl.program_id(0) != 0)
    def _():
        second_out[...] += part

    in_out[0] = mm_tn(second[...], gate_slope)
    in_out[1] = mm_tn(second[...], lift_slope)
    out_out[...] = mm_tn(hidden, slope[...])


def expert_back_split_kernel(
    sides, rows, slope, gate_up, down, gate_up_far, down_far,
    rows_out, in_keep, in_give, out_keep, out_give,
):
    sources = rows.shape[0]
    flat = rows[...].reshape(sources * CAP, D)
    flat_slope = slope[...].reshape(sources * CAP, D)

    @pl.when(pl.program_id(1) == 0)
    def _():
        for ref in (in_keep, in_give, out_keep, out_give):
            ref[...] = jnp.zeros_like(ref)

    def serve(gate_w, down_w):
        hidden, gate_slope, lift_slope = unit_back(
            flat, flat_slope, gate_w[0], gate_w[1], down_w[...]
        )
        result = (mm_nt(gate_slope, gate_w[0]) + mm_nt(lift_slope, gate_w[1])).astype(BF16)
        rows_out[...] = result.reshape(rows_out.shape)
        half = hidden.shape[1] // 2
        low = sides[0] == 0
        gate = mm_tn(flat, gate_slope)
        lift = mm_tn(flat, lift_slope)
        in_keep[0] += jnp.where(low, gate, lift)
        in_give[0] += jnp.where(low, lift, gate)
        first = mm_tn(hidden[:, :half], flat_slope)
        last = mm_tn(hidden[:, half:], flat_slope)
        out_keep[0] += jnp.where(low, first, last)
        out_give[0] += jnp.where(low, last, first)

    pl.when(pl.program_id(0) == 0)(lambda: serve(gate_up, down))
    pl.when(pl.program_id(0) == 1)(lambda: serve(gate_up_far, down_far))


def shared_back_split_kernel(
    sides, second, slope, gate_w, lift_w, down_w,
    second_out, in_keep, in_give_even, in_give_odd, out_keep, out_give, out_ref,
):
    hidden, gate_slope, lift_slope = unit_back(
        second[...], slope[...], gate_w[...], lift_w[...], down_w[...]
    )
    part = mm_nt(gate_slope, gate_w[...]) + mm_nt(lift_slope, lift_w[...])

    @pl.when(pl.program_id(0) == 0)
    def _():
        second_out[...] = part

    @pl.when(pl.program_id(0) != 0)
    def _():
        second_out[...] += part

    core, cross = sides[0], sides[1]
    low = core == 0
    gate = mm_tn(second[...], gate_slope)
    lift = mm_tn(second[...], lift_slope)
    in_keep[0] = jnp.where(low, gate, lift)
    given = jnp.where(low, lift, gate)
    even = pl.program_id(0) % 2 == 0

    @pl.when(even)
    def _():
        in_give_even[0] = given

    @pl.when(jnp.logical_not(even))
    def _():
        in_give_odd[0] = given

    out_ref[...] = mm_tn(hidden, slope[...])
    quarter = out_keep.shape[1] // 2
    for shard in range(2):
        for side in range(2):
            for ref, half in ((out_keep, core), (out_give, 1 - core)):
                piece = half * 2 + jnp.bitwise_xor(cross, side)
                start = pl.multiple_of(shard * 4 * quarter + piece * quarter, 8)
                ref[side, shard * quarter : (shard + 1) * quarter, :] = out_ref[
                    pl.ds(start, quarter), :
                ]


def coded_tile(value):
    top = jnp.max(jnp.abs(value), -1, keepdims=True)
    power = jnp.ceil(jnp.log2(jnp.maximum(top, 1e-30)))
    code = jnp.clip(jnp.round(value * jnp.exp2(15.0 - power)), -32767.0, 32767.0)
    return code, power


def encode(ref, tiles):
    lane = lanes_of(tiles[0].shape)
    powers = jnp.zeros(tiles[0].shape, F32)
    for index, tile in enumerate(tiles):
        code, power = coded_tile(tile)
        ref[:, index * 128 : (index + 1) * 128] = code.astype(jnp.int32).astype(jnp.int16)
        powers = jnp.where(lane == index, power, powers)
    ref[:, len(tiles) * 128 :] = powers.astype(jnp.int32).astype(jnp.int16)


def decode(ref):
    count = ref.shape[-1] // 128 - 1
    scale = jnp.exp2(ref[..., count * 128 :].astype(jnp.int32).astype(F32) - 15.0)
    return [
        ref[..., index * 128 : (index + 1) * 128].astype(jnp.int32).astype(F32)
        * scale[..., index : index + 1]
        for index in range(count)
    ]


def tiles_of(value):
    return [value[:, at : at + 128] for at in range(0, value.shape[1], 128)]


def fold_kernel(in_keep, in_even, in_odd, out_keep, out_other, keep, give):
    wide = in_keep.shape[2]
    half = wide // 2
    keep[:, :half] = in_keep[0, :, :half] + in_even[0]
    keep[:, half:wide] = in_keep[0, :, half:] + in_odd[0]
    keep[:, wide:] = out_keep[0] + out_other[0]
    encode(
        give,
        tiles_of(in_keep[1, :, :half] + in_even[1])
        + tiles_of(in_keep[1, :, half:] + in_odd[1])
        + tiles_of(out_keep[1] + out_other[1]),
    )


def add_code_kernel(keep, other, code):
    encode(code, [mine + theirs for mine, theirs in zip(tiles_of(keep[...]), decode(other))])


def shard_sum_kernel(codes, total):
    for index, tile in enumerate(decode(codes)):
        total[:, index * 128 : (index + 1) * 128] = jnp.sum(tile, 0)


def expert_split_kernel(sides, in_keep, in_other, out_keep, out_other, keep, code):
    wide, half = in_keep.shape[2], in_keep.shape[1] // 2
    here = pl.ds(pl.multiple_of(sides[1] * half, 8), half)
    there = pl.ds(pl.multiple_of((1 - sides[1]) * half, 8), half)
    keep[0, :, :wide] = in_keep[0, here, :] + in_other[0, here, :]
    keep[0, :, wide:] = out_keep[0, here, :] + out_other[0, here, :]
    encode(
        code.at[0],
        tiles_of(in_keep[0, there, :] + in_other[0, there, :])
        + tiles_of(out_keep[0, there, :] + out_other[0, there, :]),
    )


def expert_far_kernel(keep, codes, own, far):
    for index, tile in enumerate(decode(codes.at[0])):
        here = slice(index * 128, (index + 1) * 128)
        own[:, here] = keep[0, :, here] + tile
    encode(far, [mine + theirs for mine, theirs in zip(tiles_of(keep[1]), decode(codes.at[1]))])


def expert_total_kernel(own, code, in_total, out_total):
    split = in_total.shape[1] // 128
    for index, tile in enumerate(decode(code)):
        ref, at = (in_total, index) if index < split else (out_total, index - split)
        ref[:, at * 128 : (at + 1) * 128] = own[:, index * 128 : (index + 1) * 128] + tile


def last_code_kernel(core, keep, other, code):
    tiles = tiles_of(keep[...] + other[...])
    rough, power = coded_tile(tiles[5])
    tiles[6] = jnp.where(core[0] == 1, tiles[5] - rough * jnp.exp2(power - 15.0), tiles[6])
    encode(code, tiles)


def last_sum_kernel(core, codes, total):
    tiles = decode(codes)
    high = core[0] == 1
    fine = tiles[6]
    tiles[5] = jnp.where(high, tiles[5] + fine, tiles[5])
    tiles[6] = jnp.where(high, 0.0, fine)
    for index, tile in enumerate(tiles):
        total[:, index * 128 : (index + 1) * 128] = jnp.sum(tile, 0)


def middle_kernel(
    grouped, returned, known, slot_row, after, shared, logits, small, gains, target, ahead, weighting,
    mixer_out, shared_slope_out, slots_out, logits_slope_out, small_out, gain_out, sums_out,
):
    amount = after.shape[0]
    lane = lanes_of((amount, SMALL))
    table = known[...]
    integers = table[:, :8].astype(jnp.int32)
    chosen = [
        (lane == integers[:, CHOICE + k : CHOICE + k + 1]).astype(F32) for k in range(2)
    ]
    point = lax.broadcasted_iota(jnp.int32, (amount, SMALL), 0)
    usable = (point + 1 + ahead[...] < integers[:, FINISH : FINISH + 1]).astype(F32)
    logit = logits[...]
    routed = lane < EXPERTS
    top = jnp.max(jnp.where(routed, logit, -1e30), -1, keepdims=True)
    exponent = jnp.where(routed, jnp.exp(jnp.where(routed, logit - top, 0.0)), 0.0)
    probs = exponent / jnp.sum(exponent, -1, keepdims=True)
    gates = [jnp.sum(chosen[k] * probs, -1, keepdims=True) for k in range(2)]
    shared_gate = jax.nn.sigmoid(
        jnp.sum(jnp.where(lane == EXPERTS, logit, 0.0), -1, keepdims=True)
    )
    picked = [jnp.zeros((amount, D), F32), jnp.zeros((amount, D), F32)]
    for expert in range(EXPERTS):
        place = slot_place(grouped, expert)
        if len(returned.shape) == 2:
            rows = returned[place * CAP : (place + 1) * CAP, :]
            scale = 1.0
        else:
            rows = returned[place, :CAP, :].astype(jnp.int32).astype(F32)
            powers = returned[place, CAP:, :].astype(jnp.int32).astype(F32)
            scale = jnp.exp2(powers[0:1, :CAP] - 15.0)
        high = rows.astype(BF16)
        rest = (rows - high.astype(F32)).astype(BF16)
        for k in range(2):
            slot = expert * CAP + lax.broadcasted_iota(jnp.int32, (amount, CAP), 1)
            hot = jnp.where(integers[:, SLOT + k : SLOT + k + 1] == slot, scale, 0.0).astype(BF16)
            picked[k] = picked[k] + (mm(hot, high) + mm(hot, rest))
    mixer = (
        after[...] + shared_gate * shared[...] + (gates[0] * picked[0] + gates[1] * picked[1])
    )
    inverse = inverse_rms(mixer)
    gain = gains[4:5]
    third = (mixer * inverse * gain).astype(BF16)
    residue = mm(third, small[...]) - target[...]
    size = jnp.abs(residue)
    cost = (
        jnp.where(
            size <= KINK_THRESHOLD,
            0.5 * residue * residue,
            KINK_THRESHOLD * (size - 0.5 * KINK_THRESHOLD),
        )
        * usable
    )
    domain_hot = (lane == integers[:, DOMAIN : DOMAIN + 1]).astype(F32)
    sums_out[...] = jnp.sum(domain_hot * jnp.sum(cost, -1, keepdims=True), 0, keepdims=True)
    weight = jnp.sum(domain_hot * weighting[...], -1, keepdims=True)
    slope = (
        jnp.clip(residue, -KINK_THRESHOLD, KINK_THRESHOLD) * usable * weight
    ).astype(BF16)
    small_out[...] = mm_tn(third, slope)
    mixer_slope, gain_slope = rms_back(mixer, inverse, gain, mm_nt(slope, small[...]))
    gain_out[...] = gain_slope
    mixer_out[...] = mixer_slope
    shared_slope_out[...] = (shared_gate * mixer_slope).astype(BF16)
    gate_slope = jnp.sum(mixer_slope * shared[...], -1, keepdims=True)
    probs_slope = chosen[0] * jnp.sum(mixer_slope * picked[0], -1, keepdims=True) + chosen[
        1
    ] * jnp.sum(mixer_slope * picked[1], -1, keepdims=True)
    inner = jnp.sum(probs * probs_slope, -1, keepdims=True)
    logits_slope_out[...] = jnp.where(
        routed,
        probs * (probs_slope - inner),
        jnp.where(lane == EXPERTS, gate_slope * (shared_gate * (1.0 - shared_gate)), 0.0),
    ).astype(BF16)
    slopes = [(gates[k] * mixer_slope).astype(BF16) for k in range(2)]
    for expert in range(EXPERTS):
        place = slot_place(grouped, expert)
        slots_out[place * CAP : (place + 1) * CAP, :] = (
            mm(slot_rows_hot(slot_row[0:1, :], expert), slopes[0])
            + mm(slot_rows_hot(slot_row[1:2, :], expert), slopes[1])
        ).astype(BF16)


def attend_back_kernel(
    grouped, returned, known, second_slope, logits_slope, small, after, mixer_slope, gains, mixed, second,
    output_w, small_before,
    attend_out, mixed_out, output_out, gain_out, small_out,
):
    slope = second_slope[...] + mm_nt(logits_slope[...], small[...])
    for expert in range(EXPERTS):
        hot = slot_cols_hot(known[:, 0:1], expert) + slot_cols_hot(known[:, 1:2], expert)
        place = slot_place(grouped, expert)
        slope = slope + mm(hot, returned[place * CAP : (place + 1) * CAP, :])
    after_rows = after[...]
    part, gain_slope = rms_back(after_rows, inverse_rms(after_rows), gains[3:4], slope)
    gain_out[...] = gain_slope
    attend = mixer_slope[...] + part
    attend_out[...] = attend
    low = attend.astype(BF16)
    output_out[...] = mm_tn(mixed[...], low)
    mixed_out[...] = mm_nt(low, output_w[...]).astype(BF16)
    small_out[...] = small_before[...] + mm_tn(second[...], logits_slope[...])


def front_back_kernel(
    fast, core, mixed_slope, qkv, log_total, known, rows_table, cosine, sine, first, embedded,
    gains, input_w, attend_slope, small_before, gain_two, gain_three, output_before,
    keep_out, give_out,
    pack_out, query_acc, key_acc, held_acc, slope_ref,
):
    amount = first.shape[0]
    key_acc[...] = jnp.zeros_like(key_acc)
    held_acc[...] = jnp.zeros_like(held_acc)
    lane = lanes_of((ROW_BLOCK, 128))
    lane_all = lanes_of((amount, 128))
    for start in range(0, amount, ROW_BLOCK):
        keys = start + ROW_BLOCK
        here = slice(start, start + ROW_BLOCK)
        allowed = allowed_block(known[...], rows_table[...], start, ROW_BLOCK, keys)
        for group in range(D // 128):
            wide = slice(group * 128, (group + 1) * 128)
            query = qkv[here, group * 128 : (group + 1) * 128]
            key = qkv[:keys, D + group * 128 : D + (group + 1) * 128]
            held = qkv[:keys, 2 * D + group * 128 : 2 * D + (group + 1) * 128]
            out_slope = mixed_slope[here, wide]
            query_sum = jnp.zeros((ROW_BLOCK, 128), F32)
            key_sum = jnp.zeros((keys, 128), F32)
            held_sum = jnp.zeros((keys, 128), F32)
            for head in range(128 // HD):
                own = lane // HD == head
                own_query = jnp.where(own, query, jnp.zeros_like(query))
                own_slope = jnp.where(own, out_slope, jnp.zeros_like(out_slope))
                own_key = jnp.where(lane_all[:keys] // HD == head, key, jnp.zeros_like(key))
                at = group * (128 // HD) + head
                raw = mm_nt(own_query, key) * HD ** (-0.5)
                probs = jnp.exp(jnp.where(allowed, raw - log_total[here, at : at + 1], -1e30))
                held_sum = held_sum + mm_tn(probs.astype(BF16), own_slope)
                probs_slope = mm_nt(own_slope, held)
                inner = jnp.sum(probs_slope * probs, -1, keepdims=True)
                raw_slope = (probs * (probs_slope - inner)).astype(BF16)
                query_sum = query_sum + mm(raw_slope, own_key)
                key_sum = key_sum + mm_tn(raw_slope, own_query)
            query_acc[here, wide] = query_sum
            key_acc[:keys, wide] += key_sum
            held_acc[:keys, wide] += held_sum
    cos_rows, sin_rows = cosine[...], sine[...]
    for block in range(3):
        wide = slice(block * 128, (block + 1) * 128)
        for base, acc in ((0, query_acc), (D, key_acc)):
            part = acc[:, wide] * HD ** (-0.5)
            part = part * cos_rows + half_swap(part * sin_rows)
            slope_ref[:, base + block * 128 : base + (block + 1) * 128] = part.astype(BF16)
    slope_ref[:, 2 * D :] = held_acc[...].astype(BF16)
    projected_slope = slope_ref[...]
    pack_out[:, : 3 * D] = mm_tn(first[...], projected_slope)
    pack_out[:, 3 * D : SMALL_AT] = output_before[...]
    first_slope = mm_nt(projected_slope, input_w[...])
    rows = embedded[...]
    part, gain_one = rms_back(rows, inverse_rms(rows), gains[2:3], first_slope)
    slope = attend_slope[...] + part
    value = known[:, VALUE : VALUE + 1]
    gate = value * gains[0:1]
    bent = jax.nn.sigmoid(gate)
    gate_gradient = jnp.sum(
        slope * (value * gains[1:2]) * (bent * (1.0 + gate * (1.0 - bent))) * value,
        0,
        keepdims=True,
    )
    lift_gradient = jnp.sum(slope * (gate * bent) * value, 0, keepdims=True)
    row = lax.broadcasted_iota(jnp.int32, (128, D), 0)
    table = jnp.zeros((128, D), F32)
    for offset, piece in enumerate(
        (gate_gradient, lift_gradient, gain_one, gain_two[...], gain_three[...])
    ):
        table = jnp.where(row == VECTORS_AT + offset, piece, table)
    pack_out[:, SMALL_AT : SMALL_AT + SMALL] = small_before[...] + table.T
    if not fast:
        keep_out[...] = pack_out[:, : keep_out.shape[1]]
        give_out[...] = jnp.zeros_like(give_out)
        return
    pack_out[:, SMALL_AT + SMALL :] = jnp.zeros_like(pack_out[:, SMALL_AT + SMALL :])
    half = keep_out.shape[1]
    keep_out[...] = pack_out[:, pl.ds(pl.multiple_of(core[0] * half, 128), half)]
    give_out[...] = pack_out[:, pl.ds(pl.multiple_of((1 - core[0]) * half, 128), half)]


def lamb_direction(master, gradient, mean, square, factor):
    clipped = gradient * factor
    mean_next = BETA_ONE * mean + (1.0 - BETA_ONE) * clipped
    square_next = BETA_TWO * square + (1.0 - BETA_TWO) * clipped * clipped
    direction = (
        mean_next
        / (1.0 - BETA_ONE**STEP)
        / (jnp.sqrt(square_next / (1.0 - BETA_TWO**STEP)) + EPS_ADAM)
        + DECAY * master
    )
    return mean_next, square_next, direction


def whole(array):
    shape = array.shape
    return pl.BlockSpec(shape, lambda *unused: (0,) * len(shape))


def params(limit=VMEM):
    return pltpu.CompilerParams(vmem_limit_bytes=limit)


def cost(microseconds):
    return pl.CostEstimate(flops=int(microseconds * 1.15e9), bytes_accessed=0, transcendentals=0)


def columns(array, width, at):
    return (array, pl.BlockSpec((array.shape[0], width), lambda *unused: (0, at)))


def simple_call(kernel, outs, args, microseconds, scratch=()):
    pairs = [a if isinstance(a, tuple) else (a, whole(a)) for a in args]
    args = [a for a, spec in pairs]
    return pl.pallas_call(
        kernel,
        out_shape=outs,
        in_specs=[spec for a, spec in pairs],
        out_specs=[whole(a) for a in outs],
        scratch_shapes=list(scratch),
        grid=(1,),
        compiler_params=params(),
        cost_estimate=cost(microseconds),
    )(*args)


def out(shape, dtype=F32):
    return jax.ShapeDtypeStruct(shape, dtype)


def flip(value, axis_name, bit):
    count = lax.axis_size(axis_name)
    return lax.ppermute(value, axis_name, [(i, i ^ bit) for i in range(count)])


def bits_of(axis_name):
    count = lax.axis_size(axis_name)
    return [1 << i for i in range(count.bit_length() - 1)]


def sum_small(value, axes):
    for axis_name in axes:
        for bit in bits_of(axis_name):
            value = value + flip(value, axis_name, bit)
    return value


def halves(value, axis, take_high):
    size = value.shape[axis] // 2
    side = take_high.astype(jnp.int32)
    return (
        lax.dynamic_slice_in_dim(value, side * size, size, axis),
        lax.dynamic_slice_in_dim(value, (1 - side) * size, size, axis),
    )


def scatter_sum(value, axis, bits):
    for bit in bits:
        side = (lax.axis_index("dp") & bit) != 0
        keep, give = halves(value, axis, side)
        value = keep + flip(give, "dp", bit)
    return value


def join(value, axis, bits):
    for bit in reversed(bits):
        side = (lax.axis_index("dp") & bit) != 0
        other = flip(value, "dp", bit)
        value = jnp.concatenate(
            [jnp.where(side, other, value), jnp.where(side, value, other)], axis
        )
    return value


def ready(value, *others):
    return lax.optimization_barrier((value, *others))[0]


def exchange(value):
    return lax.all_to_all(value, "expert", split_axis=0, concat_axis=0, tiled=True)


def exchange_near(value):
    return lax.all_to_all(
        value,
        "expert",
        split_axis=0,
        concat_axis=0,
        tiled=True,
        axis_index_groups=[[0, 1, 2, 3], [4, 5, 6, 7]],
    )


def pairs_of(value, sides):
    far = flip(value, "expert", 4)
    return pl.pallas_call(
        pair_kernel,
        out_shape=out((4, 2, *value.shape), BF16),
        in_specs=[
            pl.BlockSpec(memory_space=pltpu.SMEM),
            *[pl.BlockSpec(memory_space=pltpu.VMEM)] * 2,
        ],
        out_specs=pl.BlockSpec(memory_space=pltpu.VMEM),
        compiler_params=params(),
        cost_estimate=cost(2),
    )(sides, value, far)


def spread(value):
    count = lax.axis_size("expert")
    return exchange(jnp.broadcast_to(value[None], (count, *value.shape)))


def expert_scatter(value):
    return jnp.sum(exchange(value), 0)


def squares_kernel(weights, sums, *refs):
    total = jnp.zeros((1, 1), F32)
    for weight, ref in zip(weights, refs[:-1]):
        piece = ref[...]
        part = jnp.sum(jnp.sum(piece * piece, -1, keepdims=True), 0, keepdims=True)
        total = total + part * weight
    refs[-1][0:1, :] = jnp.broadcast_to(total, (1, 128))
    refs[-1][1:2, :] = sums[...]


def sum_all(value):
    while value.ndim > 2:
        value = jnp.sum(value, 0)
    return jnp.sum(jnp.sum(value, 0, keepdims=True), -1, keepdims=True)


TILED = (4, 7, 8)


def tile_spec(index, shape, steps):
    if index == 7:
        return pl.BlockSpec((2, D // steps, shape[2]), lambda i: (0, i, 0))
    if index == 8:
        return pl.BlockSpec((shape[0] // steps, D), lambda i: (i, 0))
    if index == 4 and len(shape) == 3:
        half = steps // 2
        return pl.BlockSpec((1, shape[1], shape[2] // half), lambda i: (i // half, 0, i % half))
    if index == 4:
        return pl.BlockSpec((shape[0], shape[1] // steps), lambda i: (0, i))
    return pl.BlockSpec(shape, lambda i: (0,) * len(shape))


def tile_specs(arrays, steps):
    return [tile_spec(index, array.shape, steps) for index, array in enumerate(arrays)]


def quarter_kernel(sides, gate_up, down, quarter):
    wide = gate_up.shape[2]
    quarter[:, :wide] = gate_up[0].astype(BF16)
    quarter[:, wide:] = down[...].astype(BF16)


def prepare_kernel(count, *refs):
    masters = refs[:count]
    gate_up_low, down_low, totals = refs[count:]
    step = pl.program_id(0)
    gate_up_low[...] = masters[7][...].astype(BF16)
    down_low[...] = masters[8][...].astype(BF16)

    @pl.when(step == 0)
    def _():
        totals[...] = jnp.zeros_like(totals)

    def add(index):
        master = masters[index][...]
        totals[index : index + 1, :] += jnp.broadcast_to(sum_all(master * master), (1, 128))

    for index in TILED:
        add(index)

    @pl.when(step == 0)
    def _():
        for index in range(count):
            if index not in TILED:
                add(index)


def picked_piece(pieces, index, part):
    value = part(pieces[0])
    for other in range(1, len(pieces)):
        value = jnp.where(index == other, part(pieces[other]), value)
    return value


def moments_kernel(fast, count, small_end, sides, square_ref, *refs):
    masters, means, squares = (refs[k * count : (k + 1) * count] for k in range(3))
    results = refs[-3 * count - 1 :]
    pieces = refs[3 * count : -3 * count - 1]
    totals = results[-1]
    factor = jnp.minimum(1.0, CLIP / jnp.sqrt(square_ref[0:1, 0:1]))
    step = pl.program_id(0)

    @pl.when(step == 0)
    def _():
        totals[...] = jnp.zeros_like(totals)

    def last_rows(start, stop):
        if not fast:
            return pieces[0][:, start:stop]
        low = sides[0] == 0
        half = pieces[0].shape[1]
        parts = []
        for side in range(2):
            begin, end = max(start, side * half), min(stop, (side + 1) * half)
            if begin < end:
                begin, end = begin - side * half, end - side * half
                mine, other = pieces[0][:, begin:end], pieces[1][:, begin:end]
                parts.append(jnp.where(low == (side == 0), mine, other))
        return jnp.concatenate(parts, 1) if len(parts) > 1 else parts[0]

    def gradient_of(index):
        if index in (0, 3):
            table = last_rows(SMALL_AT, SMALL_AT + SMALL).T
            return table[VECTORS_AT : VECTORS_AT + 5] if index == 0 else table[:HORIZON_AT]
        if index == 6:
            return last_rows(SMALL_AT, SMALL_AT + SMALL)[:, HORIZON_AT:small_end]
        if index == 1:
            return last_rows(0, 3 * D)
        if index == 2:
            return last_rows(3 * D, SMALL_AT)
        if not fast:
            return pieces[{4: 1, 5: 2, 7: 3, 8: 4}[index]][...]
        me = sides[0] * 2 + sides[1]
        shared = pieces[2:6]
        wide = 2 * FFS // 4
        if index == 4:
            return picked_piece(
                shared, jnp.bitwise_xor(step, me), lambda ref: ref[:, :wide]
            )
        if index == 5:
            return jnp.concatenate(
                [
                    picked_piece(shared, jnp.bitwise_xor(piece, me), lambda ref: ref[:, wide:])
                    for piece in range(4)
                ],
                0,
            )
        routed = pieces[6:10] if index == 7 else pieces[10:14]
        if index == 7:
            rows = masters[7].shape[1]
            here = pl.ds(pl.multiple_of((step % 2) * rows, 8), rows)
            return jnp.stack(
                [
                    picked_piece(
                        routed,
                        jnp.bitwise_xor(side * 2 + step // 2, me),
                        lambda ref: ref[here, :],
                    )
                    for side in range(2)
                ]
            )
        return picked_piece(routed, jnp.bitwise_xor(step, me), lambda ref: ref[...])

    def update(index):
        gradient = gradient_of(index)
        if index == 4 and gradient.ndim == 3:
            gradient = gradient[0]
        scale = factor.reshape(1, 1, 1) if gradient.ndim == 3 else factor
        mean_next, square_next, direction = lamb_direction(
            masters[index][...], gradient, means[index][...], squares[index][...], scale
        )
        results[index][...] = direction
        results[count + index][...] = mean_next
        results[2 * count + index][...] = square_next
        totals[index : index + 1, :] += jnp.broadcast_to(sum_all(direction * direction), (1, 128))

    for index in TILED:
        update(index)
    for index in range(count):
        if index not in TILED:
            pl.when(step == min(index, 3))(functools.partial(update, index))


def step_kernel(count, totals, master_totals, *refs):
    masters, directions = refs[:count], refs[count : 2 * count]
    results = refs[2 * count :]
    step = pl.program_id(0)

    def update(index):
        ratio = jnp.sqrt(master_totals[index : index + 1, 0:1]) / jnp.sqrt(
            totals[index : index + 1, 0:1]
        )
        ratio = RATE * ratio
        if len(masters[index].shape) == 3:
            ratio = ratio.reshape(1, 1, 1)
        results[index][...] = masters[index][...] - ratio * directions[index][...]

    for index in TILED:
        update(index)
    for index in range(count):
        if index not in TILED:
            pl.when(step == min(index, 3))(functools.partial(update, index))


def shards(
    points,
    experts,
    lengths,
    domains,
    domain_weights,
    vectors,
    attend_input,
    attend_output,
    router,
    shared_input,
    shared_output,
    horizon,
    expert_input,
    expert_output,
    mean_vectors,
    mean_attend_input,
    mean_attend_output,
    mean_router,
    mean_shared_input,
    mean_shared_output,
    mean_horizon,
    mean_expert_input,
    mean_expert_output,
    square_vectors,
    square_attend_input,
    square_attend_output,
    square_router,
    square_shared_input,
    square_shared_output,
    square_horizon,
    square_expert_input,
    square_expert_output,
):
    expert_count = lax.axis_size("expert")
    group_size = expert_count // EXPERTS
    dp_count = lax.axis_size("dp")
    dp_bits = bits_of("dp")
    amount = points.shape[0]
    local_rows = attend_input.shape[0]
    head_columns = horizon.shape[1]
    hidden_local = expert_output.shape[0]
    small_end = HORIZON_AT + head_columns
    fast = (
        group_size == 1 and dp_count == 4 and local_rows % 16 == 0 and hidden_local == 2 * D
    )
    core = lax.axis_index("dp") & 1
    sides = jnp.stack(
        [core, lax.axis_index("dp") >> 1, lax.axis_index("expert") >> 2]
    ).astype(jnp.int32)
    in_smem = pl.BlockSpec(memory_space=pltpu.SMEM)
    in_vmem = pl.BlockSpec(memory_space=pltpu.VMEM)
    ahead_row = jnp.pad(
        jnp.asarray(ahead_table())[None], ((0, 0), (0, SMALL - head_columns)), constant_values=1 << 20
    )
    packed = pl.pallas_call(
        functools.partial(pack_kernel, small_end),
        out_shape=out((1 if fast else expert_count, local_rows, 2 * D + SMALL), BF16),
        in_specs=[*[in_smem] * 3, *[in_vmem] * 6],
        out_specs=in_vmem,
        compiler_params=params(),
        cost_estimate=cost(2),
    )(sides, lengths, domains, ahead_row, attend_input, attend_output, router.T, horizon, vectors)
    gathered = exchange_near(pairs_of(packed[0], sides)) if fast else exchange(packed)

    def state(group):
        return tuple(a.T if index == 3 else a for index, a in enumerate(group))

    masters = state(
        (
            vectors, attend_input, attend_output, router, shared_input, shared_output, horizon,
            expert_input, expert_output,
        )
    )
    first_moments = state(
        (
            mean_vectors, mean_attend_input, mean_attend_output, mean_router, mean_shared_input,
            mean_shared_output, mean_horizon, mean_expert_input, mean_expert_output,
        )
    )
    second_moments = state(
        (
            square_vectors, square_attend_input, square_attend_output, square_router,
            square_shared_input, square_shared_output, square_horizon, square_expert_input,
            square_expert_output,
        )
    )
    count = len(masters)
    steps = 4
    gate_up_low, down_low, master_squares = pl.pallas_call(
        functools.partial(prepare_kernel, count),
        out_shape=[
            out(expert_input.shape, BF16), out(expert_output.shape, BF16), out((16, 128)),
        ],
        grid=(steps,),
        in_specs=tile_specs(masters, steps),
        out_specs=[
            tile_spec(7, expert_input.shape, steps),
            tile_spec(8, expert_output.shape, steps),
            whole(out((16, 128))),
        ],
        compiler_params=params(),
        cost_estimate=cost(5),
    )(*masters)
    weight_quarter = points
    if fast:
        weight_quarter = pl.pallas_call(
            quarter_kernel,
            out_shape=out((D // 2, hidden_local + D), BF16),
            grid_spec=pltpu.PrefetchScalarGridSpec(
                num_scalar_prefetch=1,
                grid=(1,),
                in_specs=[
                    pl.BlockSpec(
                        (1, D // 2, hidden_local), lambda i, sides: (sides[0], sides[1], 0)
                    ),
                    pl.BlockSpec((D // 2, D), lambda i, sides: (sides[0] * 2 + sides[1], 0)),
                ],
                out_specs=pl.BlockSpec((D // 2, hidden_local + D), lambda i, sides: (0, 0)),
            ),
            compiler_params=params(),
            cost_estimate=cost(2.6),
        )(sides, expert_input, expert_output)
    frequency = jnp.exp(-jnp.log(10000.0) * jnp.arange(HD // 2, dtype=F32) / (HD // 2))
    cosine, sine, known, rows_table = pl.pallas_call(
        tables_kernel,
        out_shape=[out((amount, 128)), out((amount, 128)), out((amount, 128)), out((8, amount))],
        in_specs=[*[in_smem] * 2, *[in_vmem] * 3],
        out_specs=[in_vmem] * 4,
        compiler_params=params(),
        cost_estimate=cost(3),
    )(
        lengths,
        domains,
        jnp.tile(frequency, 128 // (HD // 2))[None],
        points.reshape(1, amount),
        experts.T,
    )
    folds = FFS // D
    shared_piece = jnp.concatenate(
        [
            shared_input,
            shared_output.reshape(folds, local_rows, D).swapaxes(0, 1).reshape(local_rows, -1),
        ],
        1,
    ).astype(BF16)
    for bit in dp_bits:
        shared_piece, unused = halves(shared_piece, 1, (lax.axis_index("dp") & bit) != 0)
    if fast:
        shared_piece = pairs_of(shared_piece, sides)
    gathered = ready(gathered, known, shared_piece, weight_quarter).reshape(D, -1)
    gathered_other = flip(gathered, "dp", 1)
    shared_piece = ready(shared_piece, gathered)
    if fast:
        shared_pieces = exchange_near(shared_piece)
        weight_pieces = [flip(weight_quarter, "expert", 4)]
    else:
        shared_pieces = spread(shared_piece)
    (
        embedded, first, qkv, log_total, mixed, after, second, logits, slots, gains, pack,
        counts_half,
    ) = simple_call(
        functools.partial(front_kernel, fast, local_rows),
        [
            out((amount, D)), out((amount, D), BF16), out((amount, 3 * D), BF16),
            out((amount, 128)), out((amount, D), BF16), out((amount, D)),
            out((amount, D), BF16), out((amount, SMALL)), out((EXPERTS * CAP, D), BF16),
            out((8, D)), out((D, SMALL_AT + SMALL), BF16), out((1, SMALL)),
        ],
        [(sides, in_smem), gathered, gathered_other, cosine, sine, known, rows_table],
        15,
    )

    def to_devices(rows):
        rows = rows.reshape(EXPERTS, CAP, D)
        return exchange(jnp.repeat(rows, group_size, 0)).reshape(-1, D)

    def to_points(rows):
        rows = exchange(rows.reshape(expert_count, CAP, D))
        if group_size > 1:
            kind = rows.dtype
            rows = rows.reshape(EXPERTS, group_size, CAP, D).astype(F32)
            rows = jnp.sum(rows, 1).astype(kind)
        return rows.reshape(-1, D)

    first_bit = dp_bits[-1]
    block = 512
    if fast:
        arrived = exchange_near(
            ready(slots, shared_pieces, weight_pieces[0]).reshape(4, 2, CAP, D)
        )
        weight_pieces.append(flip(ready(weight_pieces[0], slots), "dp", 2))
        weight_pieces += [flip(piece, "dp", 1) for piece in weight_pieces]
        gate_up_far, down_far = simple_call(
            far_weights_kernel,
            [out(expert_input.shape, BF16), out(expert_output.shape, BF16)],
            [(sides, in_smem), ready(weight_pieces[0], gate_up_low), *weight_pieces[1:]],
            3,
        )
        shared_pieces = ready(shared_pieces, weight_pieces[1])
        shared_other = flip(shared_pieces, "dp", 2)
        row_spec = pl.BlockSpec(
            (4, 1, CAP, D), lambda i, sides: (0, jnp.bitwise_xor(i, sides[2]), 0, 0)
        )
        held = [gate_up_low, down_low, gate_up_far, down_far]
        held_specs = [
            pl.BlockSpec(a.shape, lambda *unused, a=a: (0,) * len(a.shape)) for a in held
        ]
        expert_rows = pl.pallas_call(
            pair_expert_kernel,
            out_shape=out((4, 2, CAP + CODE_ROWS, D), jnp.int16),
            grid_spec=pltpu.PrefetchScalarGridSpec(
                num_scalar_prefetch=1,
                grid=(2,),
                in_specs=[row_spec, *held_specs],
                out_specs=pl.BlockSpec(
                    (4, 1, CAP + CODE_ROWS, D),
                    lambda i, sides: (0, jnp.bitwise_xor(i, sides[2]), 0, 0),
                ),
            ),
            compiler_params=params(),
            cost_estimate=cost(10),
        )(sides, arrived, *held)
        returned = exchange_near(ready(expert_rows, shared_other)).reshape(
            EXPERTS, CAP + CODE_ROWS, D
        )
        shared_pieces = ready(shared_pieces, expert_rows)
        shared_quarters = [shared_pieces, shared_other]
        shared_quarters += [flip(piece, "dp", 1) for piece in shared_quarters]
        shin_low, shout_low = simple_call(
            functools.partial(shared_weights_kernel, local_rows),
            [out((D, 2 * FFS), BF16), out((FFS, D), BF16)],
            [(sides, in_smem), *[piece.reshape(D, -1) for piece in shared_quarters]],
            4.3,
        )
    else:
        arrived = to_devices(ready(slots, shared_pieces))
        total_rows = arrived.shape[0]
        row_spec = pl.BlockSpec((block, D), lambda i: (i, 0))
        expert_rows = pl.pallas_call(
            expert_kernel,
            out_shape=out((total_rows, D)),
            grid=(total_rows // block,),
            in_specs=[row_spec, whole(gate_up_low), whole(down_low)],
            out_specs=row_spec,
            compiler_params=params(),
            cost_estimate=cost(10),
        )(arrived, gate_up_low, down_low)
        returned = to_points(expert_rows)
        shared_pack = join(ready(shared_pieces, expert_rows), 2, dp_bits)
        shin_low = shared_pack[:, :, : 2 * FFS].reshape(D, -1)
        shout_low = (
            shared_pack[:, :, 2 * FFS :]
            .reshape(expert_count, local_rows, folds, D)
            .swapaxes(1, 2)
            .reshape(FFS, D)
        )
    chunk = 512
    chunks = FFS // chunk
    shared = pl.pallas_call(
        shared_kernel,
        out_shape=out((amount, D)),
        grid=(chunks,),
        in_specs=[
            whole(second),
            pl.BlockSpec((D, chunk), lambda i: (0, i)),
            pl.BlockSpec((D, chunk), lambda i: (0, i + chunks)),
            pl.BlockSpec((chunk, D), lambda i: (i, 0)),
        ],
        out_specs=pl.BlockSpec((amount, D), lambda i: (0, 0)),
        compiler_params=params(),
        cost_estimate=cost(5.8),
    )(second, shin_low, shin_low, shout_low)
    counts = ready(counts_half, expert_rows)
    for bit in dp_bits[1:]:
        counts = counts + flip(counts, "dp", bit)
    weighting = jnp.pad(domain_weights, (0, SMALL - DOMAINS))[None] / jnp.maximum(counts, 1.0)
    side_pad = ((0, 0), (HORIZON_AT, SMALL - small_end))
    target = jnp.pad(target_columns(points), side_pad)
    ahead_small = jnp.pad(
        jnp.asarray(ahead_table())[None], ((0, 0), side_pad[1]), constant_values=1 << 20
    )
    small_low = columns(pack, SMALL, SMALL_AT // SMALL)
    (
        mixer_slope, shared_slope, slope_slots, logits_slope, small_head, gain_three, local_sums,
    ) = simple_call(
        functools.partial(middle_kernel, fast),
        [
            out((amount, D)), out((amount, D), BF16), out((EXPERTS * CAP, D), BF16),
            out((amount, SMALL), BF16), out((D, SMALL)), out((1, D)), out((1, SMALL)),
        ],
        [
            returned, known, rows_table, after, shared, logits, small_low, gains, target,
            ahead_small, weighting,
        ],
        11.4,
    )
    received = exchange_near(slope_slots.reshape(4, 2, CAP, D)) if fast else to_devices(slope_slots)
    chunk = D
    chunks = FFS // chunk
    back_in = [
        pl.BlockSpec((amount, D), lambda i, *unused: (0, 0)),
        pl.BlockSpec((amount, D), lambda i, *unused: (0, 0)),
        pl.BlockSpec((D, chunk), lambda i, *unused: (0, i)),
        pl.BlockSpec((D, chunk), lambda i, *unused: (0, i + chunks)),
        pl.BlockSpec((chunk, D), lambda i, *unused: (i, 0)),
    ]
    second_spec = pl.BlockSpec((amount, D), lambda i, *unused: (0, 0))
    back_args = (second, shared_slope, shin_low, shin_low, shout_low)
    if fast:
        in_spec = pl.BlockSpec(
            (1, D, chunk), lambda i, sides: (jnp.bitwise_xor(i // 2, sides[1]), 0, i % 2)
        )
        give_spec = pl.BlockSpec(
            (1, D, chunk), lambda i, sides: (jnp.bitwise_xor(i // 2, sides[1]), 0, 0)
        )
        out_spec = pl.BlockSpec((2, D // chunks, D), lambda i, sides: (0, i, 0))
        shared_second_slope, in_keep, in_even, in_odd, out_keep, out_give = pl.pallas_call(
            shared_back_split_kernel,
            out_shape=[
                out((amount, D)), out((2, D, FFS // 2)), *[out((2, D, D))] * 4,
            ],
            grid_spec=pltpu.PrefetchScalarGridSpec(
                num_scalar_prefetch=1,
                grid=(chunks,),
                in_specs=back_in,
                out_specs=[second_spec, in_spec, give_spec, give_spec, out_spec, out_spec],
                scratch_shapes=[pltpu.VMEM((chunk, D), F32)],
            ),
            compiler_params=params(),
            cost_estimate=cost(14),
        )(sides, *back_args)
    else:
        shared_second_slope, grad_shin, grad_shout = pl.pallas_call(
            shared_back_kernel,
            out_shape=[out((amount, D)), out((2, D, FFS)), out((FFS, D))],
            grid=(chunks,),
            in_specs=back_in,
            out_specs=[
                second_spec,
                pl.BlockSpec((2, D, chunk), lambda i: (0, 0, i)),
                pl.BlockSpec((chunk, D), lambda i: (i, 0)),
            ],
            compiler_params=params(),
            cost_estimate=cost(10),
        )(*back_args)
    if fast:
        in_even, in_odd, out_other = (flip(a, "dp", 1) for a in (in_even, in_odd, out_give))
        fold_in = pl.BlockSpec((2, D // 4, FFS // 2), lambda i: (0, i, 0))
        fold_out = pl.BlockSpec((2, D // 4, D), lambda i: (0, i, 0))
        wide = FFS // 2 + D
        fold_to = pl.BlockSpec((D // 4, wide), lambda i: (i, 0))
        code_to = pl.BlockSpec((D // 4, wide + 128), lambda i: (i, 0))
        shared_keep, shared_give = pl.pallas_call(
            fold_kernel,
            out_shape=[out((D, wide)), out((D, wide + 128), jnp.int16)],
            grid=(4,),
            in_specs=[fold_in, *[fold_out] * 4],
            out_specs=[fold_to, code_to],
            compiler_params=params(),
            cost_estimate=cost(5.3),
        )(in_keep, in_even, in_odd, out_keep, out_other)
        received = ready(received, shared_second_slope, shared_give)
        shared_other = flip(shared_give, "dp", 2)
    else:
        received = ready(received, shared_second_slope)
    if fast:
        half_shapes = [out((2, D, hidden_local))] * 2 + [out((2, D, D))] * 2
        row_spec = pl.BlockSpec(
            (2, 1, CAP, D), lambda i, j, sides: (j, jnp.bitwise_xor(i, sides[2]), 0, 0)
        )
        grad_rows, expert_in, expert_in_give, expert_out, expert_out_give = pl.pallas_call(
            expert_back_split_kernel,
            out_shape=[out((4, 2, CAP, D), BF16), *half_shapes],
            grid_spec=pltpu.PrefetchScalarGridSpec(
                num_scalar_prefetch=1,
                grid=(2, 2),
                in_specs=[row_spec, row_spec, *held_specs],
                out_specs=[
                    row_spec,
                    *[
                        pl.BlockSpec((1, *a.shape[1:]), lambda i, j, sides: (i, 0, 0))
                        for a in half_shapes
                    ],
                ],
            ),
            compiler_params=params(),
            cost_estimate=cost(19.5),
        )(sides, arrived, received, *held)
        routed_back = exchange_near(ready(grad_rows, shared_other)).reshape(-1, D)
    else:
        grad_rows, grad_expert_in, grad_expert_out = pl.pallas_call(
            expert_back_kernel,
            out_shape=[
                out((total_rows, D), BF16), out((2, D, hidden_local)), out((hidden_local, D)),
            ],
            grid=(total_rows // block,),
            in_specs=[row_spec, row_spec, whole(gate_up_low), whole(down_low)],
            out_specs=[
                row_spec,
                pl.BlockSpec((2, D, hidden_local), lambda i: (0, 0, 0)),
                pl.BlockSpec((hidden_local, D), lambda i: (0, 0)),
            ],
            compiler_params=params(),
            cost_estimate=cost(10),
        )(arrived, received, gate_up_low, down_low)
        routed_back = to_points(grad_rows)
    if fast:
        shared_code = pl.pallas_call(
            add_code_kernel,
            out_shape=out((D, wide + 128), jnp.int16),
            grid=(4,),
            in_specs=[fold_to, code_to],
            out_specs=code_to,
            compiler_params=params(),
            cost_estimate=cost(4.4),
        )(shared_keep, shared_other)
        expert_in_other = flip(expert_in_give, "dp", 1)
        expert_out_other = flip(expert_out_give, "dp", 1)
        half_in = pl.BlockSpec((1, D, hidden_local), lambda i: (i, 0, 0))
        half_out = pl.BlockSpec((1, D, D), lambda i: (i, 0, 0))
        expert_keep, expert_code = pl.pallas_call(
            expert_split_kernel,
            out_shape=[out((2, D // 2, wide)), out((2, D // 2, wide + 128), jnp.int16)],
            grid=(2,),
            in_specs=[in_smem, half_in, half_in, half_out, half_out],
            out_specs=[
                pl.BlockSpec((1, D // 2, wide), lambda i: (i, 0, 0)),
                pl.BlockSpec((1, D // 2, wide + 128), lambda i: (i, 0, 0)),
            ],
            compiler_params=params(),
            cost_estimate=cost(4.6),
        )(sides, expert_in, expert_in_other, expert_out, expert_out_other)
        sums = local_sums + flip(local_sums, "dp", 2)
        routed_plain = routed_back
        routed_back = ready(routed_back, shared_code, expert_code, sums)
    attend_slope, mixed_slope, grad_output, gain_two, small_routed = simple_call(
        functools.partial(attend_back_kernel, fast),
        [
            out((amount, D)), out((amount, D), BF16), out((D, D)), out((1, D)), out((D, SMALL)),
        ],
        [
            routed_back, known, shared_second_slope, logits_slope, small_low, after,
            mixer_slope, gains, mixed, second, columns(pack, D, 3), small_head,
        ],
        6,
    )
    if fast:
        expert_code_other = flip(expert_code, "dp", 2)
        expert_own, expert_far = simple_call(
            expert_far_kernel,
            [out((D // 2, wide)), out((D // 2, wide + 128), jnp.int16)],
            [expert_keep, expert_code_other],
            3.5,
        )
        mixed_slope = ready(mixed_slope, expert_far)
    pack_columns = SMALL_AT + SMALL
    half_columns = SMALL_AT // 2 + SMALL
    last_keep, last_give = simple_call(
        functools.partial(front_back_kernel, fast),
        [
            out((D, half_columns if fast else pack_columns)),
            out((D, half_columns) if fast else (8, 128)),
        ],
        [
            (sides, in_smem), mixed_slope, qkv, log_total, known, rows_table, cosine, sine, first,
            embedded, gains, columns(pack, 3 * D, 0), attend_slope, small_routed, gain_two,
            gain_three, grad_output,
        ],
        18.4,
        [
            pltpu.VMEM((D, 2 * half_columns), F32),
            pltpu.VMEM((amount, D), F32),
            pltpu.VMEM((amount, D), F32),
            pltpu.VMEM((amount, D), F32),
            pltpu.VMEM((amount, 3 * D), BF16),
        ],
    )

    if fast:
        shared_code = ready(shared_code, routed_plain).reshape(expert_count, local_rows, -1)
        (shared_sum,) = simple_call(
            shard_sum_kernel, [out((local_rows, wide))], [exchange(shared_code)], 2.5
        )
        expert_far_other = flip(expert_far, "expert", 4)
        last_give = ready(last_give, expert_far_other)
        (last_code,) = simple_call(
            last_code_kernel,
            [out((D, half_columns + 128), jnp.int16)],
            [(sides, in_smem), last_keep, flip(last_give, "dp", 1)],
            3.3,
        )
        last_code = ready(last_code, shared_sum).reshape(expert_count, local_rows, -1)
        (last_part,) = simple_call(
            last_sum_kernel,
            [out((local_rows, half_columns))],
            [(sides, in_smem), exchange(last_code)],
            2.2,
        )
        last_part = last_part + flip(last_part, "dp", 2)
        expert_in, expert_out = simple_call(
            expert_total_kernel,
            [out((D // 2, hidden_local)), out((D // 2, D))],
            [ready(expert_own, last_code), expert_far_other],
            2.5,
        )
        expert_in_cross = flip(expert_in, "dp", 2)
        expert_out_cross = flip(expert_out, "dp", 2)
        shared_cross = flip(shared_sum, "dp", 2)
        square_pieces = [
            expert_in, expert_in_cross, expert_out, expert_out_cross, shared_sum, shared_cross,
            last_part,
        ]
        weights = (1.0,) * 7
        square_bits = [1]
        pieces = [
            last_part, flip(last_part, "dp", 1), shared_sum, shared_cross,
            flip(shared_sum, "dp", 1), flip(shared_cross, "dp", 1),
            expert_in, expert_in_cross, flip(expert_in, "dp", 1), flip(expert_in_cross, "dp", 1),
            expert_out, expert_out_cross, flip(expert_out, "dp", 1),
            flip(expert_out_cross, "dp", 1),
        ]
        piece_specs = [whole(a) for a in pieces]
    else:
        sums = local_sums
        shin_part = scatter_sum(grad_shin, 0, [1])[0].reshape(expert_count, local_rows, FFS)
        shin_part = expert_scatter(scatter_sum(shin_part, 2, dp_bits[1:]))
        shout_part = scatter_sum(grad_shout.reshape(expert_count, -1, D), 1, dp_bits)
        shout_part = expert_scatter(shout_part)
        expert_in_part = scatter_sum(grad_expert_in.reshape(-1, hidden_local), 0, dp_bits)
        expert_out_part = scatter_sum(grad_expert_out, 0, dp_bits)
        last_part = expert_scatter(last_keep.reshape(expert_count, local_rows, -1))
        for bit in dp_bits:
            last_part = last_part + flip(last_part, "dp", bit)
        square_pieces = [expert_in_part, expert_out_part, shin_part, shout_part, last_part]
        weights = (1.0, 1.0, 1.0, 1.0, 1.0 / dp_count)
        square_bits = dp_bits
        pieces = [
            last_part,
            join(join(shin_part, 1, dp_bits[1:])[None], 0, [1]),
            join(shout_part, 0, dp_bits),
            join(expert_in_part, 0, dp_bits).reshape(expert_input.shape),
            join(expert_out_part, 0, dp_bits),
        ]
        piece_specs = [
            whole(last_part),
            *[tile_spec(i, a.shape, steps) for i, a in zip((4, 5, 7, 8), pieces[1:])],
        ]
    (both_sums,) = simple_call(
        functools.partial(squares_kernel, weights), [out((2, 128))], [sums, *square_pieces], 2.4
    )
    for bit in square_bits:
        both_sums = both_sums + flip(both_sums, "dp", bit)
    both_sums = sum_small(both_sums, ("expert",))
    domain_sums = both_sums[1, :DOMAINS]
    grad_norm = jnp.sqrt(both_sums[0, 0:1])
    shapes = [out(a.shape) for a in masters]
    state_specs = tile_specs(masters, steps)
    updates = pl.pallas_call(
        functools.partial(moments_kernel, fast, count, small_end),
        out_shape=[*shapes, *shapes, *shapes, out((16, 128))],
        grid=(steps,),
        in_specs=[
            in_smem, whole(both_sums), *state_specs, *state_specs, *state_specs, *piece_specs,
        ],
        out_specs=[*state_specs, *state_specs, *state_specs, whole(out((16, 128)))],
        compiler_params=params(),
        cost_estimate=cost(17),
    )(sides, both_sums, *masters, *first_moments, *second_moments, *pieces)
    directions = updates[:count]
    all_totals = sum_small(
        jnp.concatenate([updates[-1][:count], master_squares[:count]], 0), ("expert",)
    )
    totals, master_totals = all_totals[:count], all_totals[count:]
    next_masters = pl.pallas_call(
        functools.partial(step_kernel, count),
        out_shape=shapes,
        grid=(steps,),
        in_specs=[whole(totals), whole(master_totals), *state_specs, *state_specs],
        out_specs=state_specs,
        compiler_params=params(),
        cost_estimate=cost(7),
    )(totals, master_totals, *masters, *directions)
    results = []
    for index in range(count):
        for group in (next_masters, updates[count : 2 * count], updates[2 * count : 3 * count]):
            results.append(group[index].T if index == 3 else group[index])
    norms = jnp.sqrt(all_totals[:, 0])
    results.append(jnp.stack([domain_sums, counts[0, :DOMAINS]]))
    results.append(grad_norm)
    results.append(jnp.stack([norms[count:], norms[:count]], 1))
    return tuple(results)


def solution(mesh):
    placed = (
        P(("dp", "expert")),
        P(("dp", "expert"), None),
        P(("dp", "expert"), None),
        P(("dp", "expert"), None),
        P(),
        P(None, "expert"),
        P("expert", None),
        P("expert", None),
        P("expert", None),
        P("expert", None),
        P("expert", None),
        P("expert", None),
        P(None, None, "expert"),
        P("expert", None),
        P(None, "expert"),
        P("expert", None),
        P("expert", None),
        P("expert", None),
        P("expert", None),
        P("expert", None),
        P("expert", None),
        P(None, None, "expert"),
        P("expert", None),
        P(None, "expert"),
        P("expert", None),
        P("expert", None),
        P("expert", None),
        P("expert", None),
        P("expert", None),
        P("expert", None),
        P(None, None, "expert"),
        P("expert", None),
    )
    return jax.shard_map(
        shards,
        mesh=mesh,
        in_specs=placed,
        out_specs=(
            P(None, "expert"),
            P(None, "expert"),
            P(None, "expert"),
            P("expert", None),
            P("expert", None),
            P("expert", None),
            P("expert", None),
            P("expert", None),
            P("expert", None),
            P("expert", None),
            P("expert", None),
            P("expert", None),
            P("expert", None),
            P("expert", None),
            P("expert", None),
            P("expert", None),
            P("expert", None),
            P("expert", None),
            P("expert", None),
            P("expert", None),
            P("expert", None),
            P(None, None, "expert"),
            P(None, None, "expert"),
            P(None, None, "expert"),
            P("expert", None),
            P("expert", None),
            P("expert", None),
            P(),
            P(),
            P(),
        ),
        check_vma=False,
    )
```

```python
import functools

import jax
import jax.numpy as jnp
import numpy as np
from jax import lax
from jax.experimental import pallas as pl
from jax.experimental.pallas import tpu as pltpu
from jax.sharding import PartitionSpec as P

D = 384
HEADS = 12
HD = 32
FFS = 1536
EXPERTS = 8
DOMAINS = 9
STEP = 10
CAP = 256


HORIZONS = (1, 8, 32, 64)
REACH = 64
KINK_THRESHOLD = 2.0
EPS_NORM = 1e-06
CLIP = 0.01
BETA_ONE = 0.9
BETA_TWO = 0.99
EPS_ADAM = 1e-08
DECAY = 0.01
RATE = 0.3


def ahead_table():
    return np.concatenate([np.arange(horizon_len) for horizon_len in HORIZONS]).astype(np.int32)


def target_columns(samples):
    amount = samples.shape[0]
    padded = jnp.concatenate([samples, jnp.zeros((REACH + 1,), samples.dtype)])
    future = jnp.stack([padded[1 + offset : 1 + offset + amount] for offset in range(REACH)], 1)
    return future[:, ahead_table()]


ROW_BLOCK = 256
SMALL = 128
HORIZON_AT = EXPERTS + 1
VECTORS_AT = 120
SMALL_AT = 4 * D
COUNTS_AT = 125
CODE_ROWS = 16
VMEM = 56 * 1024 * 1024
F32 = jnp.float32
BF16 = jnp.bfloat16


def mm(left, right):
    return jnp.dot(left, right, preferred_element_type=F32)


def mm_nt(left, right):
    return lax.dot_general(left, right, (((1,), (1,)), ((), ())), preferred_element_type=F32)


def mm_tn(left, right):
    return lax.dot_general(left, right, (((0,), (0,)), ((), ())), preferred_element_type=F32)


def inverse_rms(rows):
    return lax.rsqrt(jnp.mean(rows * rows, axis=-1, keepdims=True) + EPS_NORM)


def rms_back(rows, inverse, gain, slope):
    gain_slope = jnp.sum(slope * rows * inverse, 0, keepdims=True)
    scaled = slope * gain
    return (
        inverse * scaled
        - rows * (inverse * inverse * inverse) * jnp.mean(rows * scaled, -1, keepdims=True),
        gain_slope,
    )


def lanes_of(shape):
    return lax.broadcasted_iota(jnp.int32, shape, len(shape) - 1)


def half_swap(rows):
    half_width = HD // 2
    lane = lanes_of(rows.shape)
    return jnp.where(
        lane % HD < half_width,
        pltpu.roll(rows, rows.shape[1] - half_width, 1),
        pltpu.roll(rows, half_width, 1),
    )


SLOT, SERIES_OF, FINISH, DOMAIN, CHOICE, VALUE, PLACE = 0, 2, 3, 4, 5, 7, 8


def tables_kernel(
    lengths, domains, frequency, points_row, experts_row, cosine, sine, columns_out, rows_out
):
    amount = points_row.shape[1]
    place = lax.broadcasted_iota(jnp.int32, (1, amount), 1)
    series = jnp.zeros((1, amount), jnp.int32)
    begin = jnp.zeros((1, amount), jnp.int32)
    finish = jnp.zeros((1, amount), jnp.int32)
    domain = jnp.zeros((1, amount), jnp.int32)
    start = jnp.int32(0)
    for index in range(lengths.shape[1]):
        stop = start + lengths[0, index]
        inside = (place >= start) & (place < stop)
        series = jnp.where(inside, index, series)
        begin = jnp.where(inside, start, begin)
        finish = jnp.where(inside, stop, finish)
        domain = jnp.where(inside, domains[0, index], domain)
        start = stop
    name = lax.broadcasted_iota(jnp.int32, (16, amount), 0)
    choices = [experts_row[k : k + 1, :] for k in range(2)]
    named = [(name == choice).astype(F32) for choice in choices]
    earlier = (
        lax.broadcasted_iota(jnp.int32, (amount, amount), 0)
        < lax.broadcasted_iota(jnp.int32, (amount, amount), 1)
    )
    before = mm((named[0] + named[1]).astype(BF16), earlier.astype(F32).astype(BF16))
    entries = []
    for k in range(2):
        rank = jnp.sum(named[k] * before, 0, keepdims=True)
        entries.append(choices[k].astype(F32) * CAP + rank)
    entries += [series, finish, domain, *choices, points_row[...], place - begin]
    row = lax.broadcasted_iota(jnp.int32, (128, amount), 0)
    table = jnp.zeros((128, amount), F32)
    for index, entry in enumerate(entries):
        table = jnp.where(row == index, entry.astype(F32), table)
    rows_out[...] = table[:8]
    columns = table.T
    columns_out[...] = columns
    angles = columns[:, PLACE : PLACE + 1] * frequency[...]
    cosine[...] = jnp.cos(angles)
    turned = jnp.sin(angles)
    sine[...] = jnp.where(lanes_of((amount, 128)) % HD < HD // 2, -turned, turned)


def allowed_block(table, rows_table, start, rows, keys):
    query = start + lax.broadcasted_iota(jnp.int32, (rows, keys), 0)
    key = lax.broadcasted_iota(jnp.int32, (rows, keys), 1)
    series_col = table[start : start + rows, SERIES_OF : SERIES_OF + 1]
    return (series_col == rows_table[SERIES_OF : SERIES_OF + 1, :keys]) & (key <= query)


def slot_place(grouped, expert):
    return (expert % 4) * 2 + expert // 4 if grouped else expert


def slot_rows_hot(slot_row, expert):
    slot = expert * CAP + lax.broadcasted_iota(jnp.int32, (CAP, slot_row.shape[1]), 0)
    return (slot_row.astype(jnp.int32) == slot).astype(F32).astype(BF16)


def slot_cols_hot(slot_col, expert):
    slot = expert * CAP + lax.broadcasted_iota(jnp.int32, (slot_col.shape[0], CAP), 1)
    return (slot_col.astype(jnp.int32) == slot).astype(F32).astype(BF16)


def pack_kernel(small_end, core, lengths, domains, ahead, input_w, output_w, router, horizon, vectors, out):
    rows = input_w.shape[0]

    def placed(count, at):
        row = lax.broadcasted_iota(jnp.int32, (count, SMALL), 0)
        return (row + at == lanes_of((count, SMALL))).astype(F32).astype(BF16)

    small = (
        mm_tn(router[...].astype(BF16), placed(HORIZON_AT, 0))
        + mm(horizon[...].astype(BF16), placed(small_end - HORIZON_AT, HORIZON_AT))
        + mm_tn(vectors[...].astype(BF16), placed(vectors.shape[0], VECTORS_AT))
    )
    row = lax.broadcasted_iota(jnp.int32, (rows, SMALL), 0)
    lane = lanes_of((rows, SMALL))
    counts = jnp.zeros((rows, SMALL), F32)
    for series in range(lengths.shape[1]):
        left = jnp.maximum(lengths[0, series] - 1 - ahead[...], 0).astype(F32)
        entries = jnp.sum(left, -1, keepdims=True)
        counts = counts + jnp.where(row == domains[0, series], entries, 0.0)
    high = jnp.floor(counts * (1.0 / 256.0))
    small = jnp.where(lane == COUNTS_AT, high, small)
    small = jnp.where(lane == COUNTS_AT + 1, counts - 256.0 * high, small)
    flat = jnp.concatenate([input_w[...], output_w[...]], 1)
    half = 2 * D
    mine = jnp.where(core[0] == 0, flat[:, :half], flat[:, half:]).astype(BF16)
    for target in range(out.shape[0]):
        out[target, :, :half] = mine
        out[target, :, half:] = small.astype(BF16)


def pair_kernel(sides, own, far, out):
    low = sides[2] == 0
    first = jnp.where(low, own[...], far[...])
    second = jnp.where(low, far[...], own[...])
    for target in range(out.shape[0]):
        out[target, 0] = first
        out[target, 1] = second


def front_kernel(
    grouped, local_rows, core, mine, other, cosine, sine, known, slot_row,
    embedded_out, first_out, qkv_out, log_out, mixed_out, after_out, second_out, logits_out,
    slots_out, gains_out, pack, counts_out,
):
    amount = known.shape[0]
    half = 2 * D
    low = core[0] == 0
    for index in range(D // local_rows):
        place = slot_place(grouped, index)
        here = slice(index * local_rows, (index + 1) * local_rows)
        there = slice(place * local_rows, (place + 1) * local_rows)
        left, right = mine[there, :half], other[there, :half]
        pack[here, :half] = jnp.where(low, left, right)
        pack[here, half:SMALL_AT] = jnp.where(low, right, left)
        pack[here, SMALL_AT:] = mine[there, half:]
    table = pack[:, SMALL_AT:].astype(F32).T
    gains = table[VECTORS_AT : VECTORS_AT + 8]
    gains_out[...] = gains
    other_table = other[:, half:].astype(F32).T
    row = lax.broadcasted_iota(jnp.int32, (D, SMALL), 0)
    fold = (row % local_rows == lanes_of((D, SMALL))).astype(F32).astype(BF16)
    digits = mm(table[VECTORS_AT : VECTORS_AT + 8].astype(BF16), fold) + mm(
        other_table[VECTORS_AT : VECTORS_AT + 8].astype(BF16), fold
    )
    at = COUNTS_AT - VECTORS_AT
    counts_out[...] = digits[at : at + 1] * 256.0 + digits[at + 1 : at + 2]
    value = known[:, VALUE : VALUE + 1]
    gate = value * gains[0:1]
    embedded = gate * jax.nn.sigmoid(gate) * (value * gains[1:2])
    embedded_out[...] = embedded
    first = (embedded * inverse_rms(embedded) * gains[2:3]).astype(BF16)
    first_out[...] = first
    projected = mm(first, pack[:, : 3 * D])
    cos_rows, sin_rows = cosine[...], sine[...]
    for block in range(6):
        part = projected[:, block * 128 : (block + 1) * 128]
        part = part * cos_rows + half_swap(part) * sin_rows
        qkv_out[:, block * 128 : (block + 1) * 128] = part.astype(BF16)
    qkv_out[:, 2 * D :] = projected[:, 2 * D :].astype(BF16)
    lane = lanes_of((ROW_BLOCK, 128))
    for start in range(0, amount, ROW_BLOCK):
        keys = start + ROW_BLOCK
        allowed = allowed_block(known[...], slot_row[...], start, ROW_BLOCK, keys)
        log_rows = jnp.zeros((ROW_BLOCK, 128), F32)
        for group in range(D // 128):
            query = qkv_out[start : start + ROW_BLOCK, group * 128 : (group + 1) * 128]
            key = qkv_out[:keys, D + group * 128 : D + (group + 1) * 128]
            held = qkv_out[:keys, 2 * D + group * 128 : 2 * D + (group + 1) * 128]
            gathered = jnp.zeros((ROW_BLOCK, 128), F32)
            for head in range(128 // HD):
                own = lane // HD == head
                raw = mm_nt(jnp.where(own, query, jnp.zeros_like(query)), key) * HD ** (-0.5)
                raw = jnp.where(allowed, raw, -1e30)
                top = jnp.max(raw, -1, keepdims=True)
                exponent = jnp.exp(raw - top)
                total = jnp.sum(exponent, -1, keepdims=True)
                attention = (exponent * (1.0 / total)).astype(BF16)
                gathered = jnp.where(own, mm(attention, held), gathered)
                log_rows = jnp.where(
                    lane == group * (128 // HD) + head, top + jnp.log(total), log_rows
                )
            mixed_out[start : start + ROW_BLOCK, group * 128 : (group + 1) * 128] = (
                gathered.astype(BF16)
            )
        log_out[start : start + ROW_BLOCK, :] = log_rows
    after = embedded + mm(mixed_out[...], pack[:, 3 * D : 4 * D])
    after_out[...] = after
    second = (after * inverse_rms(after) * gains[3:4]).astype(BF16)
    second_out[...] = second
    logits_out[...] = mm(second, pack[:, SMALL_AT:])
    for expert in range(EXPERTS):
        hot = slot_rows_hot(slot_row[0:1, :], expert) + slot_rows_hot(slot_row[1:2, :], expert)
        place = slot_place(grouped, expert)
        slots_out[place * CAP : (place + 1) * CAP, :] = mm(hot, second).astype(BF16)


def shared_kernel(second, gate_w, lift_w, down_w, shared_out):
    gate = mm(second[...], gate_w[...])
    lift = mm(second[...], lift_w[...])
    hidden = (gate * jax.nn.sigmoid(gate) * lift).astype(BF16)
    part = mm(hidden, down_w[...])

    @pl.when(pl.program_id(0) == 0)
    def _():
        shared_out[...] = part

    @pl.when(pl.program_id(0) != 0)
    def _():
        shared_out[...] += part


def code_rows(part, ref):
    top = jnp.max(jnp.abs(part), -1, keepdims=True)
    power = jnp.ceil(jnp.log2(jnp.maximum(top, 1e-30)))
    code = jnp.clip(jnp.round(part * jnp.exp2(15.0 - power)), -32767.0, 32767.0)
    ref[:CAP, :] = code.astype(jnp.int32).astype(jnp.int16)
    row = lax.broadcasted_iota(jnp.int32, (CAP, CAP), 0)
    column = lax.broadcasted_iota(jnp.int32, (CAP, CAP), 1)
    powers = jnp.sum(jnp.where(row == column, power, 0.0), 0, keepdims=True)
    powers = jnp.concatenate([powers, jnp.zeros((1, D - CAP), F32)], 1)
    ref[CAP:, :] = jnp.broadcast_to(powers, (CODE_ROWS, D)).astype(jnp.int32).astype(jnp.int16)


def unit(rows, gate_up, down):
    gate = mm(rows, gate_up[0])
    lift = mm(rows, gate_up[1])
    hidden = (gate * jax.nn.sigmoid(gate) * lift).astype(BF16)
    return mm(hidden, down[...])


def expert_kernel(rows, gate_up, down, rows_out):
    rows_out[...] = unit(rows[...], gate_up, down)


def pair_expert_kernel(sides, rows, gate_up, down, gate_up_far, down_far, rows_out):
    sources = rows.shape[0]
    flat = rows[...].reshape(sources * CAP, D)

    def serve(weights):
        result = unit(flat, *weights)
        for source in range(sources):
            code_rows(result[source * CAP : (source + 1) * CAP], rows_out.at[source, 0])

    pl.when(pl.program_id(0) == 0)(lambda: serve((gate_up, down)))
    pl.when(pl.program_id(0) == 1)(lambda: serve((gate_up_far, down_far)))


def far_weights_kernel(sides, *refs):
    pieces, (gate_up, down) = refs[:4], refs[4:]
    me = sides[0] * 2 + sides[1]
    half, wide = pieces[0].shape[0], gate_up.shape[2]
    for piece in range(4):
        core, cross = piece // 2, piece % 2
        value = picked_piece(pieces, jnp.bitwise_xor(piece, me), lambda ref: ref[...])
        gate_up[core, cross * half : (cross + 1) * half, :] = value[:, :wide]
        down[piece * half : (piece + 1) * half, :] = value[:, wide:]


def shared_weights_kernel(local_rows, sides, *refs):
    pieces, (both, down) = refs[:4], refs[4:]
    me = sides[0] * 2 + sides[1]
    wide = pieces[0].shape[1]
    shard = down.shape[0] // (D // local_rows)
    for piece in range(4):
        value = picked_piece(pieces, jnp.bitwise_xor(piece, me), lambda ref: ref[...])
        for index in range(D // local_rows):
            place = slot_place(True, index)
            rows = value[place * local_rows : (place + 1) * local_rows]
            for at in range(0, wide, D):
                column = piece * wide + at
                part = rows[:, at : at + D]
                if column < 2 * FFS:
                    both[index * local_rows : (index + 1) * local_rows, column : column + D] = part
                else:
                    row = index * shard + (column - 2 * FFS) // D * local_rows
                    down[row : row + local_rows, :] = part


def unit_back(rows, slope, gate_w, lift_w, down_w):
    gate = mm(rows, gate_w)
    lift = mm(rows, lift_w)
    bent = jax.nn.sigmoid(gate)
    smooth = gate * bent
    hidden = (smooth * lift).astype(BF16)
    hidden_slope = mm_nt(slope, down_w)
    gate_slope = (hidden_slope * lift * (bent * (1.0 + gate * (1.0 - bent)))).astype(BF16)
    lift_slope = (hidden_slope * smooth).astype(BF16)
    return hidden, gate_slope, lift_slope


def expert_back_kernel(rows, slope, gate_up, down, rows_out, in_out, out_out):
    hidden, gate_slope, lift_slope = unit_back(
        rows[...], slope[...], gate_up[0], gate_up[1], down[...]
    )
    rows_out[...] = (mm_nt(gate_slope, gate_up[0]) + mm_nt(lift_slope, gate_up[1])).astype(BF16)

    @pl.when(pl.program_id(0) == 0)
    def _():
        in_out[...] = jnp.zeros_like(in_out)
        out_out[...] = jnp.zeros_like(out_out)

    in_out[0] += mm_tn(rows[...], gate_slope)
    in_out[1] += mm_tn(rows[...], lift_slope)
    out_out[...] += mm_tn(hidden, slope[...])


def shared_back_kernel(second, slope, gate_w, lift_w, down_w, second_out, in_out, out_out):
    hidden, gate_slope, lift_slope = unit_back(
        second[...], slope[...], gate_w[...], lift_w[...], down_w[...]
    )
    part = mm_nt(gate_slope, gate_w[...]) + mm_nt(lift_slope, lift_w[...])

    @pl.when(pl.program_id(0) == 0)
    def _():
        second_out[...] = part

    @pl.when(pl.program_id(0) != 0)
    def _():
        second_out[...] += part

    in_out[0] = mm_tn(second[...], gate_slope)
    in_out[1] = mm_tn(second[...], lift_slope)
    out_out[...] = mm_tn(hidden, slope[...])


def expert_back_split_kernel(
    sides, rows, slope, gate_up, down, gate_up_far, down_far,
    rows_out, in_keep, in_give, out_keep, out_give,
):
    sources = rows.shape[0]
    flat = rows[...].reshape(sources * CAP, D)
    flat_slope = slope[...].reshape(sources * CAP, D)

    @pl.when(pl.program_id(1) == 0)
    def _():
        for ref in (in_keep, in_give, out_keep, out_give):
            ref[...] = jnp.zeros_like(ref)

    def serve(gate_w, down_w):
        hidden, gate_slope, lift_slope = unit_back(
            flat, flat_slope, gate_w[0], gate_w[1], down_w[...]
        )
        result = (mm_nt(gate_slope, gate_w[0]) + mm_nt(lift_slope, gate_w[1])).astype(BF16)
        rows_out[...] = result.reshape(rows_out.shape)
        half = hidden.shape[1] // 2
        low = sides[0] == 0
        gate = mm_tn(flat, gate_slope)
        lift = mm_tn(flat, lift_slope)
        in_keep[0] += jnp.where(low, gate, lift)
        in_give[0] += jnp.where(low, lift, gate)
        first = mm_tn(hidden[:, :half], flat_slope)
        last = mm_tn(hidden[:, half:], flat_slope)
        out_keep[0] += jnp.where(low, first, last)
        out_give[0] += jnp.where(low, last, first)

    pl.when(pl.program_id(0) == 0)(lambda: serve(gate_up, down))
    pl.when(pl.program_id(0) == 1)(lambda: serve(gate_up_far, down_far))


def shared_back_split_kernel(
    sides, second, slope, gate_w, lift_w, down_w,
    second_out, in_keep, in_give_even, in_give_odd, out_keep, out_give, out_ref,
):
    hidden, gate_slope, lift_slope = unit_back(
        second[...], slope[...], gate_w[...], lift_w[...], down_w[...]
    )
    part = mm_nt(gate_slope, gate_w[...]) + mm_nt(lift_slope, lift_w[...])

    @pl.when(pl.program_id(0) == 0)
    def _():
        second_out[...] = part

    @pl.when(pl.program_id(0) != 0)
    def _():
        second_out[...] += part

    core, cross = sides[0], sides[1]
    low = core == 0
    gate = mm_tn(second[...], gate_slope)
    lift = mm_tn(second[...], lift_slope)
    in_keep[0] = jnp.where(low, gate, lift)
    given = jnp.where(low, lift, gate)
    half = given.shape[1] // 2
    in_give_even[0] = given[:, :half]
    in_give_odd[0] = given[:, half:]
    out_ref[...] = mm_tn(hidden, slope[...])
    quarter = D // EXPERTS
    shards = out_keep.shape[1] // quarter
    for shard in range(shards):
        for side in range(2):
            for ref, half in ((out_keep, core), (out_give, 1 - core)):
                piece = half * 2 + jnp.bitwise_xor(cross, side)
                start = pl.multiple_of(shard * 4 * quarter + piece * quarter, 8)
                ref[side, shard * quarter : (shard + 1) * quarter, :] = out_ref[
                    pl.ds(start, quarter), :
                ]


def coded_tile(value):
    top = jnp.max(jnp.abs(value), -1, keepdims=True)
    power = jnp.ceil(jnp.log2(jnp.maximum(top, 1e-30)))
    code = jnp.clip(jnp.round(value * jnp.exp2(15.0 - power)), -32767.0, 32767.0)
    return code, power


def encode(ref, tiles):
    lane = lanes_of(tiles[0].shape)
    powers = jnp.zeros(tiles[0].shape, F32)
    for index, tile in enumerate(tiles):
        code, power = coded_tile(tile)
        ref[:, index * 128 : (index + 1) * 128] = code.astype(jnp.int32).astype(jnp.int16)
        powers = jnp.where(lane == index, power, powers)
    ref[:, len(tiles) * 128 :] = powers.astype(jnp.int32).astype(jnp.int16)


def decode(ref):
    count = ref.shape[-1] // 128 - 1
    scale = jnp.exp2(ref[..., count * 128 :].astype(jnp.int32).astype(F32) - 15.0)
    return [
        ref[..., index * 128 : (index + 1) * 128].astype(jnp.int32).astype(F32)
        * scale[..., index : index + 1]
        for index in range(count)
    ]


def tiles_of(value):
    return [value[:, at : at + 128] for at in range(0, value.shape[1], 128)]


def fold_kernel(in_keep, in_even, in_odd, out_keep, out_other, keep, give):
    wide = in_keep.shape[2]
    half = wide // 2
    keep[:, :half] = in_keep[0, :, :half] + in_even[0]
    keep[:, half:wide] = in_keep[0, :, half:] + in_odd[0]
    keep[:, wide:] = out_keep[0] + out_other[0]
    encode(
        give,
        tiles_of(in_keep[1, :, :half] + in_even[1])
        + tiles_of(in_keep[1, :, half:] + in_odd[1])
        + tiles_of(out_keep[1] + out_other[1]),
    )


def add_code_kernel(keep, other, code):
    encode(code, [mine + theirs for mine, theirs in zip(tiles_of(keep[...]), decode(other))])


def shard_sum_kernel(codes, total):
    for index, tile in enumerate(decode(codes)):
        total[:, index * 128 : (index + 1) * 128] = jnp.sum(tile, 0)


def expert_split_kernel(sides, in_keep, in_other, out_keep, out_other, keep, code):
    wide, half = in_keep.shape[2], in_keep.shape[1] // 2
    here = pl.ds(pl.multiple_of(sides[1] * half, 8), half)
    there = pl.ds(pl.multiple_of((1 - sides[1]) * half, 8), half)
    keep[0, :, :wide] = in_keep[0, here, :] + in_other[0, here, :]
    keep[0, :, wide:] = out_keep[0, here, :] + out_other[0, here, :]
    encode(
        code.at[0],
        tiles_of(in_keep[0, there, :] + in_other[0, there, :])
        + tiles_of(out_keep[0, there, :] + out_other[0, there, :]),
    )


def expert_far_kernel(keep, codes, own, far):
    for index, tile in enumerate(decode(codes.at[0])):
        here = slice(index * 128, (index + 1) * 128)
        own[:, here] = keep[0, :, here] + tile
    encode(far, [mine + theirs for mine, theirs in zip(tiles_of(keep[1]), decode(codes.at[1]))])


def expert_total_kernel(own, code, total):
    encode(
        total, [mine + theirs for mine, theirs in zip(tiles_of(own[...]), decode(code))]
    )


def last_code_kernel(core, keep, other, code):
    tiles = tiles_of(keep[...] + other[...])
    rough, power = coded_tile(tiles[5])
    tiles[6] = jnp.where(core[0] == 1, tiles[5] - rough * jnp.exp2(power - 15.0), tiles[6])
    encode(code, tiles)


def last_sum_kernel(core, codes, total):
    tiles = decode(codes)
    high = core[0] == 1
    fine = tiles[6]
    tiles[5] = jnp.where(high, tiles[5] + fine, tiles[5])
    tiles[6] = jnp.where(high, 0.0, fine)
    for index, tile in enumerate(tiles):
        total[:, index * 128 : (index + 1) * 128] = jnp.sum(tile, 0)


def middle_kernel(
    grouped, returned, known, slot_row, after, shared, logits, small, gains, target, ahead, weighting,
    mixer_out, shared_slope_out, slots_out, logits_slope_out, small_out, gain_out, sums_out,
):
    amount = after.shape[0]
    lane = lanes_of((amount, SMALL))
    table = known[...]
    integers = table[:, :8].astype(jnp.int32)
    chosen = [
        (lane == integers[:, CHOICE + k : CHOICE + k + 1]).astype(F32) for k in range(2)
    ]
    point = lax.broadcasted_iota(jnp.int32, (amount, SMALL), 0)
    usable = (point + 1 + ahead[...] < integers[:, FINISH : FINISH + 1]).astype(F32)
    logit = logits[...]
    routed = lane < EXPERTS
    top = jnp.max(jnp.where(routed, logit, -1e30), -1, keepdims=True)
    exponent = jnp.where(routed, jnp.exp(jnp.where(routed, logit - top, 0.0)), 0.0)
    probs = exponent / jnp.sum(exponent, -1, keepdims=True)
    gates = [jnp.sum(chosen[k] * probs, -1, keepdims=True) for k in range(2)]
    shared_gate = jax.nn.sigmoid(
        jnp.sum(jnp.where(lane == EXPERTS, logit, 0.0), -1, keepdims=True)
    )
    picked = [jnp.zeros((amount, D), F32), jnp.zeros((amount, D), F32)]
    for expert in range(EXPERTS):
        place = slot_place(grouped, expert)
        if len(returned.shape) == 2:
            rows = returned[place * CAP : (place + 1) * CAP, :]
            scale = 1.0
        else:
            rows = returned[place, :CAP, :].astype(jnp.int32).astype(F32)
            powers = returned[place, CAP:, :].astype(jnp.int32).astype(F32)
            scale = jnp.exp2(powers[0:1, :CAP] - 15.0)
        high = rows.astype(BF16)
        rest = (rows - high.astype(F32)).astype(BF16)
        for k in range(2):
            slot = expert * CAP + lax.broadcasted_iota(jnp.int32, (amount, CAP), 1)
            hot = jnp.where(integers[:, SLOT + k : SLOT + k + 1] == slot, scale, 0.0).astype(BF16)
            picked[k] = picked[k] + (mm(hot, high) + mm(hot, rest))
    mixer = (
        after[...] + shared_gate * shared[...] + (gates[0] * picked[0] + gates[1] * picked[1])
    )
    inverse = inverse_rms(mixer)
    gain = gains[4:5]
    third = (mixer * inverse * gain).astype(BF16)
    residue = mm(third, small[...]) - target[...]
    size = jnp.abs(residue)
    cost = (
        jnp.where(
            size <= KINK_THRESHOLD,
            0.5 * residue * residue,
            KINK_THRESHOLD * (size - 0.5 * KINK_THRESHOLD),
        )
        * usable
    )
    domain_hot = (lane == integers[:, DOMAIN : DOMAIN + 1]).astype(F32)
    sums_out[...] = jnp.sum(domain_hot * jnp.sum(cost, -1, keepdims=True), 0, keepdims=True)
    weight = jnp.sum(domain_hot * weighting[...], -1, keepdims=True)
    slope = (
        jnp.clip(residue, -KINK_THRESHOLD, KINK_THRESHOLD) * usable * weight
    ).astype(BF16)
    small_out[...] = mm_tn(third, slope)
    mixer_slope, gain_slope = rms_back(mixer, inverse, gain, mm_nt(slope, small[...]))
    gain_out[...] = gain_slope
    mixer_out[...] = mixer_slope
    shared_slope_out[...] = (shared_gate * mixer_slope).astype(BF16)
    gate_slope = jnp.sum(mixer_slope * shared[...], -1, keepdims=True)
    probs_slope = chosen[0] * jnp.sum(mixer_slope * picked[0], -1, keepdims=True) + chosen[
        1
    ] * jnp.sum(mixer_slope * picked[1], -1, keepdims=True)
    inner = jnp.sum(probs * probs_slope, -1, keepdims=True)
    logits_slope_out[...] = jnp.where(
        routed,
        probs * (probs_slope - inner),
        jnp.where(lane == EXPERTS, gate_slope * (shared_gate * (1.0 - shared_gate)), 0.0),
    ).astype(BF16)
    slopes = [(gates[k] * mixer_slope).astype(BF16) for k in range(2)]
    for expert in range(EXPERTS):
        place = slot_place(grouped, expert)
        slots_out[place * CAP : (place + 1) * CAP, :] = (
            mm(slot_rows_hot(slot_row[0:1, :], expert), slopes[0])
            + mm(slot_rows_hot(slot_row[1:2, :], expert), slopes[1])
        ).astype(BF16)


def attend_back_kernel(
    grouped, returned, known, second_slope, logits_slope, small, after, mixer_slope, gains, mixed, second,
    output_w, small_before,
    attend_out, mixed_out, output_out, gain_out, small_out,
):
    slope = second_slope[...] + mm_nt(logits_slope[...], small[...])
    for expert in range(EXPERTS):
        hot = slot_cols_hot(known[:, 0:1], expert) + slot_cols_hot(known[:, 1:2], expert)
        place = slot_place(grouped, expert)
        slope = slope + mm(hot, returned[place * CAP : (place + 1) * CAP, :])
    after_rows = after[...]
    part, gain_slope = rms_back(after_rows, inverse_rms(after_rows), gains[3:4], slope)
    gain_out[...] = gain_slope
    attend = mixer_slope[...] + part
    attend_out[...] = attend
    low = attend.astype(BF16)
    output_out[...] = mm_tn(mixed[...], low)
    mixed_out[...] = mm_nt(low, output_w[...]).astype(BF16)
    small_out[...] = small_before[...] + mm_tn(second[...], logits_slope[...])


def front_back_kernel(
    fast, core, mixed_slope, qkv, log_total, known, rows_table, cosine, sine, first, embedded,
    gains, input_w, attend_slope, small_before, gain_two, gain_three, output_before,
    keep_out, give_out,
    pack_out, query_acc, key_acc, held_acc, slope_ref,
):
    amount = first.shape[0]
    key_acc[...] = jnp.zeros_like(key_acc)
    held_acc[...] = jnp.zeros_like(held_acc)
    lane = lanes_of((ROW_BLOCK, 128))
    lane_all = lanes_of((amount, 128))
    for start in range(0, amount, ROW_BLOCK):
        keys = start + ROW_BLOCK
        here = slice(start, start + ROW_BLOCK)
        allowed = allowed_block(known[...], rows_table[...], start, ROW_BLOCK, keys)
        for group in range(D // 128):
            wide = slice(group * 128, (group + 1) * 128)
            query = qkv[here, group * 128 : (group + 1) * 128]
            key = qkv[:keys, D + group * 128 : D + (group + 1) * 128]
            held = qkv[:keys, 2 * D + group * 128 : 2 * D + (group + 1) * 128]
            out_slope = mixed_slope[here, wide]
            query_sum = jnp.zeros((ROW_BLOCK, 128), F32)
            key_sum = jnp.zeros((keys, 128), F32)
            held_sum = jnp.zeros((keys, 128), F32)
            for head in range(128 // HD):
                own = lane // HD == head
                own_query = jnp.where(own, query, jnp.zeros_like(query))
                own_slope = jnp.where(own, out_slope, jnp.zeros_like(out_slope))
                own_key = jnp.where(lane_all[:keys] // HD == head, key, jnp.zeros_like(key))
                at = group * (128 // HD) + head
                raw = mm_nt(own_query, key) * HD ** (-0.5)
                probs = jnp.exp(jnp.where(allowed, raw - log_total[here, at : at + 1], -1e30))
                held_sum = held_sum + mm_tn(probs.astype(BF16), own_slope)
                probs_slope = mm_nt(own_slope, held)
                inner = jnp.sum(probs_slope * probs, -1, keepdims=True)
                raw_slope = (probs * (probs_slope - inner)).astype(BF16)
                query_sum = query_sum + mm(raw_slope, own_key)
                key_sum = key_sum + mm_tn(raw_slope, own_query)
            query_acc[here, wide] = query_sum
            key_acc[:keys, wide] += key_sum
            held_acc[:keys, wide] += held_sum
    cos_rows, sin_rows = cosine[...], sine[...]
    for block in range(3):
        wide = slice(block * 128, (block + 1) * 128)
        for base, acc in ((0, query_acc), (D, key_acc)):
            part = acc[:, wide] * HD ** (-0.5)
            part = part * cos_rows + half_swap(part * sin_rows)
            slope_ref[:, base + block * 128 : base + (block + 1) * 128] = part.astype(BF16)
    slope_ref[:, 2 * D :] = held_acc[...].astype(BF16)
    projected_slope = slope_ref[...]
    pack_out[:, : 3 * D] = mm_tn(first[...], projected_slope)
    pack_out[:, 3 * D : SMALL_AT] = output_before[...]
    first_slope = mm_nt(projected_slope, input_w[...])
    rows = embedded[...]
    part, gain_one = rms_back(rows, inverse_rms(rows), gains[2:3], first_slope)
    slope = attend_slope[...] + part
    value = known[:, VALUE : VALUE + 1]
    gate = value * gains[0:1]
    bent = jax.nn.sigmoid(gate)
    gate_gradient = jnp.sum(
        slope * (value * gains[1:2]) * (bent * (1.0 + gate * (1.0 - bent))) * value,
        0,
        keepdims=True,
    )
    lift_gradient = jnp.sum(slope * (gate * bent) * value, 0, keepdims=True)
    row = lax.broadcasted_iota(jnp.int32, (128, D), 0)
    table = jnp.zeros((128, D), F32)
    for offset, piece in enumerate(
        (gate_gradient, lift_gradient, gain_one, gain_two[...], gain_three[...])
    ):
        table = jnp.where(row == VECTORS_AT + offset, piece, table)
    pack_out[:, SMALL_AT : SMALL_AT + SMALL] = small_before[...] + table.T
    if not fast:
        keep_out[...] = pack_out[:, : keep_out.shape[1]]
        give_out[...] = jnp.zeros_like(give_out)
        return
    pack_out[:, SMALL_AT + SMALL :] = jnp.zeros_like(pack_out[:, SMALL_AT + SMALL :])
    half = keep_out.shape[1]
    keep_out[...] = pack_out[:, pl.ds(pl.multiple_of(core[0] * half, 128), half)]
    give_out[...] = pack_out[:, pl.ds(pl.multiple_of((1 - core[0]) * half, 128), half)]


def lamb_direction(master, gradient, mean, square, factor):
    clipped = gradient * factor
    mean_next = BETA_ONE * mean + (1.0 - BETA_ONE) * clipped
    square_next = BETA_TWO * square + (1.0 - BETA_TWO) * clipped * clipped
    direction = (
        mean_next
        / (1.0 - BETA_ONE**STEP)
        / (jnp.sqrt(square_next / (1.0 - BETA_TWO**STEP)) + EPS_ADAM)
        + DECAY * master
    )
    return mean_next, square_next, direction


def whole(array):
    shape = array.shape
    return pl.BlockSpec(shape, lambda *unused: (0,) * len(shape))


def params(limit=VMEM):
    return pltpu.CompilerParams(vmem_limit_bytes=limit)


def cost(microseconds):
    return pl.CostEstimate(flops=int(microseconds * 1.15e9), bytes_accessed=0, transcendentals=0)


def columns(array, width, at):
    return (array, pl.BlockSpec((array.shape[0], width), lambda *unused: (0, at)))


def simple_call(kernel, outs, args, microseconds, scratch=()):
    pairs = [a if isinstance(a, tuple) else (a, whole(a)) for a in args]
    args = [a for a, spec in pairs]
    return pl.pallas_call(
        kernel,
        out_shape=outs,
        in_specs=[spec for a, spec in pairs],
        out_specs=[whole(a) for a in outs],
        scratch_shapes=list(scratch),
        grid=(1,),
        compiler_params=params(),
        cost_estimate=cost(microseconds),
    )(*args)


def out(shape, dtype=F32):
    return jax.ShapeDtypeStruct(shape, dtype)


def flip(value, axis_name, bit):
    count = lax.axis_size(axis_name)
    return lax.ppermute(value, axis_name, [(i, i ^ bit) for i in range(count)])


def bits_of(axis_name):
    count = lax.axis_size(axis_name)
    return [1 << i for i in range(count.bit_length() - 1)]


def sum_small(value, axes):
    for axis_name in axes:
        for bit in bits_of(axis_name):
            value = value + flip(value, axis_name, bit)
    return value


def expert_parts(value):
    if lax.axis_size("expert") != 8:
        return [sum_small(value, ("expert",))]
    value = value + flip(value, "expert", 1)
    return [value] + [flip(value, "expert", bit) for bit in (2, 4, 6)]


def ordered_sum(parts, me):
    values = [part[...] for part in parts]
    total = None
    for index in range(len(values)):
        at = jnp.bitwise_xor(index, me)
        part = values[0]
        for other in range(1, len(values)):
            part = jnp.where(at == other, values[other], part)
        total = part if total is None else total + part
    return total


def halves(value, axis, take_high):
    size = value.shape[axis] // 2
    side = take_high.astype(jnp.int32)
    return (
        lax.dynamic_slice_in_dim(value, side * size, size, axis),
        lax.dynamic_slice_in_dim(value, (1 - side) * size, size, axis),
    )


def scatter_sum(value, axis, bits):
    for bit in bits:
        side = (lax.axis_index("dp") & bit) != 0
        keep, give = halves(value, axis, side)
        value = keep + flip(give, "dp", bit)
    return value


def join(value, axis, bits):
    for bit in reversed(bits):
        side = (lax.axis_index("dp") & bit) != 0
        other = flip(value, "dp", bit)
        value = jnp.concatenate(
            [jnp.where(side, other, value), jnp.where(side, value, other)], axis
        )
    return value


def ready(value, *others):
    return lax.optimization_barrier((value, *others))[0]


def exchange(value):
    return lax.all_to_all(value, "expert", split_axis=0, concat_axis=0, tiled=True)


def exchange_near(value):
    return lax.all_to_all(
        value,
        "expert",
        split_axis=0,
        concat_axis=0,
        tiled=True,
        axis_index_groups=[[0, 1, 2, 3], [4, 5, 6, 7]],
    )


def pairs_of(value, sides):
    far = flip(value, "expert", 4)
    return pl.pallas_call(
        pair_kernel,
        out_shape=out((4, 2, *value.shape), BF16),
        in_specs=[
            pl.BlockSpec(memory_space=pltpu.SMEM),
            *[pl.BlockSpec(memory_space=pltpu.VMEM)] * 2,
        ],
        out_specs=pl.BlockSpec(memory_space=pltpu.VMEM),
        compiler_params=params(),
        cost_estimate=cost(2),
    )(sides, value, far)


def spread(value):
    count = lax.axis_size("expert")
    return exchange(jnp.broadcast_to(value[None], (count, *value.shape)))


def expert_scatter(value):
    return jnp.sum(exchange(value), 0)


def squares_kernel(weights, sums, *refs):
    total = jnp.zeros((1, 1), F32)
    for weight, ref in zip(weights, refs[:-1]):
        for piece in decode(ref) if ref.dtype == jnp.int16 else [ref[...]]:
            part = jnp.sum(jnp.sum(piece * piece, -1, keepdims=True), 0, keepdims=True)
            total = total + part * weight
    refs[-1][0:1, :] = jnp.broadcast_to(total, (1, 128))
    refs[-1][1:2, :] = sums[...]


def sum_all(value):
    while value.ndim > 2:
        value = jnp.sum(value, 0)
    return jnp.sum(jnp.sum(value, 0, keepdims=True), -1, keepdims=True)


TILED = (4, 7, 8)


def tile_spec(index, shape, steps):
    if index == 7:
        return pl.BlockSpec((2, D // steps, shape[2]), lambda i: (0, i, 0))
    if index == 8:
        return pl.BlockSpec((shape[0] // steps, D), lambda i: (i, 0))
    if index == 4 and len(shape) == 3:
        half = steps // 2
        return pl.BlockSpec((1, shape[1], shape[2] // half), lambda i: (i // half, 0, i % half))
    if index == 4:
        return pl.BlockSpec((shape[0], shape[1] // steps), lambda i: (0, i))
    return pl.BlockSpec(shape, lambda i: (0,) * len(shape))


def tile_specs(arrays, steps):
    return [tile_spec(index, array.shape, steps) for index, array in enumerate(arrays)]


def quarter_kernel(sides, gate_up, down, quarter):
    wide = gate_up.shape[2]
    quarter[:, :wide] = gate_up[0].astype(BF16)
    quarter[:, wide:] = down[...].astype(BF16)


def prepare_kernel(count, *refs):
    masters = refs[:count]
    gate_up_low, down_low, totals = refs[count:]
    step = pl.program_id(0)
    gate_up_low[...] = masters[7][...].astype(BF16)
    down_low[...] = masters[8][...].astype(BF16)

    @pl.when(step == 0)
    def _():
        totals[...] = jnp.zeros_like(totals)

    def add(index):
        master = masters[index][...]
        totals[index : index + 1, :] += jnp.broadcast_to(sum_all(master * master), (1, 128))

    for index in TILED:
        add(index)

    @pl.when(step == 0)
    def _():
        for index in range(count):
            if index not in TILED:
                add(index)


def picked_piece(pieces, index, part):
    value = part(pieces[0])
    for other in range(1, len(pieces)):
        value = jnp.where(index == other, part(pieces[other]), value)
    return value


def moments_kernel(fast, count, part_count, small_end, sides, *refs):
    square_parts, refs = refs[:part_count], refs[part_count:]
    masters, means, squares = (refs[k * count : (k + 1) * count] for k in range(3))
    results = refs[-3 * count - 2 :]
    pieces = refs[3 * count : -3 * count - 2]
    totals, sums = results[-2:]
    both_sums = ordered_sum(square_parts, sides[3])
    sums[...] = both_sums
    factor = jnp.minimum(1.0, CLIP / jnp.sqrt(both_sums[0:1, 0:1]))
    step = pl.program_id(0)

    @pl.when(step == 0)
    def _():
        totals[...] = jnp.zeros_like(totals)

    def last_rows(start, stop):
        if not fast:
            return pieces[0][:, start:stop]
        low = sides[0] == 0
        half = pieces[0].shape[1]
        parts = []
        for side in range(2):
            begin, end = max(start, side * half), min(stop, (side + 1) * half)
            if begin < end:
                begin, end = begin - side * half, end - side * half
                mine, other = pieces[0][:, begin:end], pieces[1][:, begin:end]
                parts.append(jnp.where(low == (side == 0), mine, other))
        return jnp.concatenate(parts, 1) if len(parts) > 1 else parts[0]

    def gradient_of(index):
        if index in (0, 3):
            table = last_rows(SMALL_AT, SMALL_AT + SMALL).T
            return table[VECTORS_AT : VECTORS_AT + 5] if index == 0 else table[:HORIZON_AT]
        if index == 6:
            return last_rows(SMALL_AT, SMALL_AT + SMALL)[:, HORIZON_AT:small_end]
        if index == 1:
            return last_rows(0, 3 * D)
        if index == 2:
            return last_rows(3 * D, SMALL_AT)
        if not fast:
            return pieces[{4: 1, 5: 2, 7: 3, 8: 4}[index]][...]
        me = sides[0] * 2 + sides[1]
        shared = pieces[2:6]
        wide = 2 * FFS // 4
        if index == 4:
            return picked_piece(
                shared, jnp.bitwise_xor(step, me), lambda ref: ref[:, :wide]
            )
        if index == 5:
            return jnp.concatenate(
                [
                    picked_piece(shared, jnp.bitwise_xor(piece, me), lambda ref: ref[:, wide:])
                    for piece in range(4)
                ],
                0,
            )
        routed = pieces[6:10]
        split = masters[7].shape[2] // 128
        count_tiles = routed[0].shape[1] // 128 - 1

        def decoded(at, here, first, last):
            powers = picked_piece(routed, at, lambda ref: ref[here, count_tiles * 128 :])
            scale = jnp.exp2(powers.astype(jnp.int32).astype(F32) - 15.0)
            codes = picked_piece(routed, at, lambda ref: ref[here, first * 128 : last * 128])
            codes = codes.astype(jnp.int32).astype(F32)
            return jnp.concatenate(
                [
                    codes[:, (tile - first) * 128 : (tile - first + 1) * 128]
                    * scale[:, tile : tile + 1]
                    for tile in range(first, last)
                ],
                1,
            )

        if index == 7:
            rows = masters[7].shape[1]
            here = pl.ds(pl.multiple_of((step % 2) * rows, 16), rows)
            return jnp.stack(
                [
                    decoded(jnp.bitwise_xor(side * 2 + step // 2, me), here, 0, split)
                    for side in range(2)
                ]
            )
        return decoded(jnp.bitwise_xor(step, me), slice(None), split, count_tiles)

    def update(index):
        gradient = gradient_of(index)
        if index == 4 and gradient.ndim == 3:
            gradient = gradient[0]
        scale = factor.reshape(1, 1, 1) if gradient.ndim == 3 else factor
        mean_next, square_next, direction = lamb_direction(
            masters[index][...], gradient, means[index][...], squares[index][...], scale
        )
        results[index][...] = direction
        results[count + index][...] = mean_next
        results[2 * count + index][...] = square_next
        totals[index : index + 1, :] += jnp.broadcast_to(sum_all(direction * direction), (1, 128))

    for index in TILED:
        update(index)
    for index in range(count):
        if index not in TILED:
            pl.when(step == min(index, 3))(functools.partial(update, index))


def step_kernel(count, part_count, sides, *refs):
    parts, refs = refs[:part_count], refs[part_count:]
    masters, directions = refs[:count], refs[count : 2 * count]
    results = refs[2 * count :]
    all_totals = ordered_sum(parts, sides[3])
    results[-1][...] = all_totals
    totals, master_totals = all_totals[:count], all_totals[count:]
    step = pl.program_id(0)

    def update(index):
        ratio = jnp.sqrt(master_totals[index : index + 1, 0:1]) / jnp.sqrt(
            totals[index : index + 1, 0:1]
        )
        ratio = RATE * ratio
        if len(masters[index].shape) == 3:
            ratio = ratio.reshape(1, 1, 1)
        results[index][...] = masters[index][...] - ratio * directions[index][...]

    for index in TILED:
        update(index)
    for index in range(count):
        if index not in TILED:
            pl.when(step == min(index, 3))(functools.partial(update, index))


def shards(
    points,
    experts,
    lengths,
    domains,
    domain_weights,
    vectors,
    attend_input,
    attend_output,
    router,
    shared_input,
    shared_output,
    horizon,
    expert_input,
    expert_output,
    mean_vectors,
    mean_attend_input,
    mean_attend_output,
    mean_router,
    mean_shared_input,
    mean_shared_output,
    mean_horizon,
    mean_expert_input,
    mean_expert_output,
    square_vectors,
    square_attend_input,
    square_attend_output,
    square_router,
    square_shared_input,
    square_shared_output,
    square_horizon,
    square_expert_input,
    square_expert_output,
):
    expert_count = lax.axis_size("expert")
    group_size = expert_count // EXPERTS
    dp_count = lax.axis_size("dp")
    dp_bits = bits_of("dp")
    amount = points.shape[0]
    local_rows = attend_input.shape[0]
    head_columns = horizon.shape[1]
    hidden_local = expert_output.shape[0]
    small_end = HORIZON_AT + head_columns
    fast = (
        group_size == 1 and dp_count == 4 and local_rows % 16 == 0 and hidden_local == 2 * D
    )
    core = lax.axis_index("dp") & 1
    sides = jnp.stack(
        [
            core, lax.axis_index("dp") >> 1, lax.axis_index("expert") >> 2,
            lax.axis_index("expert") >> 1 if fast else core * 0,
        ]
    ).astype(jnp.int32)
    in_smem = pl.BlockSpec(memory_space=pltpu.SMEM)
    in_vmem = pl.BlockSpec(memory_space=pltpu.VMEM)
    ahead_row = jnp.pad(
        jnp.asarray(ahead_table())[None], ((0, 0), (0, SMALL - head_columns)), constant_values=1 << 20
    )
    packed = pl.pallas_call(
        functools.partial(pack_kernel, small_end),
        out_shape=out((1 if fast else expert_count, local_rows, 2 * D + SMALL), BF16),
        in_specs=[*[in_smem] * 3, *[in_vmem] * 6],
        out_specs=in_vmem,
        compiler_params=params(),
        cost_estimate=cost(2),
    )(sides, lengths, domains, ahead_row, attend_input, attend_output, router.T, horizon, vectors)
    gathered = exchange_near(pairs_of(packed[0], sides)) if fast else exchange(packed)

    def state(group):
        return tuple(a.T if index == 3 else a for index, a in enumerate(group))

    masters = state(
        (
            vectors, attend_input, attend_output, router, shared_input, shared_output, horizon,
            expert_input, expert_output,
        )
    )
    first_moments = state(
        (
            mean_vectors, mean_attend_input, mean_attend_output, mean_router, mean_shared_input,
            mean_shared_output, mean_horizon, mean_expert_input, mean_expert_output,
        )
    )
    second_moments = state(
        (
            square_vectors, square_attend_input, square_attend_output, square_router,
            square_shared_input, square_shared_output, square_horizon, square_expert_input,
            square_expert_output,
        )
    )
    count = len(masters)
    steps = 4
    gate_up_low, down_low, master_squares = pl.pallas_call(
        functools.partial(prepare_kernel, count),
        out_shape=[
            out(expert_input.shape, BF16), out(expert_output.shape, BF16), out((16, 128)),
        ],
        grid=(steps,),
        in_specs=tile_specs(masters, steps),
        out_specs=[
            tile_spec(7, expert_input.shape, steps),
            tile_spec(8, expert_output.shape, steps),
            whole(out((16, 128))),
        ],
        compiler_params=params(),
        cost_estimate=cost(5),
    )(*masters)
    weight_quarter = points
    if fast:
        weight_quarter = pl.pallas_call(
            quarter_kernel,
            out_shape=out((D // 2, hidden_local + D), BF16),
            grid_spec=pltpu.PrefetchScalarGridSpec(
                num_scalar_prefetch=1,
                grid=(1,),
                in_specs=[
                    pl.BlockSpec(
                        (1, D // 2, hidden_local), lambda i, sides: (sides[0], sides[1], 0)
                    ),
                    pl.BlockSpec((D // 2, D), lambda i, sides: (sides[0] * 2 + sides[1], 0)),
                ],
                out_specs=pl.BlockSpec((D // 2, hidden_local + D), lambda i, sides: (0, 0)),
            ),
            compiler_params=params(),
            cost_estimate=cost(2.6),
        )(sides, expert_input, expert_output)
    frequency = jnp.exp(-jnp.log(10000.0) * jnp.arange(HD // 2, dtype=F32) / (HD // 2))
    cosine, sine, known, rows_table = pl.pallas_call(
        tables_kernel,
        out_shape=[out((amount, 128)), out((amount, 128)), out((amount, 128)), out((8, amount))],
        in_specs=[*[in_smem] * 2, *[in_vmem] * 3],
        out_specs=[in_vmem] * 4,
        compiler_params=params(),
        cost_estimate=cost(3),
    )(
        lengths,
        domains,
        jnp.tile(frequency, 128 // (HD // 2))[None],
        points.reshape(1, amount),
        experts.T,
    )
    folds = FFS // D
    shared_piece = jnp.concatenate(
        [
            shared_input,
            shared_output.reshape(folds, local_rows, D).swapaxes(0, 1).reshape(local_rows, -1),
        ],
        1,
    ).astype(BF16)
    for bit in dp_bits:
        shared_piece, unused = halves(shared_piece, 1, (lax.axis_index("dp") & bit) != 0)
    if fast:
        shared_piece = pairs_of(shared_piece, sides)
    gathered = ready(gathered, known, shared_piece, weight_quarter).reshape(D, -1)
    gathered_other = flip(gathered, "dp", 1)
    shared_piece = ready(shared_piece, gathered)
    if fast:
        shared_pieces = exchange_near(shared_piece)
        weight_pieces = [flip(weight_quarter, "expert", 4)]
    else:
        shared_pieces = spread(shared_piece)
    (
        embedded, first, qkv, log_total, mixed, after, second, logits, slots, gains, pack,
        counts_half,
    ) = simple_call(
        functools.partial(front_kernel, fast, local_rows),
        [
            out((amount, D)), out((amount, D), BF16), out((amount, 3 * D), BF16),
            out((amount, 128)), out((amount, D), BF16), out((amount, D)),
            out((amount, D), BF16), out((amount, SMALL)), out((EXPERTS * CAP, D), BF16),
            out((8, D)), out((D, SMALL_AT + SMALL), BF16), out((1, SMALL)),
        ],
        [(sides, in_smem), gathered, gathered_other, cosine, sine, known, rows_table],
        15,
    )

    def to_devices(rows):
        rows = rows.reshape(EXPERTS, CAP, D)
        return exchange(jnp.repeat(rows, group_size, 0)).reshape(-1, D)

    def to_points(rows):
        rows = exchange(rows.reshape(expert_count, CAP, D))
        if group_size > 1:
            kind = rows.dtype
            rows = rows.reshape(EXPERTS, group_size, CAP, D).astype(F32)
            rows = jnp.sum(rows, 1).astype(kind)
        return rows.reshape(-1, D)

    first_bit = dp_bits[-1]
    block = 512
    if fast:
        arrived = exchange_near(
            ready(slots, shared_pieces, weight_pieces[0]).reshape(4, 2, CAP, D)
        )
        weight_pieces.append(flip(ready(weight_pieces[0], slots), "dp", 2))
        weight_pieces += [flip(piece, "dp", 1) for piece in weight_pieces]
        gate_up_far, down_far = simple_call(
            far_weights_kernel,
            [out(expert_input.shape, BF16), out(expert_output.shape, BF16)],
            [(sides, in_smem), ready(weight_pieces[0], gate_up_low), *weight_pieces[1:]],
            3,
        )
        shared_pieces = ready(shared_pieces, weight_pieces[1])
        shared_other = flip(shared_pieces, "dp", 2)
        row_spec = pl.BlockSpec(
            (4, 1, CAP, D), lambda i, sides: (0, jnp.bitwise_xor(i, sides[2]), 0, 0)
        )
        held = [gate_up_low, down_low, gate_up_far, down_far]
        held_specs = [
            pl.BlockSpec(a.shape, lambda *unused, a=a: (0,) * len(a.shape)) for a in held
        ]
        expert_rows = pl.pallas_call(
            pair_expert_kernel,
            out_shape=out((4, 2, CAP + CODE_ROWS, D), jnp.int16),
            grid_spec=pltpu.PrefetchScalarGridSpec(
                num_scalar_prefetch=1,
                grid=(2,),
                in_specs=[row_spec, *held_specs],
                out_specs=pl.BlockSpec(
                    (4, 1, CAP + CODE_ROWS, D),
                    lambda i, sides: (0, jnp.bitwise_xor(i, sides[2]), 0, 0),
                ),
            ),
            compiler_params=params(),
            cost_estimate=cost(10),
        )(sides, arrived, *held)
        returned = exchange_near(expert_rows).reshape(
            EXPERTS, CAP + CODE_ROWS, D
        )
        shared_pieces = ready(shared_pieces, expert_rows)
        shared_quarters = [shared_pieces, shared_other]
        shared_quarters += [flip(piece, "dp", 1) for piece in shared_quarters]
        shin_low, shout_low = simple_call(
            functools.partial(shared_weights_kernel, local_rows),
            [out((D, 2 * FFS), BF16), out((FFS, D), BF16)],
            [(sides, in_smem), *[piece.reshape(D, -1) for piece in shared_quarters]],
            4.3,
        )
    else:
        arrived = to_devices(ready(slots, shared_pieces))
        total_rows = arrived.shape[0]
        row_spec = pl.BlockSpec((block, D), lambda i: (i, 0))
        expert_rows = pl.pallas_call(
            expert_kernel,
            out_shape=out((total_rows, D)),
            grid=(total_rows // block,),
            in_specs=[row_spec, whole(gate_up_low), whole(down_low)],
            out_specs=row_spec,
            compiler_params=params(),
            cost_estimate=cost(10),
        )(arrived, gate_up_low, down_low)
        returned = to_points(expert_rows)
        shared_pack = join(ready(shared_pieces, expert_rows), 2, dp_bits)
        shin_low = shared_pack[:, :, : 2 * FFS].reshape(D, -1)
        shout_low = (
            shared_pack[:, :, 2 * FFS :]
            .reshape(expert_count, local_rows, folds, D)
            .swapaxes(1, 2)
            .reshape(FFS, D)
        )
    chunk = 512
    chunks = FFS // chunk
    shared = pl.pallas_call(
        shared_kernel,
        out_shape=out((amount, D)),
        grid=(chunks,),
        in_specs=[
            whole(second),
            pl.BlockSpec((D, chunk), lambda i: (0, i)),
            pl.BlockSpec((D, chunk), lambda i: (0, i + chunks)),
            pl.BlockSpec((chunk, D), lambda i: (i, 0)),
        ],
        out_specs=pl.BlockSpec((amount, D), lambda i: (0, 0)),
        compiler_params=params(),
        cost_estimate=cost(5.8),
    )(second, shin_low, shin_low, shout_low)
    counts = ready(counts_half, expert_rows)
    for bit in dp_bits[1:]:
        counts = counts + flip(counts, "dp", bit)
    weighting = jnp.pad(domain_weights, (0, SMALL - DOMAINS))[None] / jnp.maximum(counts, 1.0)
    side_pad = ((0, 0), (HORIZON_AT, SMALL - small_end))
    target = jnp.pad(target_columns(points), side_pad)
    ahead_small = jnp.pad(
        jnp.asarray(ahead_table())[None], ((0, 0), side_pad[1]), constant_values=1 << 20
    )
    small_low = columns(pack, SMALL, SMALL_AT // SMALL)
    (
        mixer_slope, shared_slope, slope_slots, logits_slope, small_head, gain_three, local_sums,
    ) = simple_call(
        functools.partial(middle_kernel, fast),
        [
            out((amount, D)), out((amount, D), BF16), out((EXPERTS * CAP, D), BF16),
            out((amount, SMALL), BF16), out((D, SMALL)), out((1, D)), out((1, SMALL)),
        ],
        [
            returned, known, rows_table, after, shared, logits, small_low, gains, target,
            ahead_small, weighting,
        ],
        11.4,
    )
    received = exchange_near(slope_slots.reshape(4, 2, CAP, D)) if fast else to_devices(slope_slots)
    chunk = 2 * D
    chunks = FFS // chunk
    back_in = [
        pl.BlockSpec((amount, D), lambda i, *unused: (0, 0)),
        pl.BlockSpec((amount, D), lambda i, *unused: (0, 0)),
        pl.BlockSpec((D, chunk), lambda i, *unused: (0, i)),
        pl.BlockSpec((D, chunk), lambda i, *unused: (0, i + chunks)),
        pl.BlockSpec((chunk, D), lambda i, *unused: (i, 0)),
    ]
    second_spec = pl.BlockSpec((amount, D), lambda i, *unused: (0, 0))
    back_args = (second, shared_slope, shin_low, shin_low, shout_low)
    if fast:
        in_spec = pl.BlockSpec(
            (1, D, chunk), lambda i, sides: (jnp.bitwise_xor(i, sides[1]), 0, 0)
        )
        give_spec = pl.BlockSpec(
            (1, D, D), lambda i, sides: (jnp.bitwise_xor(i, sides[1]), 0, 0)
        )
        out_spec = pl.BlockSpec((2, D // chunks, D), lambda i, sides: (0, i, 0))
        shared_second_slope, in_keep, in_even, in_odd, out_keep, out_give = pl.pallas_call(
            shared_back_split_kernel,
            out_shape=[
                out((amount, D)), out((2, D, FFS // 2)), *[out((2, D, D))] * 4,
            ],
            grid_spec=pltpu.PrefetchScalarGridSpec(
                num_scalar_prefetch=1,
                grid=(chunks,),
                in_specs=back_in,
                out_specs=[second_spec, in_spec, give_spec, give_spec, out_spec, out_spec],
                scratch_shapes=[pltpu.VMEM((chunk, D), F32)],
            ),
            compiler_params=params(),
            cost_estimate=cost(14),
        )(sides, *back_args)
    else:
        shared_second_slope, grad_shin, grad_shout = pl.pallas_call(
            shared_back_kernel,
            out_shape=[out((amount, D)), out((2, D, FFS)), out((FFS, D))],
            grid=(chunks,),
            in_specs=back_in,
            out_specs=[
                second_spec,
                pl.BlockSpec((2, D, chunk), lambda i: (0, 0, i)),
                pl.BlockSpec((chunk, D), lambda i: (i, 0)),
            ],
            compiler_params=params(),
            cost_estimate=cost(10),
        )(*back_args)
    if fast:
        in_even, in_odd, out_other = (flip(a, "dp", 1) for a in (in_even, in_odd, out_give))
        fold_in = pl.BlockSpec((2, D // 4, FFS // 2), lambda i: (0, i, 0))
        fold_out = pl.BlockSpec((2, D // 4, D), lambda i: (0, i, 0))
        wide = FFS // 2 + D
        fold_to = pl.BlockSpec((D // 4, wide), lambda i: (i, 0))
        code_to = pl.BlockSpec((D // 4, wide + 128), lambda i: (i, 0))
        shared_keep, shared_give = pl.pallas_call(
            fold_kernel,
            out_shape=[out((D, wide)), out((D, wide + 128), jnp.int16)],
            grid=(4,),
            in_specs=[fold_in, *[fold_out] * 4],
            out_specs=[fold_to, code_to],
            compiler_params=params(),
            cost_estimate=cost(5.3),
        )(in_keep, in_even, in_odd, out_keep, out_other)
        received = ready(received, shared_second_slope, shared_give)
        shared_other = flip(shared_give, "dp", 2)
    else:
        received = ready(received, shared_second_slope)
    if fast:
        half_shapes = [out((2, D, hidden_local))] * 2 + [out((2, D, D))] * 2
        row_spec = pl.BlockSpec(
            (2, 1, CAP, D), lambda i, j, sides: (j, jnp.bitwise_xor(i, sides[2]), 0, 0)
        )
        grad_rows, expert_in, expert_in_give, expert_out, expert_out_give = pl.pallas_call(
            expert_back_split_kernel,
            out_shape=[out((4, 2, CAP, D), BF16), *half_shapes],
            grid_spec=pltpu.PrefetchScalarGridSpec(
                num_scalar_prefetch=1,
                grid=(2, 2),
                in_specs=[row_spec, row_spec, *held_specs],
                out_specs=[
                    row_spec,
                    *[
                        pl.BlockSpec((1, *a.shape[1:]), lambda i, j, sides: (i, 0, 0))
                        for a in half_shapes
                    ],
                ],
            ),
            compiler_params=params(),
            cost_estimate=cost(19.5),
        )(sides, arrived, received, *held)
        routed_back = exchange_near(ready(grad_rows, shared_other)).reshape(-1, D)
    else:
        grad_rows, grad_expert_in, grad_expert_out = pl.pallas_call(
            expert_back_kernel,
            out_shape=[
                out((total_rows, D), BF16), out((2, D, hidden_local)), out((hidden_local, D)),
            ],
            grid=(total_rows // block,),
            in_specs=[row_spec, row_spec, whole(gate_up_low), whole(down_low)],
            out_specs=[
                row_spec,
                pl.BlockSpec((2, D, hidden_local), lambda i: (0, 0, 0)),
                pl.BlockSpec((hidden_local, D), lambda i: (0, 0)),
            ],
            compiler_params=params(),
            cost_estimate=cost(10),
        )(arrived, received, gate_up_low, down_low)
        routed_back = to_points(grad_rows)
    if fast:
        shared_code = pl.pallas_call(
            add_code_kernel,
            out_shape=out((D, wide + 128), jnp.int16),
            grid=(4,),
            in_specs=[fold_to, code_to],
            out_specs=code_to,
            compiler_params=params(),
            cost_estimate=cost(4.4),
        )(shared_keep, shared_other)
        expert_in_other = flip(expert_in_give, "dp", 1)
        expert_out_other = flip(expert_out_give, "dp", 1)
        half_in = pl.BlockSpec((1, D, hidden_local), lambda i: (i, 0, 0))
        half_out = pl.BlockSpec((1, D, D), lambda i: (i, 0, 0))
        expert_keep, expert_code = pl.pallas_call(
            expert_split_kernel,
            out_shape=[out((2, D // 2, wide)), out((2, D // 2, wide + 128), jnp.int16)],
            grid=(2,),
            in_specs=[in_smem, half_in, half_in, half_out, half_out],
            out_specs=[
                pl.BlockSpec((1, D // 2, wide), lambda i: (i, 0, 0)),
                pl.BlockSpec((1, D // 2, wide + 128), lambda i: (i, 0, 0)),
            ],
            compiler_params=params(),
            cost_estimate=cost(4.6),
        )(sides, expert_in, expert_in_other, expert_out, expert_out_other)
        sums = local_sums + flip(local_sums, "dp", 2)
        routed_plain = routed_back
        routed_back = ready(routed_back, shared_code, expert_code, sums)
    attend_slope, mixed_slope, grad_output, gain_two, small_routed = simple_call(
        functools.partial(attend_back_kernel, fast),
        [
            out((amount, D)), out((amount, D), BF16), out((D, D)), out((1, D)), out((D, SMALL)),
        ],
        [
            routed_back, known, shared_second_slope, logits_slope, small_low, after,
            mixer_slope, gains, mixed, second, columns(pack, D, 3), small_head,
        ],
        6,
    )
    if fast:
        expert_code_other = flip(expert_code, "dp", 2)
        expert_own, expert_far = simple_call(
            expert_far_kernel,
            [out((D // 2, wide)), out((D // 2, wide + 128), jnp.int16)],
            [expert_keep, expert_code_other],
            3.5,
        )
        mixed_slope = ready(mixed_slope, expert_far)
    pack_columns = SMALL_AT + SMALL
    half_columns = SMALL_AT // 2 + SMALL
    last_keep, last_give = simple_call(
        functools.partial(front_back_kernel, fast),
        [
            out((D, half_columns if fast else pack_columns)),
            out((D, half_columns) if fast else (8, 128)),
        ],
        [
            (sides, in_smem), mixed_slope, qkv, log_total, known, rows_table, cosine, sine, first,
            embedded, gains, columns(pack, 3 * D, 0), attend_slope, small_routed, gain_two,
            gain_three, grad_output,
        ],
        18.4,
        [
            pltpu.VMEM((D, 2 * half_columns), F32),
            pltpu.VMEM((amount, D), F32),
            pltpu.VMEM((amount, D), F32),
            pltpu.VMEM((amount, D), F32),
            pltpu.VMEM((amount, 3 * D), BF16),
        ],
    )

    if fast:
        shared_code = ready(shared_code, routed_plain, expert_code).reshape(expert_count, local_rows, -1)
        shared_code = exchange(shared_code)
        expert_far_other = flip(expert_far, "expert", 4)
        last_give = ready(last_give, expert_far_other, shared_code)
        (last_code,) = simple_call(
            last_code_kernel,
            [out((D, half_columns + 128), jnp.int16)],
            [(sides, in_smem), last_keep, flip(last_give, "dp", 1)],
            3.3,
        )
        (shared_sum,) = simple_call(
            shard_sum_kernel, [out((local_rows, wide))], [ready(shared_code, last_code)], 2.5
        )
        last_code = ready(last_code, shared_code).reshape(expert_count, local_rows, -1)
        (last_part,) = simple_call(
            last_sum_kernel,
            [out((local_rows, half_columns))],
            [(sides, in_smem), exchange(last_code)],
            2.2,
        )
        last_part = last_part + flip(last_part, "dp", 2)
        (expert_total,) = simple_call(
            expert_total_kernel,
            [out((D // 2, wide + 128), jnp.int16)],
            [ready(expert_own, last_code), expert_far_other],
            2.5,
        )
        expert_cross = flip(expert_total, "dp", 2)
        shared_cross = flip(shared_sum, "dp", 2)
        square_pieces = [
            shared_sum, shared_cross, last_part, expert_total, expert_cross,
        ]
        weights = (1.0,) * 5
        square_bits = [1]
        pieces = [
            last_part, flip(last_part, "dp", 1), shared_sum, shared_cross,
            flip(shared_sum, "dp", 1), flip(shared_cross, "dp", 1),
            expert_total, expert_cross, flip(expert_total, "dp", 1), flip(expert_cross, "dp", 1),
        ]
        piece_specs = [whole(a) for a in pieces]
    else:
        sums = local_sums
        shin_part = scatter_sum(grad_shin, 0, [1])[0].reshape(expert_count, local_rows, FFS)
        shin_part = expert_scatter(scatter_sum(shin_part, 2, dp_bits[1:]))
        shout_part = scatter_sum(grad_shout.reshape(expert_count, -1, D), 1, dp_bits)
        shout_part = expert_scatter(shout_part)
        expert_in_part = scatter_sum(grad_expert_in.reshape(-1, hidden_local), 0, dp_bits)
        expert_out_part = scatter_sum(grad_expert_out, 0, dp_bits)
        last_part = expert_scatter(last_keep.reshape(expert_count, local_rows, -1))
        for bit in dp_bits:
            last_part = last_part + flip(last_part, "dp", bit)
        square_pieces = [expert_in_part, expert_out_part, shin_part, shout_part, last_part]
        weights = (1.0, 1.0, 1.0, 1.0, 1.0 / dp_count)
        square_bits = dp_bits
        pieces = [
            last_part,
            join(join(shin_part, 1, dp_bits[1:])[None], 0, [1]),
            join(shout_part, 0, dp_bits),
            join(expert_in_part, 0, dp_bits).reshape(expert_input.shape),
            join(expert_out_part, 0, dp_bits),
        ]
        piece_specs = [
            whole(last_part),
            *[tile_spec(i, a.shape, steps) for i, a in zip((4, 5, 7, 8), pieces[1:])],
        ]
    (both_sums,) = simple_call(
        functools.partial(squares_kernel, weights), [out((2, 128))], [sums, *square_pieces], 2.4
    )
    for bit in square_bits:
        both_sums = both_sums + flip(both_sums, "dp", bit)
    square_parts = expert_parts(both_sums)
    part_count = len(square_parts)
    shapes = [out(a.shape) for a in masters]
    state_specs = tile_specs(masters, steps)
    updates = pl.pallas_call(
        functools.partial(moments_kernel, fast, count, part_count, small_end),
        out_shape=[*shapes, *shapes, *shapes, out((16, 128)), out((2, 128))],
        grid=(steps,),
        in_specs=[
            in_smem, *[whole(a) for a in square_parts], *state_specs, *state_specs, *state_specs,
            *piece_specs,
        ],
        out_specs=[
            *state_specs, *state_specs, *state_specs, whole(out((16, 128))), whole(out((2, 128))),
        ],
        compiler_params=params(),
        cost_estimate=cost(17),
    )(sides, *square_parts, *masters, *first_moments, *second_moments, *pieces)
    both_sums = updates[-1]
    domain_sums = both_sums[1, :DOMAINS]
    grad_norm = jnp.sqrt(both_sums[0, 0:1])
    directions = updates[:count]
    total_parts = expert_parts(
        jnp.concatenate([updates[-2][:count], master_squares[:count]], 0)
    )
    *next_masters, all_totals = pl.pallas_call(
        functools.partial(step_kernel, count, part_count),
        out_shape=[*shapes, out((2 * count, 128))],
        grid=(steps,),
        in_specs=[in_smem, *[whole(a) for a in total_parts], *state_specs, *state_specs],
        out_specs=[*state_specs, whole(out((2 * count, 128)))],
        compiler_params=params(),
        cost_estimate=cost(7),
    )(sides, *total_parts, *masters, *directions)
    results = []
    for index in range(count):
        for group in (next_masters, updates[count : 2 * count], updates[2 * count : 3 * count]):
            results.append(group[index].T if index == 3 else group[index])
    norms = jnp.sqrt(all_totals[:, 0])
    results.append(jnp.stack([domain_sums, counts[0, :DOMAINS]]))
    results.append(grad_norm)
    results.append(jnp.stack([norms[count:], norms[:count]], 1))
    return tuple(results)


def solution(mesh):
    placed = (
        P(("dp", "expert")),
        P(("dp", "expert"), None),
        P(("dp", "expert"), None),
        P(("dp", "expert"), None),
        P(),
        P(None, "expert"),
        P("expert", None),
        P("expert", None),
        P("expert", None),
        P("expert", None),
        P("expert", None),
        P("expert", None),
        P(None, None, "expert"),
        P("expert", None),
        P(None, "expert"),
        P("expert", None),
        P("expert", None),
        P("expert", None),
        P("expert", None),
        P("expert", None),
        P("expert", None),
        P(None, None, "expert"),
        P("expert", None),
        P(None, "expert"),
        P("expert", None),
        P("expert", None),
        P("expert", None),
        P("expert", None),
        P("expert", None),
        P("expert", None),
        P(None, None, "expert"),
        P("expert", None),
    )
    return jax.shard_map(
        shards,
        mesh=mesh,
        in_specs=placed,
        out_specs=(
            P(None, "expert"),
            P(None, "expert"),
            P(None, "expert"),
            P("expert", None),
            P("expert", None),
            P("expert", None),
            P("expert", None),
            P("expert", None),
            P("expert", None),
            P("expert", None),
            P("expert", None),
            P("expert", None),
            P("expert", None),
            P("expert", None),
            P("expert", None),
            P("expert", None),
            P("expert", None),
            P("expert", None),
            P("expert", None),
            P("expert", None),
            P("expert", None),
            P(None, None, "expert"),
            P(None, None, "expert"),
            P(None, None, "expert"),
            P("expert", None),
            P("expert", None),
            P("expert", None),
            P(),
            P(),
            P(),
        ),
        check_vma=False,
    )
```

```python
import functools

import jax
import jax.numpy as jnp
import numpy as np
from jax import lax
from jax.experimental import pallas as pl
from jax.experimental.pallas import tpu as pltpu
from jax.sharding import PartitionSpec as P

D = 384
HEADS = 12
HD = 32
FFS = 1536
EXPERTS = 8
DOMAINS = 9
STEP = 10
CAP = 256


HORIZONS = (1, 8, 32, 64)
REACH = 64
KINK_THRESHOLD = 2.0
EPS_NORM = 1e-06
CLIP = 0.01
BETA_ONE = 0.9
BETA_TWO = 0.99
EPS_ADAM = 1e-08
DECAY = 0.01
RATE = 0.3


def ahead_table():
    return np.concatenate([np.arange(horizon_len) for horizon_len in HORIZONS]).astype(np.int32)


def target_columns(samples):
    amount = samples.shape[0]
    padded = jnp.concatenate([samples, jnp.zeros((REACH + 1,), samples.dtype)])
    future = jnp.stack([padded[1 + offset : 1 + offset + amount] for offset in range(REACH)], 1)
    return future[:, ahead_table()]


ROW_BLOCK = 256
SMALL = 128
HORIZON_AT = EXPERTS + 1
VECTORS_AT = 120
SMALL_AT = 4 * D
COUNTS_AT = 125
CODE_ROWS = 16
VMEM = 56 * 1024 * 1024
F32 = jnp.float32
BF16 = jnp.bfloat16


def mm(left, right):
    return jnp.dot(left, right, preferred_element_type=F32)


def mm_nt(left, right):
    return lax.dot_general(left, right, (((1,), (1,)), ((), ())), preferred_element_type=F32)


def mm_tn(left, right):
    return lax.dot_general(left, right, (((0,), (0,)), ((), ())), preferred_element_type=F32)


def inverse_rms(rows):
    return lax.rsqrt(jnp.mean(rows * rows, axis=-1, keepdims=True) + EPS_NORM)


def rms_back(rows, inverse, gain, slope):
    gain_slope = jnp.sum(slope * rows * inverse, 0, keepdims=True)
    scaled = slope * gain
    return (
        inverse * scaled
        - rows * (inverse * inverse * inverse) * jnp.mean(rows * scaled, -1, keepdims=True),
        gain_slope,
    )


def lanes_of(shape):
    return lax.broadcasted_iota(jnp.int32, shape, len(shape) - 1)


def half_swap(rows):
    half_width = HD // 2
    lane = lanes_of(rows.shape)
    return jnp.where(
        lane % HD < half_width,
        pltpu.roll(rows, rows.shape[1] - half_width, 1),
        pltpu.roll(rows, half_width, 1),
    )


SLOT, SERIES_OF, FINISH, DOMAIN, CHOICE, VALUE, PLACE = 0, 2, 3, 4, 5, 7, 8


def tables_kernel(
    lengths, domains, frequency, points_row, experts_row, cosine, sine, columns_out, rows_out
):
    amount = points_row.shape[1]
    place = lax.broadcasted_iota(jnp.int32, (1, amount), 1)
    series = jnp.zeros((1, amount), jnp.int32)
    begin = jnp.zeros((1, amount), jnp.int32)
    finish = jnp.zeros((1, amount), jnp.int32)
    domain = jnp.zeros((1, amount), jnp.int32)
    start = jnp.int32(0)
    for index in range(lengths.shape[1]):
        stop = start + lengths[0, index]
        inside = (place >= start) & (place < stop)
        series = jnp.where(inside, index, series)
        begin = jnp.where(inside, start, begin)
        finish = jnp.where(inside, stop, finish)
        domain = jnp.where(inside, domains[0, index], domain)
        start = stop
    name = lax.broadcasted_iota(jnp.int32, (16, amount), 0)
    choices = [experts_row[k : k + 1, :] for k in range(2)]
    named = [(name == choice).astype(F32) for choice in choices]
    earlier = (
        lax.broadcasted_iota(jnp.int32, (amount, amount), 0)
        < lax.broadcasted_iota(jnp.int32, (amount, amount), 1)
    )
    before = mm((named[0] + named[1]).astype(BF16), earlier.astype(F32).astype(BF16))
    entries = []
    for k in range(2):
        rank = jnp.sum(named[k] * before, 0, keepdims=True)
        entries.append(choices[k].astype(F32) * CAP + rank)
    entries += [series, finish, domain, *choices, points_row[...], place - begin]
    row = lax.broadcasted_iota(jnp.int32, (128, amount), 0)
    table = jnp.zeros((128, amount), F32)
    for index, entry in enumerate(entries):
        table = jnp.where(row == index, entry.astype(F32), table)
    rows_out[...] = table[:8]
    columns = table.T
    columns_out[...] = columns
    angles = columns[:, PLACE : PLACE + 1] * frequency[...]
    cosine[...] = jnp.cos(angles)
    turned = jnp.sin(angles)
    sine[...] = jnp.where(lanes_of((amount, 128)) % HD < HD // 2, -turned, turned)


def allowed_block(table, rows_table, start, rows, keys):
    query = start + lax.broadcasted_iota(jnp.int32, (rows, keys), 0)
    key = lax.broadcasted_iota(jnp.int32, (rows, keys), 1)
    series_col = table[start : start + rows, SERIES_OF : SERIES_OF + 1]
    return (series_col == rows_table[SERIES_OF : SERIES_OF + 1, :keys]) & (key <= query)


def slot_place(grouped, expert):
    return (expert % 4) * 2 + expert // 4 if grouped else expert


def slot_rows_hot(slot_row, expert):
    slot = expert * CAP + lax.broadcasted_iota(jnp.int32, (CAP, slot_row.shape[1]), 0)
    return (slot_row.astype(jnp.int32) == slot).astype(F32).astype(BF16)


def slot_cols_hot(slot_col, expert):
    slot = expert * CAP + lax.broadcasted_iota(jnp.int32, (slot_col.shape[0], CAP), 1)
    return (slot_col.astype(jnp.int32) == slot).astype(F32).astype(BF16)


def pack_kernel(small_end, core, lengths, domains, ahead, input_w, output_w, router, horizon, vectors, out):
    rows = input_w.shape[0]

    def placed(count, at):
        row = lax.broadcasted_iota(jnp.int32, (count, SMALL), 0)
        return (row + at == lanes_of((count, SMALL))).astype(F32).astype(BF16)

    small = (
        mm_tn(router[...].astype(BF16), placed(HORIZON_AT, 0))
        + mm(horizon[...].astype(BF16), placed(small_end - HORIZON_AT, HORIZON_AT))
        + mm_tn(vectors[...].astype(BF16), placed(vectors.shape[0], VECTORS_AT))
    )
    row = lax.broadcasted_iota(jnp.int32, (rows, SMALL), 0)
    lane = lanes_of((rows, SMALL))
    counts = jnp.zeros((rows, SMALL), F32)
    for series in range(lengths.shape[1]):
        left = jnp.maximum(lengths[0, series] - 1 - ahead[...], 0).astype(F32)
        entries = jnp.sum(left, -1, keepdims=True)
        counts = counts + jnp.where(row == domains[0, series], entries, 0.0)
    high = jnp.floor(counts * (1.0 / 256.0))
    small = jnp.where(lane == COUNTS_AT, high, small)
    small = jnp.where(lane == COUNTS_AT + 1, counts - 256.0 * high, small)
    flat = jnp.concatenate([input_w[...], output_w[...]], 1)
    half = 2 * D
    mine = jnp.where(core[0] == 0, flat[:, :half], flat[:, half:]).astype(BF16)
    for target in range(out.shape[0]):
        out[target, :, :half] = mine
        out[target, :, half:] = small.astype(BF16)


def pair_kernel(sides, own, far, out):
    low = sides[2] == 0
    first = jnp.where(low, own[...], far[...])
    second = jnp.where(low, far[...], own[...])
    for target in range(out.shape[0]):
        out[target, 0] = first
        out[target, 1] = second


def front_kernel(
    grouped, local_rows, core, mine, other, cosine, sine, known, slot_row,
    embedded_out, first_out, qkv_out, log_out, mixed_out, after_out, second_out, logits_out,
    slots_out, gains_out, pack, counts_out,
):
    amount = known.shape[0]
    half = 2 * D
    low = core[0] == 0
    for index in range(D // local_rows):
        place = slot_place(grouped, index)
        here = slice(index * local_rows, (index + 1) * local_rows)
        there = slice(place * local_rows, (place + 1) * local_rows)
        left, right = mine[there, :half], other[there, :half]
        pack[here, :half] = jnp.where(low, left, right)
        pack[here, half:SMALL_AT] = jnp.where(low, right, left)
        pack[here, SMALL_AT:] = mine[there, half:]
    table = pack[:, SMALL_AT:].astype(F32).T
    gains = table[VECTORS_AT : VECTORS_AT + 8]
    gains_out[...] = gains
    other_table = other[:, half:].astype(F32).T
    row = lax.broadcasted_iota(jnp.int32, (D, SMALL), 0)
    fold = (row % local_rows == lanes_of((D, SMALL))).astype(F32).astype(BF16)
    digits = mm(table[VECTORS_AT : VECTORS_AT + 8].astype(BF16), fold) + mm(
        other_table[VECTORS_AT : VECTORS_AT + 8].astype(BF16), fold
    )
    at = COUNTS_AT - VECTORS_AT
    counts_out[...] = digits[at : at + 1] * 256.0 + digits[at + 1 : at + 2]
    value = known[:, VALUE : VALUE + 1]
    gate = value * gains[0:1]
    embedded = gate * jax.nn.sigmoid(gate) * (value * gains[1:2])
    embedded_out[...] = embedded
    first = (embedded * inverse_rms(embedded) * gains[2:3]).astype(BF16)
    first_out[...] = first
    projected = mm(first, pack[:, : 3 * D])
    cos_rows, sin_rows = cosine[...], sine[...]
    for block in range(6):
        part = projected[:, block * 128 : (block + 1) * 128]
        part = part * cos_rows + half_swap(part) * sin_rows
        qkv_out[:, block * 128 : (block + 1) * 128] = part.astype(BF16)
    qkv_out[:, 2 * D :] = projected[:, 2 * D :].astype(BF16)
    lane = lanes_of((ROW_BLOCK, 128))
    for start in range(0, amount, ROW_BLOCK):
        keys = start + ROW_BLOCK
        allowed = allowed_block(known[...], slot_row[...], start, ROW_BLOCK, keys)
        log_rows = jnp.zeros((ROW_BLOCK, 128), F32)
        for group in range(D // 128):
            query = qkv_out[start : start + ROW_BLOCK, group * 128 : (group + 1) * 128]
            key = qkv_out[:keys, D + group * 128 : D + (group + 1) * 128]
            held = qkv_out[:keys, 2 * D + group * 128 : 2 * D + (group + 1) * 128]
            gathered = jnp.zeros((ROW_BLOCK, 128), F32)
            for head in range(128 // HD):
                own = lane // HD == head
                raw = mm_nt(jnp.where(own, query, jnp.zeros_like(query)), key) * HD ** (-0.5)
                raw = jnp.where(allowed, raw, -1e30)
                top = jnp.max(raw, -1, keepdims=True)
                exponent = jnp.exp(raw - top)
                total = jnp.sum(exponent, -1, keepdims=True)
                attention = (exponent * (1.0 / total)).astype(BF16)
                gathered = jnp.where(own, mm(attention, held), gathered)
                log_rows = jnp.where(
                    lane == group * (128 // HD) + head, top + jnp.log(total), log_rows
                )
            mixed_out[start : start + ROW_BLOCK, group * 128 : (group + 1) * 128] = (
                gathered.astype(BF16)
            )
        log_out[start : start + ROW_BLOCK, :] = log_rows
    after = embedded + mm(mixed_out[...], pack[:, 3 * D : 4 * D])
    after_out[...] = after
    second = (after * inverse_rms(after) * gains[3:4]).astype(BF16)
    second_out[...] = second
    logits_out[...] = mm(second, pack[:, SMALL_AT:])
    for expert in range(EXPERTS):
        hot = slot_rows_hot(slot_row[0:1, :], expert) + slot_rows_hot(slot_row[1:2, :], expert)
        place = slot_place(grouped, expert)
        slots_out[place * CAP : (place + 1) * CAP, :] = mm(hot, second).astype(BF16)


def shared_kernel(second, gate_w, lift_w, down_w, shared_out):
    gate = mm(second[...], gate_w[...])
    lift = mm(second[...], lift_w[...])
    hidden = (gate * jax.nn.sigmoid(gate) * lift).astype(BF16)
    part = mm(hidden, down_w[...])

    @pl.when(pl.program_id(0) == 0)
    def _():
        shared_out[...] = part

    @pl.when(pl.program_id(0) != 0)
    def _():
        shared_out[...] += part


def code_rows(part, ref):
    top = jnp.max(jnp.abs(part), -1, keepdims=True)
    power = jnp.ceil(jnp.log2(jnp.maximum(top, 1e-30)))
    code = jnp.clip(jnp.round(part * jnp.exp2(15.0 - power)), -32767.0, 32767.0)
    ref[:CAP, :] = code.astype(jnp.int32).astype(jnp.int16)
    row = lax.broadcasted_iota(jnp.int32, (CAP, CAP), 0)
    column = lax.broadcasted_iota(jnp.int32, (CAP, CAP), 1)
    powers = jnp.sum(jnp.where(row == column, power, 0.0), 0, keepdims=True)
    powers = jnp.concatenate([powers, jnp.zeros((1, D - CAP), F32)], 1)
    ref[CAP:, :] = jnp.broadcast_to(powers, (CODE_ROWS, D)).astype(jnp.int32).astype(jnp.int16)


def unit(rows, gate_up, down):
    gate = mm(rows, gate_up[0])
    lift = mm(rows, gate_up[1])
    hidden = (gate * jax.nn.sigmoid(gate) * lift).astype(BF16)
    return mm(hidden, down[...])


def expert_kernel(rows, gate_up, down, rows_out):
    rows_out[...] = unit(rows[...], gate_up, down)


def pair_expert_kernel(sides, rows, gate_up, down, gate_up_far, down_far, rows_out):
    sources = rows.shape[0]
    flat = rows[...].reshape(sources * CAP, D)

    def serve(weights):
        result = unit(flat, *weights)
        for source in range(sources):
            code_rows(result[source * CAP : (source + 1) * CAP], rows_out.at[source, 0])

    pl.when(pl.program_id(0) == 0)(lambda: serve((gate_up, down)))
    pl.when(pl.program_id(0) == 1)(lambda: serve((gate_up_far, down_far)))


def far_weights_kernel(sides, *refs):
    pieces, (gate_up, down) = refs[:4], refs[4:]
    me = sides[0] * 2 + sides[1]
    half, wide = pieces[0].shape[0], gate_up.shape[2]
    for piece in range(4):
        core, cross = piece // 2, piece % 2
        value = picked_piece(pieces, jnp.bitwise_xor(piece, me), lambda ref: ref[...])
        gate_up[core, cross * half : (cross + 1) * half, :] = value[:, :wide]
        down[piece * half : (piece + 1) * half, :] = value[:, wide:]


def shared_weights_kernel(local_rows, sides, *refs):
    pieces, (both, down) = refs[:4], refs[4:]
    me = sides[0] * 2 + sides[1]
    wide = pieces[0].shape[1]
    shard = down.shape[0] // (D // local_rows)
    for piece in range(4):
        value = picked_piece(pieces, jnp.bitwise_xor(piece, me), lambda ref: ref[...])
        for index in range(D // local_rows):
            place = slot_place(True, index)
            rows = value[place * local_rows : (place + 1) * local_rows]
            for at in range(0, wide, D):
                column = piece * wide + at
                part = rows[:, at : at + D]
                if column < 2 * FFS:
                    both[index * local_rows : (index + 1) * local_rows, column : column + D] = part
                else:
                    row = index * shard + (column - 2 * FFS) // D * local_rows
                    down[row : row + local_rows, :] = part


def unit_back(rows, slope, gate_w, lift_w, down_w):
    gate = mm(rows, gate_w)
    lift = mm(rows, lift_w)
    bent = jax.nn.sigmoid(gate)
    smooth = gate * bent
    hidden = (smooth * lift).astype(BF16)
    hidden_slope = mm_nt(slope, down_w)
    gate_slope = (hidden_slope * lift * (bent * (1.0 + gate * (1.0 - bent)))).astype(BF16)
    lift_slope = (hidden_slope * smooth).astype(BF16)
    return hidden, gate_slope, lift_slope


def expert_back_kernel(rows, slope, gate_up, down, rows_out, in_out, out_out):
    hidden, gate_slope, lift_slope = unit_back(
        rows[...], slope[...], gate_up[0], gate_up[1], down[...]
    )
    rows_out[...] = (mm_nt(gate_slope, gate_up[0]) + mm_nt(lift_slope, gate_up[1])).astype(BF16)

    @pl.when(pl.program_id(0) == 0)
    def _():
        in_out[...] = jnp.zeros_like(in_out)
        out_out[...] = jnp.zeros_like(out_out)

    in_out[0] += mm_tn(rows[...], gate_slope)
    in_out[1] += mm_tn(rows[...], lift_slope)
    out_out[...] += mm_tn(hidden, slope[...])


def shared_back_kernel(second, slope, gate_w, lift_w, down_w, second_out, in_out, out_out):
    hidden, gate_slope, lift_slope = unit_back(
        second[...], slope[...], gate_w[...], lift_w[...], down_w[...]
    )
    part = mm_nt(gate_slope, gate_w[...]) + mm_nt(lift_slope, lift_w[...])

    @pl.when(pl.program_id(0) == 0)
    def _():
        second_out[...] = part

    @pl.when(pl.program_id(0) != 0)
    def _():
        second_out[...] += part

    in_out[0] = mm_tn(second[...], gate_slope)
    in_out[1] = mm_tn(second[...], lift_slope)
    out_out[...] = mm_tn(hidden, slope[...])


def expert_back_split_kernel(
    sides, rows, slope, gate_up, down, gate_up_far, down_far,
    rows_out, in_keep, in_give, out_keep, out_give,
):
    sources = rows.shape[0]
    flat = rows[...].reshape(sources * CAP, D)
    flat_slope = slope[...].reshape(sources * CAP, D)

    @pl.when(pl.program_id(1) == 0)
    def _():
        for ref in (in_keep, in_give, out_keep, out_give):
            ref[...] = jnp.zeros_like(ref)

    def serve(gate_w, down_w):
        hidden, gate_slope, lift_slope = unit_back(
            flat, flat_slope, gate_w[0], gate_w[1], down_w[...]
        )
        result = (mm_nt(gate_slope, gate_w[0]) + mm_nt(lift_slope, gate_w[1])).astype(BF16)
        rows_out[...] = result.reshape(rows_out.shape)
        half = hidden.shape[1] // 2
        low = sides[0] == 0
        gate = mm_tn(flat, gate_slope)
        lift = mm_tn(flat, lift_slope)
        in_keep[0] += jnp.where(low, gate, lift)
        in_give[0] += jnp.where(low, lift, gate)
        first = mm_tn(hidden[:, :half], flat_slope)
        last = mm_tn(hidden[:, half:], flat_slope)
        out_keep[0] += jnp.where(low, first, last)
        out_give[0] += jnp.where(low, last, first)

    pl.when(pl.program_id(0) == 0)(lambda: serve(gate_up, down))
    pl.when(pl.program_id(0) == 1)(lambda: serve(gate_up_far, down_far))


def shared_back_split_kernel(
    sides, second, slope, gate_w, lift_w, down_w,
    second_out, in_keep, in_give_even, in_give_odd, out_keep, out_give, out_ref,
):
    hidden, gate_slope, lift_slope = unit_back(
        second[...], slope[...], gate_w[...], lift_w[...], down_w[...]
    )
    part = mm_nt(gate_slope, gate_w[...]) + mm_nt(lift_slope, lift_w[...])

    @pl.when(pl.program_id(0) == 0)
    def _():
        second_out[...] = part

    @pl.when(pl.program_id(0) != 0)
    def _():
        second_out[...] += part

    core, cross = sides[0], sides[1]
    low = core == 0
    gate = mm_tn(second[...], gate_slope)
    lift = mm_tn(second[...], lift_slope)
    in_keep[0] = jnp.where(low, gate, lift)
    given = jnp.where(low, lift, gate)
    half = given.shape[1] // 2
    in_give_even[0] = given[:, :half]
    in_give_odd[0] = given[:, half:]
    out_ref[...] = mm_tn(hidden, slope[...])
    quarter = D // EXPERTS
    shards = out_keep.shape[1] // quarter
    for shard in range(shards):
        for side in range(2):
            for ref, half in ((out_keep, core), (out_give, 1 - core)):
                piece = half * 2 + jnp.bitwise_xor(cross, side)
                start = pl.multiple_of(shard * 4 * quarter + piece * quarter, 8)
                ref[side, shard * quarter : (shard + 1) * quarter, :] = out_ref[
                    pl.ds(start, quarter), :
                ]


def coded_tile(value):
    top = jnp.max(jnp.abs(value), -1, keepdims=True)
    power = jnp.ceil(jnp.log2(jnp.maximum(top, 1e-30)))
    code = jnp.clip(jnp.round(value * jnp.exp2(15.0 - power)), -32767.0, 32767.0)
    return code, power


def encode(ref, tiles):
    lane = lanes_of(tiles[0].shape)
    powers = jnp.zeros(tiles[0].shape, F32)
    for index, tile in enumerate(tiles):
        code, power = coded_tile(tile)
        ref[:, index * 128 : (index + 1) * 128] = code.astype(jnp.int32).astype(jnp.int16)
        powers = jnp.where(lane == index, power, powers)
    ref[:, len(tiles) * 128 :] = powers.astype(jnp.int32).astype(jnp.int16)


def decode(ref):
    count = ref.shape[-1] // 128 - 1
    scale = jnp.exp2(ref[..., count * 128 :].astype(jnp.int32).astype(F32) - 15.0)
    return [
        ref[..., index * 128 : (index + 1) * 128].astype(jnp.int32).astype(F32)
        * scale[..., index : index + 1]
        for index in range(count)
    ]


def tiles_of(value):
    return [value[:, at : at + 128] for at in range(0, value.shape[1], 128)]


def fold_kernel(in_keep, in_even, in_odd, out_keep, out_other, keep, give):
    wide = in_keep.shape[2]
    half = wide // 2
    keep[:, :half] = in_keep[0, :, :half] + in_even[0]
    keep[:, half:wide] = in_keep[0, :, half:] + in_odd[0]
    keep[:, wide:] = out_keep[0] + out_other[0]
    encode(
        give,
        tiles_of(in_keep[1, :, :half] + in_even[1])
        + tiles_of(in_keep[1, :, half:] + in_odd[1])
        + tiles_of(out_keep[1] + out_other[1]),
    )


def add_code_kernel(rows, keep, other, code):
    for index in range(keep.shape[0] // rows):
        here = slice(index * rows, (index + 1) * rows)
        place = slot_place(True, index)
        encode(
            code.at[place * rows : (place + 1) * rows],
            [
                mine + theirs
                for mine, theirs in zip(tiles_of(keep[here, :]), decode(other.at[here]))
            ],
        )


def near_sum_kernel(sides, codes, own, far):
    mine = [jnp.sum(tile, 0) for tile in decode(codes.at[:, sides[2]])]
    for index, tile in enumerate(mine):
        own[:, index * 128 : (index + 1) * 128] = tile
    encode(far, [jnp.sum(tile, 0) for tile in decode(codes.at[:, 1 - sides[2]])])


def add_kernel(own, code, total):
    for index, tile in enumerate(decode(code)):
        here = slice(index * 128, (index + 1) * 128)
        total[:, here] = own[:, here] + tile


def expert_split_kernel(sides, in_keep, in_other, out_keep, out_other, keep, code):
    wide, half = in_keep.shape[2], in_keep.shape[1] // 2
    here = pl.ds(pl.multiple_of(sides[1] * half, 8), half)
    there = pl.ds(pl.multiple_of((1 - sides[1]) * half, 8), half)
    keep[0, :, :wide] = in_keep[0, here, :] + in_other[0, here, :]
    keep[0, :, wide:] = out_keep[0, here, :] + out_other[0, here, :]
    encode(
        code.at[0],
        tiles_of(in_keep[0, there, :] + in_other[0, there, :])
        + tiles_of(out_keep[0, there, :] + out_other[0, there, :]),
    )


def expert_far_kernel(keep, codes, own, far):
    for index, tile in enumerate(decode(codes.at[0])):
        here = slice(index * 128, (index + 1) * 128)
        own[:, here] = keep[0, :, here] + tile
    encode(far, [mine + theirs for mine, theirs in zip(tiles_of(keep[1]), decode(codes.at[1]))])


def expert_total_kernel(own, code, total):
    encode(
        total, [mine + theirs for mine, theirs in zip(tiles_of(own[...]), decode(code))]
    )


def encode_last(ref, tiles, high):
    rough, power = coded_tile(tiles[5])
    rest = tiles[5] - rough * jnp.exp2(power - 15.0)
    encode(ref, [*tiles[:6], jnp.where(high, rest, tiles[6])])


def whole_tiles(tiles, high):
    return [
        *tiles[:5],
        jnp.where(high, tiles[5] + tiles[6], tiles[5]),
        jnp.where(high, 0.0, tiles[6]),
    ]


def last_code_kernel(rows, sides, keep, other, *codes):
    for target, code in enumerate(codes):
        for half in range(2):
            shard = jnp.bitwise_xor(sides[4], target) + 4 * half
            here = pl.ds(pl.multiple_of(shard * rows, 8), rows)
            tiles = tiles_of(keep[here, :] + other[here, :])
            encode_last(code.at[half * rows : (half + 1) * rows], tiles, sides[0] == 1)


def last_near_kernel(rows, sides, *refs):
    codes, (own, far) = refs[:-2], refs[-2:]
    high = sides[0] == 1

    def gathered(half):
        here = pl.ds(pl.multiple_of(half * rows, 16), rows)
        sums = None
        for code in codes:
            tiles = decode(code.at[here])
            sums = tiles if sums is None else [a + b for a, b in zip(sums, tiles)]
        return whole_tiles(sums, high)

    for index, tile in enumerate(gathered(sides[2])):
        own[:, index * 128 : (index + 1) * 128] = tile
    encode_last(far, gathered(1 - sides[2]), high)


def last_sum_kernel(sides, own, code, total):
    for index, tile in enumerate(whole_tiles(decode(code), sides[0] == 1)):
        here = slice(index * 128, (index + 1) * 128)
        total[:, here] = own[:, here] + tile


def middle_kernel(
    grouped, returned, known, slot_row, after, shared, logits, small, gains, target, ahead, weighting,
    mixer_out, shared_slope_out, slots_out, logits_slope_out, small_out, gain_out, sums_out,
):
    amount = after.shape[0]
    lane = lanes_of((amount, SMALL))
    table = known[...]
    integers = table[:, :8].astype(jnp.int32)
    chosen = [
        (lane == integers[:, CHOICE + k : CHOICE + k + 1]).astype(F32) for k in range(2)
    ]
    point = lax.broadcasted_iota(jnp.int32, (amount, SMALL), 0)
    usable = (point + 1 + ahead[...] < integers[:, FINISH : FINISH + 1]).astype(F32)
    logit = logits[...]
    routed = lane < EXPERTS
    top = jnp.max(jnp.where(routed, logit, -1e30), -1, keepdims=True)
    exponent = jnp.where(routed, jnp.exp(jnp.where(routed, logit - top, 0.0)), 0.0)
    probs = exponent / jnp.sum(exponent, -1, keepdims=True)
    gates = [jnp.sum(chosen[k] * probs, -1, keepdims=True) for k in range(2)]
    shared_gate = jax.nn.sigmoid(
        jnp.sum(jnp.where(lane == EXPERTS, logit, 0.0), -1, keepdims=True)
    )
    picked = [jnp.zeros((amount, D), F32), jnp.zeros((amount, D), F32)]
    for expert in range(EXPERTS):
        place = slot_place(grouped, expert)
        if len(returned.shape) == 2:
            rows = returned[place * CAP : (place + 1) * CAP, :]
            scale = 1.0
        else:
            rows = returned[place, :CAP, :].astype(jnp.int32).astype(F32)
            powers = returned[place, CAP:, :].astype(jnp.int32).astype(F32)
            scale = jnp.exp2(powers[0:1, :CAP] - 15.0)
        high = rows.astype(BF16)
        rest = (rows - high.astype(F32)).astype(BF16)
        halves_of_rows = jnp.concatenate([high, rest], 1)
        for k in range(2):
            slot = expert * CAP + lax.broadcasted_iota(jnp.int32, (amount, CAP), 1)
            hot = jnp.where(integers[:, SLOT + k : SLOT + k + 1] == slot, scale, 0.0).astype(BF16)
            both = mm(hot, halves_of_rows)
            picked[k] = picked[k] + (both[:, :D] + both[:, D:])
    mixer = (
        after[...] + shared_gate * shared[...] + (gates[0] * picked[0] + gates[1] * picked[1])
    )
    inverse = inverse_rms(mixer)
    gain = gains[4:5]
    third = (mixer * inverse * gain).astype(BF16)
    residue = mm(third, small[...]) - target[...]
    size = jnp.abs(residue)
    cost = (
        jnp.where(
            size <= KINK_THRESHOLD,
            0.5 * residue * residue,
            KINK_THRESHOLD * (size - 0.5 * KINK_THRESHOLD),
        )
        * usable
    )
    domain_hot = (lane == integers[:, DOMAIN : DOMAIN + 1]).astype(F32)
    sums_out[...] = jnp.sum(domain_hot * jnp.sum(cost, -1, keepdims=True), 0, keepdims=True)
    weight = jnp.sum(domain_hot * weighting[...], -1, keepdims=True)
    slope = (
        jnp.clip(residue, -KINK_THRESHOLD, KINK_THRESHOLD) * usable * weight
    ).astype(BF16)
    small_out[...] = mm_tn(third, slope)
    mixer_slope, gain_slope = rms_back(mixer, inverse, gain, mm_nt(slope, small[...]))
    gain_out[...] = gain_slope
    mixer_out[...] = mixer_slope
    shared_slope_out[...] = (shared_gate * mixer_slope).astype(BF16)
    gate_slope = jnp.sum(mixer_slope * shared[...], -1, keepdims=True)
    probs_slope = chosen[0] * jnp.sum(mixer_slope * picked[0], -1, keepdims=True) + chosen[
        1
    ] * jnp.sum(mixer_slope * picked[1], -1, keepdims=True)
    inner = jnp.sum(probs * probs_slope, -1, keepdims=True)
    logits_slope_out[...] = jnp.where(
        routed,
        probs * (probs_slope - inner),
        jnp.where(lane == EXPERTS, gate_slope * (shared_gate * (1.0 - shared_gate)), 0.0),
    ).astype(BF16)
    slopes = [(gates[k] * mixer_slope).astype(BF16) for k in range(2)]
    for expert in range(EXPERTS):
        place = slot_place(grouped, expert)
        slots_out[place * CAP : (place + 1) * CAP, :] = (
            mm(slot_rows_hot(slot_row[0:1, :], expert), slopes[0])
            + mm(slot_rows_hot(slot_row[1:2, :], expert), slopes[1])
        ).astype(BF16)


def attend_back_kernel(
    grouped, returned, known, second_slope, logits_slope, small, after, mixer_slope, gains, mixed, second,
    output_w, small_before,
    attend_out, mixed_out, output_out, gain_out, small_out,
):
    slope = second_slope[...] + mm_nt(logits_slope[...], small[...])
    for expert in range(EXPERTS):
        hot = slot_cols_hot(known[:, 0:1], expert) + slot_cols_hot(known[:, 1:2], expert)
        place = slot_place(grouped, expert)
        slope = slope + mm(hot, returned[place * CAP : (place + 1) * CAP, :])
    after_rows = after[...]
    part, gain_slope = rms_back(after_rows, inverse_rms(after_rows), gains[3:4], slope)
    gain_out[...] = gain_slope
    attend = mixer_slope[...] + part
    attend_out[...] = attend
    low = attend.astype(BF16)
    output_out[...] = mm_tn(mixed[...], low)
    mixed_out[...] = mm_nt(low, output_w[...]).astype(BF16)
    small_out[...] = small_before[...] + mm_tn(second[...], logits_slope[...])


def front_back_kernel(
    fast, core, mixed_slope, qkv, log_total, known, rows_table, cosine, sine, first, embedded,
    gains, input_w, attend_slope, small_before, gain_two, gain_three, output_before,
    keep_out, give_out,
    pack_out, query_acc, key_acc, held_acc, slope_ref,
):
    amount = first.shape[0]
    key_acc[...] = jnp.zeros_like(key_acc)
    held_acc[...] = jnp.zeros_like(held_acc)
    lane = lanes_of((ROW_BLOCK, 128))
    lane_all = lanes_of((amount, 128))
    for start in range(0, amount, ROW_BLOCK):
        keys = start + ROW_BLOCK
        here = slice(start, start + ROW_BLOCK)
        allowed = allowed_block(known[...], rows_table[...], start, ROW_BLOCK, keys)
        for group in range(D // 128):
            wide = slice(group * 128, (group + 1) * 128)
            query = qkv[here, group * 128 : (group + 1) * 128]
            key = qkv[:keys, D + group * 128 : D + (group + 1) * 128]
            held = qkv[:keys, 2 * D + group * 128 : 2 * D + (group + 1) * 128]
            out_slope = mixed_slope[here, wide]
            query_sum = jnp.zeros((ROW_BLOCK, 128), F32)
            key_sum = jnp.zeros((keys, 128), F32)
            held_sum = jnp.zeros((keys, 128), F32)
            for head in range(128 // HD):
                own = lane // HD == head
                own_query = jnp.where(own, query, jnp.zeros_like(query))
                own_slope = jnp.where(own, out_slope, jnp.zeros_like(out_slope))
                own_key = jnp.where(lane_all[:keys] // HD == head, key, jnp.zeros_like(key))
                at = group * (128 // HD) + head
                raw = mm_nt(own_query, key) * HD ** (-0.5)
                probs = jnp.exp(jnp.where(allowed, raw - log_total[here, at : at + 1], -1e30))
                held_sum = held_sum + mm_tn(probs.astype(BF16), own_slope)
                probs_slope = mm_nt(own_slope, held)
                inner = jnp.sum(probs_slope * probs, -1, keepdims=True)
                raw_slope = (probs * (probs_slope - inner)).astype(BF16)
                query_sum = query_sum + mm(raw_slope, own_key)
                key_sum = key_sum + mm_tn(raw_slope, own_query)
            query_acc[here, wide] = query_sum
            key_acc[:keys, wide] += key_sum
            held_acc[:keys, wide] += held_sum
    cos_rows, sin_rows = cosine[...], sine[...]
    for block in range(3):
        wide = slice(block * 128, (block + 1) * 128)
        for base, acc in ((0, query_acc), (D, key_acc)):
            part = acc[:, wide] * HD ** (-0.5)
            part = part * cos_rows + half_swap(part * sin_rows)
            slope_ref[:, base + block * 128 : base + (block + 1) * 128] = part.astype(BF16)
    slope_ref[:, 2 * D :] = held_acc[...].astype(BF16)
    projected_slope = slope_ref[...]
    pack_out[:, : 3 * D] = mm_tn(first[...], projected_slope)
    pack_out[:, 3 * D : SMALL_AT] = output_before[...]
    first_slope = mm_nt(projected_slope, input_w[...])
    rows = embedded[...]
    part, gain_one = rms_back(rows, inverse_rms(rows), gains[2:3], first_slope)
    slope = attend_slope[...] + part
    value = known[:, VALUE : VALUE + 1]
    gate = value * gains[0:1]
    bent = jax.nn.sigmoid(gate)
    gate_gradient = jnp.sum(
        slope * (value * gains[1:2]) * (bent * (1.0 + gate * (1.0 - bent))) * value,
        0,
        keepdims=True,
    )
    lift_gradient = jnp.sum(slope * (gate * bent) * value, 0, keepdims=True)
    row = lax.broadcasted_iota(jnp.int32, (128, D), 0)
    table = jnp.zeros((128, D), F32)
    for offset, piece in enumerate(
        (gate_gradient, lift_gradient, gain_one, gain_two[...], gain_three[...])
    ):
        table = jnp.where(row == VECTORS_AT + offset, piece, table)
    pack_out[:, SMALL_AT : SMALL_AT + SMALL] = small_before[...] + table.T
    if not fast:
        keep_out[...] = pack_out[:, : keep_out.shape[1]]
        give_out[...] = jnp.zeros_like(give_out)
        return
    pack_out[:, SMALL_AT + SMALL :] = jnp.zeros_like(pack_out[:, SMALL_AT + SMALL :])
    half = keep_out.shape[1]
    keep_out[...] = pack_out[:, pl.ds(pl.multiple_of(core[0] * half, 128), half)]
    give_out[...] = pack_out[:, pl.ds(pl.multiple_of((1 - core[0]) * half, 128), half)]


def lamb_direction(master, gradient, mean, square, factor):
    clipped = gradient * factor
    mean_next = BETA_ONE * mean + (1.0 - BETA_ONE) * clipped
    square_next = BETA_TWO * square + (1.0 - BETA_TWO) * clipped * clipped
    direction = (
        mean_next
        / (1.0 - BETA_ONE**STEP)
        / (jnp.sqrt(square_next / (1.0 - BETA_TWO**STEP)) + EPS_ADAM)
        + DECAY * master
    )
    return mean_next, square_next, direction


def whole(array):
    shape = array.shape
    return pl.BlockSpec(shape, lambda *unused: (0,) * len(shape))


def params(limit=VMEM):
    return pltpu.CompilerParams(vmem_limit_bytes=limit)


def cost(microseconds):
    return pl.CostEstimate(flops=int(microseconds * 1.15e9), bytes_accessed=0, transcendentals=0)


def columns(array, width, at):
    return (array, pl.BlockSpec((array.shape[0], width), lambda *unused: (0, at)))


def simple_call(kernel, outs, args, microseconds, scratch=()):
    pairs = [a if isinstance(a, tuple) else (a, whole(a)) for a in args]
    args = [a for a, spec in pairs]
    return pl.pallas_call(
        kernel,
        out_shape=outs,
        in_specs=[spec for a, spec in pairs],
        out_specs=[whole(a) for a in outs],
        scratch_shapes=list(scratch),
        grid=(1,),
        compiler_params=params(),
        cost_estimate=cost(microseconds),
    )(*args)


def out(shape, dtype=F32):
    return jax.ShapeDtypeStruct(shape, dtype)


def flip(value, axis_name, bit):
    count = lax.axis_size(axis_name)
    return lax.ppermute(value, axis_name, [(i, i ^ bit) for i in range(count)])


def bits_of(axis_name):
    count = lax.axis_size(axis_name)
    return [1 << i for i in range(count.bit_length() - 1)]


def sum_small(value, axes):
    for axis_name in axes:
        for bit in bits_of(axis_name):
            value = value + flip(value, axis_name, bit)
    return value


def expert_parts(value):
    if lax.axis_size("expert") != 8:
        return [sum_small(value, ("expert",))]
    value = value + flip(value, "expert", 1)
    return [value] + [flip(value, "expert", bit) for bit in (2, 4, 6)]


def ordered_sum(parts, me):
    values = [part[...] for part in parts]
    total = None
    for index in range(len(values)):
        at = jnp.bitwise_xor(index, me)
        part = values[0]
        for other in range(1, len(values)):
            part = jnp.where(at == other, values[other], part)
        total = part if total is None else total + part
    return total


def halves(value, axis, take_high):
    size = value.shape[axis] // 2
    side = take_high.astype(jnp.int32)
    return (
        lax.dynamic_slice_in_dim(value, side * size, size, axis),
        lax.dynamic_slice_in_dim(value, (1 - side) * size, size, axis),
    )


def scatter_sum(value, axis, bits):
    for bit in bits:
        side = (lax.axis_index("dp") & bit) != 0
        keep, give = halves(value, axis, side)
        value = keep + flip(give, "dp", bit)
    return value


def join(value, axis, bits):
    for bit in reversed(bits):
        side = (lax.axis_index("dp") & bit) != 0
        other = flip(value, "dp", bit)
        value = jnp.concatenate(
            [jnp.where(side, other, value), jnp.where(side, value, other)], axis
        )
    return value


def ready(value, *others):
    return lax.optimization_barrier((value, *others))[0]


def exchange(value):
    return lax.all_to_all(value, "expert", split_axis=0, concat_axis=0, tiled=True)


def exchange_near(value):
    return lax.all_to_all(
        value,
        "expert",
        split_axis=0,
        concat_axis=0,
        tiled=True,
        axis_index_groups=[[0, 1, 2, 3], [4, 5, 6, 7]],
    )


def pairs_of(value, sides):
    far = flip(value, "expert", 4)
    return pl.pallas_call(
        pair_kernel,
        out_shape=out((4, 2, *value.shape), BF16),
        in_specs=[
            pl.BlockSpec(memory_space=pltpu.SMEM),
            *[pl.BlockSpec(memory_space=pltpu.VMEM)] * 2,
        ],
        out_specs=pl.BlockSpec(memory_space=pltpu.VMEM),
        compiler_params=params(),
        cost_estimate=cost(2),
    )(sides, value, far)


def spread(value):
    count = lax.axis_size("expert")
    return exchange(jnp.broadcast_to(value[None], (count, *value.shape)))


def expert_scatter(value):
    return jnp.sum(exchange(value), 0)


def squares_kernel(weights, sums, last, last_other, *refs):
    total_last, both = refs[-2:]
    total_last[...] = last[...] + last_other[...]
    total = jnp.zeros((1, 1), F32)
    for weight, ref in zip(weights, (total_last, *refs[:-2])):
        for piece in decode(ref) if ref.dtype == jnp.int16 else [ref[...]]:
            part = jnp.sum(jnp.sum(piece * piece, -1, keepdims=True), 0, keepdims=True)
            total = total + part * weight
    both[0:1, :] = jnp.broadcast_to(total, (1, 128))
    both[1:2, :] = sums[...]


def sum_all(value):
    while value.ndim > 2:
        value = jnp.sum(value, 0)
    return jnp.sum(jnp.sum(value, 0, keepdims=True), -1, keepdims=True)


TILED = (4, 7, 8)


def tile_spec(index, shape, steps):
    if index == 7:
        return pl.BlockSpec((2, D // steps, shape[2]), lambda i: (0, i, 0))
    if index == 8:
        return pl.BlockSpec((shape[0] // steps, D), lambda i: (i, 0))
    if index == 4 and len(shape) == 3:
        half = steps // 2
        return pl.BlockSpec((1, shape[1], shape[2] // half), lambda i: (i // half, 0, i % half))
    if index == 4:
        return pl.BlockSpec((shape[0], shape[1] // steps), lambda i: (0, i))
    return pl.BlockSpec(shape, lambda i: (0,) * len(shape))


def tile_specs(arrays, steps):
    return [tile_spec(index, array.shape, steps) for index, array in enumerate(arrays)]


def quarter_kernel(sides, gate_up, down, quarter):
    wide = gate_up.shape[2]
    quarter[:, :wide] = gate_up[0].astype(BF16)
    quarter[:, wide:] = down[...].astype(BF16)


def prepare_kernel(count, *refs):
    masters = refs[:count]
    gate_up_low, down_low, totals = refs[count:]
    step = pl.program_id(0)
    gate_up_low[...] = masters[7][...].astype(BF16)
    down_low[...] = masters[8][...].astype(BF16)

    @pl.when(step == 0)
    def _():
        totals[...] = jnp.zeros_like(totals)

    def add(index):
        master = masters[index][...]
        totals[index : index + 1, :] += jnp.broadcast_to(sum_all(master * master), (1, 128))

    for index in TILED:
        add(index)

    @pl.when(step == 0)
    def _():
        for index in range(count):
            if index not in TILED:
                add(index)


def picked_piece(pieces, index, part):
    value = part(pieces[0])
    for other in range(1, len(pieces)):
        value = jnp.where(index == other, part(pieces[other]), value)
    return value


def moments_kernel(fast, count, part_count, small_end, sides, master_squares, *refs):
    square_parts, refs = refs[:part_count], refs[part_count:]
    masters, means, squares = (refs[k * count : (k + 1) * count] for k in range(3))
    results = refs[-3 * count - 2 :]
    pieces = refs[3 * count : -3 * count - 2]
    totals, sums = results[-2:]
    both_sums = ordered_sum(square_parts, sides[3])
    sums[...] = both_sums
    factor = jnp.minimum(1.0, CLIP / jnp.sqrt(both_sums[0:1, 0:1]))
    step = pl.program_id(0)

    @pl.when(step == 0)
    def _():
        totals[:16] = jnp.zeros_like(master_squares)
        totals[16:] = master_squares[...]

    def last_rows(start, stop):
        if not fast:
            return pieces[0][:, start:stop]
        low = sides[0] == 0
        half = pieces[0].shape[1]
        parts = []
        for side in range(2):
            begin, end = max(start, side * half), min(stop, (side + 1) * half)
            if begin < end:
                begin, end = begin - side * half, end - side * half
                mine, other = pieces[0][:, begin:end], pieces[1][:, begin:end]
                parts.append(jnp.where(low == (side == 0), mine, other))
        return jnp.concatenate(parts, 1) if len(parts) > 1 else parts[0]

    def gradient_of(index):
        if index in (0, 3):
            table = last_rows(SMALL_AT, SMALL_AT + SMALL).T
            return table[VECTORS_AT : VECTORS_AT + 5] if index == 0 else table[:HORIZON_AT]
        if index == 6:
            return last_rows(SMALL_AT, SMALL_AT + SMALL)[:, HORIZON_AT:small_end]
        if index == 1:
            return last_rows(0, 3 * D)
        if index == 2:
            return last_rows(3 * D, SMALL_AT)
        if not fast:
            return pieces[{4: 1, 5: 2, 7: 3, 8: 4}[index]][...]
        me = sides[0] * 2 + sides[1]
        shared = pieces[2:6]
        wide = 2 * FFS // 4
        if index == 4:
            return picked_piece(
                shared, jnp.bitwise_xor(step, me), lambda ref: ref[:, :wide]
            )
        if index == 5:
            return jnp.concatenate(
                [
                    picked_piece(shared, jnp.bitwise_xor(piece, me), lambda ref: ref[:, wide:])
                    for piece in range(4)
                ],
                0,
            )
        routed = pieces[6:10]
        split = masters[7].shape[2] // 128
        count_tiles = routed[0].shape[1] // 128 - 1

        def decoded(at, here, first, last):
            powers = picked_piece(routed, at, lambda ref: ref[here, count_tiles * 128 :])
            scale = jnp.exp2(powers.astype(jnp.int32).astype(F32) - 15.0)
            codes = picked_piece(routed, at, lambda ref: ref[here, first * 128 : last * 128])
            codes = codes.astype(jnp.int32).astype(F32)
            return jnp.concatenate(
                [
                    codes[:, (tile - first) * 128 : (tile - first + 1) * 128]
                    * scale[:, tile : tile + 1]
                    for tile in range(first, last)
                ],
                1,
            )

        if index == 7:
            rows = masters[7].shape[1]
            here = pl.ds(pl.multiple_of((step % 2) * rows, 16), rows)
            return jnp.stack(
                [
                    decoded(jnp.bitwise_xor(side * 2 + step // 2, me), here, 0, split)
                    for side in range(2)
                ]
            )
        return decoded(jnp.bitwise_xor(step, me), slice(None), split, count_tiles)

    def update(index):
        gradient = gradient_of(index)
        if index == 4 and gradient.ndim == 3:
            gradient = gradient[0]
        scale = factor.reshape(1, 1, 1) if gradient.ndim == 3 else factor
        mean_next, square_next, direction = lamb_direction(
            masters[index][...], gradient, means[index][...], squares[index][...], scale
        )
        results[index][...] = direction
        results[count + index][...] = mean_next
        results[2 * count + index][...] = square_next
        totals[index : index + 1, :] += jnp.broadcast_to(sum_all(direction * direction), (1, 128))

    for index in TILED:
        update(index)
    for index in range(count):
        if index not in TILED:
            pl.when(step == min(index, 3))(functools.partial(update, index))


def step_kernel(count, part_count, sides, *refs):
    parts, refs = refs[:part_count], refs[part_count:]
    masters, directions = refs[:count], refs[count : 2 * count]
    results = refs[2 * count :]
    all_totals = ordered_sum(parts, sides[3])
    totals, master_totals = all_totals[:count], all_totals[16 : 16 + count]
    diagonal = lax.broadcasted_iota(jnp.int32, (count, 128), 0) == lanes_of((count, 128))
    for row, sums in enumerate((master_totals, totals)):
        flat = jnp.sum(jnp.where(diagonal, jnp.sqrt(sums[:, 0:1]), 0.0), 0, keepdims=True)
        results[-1][row : row + 1, :] = flat[:, :count]
    step = pl.program_id(0)

    def update(index):
        ratio = jnp.sqrt(master_totals[index : index + 1, 0:1]) / jnp.sqrt(
            totals[index : index + 1, 0:1]
        )
        ratio = RATE * ratio
        if len(masters[index].shape) == 3:
            ratio = ratio.reshape(1, 1, 1)
        results[index][...] = masters[index][...] - ratio * directions[index][...]

    for index in TILED:
        update(index)
    for index in range(count):
        if index not in TILED:
            pl.when(step == min(index, 3))(functools.partial(update, index))


def shards(
    points,
    experts,
    lengths,
    domains,
    domain_weights,
    vectors,
    attend_input,
    attend_output,
    router,
    shared_input,
    shared_output,
    horizon,
    expert_input,
    expert_output,
    mean_vectors,
    mean_attend_input,
    mean_attend_output,
    mean_router,
    mean_shared_input,
    mean_shared_output,
    mean_horizon,
    mean_expert_input,
    mean_expert_output,
    square_vectors,
    square_attend_input,
    square_attend_output,
    square_router,
    square_shared_input,
    square_shared_output,
    square_horizon,
    square_expert_input,
    square_expert_output,
):
    expert_count = lax.axis_size("expert")
    group_size = expert_count // EXPERTS
    dp_count = lax.axis_size("dp")
    dp_bits = bits_of("dp")
    amount = points.shape[0]
    local_rows = attend_input.shape[0]
    head_columns = horizon.shape[1]
    hidden_local = expert_output.shape[0]
    small_end = HORIZON_AT + head_columns
    fast = (
        group_size == 1 and dp_count == 4 and local_rows % 16 == 0 and hidden_local == 2 * D
    )
    core = lax.axis_index("dp") & 1
    sides = jnp.stack(
        [
            core, lax.axis_index("dp") >> 1, lax.axis_index("expert") >> 2,
            lax.axis_index("expert") >> 1 if fast else core * 0, lax.axis_index("expert") & 3,
        ]
    ).astype(jnp.int32)
    in_smem = pl.BlockSpec(memory_space=pltpu.SMEM)
    in_vmem = pl.BlockSpec(memory_space=pltpu.VMEM)
    ahead_row = jnp.pad(
        jnp.asarray(ahead_table())[None], ((0, 0), (0, SMALL - head_columns)), constant_values=1 << 20
    )
    packed = pl.pallas_call(
        functools.partial(pack_kernel, small_end),
        out_shape=out((1 if fast else expert_count, local_rows, 2 * D + SMALL), BF16),
        in_specs=[*[in_smem] * 3, *[in_vmem] * 6],
        out_specs=in_vmem,
        compiler_params=params(),
        cost_estimate=cost(2),
    )(sides, lengths, domains, ahead_row, attend_input, attend_output, router.T, horizon, vectors)
    gathered = exchange_near(pairs_of(packed[0], sides)) if fast else exchange(packed)

    def state(group):
        return tuple(a.T if index == 3 else a for index, a in enumerate(group))

    masters = state(
        (
            vectors, attend_input, attend_output, router, shared_input, shared_output, horizon,
            expert_input, expert_output,
        )
    )
    first_moments = state(
        (
            mean_vectors, mean_attend_input, mean_attend_output, mean_router, mean_shared_input,
            mean_shared_output, mean_horizon, mean_expert_input, mean_expert_output,
        )
    )
    second_moments = state(
        (
            square_vectors, square_attend_input, square_attend_output, square_router,
            square_shared_input, square_shared_output, square_horizon, square_expert_input,
            square_expert_output,
        )
    )
    count = len(masters)
    steps = 4
    gate_up_low, down_low, master_squares = pl.pallas_call(
        functools.partial(prepare_kernel, count),
        out_shape=[
            out(expert_input.shape, BF16), out(expert_output.shape, BF16), out((16, 128)),
        ],
        grid=(steps,),
        in_specs=tile_specs(masters, steps),
        out_specs=[
            tile_spec(7, expert_input.shape, steps),
            tile_spec(8, expert_output.shape, steps),
            whole(out((16, 128))),
        ],
        compiler_params=params(),
        cost_estimate=cost(5),
    )(*masters)
    weight_quarter = points
    if fast:
        weight_quarter = pl.pallas_call(
            quarter_kernel,
            out_shape=out((D // 2, hidden_local + D), BF16),
            grid_spec=pltpu.PrefetchScalarGridSpec(
                num_scalar_prefetch=1,
                grid=(1,),
                in_specs=[
                    pl.BlockSpec(
                        (1, D // 2, hidden_local), lambda i, sides: (sides[0], sides[1], 0)
                    ),
                    pl.BlockSpec((D // 2, D), lambda i, sides: (sides[0] * 2 + sides[1], 0)),
                ],
                out_specs=pl.BlockSpec((D // 2, hidden_local + D), lambda i, sides: (0, 0)),
            ),
            compiler_params=params(),
            cost_estimate=cost(2.6),
        )(sides, expert_input, expert_output)
    frequency = jnp.exp(-jnp.log(10000.0) * jnp.arange(HD // 2, dtype=F32) / (HD // 2))
    cosine, sine, known, rows_table = pl.pallas_call(
        tables_kernel,
        out_shape=[out((amount, 128)), out((amount, 128)), out((amount, 128)), out((8, amount))],
        in_specs=[*[in_smem] * 2, *[in_vmem] * 3],
        out_specs=[in_vmem] * 4,
        compiler_params=params(),
        cost_estimate=cost(3),
    )(
        lengths,
        domains,
        jnp.tile(frequency, 128 // (HD // 2))[None],
        points.reshape(1, amount),
        experts.T,
    )
    folds = FFS // D
    shared_piece = jnp.concatenate(
        [
            shared_input,
            shared_output.reshape(folds, local_rows, D).swapaxes(0, 1).reshape(local_rows, -1),
        ],
        1,
    ).astype(BF16)
    for bit in dp_bits:
        shared_piece, unused = halves(shared_piece, 1, (lax.axis_index("dp") & bit) != 0)
    if fast:
        shared_piece = pairs_of(shared_piece, sides)
    gathered = ready(gathered, known, shared_piece, weight_quarter).reshape(D, -1)
    gathered_other = flip(gathered, "dp", 1)
    shared_piece = ready(shared_piece, gathered)
    if fast:
        shared_pieces = exchange_near(shared_piece)
        weight_pieces = [flip(weight_quarter, "expert", 4)]
    else:
        shared_pieces = spread(shared_piece)
    (
        embedded, first, qkv, log_total, mixed, after, second, logits, slots, gains, pack,
        counts_half,
    ) = simple_call(
        functools.partial(front_kernel, fast, local_rows),
        [
            out((amount, D)), out((amount, D), BF16), out((amount, 3 * D), BF16),
            out((amount, 128)), out((amount, D), BF16), out((amount, D)),
            out((amount, D), BF16), out((amount, SMALL)), out((EXPERTS * CAP, D), BF16),
            out((8, D)), out((D, SMALL_AT + SMALL), BF16), out((1, SMALL)),
        ],
        [(sides, in_smem), gathered, gathered_other, cosine, sine, known, rows_table],
        15,
    )

    def to_devices(rows):
        rows = rows.reshape(EXPERTS, CAP, D)
        return exchange(jnp.repeat(rows, group_size, 0)).reshape(-1, D)

    def to_points(rows):
        rows = exchange(rows.reshape(expert_count, CAP, D))
        if group_size > 1:
            kind = rows.dtype
            rows = rows.reshape(EXPERTS, group_size, CAP, D).astype(F32)
            rows = jnp.sum(rows, 1).astype(kind)
        return rows.reshape(-1, D)

    first_bit = dp_bits[-1]
    block = 512
    if fast:
        arrived = exchange_near(
            ready(slots, shared_pieces, weight_pieces[0]).reshape(4, 2, CAP, D)
        )
        weight_pieces.append(flip(ready(weight_pieces[0], slots), "dp", 2))
        weight_pieces += [flip(piece, "dp", 1) for piece in weight_pieces]
        gate_up_far, down_far = simple_call(
            far_weights_kernel,
            [out(expert_input.shape, BF16), out(expert_output.shape, BF16)],
            [(sides, in_smem), ready(weight_pieces[0], gate_up_low), *weight_pieces[1:]],
            3,
        )
        shared_pieces = ready(shared_pieces, weight_pieces[1])
        shared_other = flip(shared_pieces, "dp", 2)
        row_spec = pl.BlockSpec(
            (4, 1, CAP, D), lambda i, sides: (0, jnp.bitwise_xor(i, sides[2]), 0, 0)
        )
        held = [gate_up_low, down_low, gate_up_far, down_far]
        held_specs = [
            pl.BlockSpec(a.shape, lambda *unused, a=a: (0,) * len(a.shape)) for a in held
        ]
        expert_rows = pl.pallas_call(
            pair_expert_kernel,
            out_shape=out((4, 2, CAP + CODE_ROWS, D), jnp.int16),
            grid_spec=pltpu.PrefetchScalarGridSpec(
                num_scalar_prefetch=1,
                grid=(2,),
                in_specs=[row_spec, *held_specs],
                out_specs=pl.BlockSpec(
                    (4, 1, CAP + CODE_ROWS, D),
                    lambda i, sides: (0, jnp.bitwise_xor(i, sides[2]), 0, 0),
                ),
            ),
            compiler_params=params(),
            cost_estimate=cost(10),
        )(sides, arrived, *held)
        returned = exchange_near(expert_rows).reshape(
            EXPERTS, CAP + CODE_ROWS, D
        )
        shared_pieces = ready(shared_pieces, expert_rows)
        shared_quarters = [shared_pieces, shared_other]
        shared_quarters += [flip(piece, "dp", 1) for piece in shared_quarters]
        shin_low, shout_low = simple_call(
            functools.partial(shared_weights_kernel, local_rows),
            [out((D, 2 * FFS), BF16), out((FFS, D), BF16)],
            [(sides, in_smem), *[piece.reshape(D, -1) for piece in shared_quarters]],
            4.3,
        )
    else:
        arrived = to_devices(ready(slots, shared_pieces))
        total_rows = arrived.shape[0]
        row_spec = pl.BlockSpec((block, D), lambda i: (i, 0))
        expert_rows = pl.pallas_call(
            expert_kernel,
            out_shape=out((total_rows, D)),
            grid=(total_rows // block,),
            in_specs=[row_spec, whole(gate_up_low), whole(down_low)],
            out_specs=row_spec,
            compiler_params=params(),
            cost_estimate=cost(10),
        )(arrived, gate_up_low, down_low)
        returned = to_points(expert_rows)
        shared_pack = join(ready(shared_pieces, expert_rows), 2, dp_bits)
        shin_low = shared_pack[:, :, : 2 * FFS].reshape(D, -1)
        shout_low = (
            shared_pack[:, :, 2 * FFS :]
            .reshape(expert_count, local_rows, folds, D)
            .swapaxes(1, 2)
            .reshape(FFS, D)
        )
    chunk = 512
    chunks = FFS // chunk
    shared = pl.pallas_call(
        shared_kernel,
        out_shape=out((amount, D)),
        grid=(chunks,),
        in_specs=[
            whole(second),
            pl.BlockSpec((D, chunk), lambda i: (0, i)),
            pl.BlockSpec((D, chunk), lambda i: (0, i + chunks)),
            pl.BlockSpec((chunk, D), lambda i: (i, 0)),
        ],
        out_specs=pl.BlockSpec((amount, D), lambda i: (0, 0)),
        compiler_params=params(),
        cost_estimate=cost(5.8),
    )(second, shin_low, shin_low, shout_low)
    counts = ready(counts_half, expert_rows)
    for bit in dp_bits[1:]:
        counts = counts + flip(counts, "dp", bit)
    weighting = jnp.pad(domain_weights, (0, SMALL - DOMAINS))[None] / jnp.maximum(counts, 1.0)
    side_pad = ((0, 0), (HORIZON_AT, SMALL - small_end))
    target = jnp.pad(target_columns(points), side_pad)
    ahead_small = jnp.pad(
        jnp.asarray(ahead_table())[None], ((0, 0), side_pad[1]), constant_values=1 << 20
    )
    small_low = columns(pack, SMALL, SMALL_AT // SMALL)
    (
        mixer_slope, shared_slope, slope_slots, logits_slope, small_head, gain_three, local_sums,
    ) = simple_call(
        functools.partial(middle_kernel, fast),
        [
            out((amount, D)), out((amount, D), BF16), out((EXPERTS * CAP, D), BF16),
            out((amount, SMALL), BF16), out((D, SMALL)), out((1, D)), out((1, SMALL)),
        ],
        [
            returned, known, rows_table, after, shared, logits, small_low, gains, target,
            ahead_small, weighting,
        ],
        11.4,
    )
    received = exchange_near(slope_slots.reshape(4, 2, CAP, D)) if fast else to_devices(slope_slots)
    chunk = 2 * D
    chunks = FFS // chunk
    back_in = [
        pl.BlockSpec((amount, D), lambda i, *unused: (0, 0)),
        pl.BlockSpec((amount, D), lambda i, *unused: (0, 0)),
        pl.BlockSpec((D, chunk), lambda i, *unused: (0, i)),
        pl.BlockSpec((D, chunk), lambda i, *unused: (0, i + chunks)),
        pl.BlockSpec((chunk, D), lambda i, *unused: (i, 0)),
    ]
    second_spec = pl.BlockSpec((amount, D), lambda i, *unused: (0, 0))
    back_args = (second, shared_slope, shin_low, shin_low, shout_low)
    if fast:
        in_spec = pl.BlockSpec(
            (1, D, chunk), lambda i, sides: (jnp.bitwise_xor(i, sides[1]), 0, 0)
        )
        give_spec = pl.BlockSpec(
            (1, D, D), lambda i, sides: (jnp.bitwise_xor(i, sides[1]), 0, 0)
        )
        out_spec = pl.BlockSpec((2, D // chunks, D), lambda i, sides: (0, i, 0))
        shared_second_slope, in_keep, in_even, in_odd, out_keep, out_give = pl.pallas_call(
            shared_back_split_kernel,
            out_shape=[
                out((amount, D)), out((2, D, FFS // 2)), *[out((2, D, D))] * 4,
            ],
            grid_spec=pltpu.PrefetchScalarGridSpec(
                num_scalar_prefetch=1,
                grid=(chunks,),
                in_specs=back_in,
                out_specs=[second_spec, in_spec, give_spec, give_spec, out_spec, out_spec],
                scratch_shapes=[pltpu.VMEM((chunk, D), F32)],
            ),
            compiler_params=params(),
            cost_estimate=cost(14),
        )(sides, *back_args)
    else:
        shared_second_slope, grad_shin, grad_shout = pl.pallas_call(
            shared_back_kernel,
            out_shape=[out((amount, D)), out((2, D, FFS)), out((FFS, D))],
            grid=(chunks,),
            in_specs=back_in,
            out_specs=[
                second_spec,
                pl.BlockSpec((2, D, chunk), lambda i: (0, 0, i)),
                pl.BlockSpec((chunk, D), lambda i: (i, 0)),
            ],
            compiler_params=params(),
            cost_estimate=cost(10),
        )(*back_args)
    if fast:
        in_even, in_odd, out_other = (flip(a, "dp", 1) for a in (in_even, in_odd, out_give))
        fold_in = pl.BlockSpec((2, D // 4, FFS // 2), lambda i: (0, i, 0))
        fold_out = pl.BlockSpec((2, D // 4, D), lambda i: (0, i, 0))
        wide = FFS // 2 + D
        fold_to = pl.BlockSpec((D // 4, wide), lambda i: (i, 0))
        code_to = pl.BlockSpec((D // 4, wide + 128), lambda i: (i, 0))
        shared_keep, shared_give = pl.pallas_call(
            fold_kernel,
            out_shape=[out((D, wide)), out((D, wide + 128), jnp.int16)],
            grid=(4,),
            in_specs=[fold_in, *[fold_out] * 4],
            out_specs=[fold_to, code_to],
            compiler_params=params(),
            cost_estimate=cost(5.3),
        )(in_keep, in_even, in_odd, out_keep, out_other)
        received = ready(received, shared_second_slope, shared_give)
        shared_other = flip(shared_give, "dp", 2)
    else:
        received = ready(received, shared_second_slope)
    if fast:
        half_shapes = [out((2, D, hidden_local))] * 2 + [out((2, D, D))] * 2
        row_spec = pl.BlockSpec(
            (2, 1, CAP, D), lambda i, j, sides: (j, jnp.bitwise_xor(i, sides[2]), 0, 0)
        )
        grad_rows, expert_in, expert_in_give, expert_out, expert_out_give = pl.pallas_call(
            expert_back_split_kernel,
            out_shape=[out((4, 2, CAP, D), BF16), *half_shapes],
            grid_spec=pltpu.PrefetchScalarGridSpec(
                num_scalar_prefetch=1,
                grid=(2, 2),
                in_specs=[row_spec, row_spec, *held_specs],
                out_specs=[
                    row_spec,
                    *[
                        pl.BlockSpec((1, *a.shape[1:]), lambda i, j, sides: (i, 0, 0))
                        for a in half_shapes
                    ],
                ],
            ),
            compiler_params=params(),
            cost_estimate=cost(19.5),
        )(sides, arrived, received, *held)
        routed_back = exchange_near(ready(grad_rows, shared_other)).reshape(-1, D)
    else:
        grad_rows, grad_expert_in, grad_expert_out = pl.pallas_call(
            expert_back_kernel,
            out_shape=[
                out((total_rows, D), BF16), out((2, D, hidden_local)), out((hidden_local, D)),
            ],
            grid=(total_rows // block,),
            in_specs=[row_spec, row_spec, whole(gate_up_low), whole(down_low)],
            out_specs=[
                row_spec,
                pl.BlockSpec((2, D, hidden_local), lambda i: (0, 0, 0)),
                pl.BlockSpec((hidden_local, D), lambda i: (0, 0)),
            ],
            compiler_params=params(),
            cost_estimate=cost(10),
        )(arrived, received, gate_up_low, down_low)
        routed_back = to_points(grad_rows)
    if fast:
        (shared_code,) = simple_call(
            functools.partial(add_code_kernel, local_rows),
            [out((D, wide + 128), jnp.int16)],
            [shared_keep, shared_other],
            4.4,
        )
        expert_in_other = flip(expert_in_give, "dp", 1)
        expert_out_other = flip(expert_out_give, "dp", 1)
        half_in = pl.BlockSpec((1, D, hidden_local), lambda i: (i, 0, 0))
        half_out = pl.BlockSpec((1, D, D), lambda i: (i, 0, 0))
        expert_keep, expert_code = pl.pallas_call(
            expert_split_kernel,
            out_shape=[out((2, D // 2, wide)), out((2, D // 2, wide + 128), jnp.int16)],
            grid=(2,),
            in_specs=[in_smem, half_in, half_in, half_out, half_out],
            out_specs=[
                pl.BlockSpec((1, D // 2, wide), lambda i: (i, 0, 0)),
                pl.BlockSpec((1, D // 2, wide + 128), lambda i: (i, 0, 0)),
            ],
            compiler_params=params(),
            cost_estimate=cost(4.6),
        )(sides, expert_in, expert_in_other, expert_out, expert_out_other)
        sums = local_sums + flip(local_sums, "dp", 2)
        routed_plain = routed_back
        routed_back = ready(routed_back, shared_code, expert_code, sums)
    attend_slope, mixed_slope, grad_output, gain_two, small_routed = simple_call(
        functools.partial(attend_back_kernel, fast),
        [
            out((amount, D)), out((amount, D), BF16), out((D, D)), out((1, D)), out((D, SMALL)),
        ],
        [
            routed_back, known, shared_second_slope, logits_slope, small_low, after,
            mixer_slope, gains, mixed, second, columns(pack, D, 3), small_head,
        ],
        6,
    )
    if fast:
        expert_code_other = flip(expert_code, "dp", 2)
        expert_own, expert_far = simple_call(
            expert_far_kernel,
            [out((D // 2, wide)), out((D // 2, wide + 128), jnp.int16)],
            [expert_keep, expert_code_other],
            3.5,
        )
        mixed_slope = ready(mixed_slope, expert_far)
    pack_columns = SMALL_AT + SMALL
    half_columns = SMALL_AT // 2 + SMALL
    last_keep, last_give = simple_call(
        functools.partial(front_back_kernel, fast),
        [
            out((D, half_columns if fast else pack_columns)),
            out((D, half_columns) if fast else (8, 128)),
        ],
        [
            (sides, in_smem), mixed_slope, qkv, log_total, known, rows_table, cosine, sine, first,
            embedded, gains, columns(pack, 3 * D, 0), attend_slope, small_routed, gain_two,
            gain_three, grad_output,
        ],
        18.4,
        [
            pltpu.VMEM((D, 2 * half_columns), F32),
            pltpu.VMEM((amount, D), F32),
            pltpu.VMEM((amount, D), F32),
            pltpu.VMEM((amount, D), F32),
            pltpu.VMEM((amount, 3 * D), BF16),
        ],
    )

    if fast:
        shared_code = ready(shared_code, routed_plain, expert_code)
        shared_code = exchange_near(shared_code.reshape(4, 2, local_rows, wide + 128))
        expert_far_other = flip(expert_far, "expert", 4)
        last_give = ready(last_give, expert_far_other, shared_code)
        shared_own, shared_far = simple_call(
            near_sum_kernel,
            [out((local_rows, wide)), out((local_rows, wide + 128), jnp.int16)],
            [(sides, in_smem), ready(shared_code, last_keep)],
            2.5,
        )
        last_keep = ready(last_keep, shared_far)
        last_codes = simple_call(
            functools.partial(last_code_kernel, local_rows),
            [out((2 * local_rows, half_columns + 128), jnp.int16)] * 4,
            [(sides, in_smem), last_keep, flip(last_give, "dp", 1)],
            3.3,
        )
        (shared_sum,) = simple_call(
            add_kernel, [out((local_rows, wide))], [shared_own, flip(shared_far, "expert", 4)], 1.5
        )
        last_code = last_codes[0]
        last_codes = [last_code] + [
            flip(ready(code, shared_code), "expert", bit)
            for bit, code in enumerate(last_codes)
            if bit
        ]
        last_own, last_far = simple_call(
            functools.partial(last_near_kernel, local_rows),
            [
                out((local_rows, half_columns)),
                out((local_rows, half_columns + 128), jnp.int16),
            ],
            [(sides, in_smem), *last_codes],
            2.5,
        )
        (last_part,) = simple_call(
            last_sum_kernel,
            [out((local_rows, half_columns))],
            [(sides, in_smem), last_own, flip(last_far, "expert", 4)],
            1.5,
        )
        last_other = flip(last_part, "dp", 2)
        (expert_total,) = simple_call(
            expert_total_kernel,
            [out((D // 2, wide + 128), jnp.int16)],
            [ready(expert_own, last_code), expert_far_other],
            2.5,
        )
        expert_cross = flip(expert_total, "dp", 2)
        shared_cross = flip(shared_sum, "dp", 2)
        square_pieces = [
            shared_sum, shared_cross, expert_total, expert_cross,
        ]
        weights = (1.0,) * 5
        square_bits = [1]
        pieces = [
            shared_sum, shared_cross, flip(shared_sum, "dp", 1), flip(shared_cross, "dp", 1),
            expert_total, expert_cross, flip(expert_total, "dp", 1), flip(expert_cross, "dp", 1),
        ]
        piece_specs = [whole(a) for a in pieces]
    else:
        sums = local_sums
        shin_part = scatter_sum(grad_shin, 0, [1])[0].reshape(expert_count, local_rows, FFS)
        shin_part = expert_scatter(scatter_sum(shin_part, 2, dp_bits[1:]))
        shout_part = scatter_sum(grad_shout.reshape(expert_count, -1, D), 1, dp_bits)
        shout_part = expert_scatter(shout_part)
        expert_in_part = scatter_sum(grad_expert_in.reshape(-1, hidden_local), 0, dp_bits)
        expert_out_part = scatter_sum(grad_expert_out, 0, dp_bits)
        last_part = expert_scatter(last_keep.reshape(expert_count, local_rows, -1))
        for bit in dp_bits:
            last_other = flip(last_part, "dp", bit)
            if bit != dp_bits[-1]:
                last_part = last_part + last_other
        square_pieces = [expert_in_part, expert_out_part, shin_part, shout_part]
        weights = (1.0 / dp_count, 1.0, 1.0, 1.0, 1.0)
        square_bits = dp_bits
        pieces = [
            join(join(shin_part, 1, dp_bits[1:])[None], 0, [1]),
            join(shout_part, 0, dp_bits),
            join(expert_in_part, 0, dp_bits).reshape(expert_input.shape),
            join(expert_out_part, 0, dp_bits),
        ]
        piece_specs = [tile_spec(i, a.shape, steps) for i, a in zip((4, 5, 7, 8), pieces)]
    last_part, both_sums = simple_call(
        functools.partial(squares_kernel, weights),
        [out(last_part.shape), out((2, 128))],
        [sums, last_part, last_other, *square_pieces],
        3.5,
    )
    last_pieces = [last_part] + ([flip(last_part, "dp", 1)] if fast else [])
    pieces = last_pieces + pieces
    piece_specs = [whole(a) for a in last_pieces] + piece_specs
    for bit in square_bits:
        both_sums = both_sums + flip(both_sums, "dp", bit)
    square_parts = expert_parts(both_sums)
    part_count = len(square_parts)
    shapes = [out(a.shape) for a in masters]
    state_specs = tile_specs(masters, steps)
    updates = pl.pallas_call(
        functools.partial(moments_kernel, fast, count, part_count, small_end),
        out_shape=[*shapes, *shapes, *shapes, out((32, 128)), out((2, 128))],
        grid=(steps,),
        in_specs=[
            in_smem, whole(master_squares), *[whole(a) for a in square_parts], *state_specs, *state_specs, *state_specs,
            *piece_specs,
        ],
        out_specs=[
            *state_specs, *state_specs, *state_specs, whole(out((32, 128))), whole(out((2, 128))),
        ],
        compiler_params=params(),
        cost_estimate=cost(17),
    )(sides, master_squares, *square_parts, *masters, *first_moments, *second_moments, *pieces)
    both_sums = updates[-1]
    domain_sums = both_sums[1, :DOMAINS]
    grad_norm = jnp.sqrt(both_sums[0, 0:1])
    directions = updates[:count]
    total_parts = expert_parts(updates[-2])
    *next_masters, trust = pl.pallas_call(
        functools.partial(step_kernel, count, part_count),
        out_shape=[*shapes, out((2, count))],
        grid=(steps,),
        in_specs=[in_smem, *[whole(a) for a in total_parts], *state_specs, *state_specs],
        out_specs=[*state_specs, whole(out((2, count)))],
        compiler_params=params(),
        cost_estimate=cost(7),
    )(sides, *total_parts, *masters, *directions)
    results = []
    for index in range(count):
        for group in (next_masters, updates[count : 2 * count], updates[2 * count : 3 * count]):
            results.append(group[index].T if index == 3 else group[index])
    results.append(jnp.stack([domain_sums, counts[0, :DOMAINS]]))
    results.append(grad_norm)
    results.append(trust.T)
    return tuple(results)


def solution(mesh):
    placed = (
        P(("dp", "expert")),
        P(("dp", "expert"), None),
        P(("dp", "expert"), None),
        P(("dp", "expert"), None),
        P(),
        P(None, "expert"),
        P("expert", None),
        P("expert", None),
        P("expert", None),
        P("expert", None),
        P("expert", None),
        P("expert", None),
        P(None, None, "expert"),
        P("expert", None),
        P(None, "expert"),
        P("expert", None),
        P("expert", None),
        P("expert", None),
        P("expert", None),
        P("expert", None),
        P("expert", None),
        P(None, None, "expert"),
        P("expert", None),
        P(None, "expert"),
        P("expert", None),
        P("expert", None),
        P("expert", None),
        P("expert", None),
        P("expert", None),
        P("expert", None),
        P(None, None, "expert"),
        P("expert", None),
    )
    return jax.shard_map(
        shards,
        mesh=mesh,
        in_specs=placed,
        out_specs=(
            P(None, "expert"),
            P(None, "expert"),
            P(None, "expert"),
            P("expert", None),
            P("expert", None),
            P("expert", None),
            P("expert", None),
            P("expert", None),
            P("expert", None),
            P("expert", None),
            P("expert", None),
            P("expert", None),
            P("expert", None),
            P("expert", None),
            P("expert", None),
            P("expert", None),
            P("expert", None),
            P("expert", None),
            P("expert", None),
            P("expert", None),
            P("expert", None),
            P(None, None, "expert"),
            P(None, None, "expert"),
            P(None, None, "expert"),
            P("expert", None),
            P("expert", None),
            P("expert", None),
            P(),
            P(),
            P(),
        ),
        check_vma=False,
    )
```

```python
import functools

import jax
import jax.numpy as jnp
import numpy as np
from jax import lax
from jax.experimental import pallas as pl
from jax.experimental.pallas import tpu as pltpu
from jax.sharding import PartitionSpec as P

D = 384
HEADS = 12
HD = 32
FFS = 1536
EXPERTS = 8
DOMAINS = 9
STEP = 10
CAP = 256


HORIZONS = (1, 8, 32, 64)
REACH = 64
KINK_THRESHOLD = 2.0
EPS_NORM = 1e-06
CLIP = 0.01
BETA_ONE = 0.9
BETA_TWO = 0.99
EPS_ADAM = 1e-08
DECAY = 0.01
RATE = 0.3


def ahead_table():
    return np.concatenate([np.arange(horizon_len) for horizon_len in HORIZONS]).astype(np.int32)


def target_columns(samples):
    amount = samples.shape[0]
    padded = jnp.concatenate([samples, jnp.zeros((REACH + 1,), samples.dtype)])
    future = jnp.stack([padded[1 + offset : 1 + offset + amount] for offset in range(REACH)], 1)
    return future[:, ahead_table()]


ROW_BLOCK = 256
SCORE_SCALE = HD ** (-0.5) * 1.4426950408889634
SMALL = 128
HORIZON_AT = EXPERTS + 1
VECTORS_AT = 120
SMALL_AT = 4 * D
COUNTS_AT = 125
CODE_ROWS = 16
VMEM = 56 * 1024 * 1024
F32 = jnp.float32
BF16 = jnp.bfloat16


def mm(left, right):
    return jnp.dot(left, right, preferred_element_type=F32)


def mm_nt(left, right):
    return lax.dot_general(left, right, (((1,), (1,)), ((), ())), preferred_element_type=F32)


def mm_tn(left, right):
    return lax.dot_general(left, right, (((0,), (0,)), ((), ())), preferred_element_type=F32)


def inverse_rms(rows):
    return lax.rsqrt(jnp.mean(rows * rows, axis=-1, keepdims=True) + EPS_NORM)


def rms_back(rows, inverse, gain, slope):
    gain_slope = jnp.sum(slope * rows * inverse, 0, keepdims=True)
    scaled = slope * gain
    return (
        inverse * scaled
        - rows * (inverse * inverse * inverse) * jnp.mean(rows * scaled, -1, keepdims=True),
        gain_slope,
    )


def lanes_of(shape):
    return lax.broadcasted_iota(jnp.int32, shape, len(shape) - 1)


def half_swap(rows):
    half_width = HD // 2
    lane = lanes_of(rows.shape)
    return jnp.where(
        lane % HD < half_width,
        pltpu.roll(rows, rows.shape[1] - half_width, 1),
        pltpu.roll(rows, half_width, 1),
    )


SLOT, SERIES_OF, FINISH, DOMAIN, CHOICE, VALUE, PLACE = 0, 2, 3, 4, 5, 7, 8


def tables_kernel(
    lengths, domains, frequency, points_row, experts_row, cosine, sine, columns_out, rows_out
):
    amount = points_row.shape[1]
    place = lax.broadcasted_iota(jnp.int32, (1, amount), 1)
    series = jnp.zeros((1, amount), jnp.int32)
    begin = jnp.zeros((1, amount), jnp.int32)
    finish = jnp.zeros((1, amount), jnp.int32)
    domain = jnp.zeros((1, amount), jnp.int32)
    start = jnp.int32(0)
    for index in range(lengths.shape[1]):
        stop = start + lengths[0, index]
        inside = (place >= start) & (place < stop)
        series = jnp.where(inside, index, series)
        begin = jnp.where(inside, start, begin)
        finish = jnp.where(inside, stop, finish)
        domain = jnp.where(inside, domains[0, index], domain)
        start = stop
    name = lax.broadcasted_iota(jnp.int32, (16, amount), 0)
    choices = [experts_row[k : k + 1, :] for k in range(2)]
    named = [(name == choice).astype(F32) for choice in choices]
    earlier = (
        lax.broadcasted_iota(jnp.int32, (amount, amount), 0)
        < lax.broadcasted_iota(jnp.int32, (amount, amount), 1)
    )
    before = mm((named[0] + named[1]).astype(BF16), earlier.astype(F32).astype(BF16))
    entries = []
    for k in range(2):
        rank = jnp.sum(named[k] * before, 0, keepdims=True)
        entries.append(choices[k].astype(F32) * CAP + rank)
    entries += [series, finish, domain, *choices, points_row[...], place - begin]
    row = lax.broadcasted_iota(jnp.int32, (128, amount), 0)
    table = jnp.zeros((128, amount), F32)
    for index, entry in enumerate(entries):
        table = jnp.where(row == index, entry.astype(F32), table)
    rows_out[...] = table[:8]
    columns = table.T
    columns_out[...] = columns
    angles = columns[:, PLACE : PLACE + 1] * frequency[...]
    cosine[...] = jnp.cos(angles)
    turned = jnp.sin(angles)
    sine[...] = jnp.where(lanes_of((amount, 128)) % HD < HD // 2, -turned, turned)


def allowed_block(table, rows_table, start, rows, keys):
    query = start + lax.broadcasted_iota(jnp.int32, (rows, keys), 0)
    key = lax.broadcasted_iota(jnp.int32, (rows, keys), 1)
    series_col = table[start : start + rows, SERIES_OF : SERIES_OF + 1]
    return (series_col == rows_table[SERIES_OF : SERIES_OF + 1, :keys]) & (key <= query)


def slot_place(grouped, expert):
    return (expert % 4) * 2 + expert // 4 if grouped else expert


def slot_rows_hot(slot_row, expert):
    slot = expert * CAP + lax.broadcasted_iota(jnp.int32, (CAP, slot_row.shape[1]), 0)
    return (slot_row.astype(jnp.int32) == slot).astype(F32).astype(BF16)


def slot_cols_hot(slot_col, expert):
    slot = expert * CAP + lax.broadcasted_iota(jnp.int32, (slot_col.shape[0], CAP), 1)
    return (slot_col.astype(jnp.int32) == slot).astype(F32).astype(BF16)


def pack_kernel(small_end, core, lengths, domains, ahead, input_w, output_w, router, horizon, vectors, out):
    rows = input_w.shape[0]

    def placed(count, at):
        row = lax.broadcasted_iota(jnp.int32, (count, SMALL), 0)
        return (row + at == lanes_of((count, SMALL))).astype(F32).astype(BF16)

    small = (
        mm_tn(router[...].astype(BF16), placed(HORIZON_AT, 0))
        + mm(horizon[...].astype(BF16), placed(small_end - HORIZON_AT, HORIZON_AT))
        + mm_tn(vectors[...].astype(BF16), placed(vectors.shape[0], VECTORS_AT))
    )
    row = lax.broadcasted_iota(jnp.int32, (rows, SMALL), 0)
    lane = lanes_of((rows, SMALL))
    counts = jnp.zeros((rows, SMALL), F32)
    for series in range(lengths.shape[1]):
        left = jnp.maximum(lengths[0, series] - 1 - ahead[...], 0).astype(F32)
        entries = jnp.sum(left, -1, keepdims=True)
        counts = counts + jnp.where(row == domains[0, series], entries, 0.0)
    high = jnp.floor(counts * (1.0 / 256.0))
    small = jnp.where(lane == COUNTS_AT, high, small)
    small = jnp.where(lane == COUNTS_AT + 1, counts - 256.0 * high, small)
    flat = jnp.concatenate([input_w[...], output_w[...]], 1)
    half = 2 * D
    mine = jnp.where(core[0] == 0, flat[:, :half], flat[:, half:]).astype(BF16)
    for target in range(out.shape[0]):
        out[target, :, :half] = mine
        out[target, :, half:] = small.astype(BF16)


def pair_kernel(sides, own, far, out):
    low = sides[2] == 0
    first = jnp.where(low, own[...], far[...])
    second = jnp.where(low, far[...], own[...])
    for target in range(out.shape[0]):
        out[target, 0] = first
        out[target, 1] = second


def front_kernel(
    grouped, local_rows, core, mine, other, cosine, sine, known, slot_row,
    embedded_out, first_out, qkv_out, log_out, mixed_out, after_out, second_out, logits_out,
    slots_out, gains_out, pack, counts_out,
):
    amount = known.shape[0]
    half = 2 * D
    low = core[0] == 0
    for index in range(D // local_rows):
        place = slot_place(grouped, index)
        here = slice(index * local_rows, (index + 1) * local_rows)
        there = slice(place * local_rows, (place + 1) * local_rows)
        left, right = mine[there, :half], other[there, :half]
        pack[here, :half] = jnp.where(low, left, right)
        pack[here, half:SMALL_AT] = jnp.where(low, right, left)
        pack[here, SMALL_AT:] = mine[there, half:]
    table = pack[:, SMALL_AT:].astype(F32).T
    gains = table[VECTORS_AT : VECTORS_AT + 8]
    gains_out[...] = gains
    other_table = other[:, half:].astype(F32).T
    row = lax.broadcasted_iota(jnp.int32, (D, SMALL), 0)
    fold = (row % local_rows == lanes_of((D, SMALL))).astype(F32).astype(BF16)
    digits = mm(table[VECTORS_AT : VECTORS_AT + 8].astype(BF16), fold) + mm(
        other_table[VECTORS_AT : VECTORS_AT + 8].astype(BF16), fold
    )
    at = COUNTS_AT - VECTORS_AT
    counts_out[...] = digits[at : at + 1] * 256.0 + digits[at + 1 : at + 2]
    value = known[:, VALUE : VALUE + 1]
    gate = value * gains[0:1]
    embedded = gate * jax.nn.sigmoid(gate) * (value * gains[1:2])
    embedded_out[...] = embedded
    first = (embedded * inverse_rms(embedded) * gains[2:3]).astype(BF16)
    first_out[...] = first
    projected = mm(first, pack[:, : 3 * D])
    cos_rows, sin_rows = cosine[...], sine[...]
    for block in range(6):
        part = projected[:, block * 128 : (block + 1) * 128]
        part = part * cos_rows + half_swap(part) * sin_rows
        qkv_out[:, block * 128 : (block + 1) * 128] = part.astype(BF16)
    qkv_out[:, 2 * D :] = projected[:, 2 * D :].astype(BF16)
    lane = lanes_of((ROW_BLOCK, 128))
    for start in range(0, amount, ROW_BLOCK):
        keys = start + ROW_BLOCK
        allowed = allowed_block(known[...], slot_row[...], start, ROW_BLOCK, keys)
        log_rows = jnp.zeros((ROW_BLOCK, 128), F32)
        for group in range(D // 128):
            query = qkv_out[start : start + ROW_BLOCK, group * 128 : (group + 1) * 128]
            key = qkv_out[:keys, D + group * 128 : D + (group + 1) * 128]
            held = qkv_out[:keys, 2 * D + group * 128 : 2 * D + (group + 1) * 128]
            gathered = jnp.zeros((ROW_BLOCK, 128), F32)
            for head in range(128 // HD):
                own = lane // HD == head
                raw = mm_nt(jnp.where(own, query, jnp.zeros_like(query)), key) * SCORE_SCALE
                raw = jnp.where(allowed, raw, -1e30)
                top = jnp.max(raw, -1, keepdims=True)
                exponent = jnp.exp2(raw - top)
                total = jnp.sum(exponent, -1, keepdims=True)
                attention = (exponent * (1.0 / total)).astype(BF16)
                gathered = jnp.where(own, mm(attention, held), gathered)
                log_rows = jnp.where(
                    lane == group * (128 // HD) + head, top + jnp.log2(total), log_rows
                )
            mixed_out[start : start + ROW_BLOCK, group * 128 : (group + 1) * 128] = (
                gathered.astype(BF16)
            )
        log_out[start : start + ROW_BLOCK, :] = log_rows
    after = embedded + mm(mixed_out[...], pack[:, 3 * D : 4 * D])
    after_out[...] = after
    second = (after * inverse_rms(after) * gains[3:4]).astype(BF16)
    second_out[...] = second
    logits_out[...] = mm(second, pack[:, SMALL_AT:])
    for expert in range(EXPERTS):
        hot = slot_rows_hot(slot_row[0:1, :], expert) + slot_rows_hot(slot_row[1:2, :], expert)
        place = slot_place(grouped, expert)
        slots_out[place * CAP : (place + 1) * CAP, :] = mm(hot, second).astype(BF16)


def shared_kernel(second, gate_w, lift_w, down_w, shared_out):
    gate = mm(second[...], gate_w[...])
    lift = mm(second[...], lift_w[...])
    hidden = (gate * jax.nn.sigmoid(gate) * lift).astype(BF16)
    part = mm(hidden, down_w[...])

    @pl.when(pl.program_id(0) == 0)
    def _():
        shared_out[...] = part

    @pl.when(pl.program_id(0) != 0)
    def _():
        shared_out[...] += part


def code_rows(part, ref):
    top = jnp.max(jnp.abs(part), -1, keepdims=True)
    power = jnp.ceil(jnp.log2(jnp.maximum(top, 1e-30)))
    code = jnp.clip(jnp.round(part * jnp.exp2(15.0 - power)), -32767.0, 32767.0)
    ref[:CAP, :] = code.astype(jnp.int32).astype(jnp.int16)
    row = lax.broadcasted_iota(jnp.int32, (CAP, CAP), 0)
    column = lax.broadcasted_iota(jnp.int32, (CAP, CAP), 1)
    powers = jnp.sum(jnp.where(row == column, power, 0.0), 0, keepdims=True)
    powers = jnp.concatenate([powers, jnp.zeros((1, D - CAP), F32)], 1)
    ref[CAP:, :] = jnp.broadcast_to(powers, (CODE_ROWS, D)).astype(jnp.int32).astype(jnp.int16)


def unit(rows, gate_up, down):
    gate = mm(rows, gate_up[0])
    lift = mm(rows, gate_up[1])
    hidden = (gate * jax.nn.sigmoid(gate) * lift).astype(BF16)
    return mm(hidden, down[...])


def expert_kernel(rows, gate_up, down, rows_out):
    rows_out[...] = unit(rows[...], gate_up, down)


def pair_expert_kernel(sides, rows, gate_up, down, gate_up_far, down_far, rows_out):
    sources = rows.shape[0]
    flat = rows[...].reshape(sources * CAP, D)

    def serve(weights):
        result = unit(flat, *weights)
        for source in range(sources):
            code_rows(result[source * CAP : (source + 1) * CAP], rows_out.at[source, 0])

    pl.when(pl.program_id(0) == 0)(lambda: serve((gate_up, down)))
    pl.when(pl.program_id(0) == 1)(lambda: serve((gate_up_far, down_far)))


def far_weights_kernel(sides, *refs):
    pieces, (gate_up, down) = refs[:4], refs[4:]
    me = sides[0] * 2 + sides[1]
    half, wide = pieces[0].shape[0], gate_up.shape[2]
    for piece in range(4):
        core, cross = piece // 2, piece % 2
        value = picked_piece(pieces, jnp.bitwise_xor(piece, me), lambda ref: ref[...])
        gate_up[core, cross * half : (cross + 1) * half, :] = value[:, :wide]
        down[piece * half : (piece + 1) * half, :] = value[:, wide:]


def shared_weights_kernel(local_rows, sides, *refs):
    pieces, (both, down) = refs[:4], refs[4:]
    me = sides[0] * 2 + sides[1]
    wide = pieces[0].shape[1]
    shard = down.shape[0] // (D // local_rows)
    for piece in range(4):
        value = picked_piece(pieces, jnp.bitwise_xor(piece, me), lambda ref: ref[...])
        for index in range(D // local_rows):
            place = slot_place(True, index)
            rows = value[place * local_rows : (place + 1) * local_rows]
            for at in range(0, wide, D):
                column = piece * wide + at
                part = rows[:, at : at + D]
                if column < 2 * FFS:
                    both[index * local_rows : (index + 1) * local_rows, column : column + D] = part
                else:
                    row = index * shard + (column - 2 * FFS) // D * local_rows
                    down[row : row + local_rows, :] = part


def unit_back(rows, slope, gate_w, lift_w, down_w):
    gate = mm(rows, gate_w)
    lift = mm(rows, lift_w)
    bent = jax.nn.sigmoid(gate)
    smooth = gate * bent
    hidden = (smooth * lift).astype(BF16)
    hidden_slope = mm_nt(slope, down_w)
    gate_slope = (hidden_slope * lift * (bent * (1.0 + gate * (1.0 - bent)))).astype(BF16)
    lift_slope = (hidden_slope * smooth).astype(BF16)
    return hidden, gate_slope, lift_slope


def expert_back_kernel(rows, slope, gate_up, down, rows_out, in_out, out_out):
    hidden, gate_slope, lift_slope = unit_back(
        rows[...], slope[...], gate_up[0], gate_up[1], down[...]
    )
    rows_out[...] = (mm_nt(gate_slope, gate_up[0]) + mm_nt(lift_slope, gate_up[1])).astype(BF16)

    @pl.when(pl.program_id(0) == 0)
    def _():
        in_out[...] = jnp.zeros_like(in_out)
        out_out[...] = jnp.zeros_like(out_out)

    in_out[0] += mm_tn(rows[...], gate_slope)
    in_out[1] += mm_tn(rows[...], lift_slope)
    out_out[...] += mm_tn(hidden, slope[...])


def shared_back_kernel(second, slope, gate_w, lift_w, down_w, second_out, in_out, out_out):
    hidden, gate_slope, lift_slope = unit_back(
        second[...], slope[...], gate_w[...], lift_w[...], down_w[...]
    )
    part = mm_nt(gate_slope, gate_w[...]) + mm_nt(lift_slope, lift_w[...])

    @pl.when(pl.program_id(0) == 0)
    def _():
        second_out[...] = part

    @pl.when(pl.program_id(0) != 0)
    def _():
        second_out[...] += part

    in_out[0] = mm_tn(second[...], gate_slope)
    in_out[1] = mm_tn(second[...], lift_slope)
    out_out[...] = mm_tn(hidden, slope[...])


def expert_back_split_kernel(
    sides, rows, slope, gate_up, down, gate_up_far, down_far,
    rows_out, in_keep, in_give, out_keep, out_give,
):
    sources = rows.shape[0]
    flat = rows[...].reshape(sources * CAP, D)
    flat_slope = slope[...].reshape(sources * CAP, D)

    @pl.when(pl.program_id(1) == 0)
    def _():
        for ref in (in_keep, in_give, out_keep, out_give):
            ref[...] = jnp.zeros_like(ref)

    def serve(gate_w, down_w):
        hidden, gate_slope, lift_slope = unit_back(
            flat, flat_slope, gate_w[0], gate_w[1], down_w[...]
        )
        result = (mm_nt(gate_slope, gate_w[0]) + mm_nt(lift_slope, gate_w[1])).astype(BF16)
        rows_out[...] = result.reshape(rows_out.shape)
        half = hidden.shape[1] // 2
        low = sides[0] == 0
        gate = mm_tn(flat, gate_slope)
        lift = mm_tn(flat, lift_slope)
        in_keep[0] += jnp.where(low, gate, lift)
        in_give[0] += jnp.where(low, lift, gate)
        first = mm_tn(hidden[:, :half], flat_slope)
        last = mm_tn(hidden[:, half:], flat_slope)
        out_keep[0] += jnp.where(low, first, last)
        out_give[0] += jnp.where(low, last, first)

    pl.when(pl.program_id(0) == 0)(lambda: serve(gate_up, down))
    pl.when(pl.program_id(0) == 1)(lambda: serve(gate_up_far, down_far))


def shared_back_split_kernel(
    sides, second, slope, gate_w, lift_w, down_w,
    second_out, in_keep, in_give_even, in_give_odd, out_keep, out_give, out_ref,
):
    hidden, gate_slope, lift_slope = unit_back(
        second[...], slope[...], gate_w[...], lift_w[...], down_w[...]
    )
    part = mm_nt(gate_slope, gate_w[...]) + mm_nt(lift_slope, lift_w[...])

    @pl.when(pl.program_id(0) == 0)
    def _():
        second_out[...] = part

    @pl.when(pl.program_id(0) != 0)
    def _():
        second_out[...] += part

    core, cross = sides[0], sides[1]
    low = core == 0
    gate = mm_tn(second[...], gate_slope)
    lift = mm_tn(second[...], lift_slope)
    in_keep[0] = jnp.where(low, gate, lift)
    given = jnp.where(low, lift, gate)
    half = given.shape[1] // 2
    in_give_even[0] = given[:, :half]
    in_give_odd[0] = given[:, half:]
    out_ref[...] = mm_tn(hidden, slope[...])
    quarter = D // EXPERTS
    shards = out_keep.shape[1] // quarter
    for shard in range(shards):
        for side in range(2):
            for ref, half in ((out_keep, core), (out_give, 1 - core)):
                piece = half * 2 + jnp.bitwise_xor(cross, side)
                start = pl.multiple_of(shard * 4 * quarter + piece * quarter, 8)
                ref[side, shard * quarter : (shard + 1) * quarter, :] = out_ref[
                    pl.ds(start, quarter), :
                ]


def coded_tile(value):
    top = jnp.max(jnp.abs(value), -1, keepdims=True)
    power = jnp.ceil(jnp.log2(jnp.maximum(top, 1e-30)))
    code = jnp.clip(jnp.round(value * jnp.exp2(15.0 - power)), -32767.0, 32767.0)
    return code, power


def encode(ref, tiles):
    lane = lanes_of(tiles[0].shape)
    powers = jnp.zeros(tiles[0].shape, F32)
    for index, tile in enumerate(tiles):
        code, power = coded_tile(tile)
        ref[:, index * 128 : (index + 1) * 128] = code.astype(jnp.int32).astype(jnp.int16)
        powers = jnp.where(lane == index, power, powers)
    ref[:, len(tiles) * 128 :] = powers.astype(jnp.int32).astype(jnp.int16)


def decode(ref):
    count = ref.shape[-1] // 128 - 1
    scale = jnp.exp2(ref[..., count * 128 :].astype(jnp.int32).astype(F32) - 15.0)
    return [
        ref[..., index * 128 : (index + 1) * 128].astype(jnp.int32).astype(F32)
        * scale[..., index : index + 1]
        for index in range(count)
    ]


def tiles_of(value):
    return [value[:, at : at + 128] for at in range(0, value.shape[1], 128)]


def fold_kernel(in_keep, in_even, in_odd, out_keep, out_other, keep, give):
    wide = in_keep.shape[2]
    half = wide // 2
    keep[:, :half] = in_keep[0, :, :half] + in_even[0]
    keep[:, half:wide] = in_keep[0, :, half:] + in_odd[0]
    keep[:, wide:] = out_keep[0] + out_other[0]
    encode(
        give,
        tiles_of(in_keep[1, :, :half] + in_even[1])
        + tiles_of(in_keep[1, :, half:] + in_odd[1])
        + tiles_of(out_keep[1] + out_other[1]),
    )


def add_code_kernel(rows, keep, other, code):
    for index in range(keep.shape[0] // rows):
        here = slice(index * rows, (index + 1) * rows)
        place = slot_place(True, index)
        encode(
            code.at[place * rows : (place + 1) * rows],
            [
                mine + theirs
                for mine, theirs in zip(tiles_of(keep[here, :]), decode(other.at[here]))
            ],
        )


def near_sum_kernel(sides, codes, own, far):
    mine = [jnp.sum(tile, 0) for tile in decode(codes.at[:, sides[2]])]
    for index, tile in enumerate(mine):
        own[:, index * 128 : (index + 1) * 128] = tile
    encode(far, [jnp.sum(tile, 0) for tile in decode(codes.at[:, 1 - sides[2]])])


def add_kernel(own, code, total):
    for index, tile in enumerate(decode(code)):
        here = slice(index * 128, (index + 1) * 128)
        total[:, here] = own[:, here] + tile


def expert_split_kernel(sides, in_keep, in_other, out_keep, out_other, keep, code):
    wide, half = in_keep.shape[2], in_keep.shape[1] // 2
    here = pl.ds(pl.multiple_of(sides[1] * half, 8), half)
    there = pl.ds(pl.multiple_of((1 - sides[1]) * half, 8), half)
    keep[0, :, :wide] = in_keep[0, here, :] + in_other[0, here, :]
    keep[0, :, wide:] = out_keep[0, here, :] + out_other[0, here, :]
    encode(
        code.at[0],
        tiles_of(in_keep[0, there, :] + in_other[0, there, :])
        + tiles_of(out_keep[0, there, :] + out_other[0, there, :]),
    )


def expert_far_kernel(keep, codes, own, far):
    for index, tile in enumerate(decode(codes.at[0])):
        here = slice(index * 128, (index + 1) * 128)
        own[:, here] = keep[0, :, here] + tile
    encode(far, [mine + theirs for mine, theirs in zip(tiles_of(keep[1]), decode(codes.at[1]))])


def expert_total_kernel(own, code, total):
    encode(
        total, [mine + theirs for mine, theirs in zip(tiles_of(own[...]), decode(code))]
    )


def encode_last(ref, tiles, high):
    rough, power = coded_tile(tiles[5])
    rest = tiles[5] - rough * jnp.exp2(power - 15.0)
    encode(ref, [*tiles[:6], jnp.where(high, rest, tiles[6])])


def whole_tiles(tiles, high):
    return [
        *tiles[:5],
        jnp.where(high, tiles[5] + tiles[6], tiles[5]),
        jnp.where(high, 0.0, tiles[6]),
    ]


def last_code_kernel(rows, sides, keep, other, *codes):
    for target, code in enumerate(codes):
        for half in range(2):
            shard = jnp.bitwise_xor(sides[4], target) + 4 * half
            here = pl.ds(pl.multiple_of(shard * rows, 8), rows)
            tiles = tiles_of(keep[here, :] + other[here, :])
            encode_last(code.at[half * rows : (half + 1) * rows], tiles, sides[0] == 1)


def last_near_kernel(rows, sides, *refs):
    codes, (own, far) = refs[:-2], refs[-2:]
    high = sides[0] == 1

    def gathered(half):
        here = pl.ds(pl.multiple_of(half * rows, 16), rows)
        sums = None
        for code in codes:
            tiles = decode(code.at[here])
            sums = tiles if sums is None else [a + b for a, b in zip(sums, tiles)]
        return whole_tiles(sums, high)

    for index, tile in enumerate(gathered(sides[2])):
        own[:, index * 128 : (index + 1) * 128] = tile
    encode_last(far, gathered(1 - sides[2]), high)


def last_sum_kernel(sides, own, code, total):
    for index, tile in enumerate(whole_tiles(decode(code), sides[0] == 1)):
        here = slice(index * 128, (index + 1) * 128)
        total[:, here] = own[:, here] + tile


def middle_kernel(
    grouped, returned, known, slot_row, after, shared, logits, small, gains, target, ahead, weighting,
    mixer_out, shared_slope_out, slots_out, logits_slope_out, small_out, gain_out, sums_out,
):
    amount = after.shape[0]
    lane = lanes_of((amount, SMALL))
    table = known[...]
    integers = table[:, :8].astype(jnp.int32)
    chosen = [
        (lane == integers[:, CHOICE + k : CHOICE + k + 1]).astype(F32) for k in range(2)
    ]
    point = lax.broadcasted_iota(jnp.int32, (amount, SMALL), 0)
    usable = (point + 1 + ahead[...] < integers[:, FINISH : FINISH + 1]).astype(F32)
    logit = logits[...]
    routed = lane < EXPERTS
    top = jnp.max(jnp.where(routed, logit, -1e30), -1, keepdims=True)
    exponent = jnp.where(routed, jnp.exp(jnp.where(routed, logit - top, 0.0)), 0.0)
    probs = exponent / jnp.sum(exponent, -1, keepdims=True)
    gates = [jnp.sum(chosen[k] * probs, -1, keepdims=True) for k in range(2)]
    shared_gate = jax.nn.sigmoid(
        jnp.sum(jnp.where(lane == EXPERTS, logit, 0.0), -1, keepdims=True)
    )
    picked = [jnp.zeros((amount, D), F32), jnp.zeros((amount, D), F32)]
    for expert in range(EXPERTS):
        place = slot_place(grouped, expert)
        if len(returned.shape) == 2:
            rows = returned[place * CAP : (place + 1) * CAP, :]
            scale = 1.0
        else:
            rows = returned[place, :CAP, :].astype(jnp.int32).astype(F32)
            powers = returned[place, CAP:, :].astype(jnp.int32).astype(F32)
            scale = jnp.exp2(powers[0:1, :CAP] - 15.0)
        high = rows.astype(BF16)
        rest = (rows - high.astype(F32)).astype(BF16)
        halves_of_rows = jnp.concatenate([high, rest], 1)
        for k in range(2):
            slot = expert * CAP + lax.broadcasted_iota(jnp.int32, (amount, CAP), 1)
            hot = jnp.where(integers[:, SLOT + k : SLOT + k + 1] == slot, scale, 0.0).astype(BF16)
            both = mm(hot, halves_of_rows)
            picked[k] = picked[k] + (both[:, :D] + both[:, D:])
    mixer = (
        after[...] + shared_gate * shared[...] + (gates[0] * picked[0] + gates[1] * picked[1])
    )
    inverse = inverse_rms(mixer)
    gain = gains[4:5]
    third = (mixer * inverse * gain).astype(BF16)
    residue = mm(third, small[...]) - target[...]
    size = jnp.abs(residue)
    cost = (
        jnp.where(
            size <= KINK_THRESHOLD,
            0.5 * residue * residue,
            KINK_THRESHOLD * (size - 0.5 * KINK_THRESHOLD),
        )
        * usable
    )
    domain_hot = (lane == integers[:, DOMAIN : DOMAIN + 1]).astype(F32)
    sums_out[...] = jnp.sum(domain_hot * jnp.sum(cost, -1, keepdims=True), 0, keepdims=True)
    weight = jnp.sum(domain_hot * weighting[...], -1, keepdims=True)
    slope = (
        jnp.clip(residue, -KINK_THRESHOLD, KINK_THRESHOLD) * usable * weight
    ).astype(BF16)
    small_out[...] = mm_tn(third, slope)
    mixer_slope, gain_slope = rms_back(mixer, inverse, gain, mm_nt(slope, small[...]))
    gain_out[...] = gain_slope
    mixer_out[...] = mixer_slope
    shared_slope_out[...] = (shared_gate * mixer_slope).astype(BF16)
    gate_slope = jnp.sum(mixer_slope * shared[...], -1, keepdims=True)
    probs_slope = chosen[0] * jnp.sum(mixer_slope * picked[0], -1, keepdims=True) + chosen[
        1
    ] * jnp.sum(mixer_slope * picked[1], -1, keepdims=True)
    inner = jnp.sum(probs * probs_slope, -1, keepdims=True)
    logits_slope_out[...] = jnp.where(
        routed,
        probs * (probs_slope - inner),
        jnp.where(lane == EXPERTS, gate_slope * (shared_gate * (1.0 - shared_gate)), 0.0),
    ).astype(BF16)
    slopes = [(gates[k] * mixer_slope).astype(BF16) for k in range(2)]
    for expert in range(EXPERTS):
        place = slot_place(grouped, expert)
        slots_out[place * CAP : (place + 1) * CAP, :] = (
            mm(slot_rows_hot(slot_row[0:1, :], expert), slopes[0])
            + mm(slot_rows_hot(slot_row[1:2, :], expert), slopes[1])
        ).astype(BF16)


def attend_back_kernel(
    grouped, returned, known, second_slope, logits_slope, small, after, mixer_slope, gains, mixed, second,
    output_w, small_before,
    attend_out, mixed_out, output_out, gain_out, small_out,
):
    slope = second_slope[...] + mm_nt(logits_slope[...], small[...])
    for expert in range(EXPERTS):
        hot = slot_cols_hot(known[:, 0:1], expert) + slot_cols_hot(known[:, 1:2], expert)
        place = slot_place(grouped, expert)
        slope = slope + mm(hot, returned[place * CAP : (place + 1) * CAP, :])
    after_rows = after[...]
    part, gain_slope = rms_back(after_rows, inverse_rms(after_rows), gains[3:4], slope)
    gain_out[...] = gain_slope
    attend = mixer_slope[...] + part
    attend_out[...] = attend
    low = attend.astype(BF16)
    output_out[...] = mm_tn(mixed[...], low)
    mixed_out[...] = mm_nt(low, output_w[...]).astype(BF16)
    small_out[...] = small_before[...] + mm_tn(second[...], logits_slope[...])


def front_back_kernel(
    fast, core, mixed_slope, qkv, log_total, known, rows_table, cosine, sine, first, embedded,
    gains, input_w, attend_slope, small_before, gain_two, gain_three, output_before,
    keep_out, give_out,
    pack_out, query_acc, key_acc, held_acc, slope_ref,
):
    amount = first.shape[0]
    key_acc[...] = jnp.zeros_like(key_acc)
    held_acc[...] = jnp.zeros_like(held_acc)
    lane = lanes_of((ROW_BLOCK, 128))
    lane_all = lanes_of((amount, 128))
    for start in range(0, amount, ROW_BLOCK):
        keys = start + ROW_BLOCK
        here = slice(start, start + ROW_BLOCK)
        allowed = allowed_block(known[...], rows_table[...], start, ROW_BLOCK, keys)
        for group in range(D // 128):
            wide = slice(group * 128, (group + 1) * 128)
            query = qkv[here, group * 128 : (group + 1) * 128]
            key = qkv[:keys, D + group * 128 : D + (group + 1) * 128]
            held = qkv[:keys, 2 * D + group * 128 : 2 * D + (group + 1) * 128]
            out_slope = mixed_slope[here, wide]
            query_sum = jnp.zeros((ROW_BLOCK, 128), F32)
            key_sum = jnp.zeros((keys, 128), F32)
            held_sum = jnp.zeros((keys, 128), F32)
            for head in range(128 // HD):
                own = lane // HD == head
                own_query = jnp.where(own, query, jnp.zeros_like(query))
                own_slope = jnp.where(own, out_slope, jnp.zeros_like(out_slope))
                own_key = jnp.where(lane_all[:keys] // HD == head, key, jnp.zeros_like(key))
                at = group * (128 // HD) + head
                raw = mm_nt(own_query, key) * SCORE_SCALE
                probs = jnp.exp2(jnp.where(allowed, raw - log_total[here, at : at + 1], -1e30))
                held_sum = held_sum + mm_tn(probs.astype(BF16), own_slope)
                probs_slope = mm_nt(own_slope, held)
                inner = jnp.sum(probs_slope * probs, -1, keepdims=True)
                raw_slope = (probs * (probs_slope - inner)).astype(BF16)
                query_sum = query_sum + mm(raw_slope, own_key)
                key_sum = key_sum + mm_tn(raw_slope, own_query)
            query_acc[here, wide] = query_sum
            key_acc[:keys, wide] += key_sum
            held_acc[:keys, wide] += held_sum
    cos_rows, sin_rows = cosine[...], sine[...]
    for block in range(3):
        wide = slice(block * 128, (block + 1) * 128)
        for base, acc in ((0, query_acc), (D, key_acc)):
            part = acc[:, wide] * HD ** (-0.5)
            part = part * cos_rows + half_swap(part * sin_rows)
            slope_ref[:, base + block * 128 : base + (block + 1) * 128] = part.astype(BF16)
    slope_ref[:, 2 * D :] = held_acc[...].astype(BF16)
    projected_slope = slope_ref[...]
    pack_out[:, : 3 * D] = mm_tn(first[...], projected_slope)
    pack_out[:, 3 * D : SMALL_AT] = output_before[...]
    first_slope = mm_nt(projected_slope, input_w[...])
    rows = embedded[...]
    part, gain_one = rms_back(rows, inverse_rms(rows), gains[2:3], first_slope)
    slope = attend_slope[...] + part
    value = known[:, VALUE : VALUE + 1]
    gate = value * gains[0:1]
    bent = jax.nn.sigmoid(gate)
    gate_gradient = jnp.sum(
        slope * (value * gains[1:2]) * (bent * (1.0 + gate * (1.0 - bent))) * value,
        0,
        keepdims=True,
    )
    lift_gradient = jnp.sum(slope * (gate * bent) * value, 0, keepdims=True)
    row = lax.broadcasted_iota(jnp.int32, (128, D), 0)
    table = jnp.zeros((128, D), F32)
    for offset, piece in enumerate(
        (gate_gradient, lift_gradient, gain_one, gain_two[...], gain_three[...])
    ):
        table = jnp.where(row == VECTORS_AT + offset, piece, table)
    pack_out[:, SMALL_AT : SMALL_AT + SMALL] = small_before[...] + table.T
    if not fast:
        keep_out[...] = pack_out[:, : keep_out.shape[1]]
        give_out[...] = jnp.zeros_like(give_out)
        return
    pack_out[:, SMALL_AT + SMALL :] = jnp.zeros_like(pack_out[:, SMALL_AT + SMALL :])
    half = keep_out.shape[1]
    keep_out[...] = pack_out[:, pl.ds(pl.multiple_of(core[0] * half, 128), half)]
    give_out[...] = pack_out[:, pl.ds(pl.multiple_of((1 - core[0]) * half, 128), half)]


def lamb_direction(master, gradient, mean, square, factor):
    clipped = gradient * factor
    mean_next = BETA_ONE * mean + (1.0 - BETA_ONE) * clipped
    square_next = BETA_TWO * square + (1.0 - BETA_TWO) * clipped * clipped
    direction = (
        mean_next
        / (1.0 - BETA_ONE**STEP)
        / (jnp.sqrt(square_next / (1.0 - BETA_TWO**STEP)) + EPS_ADAM)
        + DECAY * master
    )
    return mean_next, square_next, direction


def whole(array):
    shape = array.shape
    return pl.BlockSpec(shape, lambda *unused: (0,) * len(shape))


def params(limit=VMEM):
    return pltpu.CompilerParams(vmem_limit_bytes=limit)


def cost(microseconds):
    return pl.CostEstimate(flops=int(microseconds * 1.15e9), bytes_accessed=0, transcendentals=0)


def columns(array, width, at):
    return (array, pl.BlockSpec((array.shape[0], width), lambda *unused: (0, at)))


def simple_call(kernel, outs, args, microseconds, scratch=()):
    pairs = [a if isinstance(a, tuple) else (a, whole(a)) for a in args]
    args = [a for a, spec in pairs]
    return pl.pallas_call(
        kernel,
        out_shape=outs,
        in_specs=[spec for a, spec in pairs],
        out_specs=[whole(a) for a in outs],
        scratch_shapes=list(scratch),
        grid=(1,),
        compiler_params=params(),
        cost_estimate=cost(microseconds),
    )(*args)


def out(shape, dtype=F32):
    return jax.ShapeDtypeStruct(shape, dtype)


def flip(value, axis_name, bit):
    count = lax.axis_size(axis_name)
    return lax.ppermute(value, axis_name, [(i, i ^ bit) for i in range(count)])


def bits_of(axis_name):
    count = lax.axis_size(axis_name)
    return [1 << i for i in range(count.bit_length() - 1)]


def sum_small(value, axes):
    for axis_name in axes:
        for bit in bits_of(axis_name):
            value = value + flip(value, axis_name, bit)
    return value


def expert_parts(value):
    if lax.axis_size("expert") != 8:
        return [sum_small(value, ("expert",))]
    value = value + flip(value, "expert", 1)
    return [value] + [flip(value, "expert", bit) for bit in (2, 4, 6)]


def ordered_sum(parts, me):
    values = [part[...] for part in parts]
    total = None
    for index in range(len(values)):
        at = jnp.bitwise_xor(index, me)
        part = values[0]
        for other in range(1, len(values)):
            part = jnp.where(at == other, values[other], part)
        total = part if total is None else total + part
    return total


def halves(value, axis, take_high):
    size = value.shape[axis] // 2
    side = take_high.astype(jnp.int32)
    return (
        lax.dynamic_slice_in_dim(value, side * size, size, axis),
        lax.dynamic_slice_in_dim(value, (1 - side) * size, size, axis),
    )


def scatter_sum(value, axis, bits):
    for bit in bits:
        side = (lax.axis_index("dp") & bit) != 0
        keep, give = halves(value, axis, side)
        value = keep + flip(give, "dp", bit)
    return value


def join(value, axis, bits):
    for bit in reversed(bits):
        side = (lax.axis_index("dp") & bit) != 0
        other = flip(value, "dp", bit)
        value = jnp.concatenate(
            [jnp.where(side, other, value), jnp.where(side, value, other)], axis
        )
    return value


def ready(value, *others):
    return lax.optimization_barrier((value, *others))[0]


def exchange(value):
    return lax.all_to_all(value, "expert", split_axis=0, concat_axis=0, tiled=True)


def exchange_near(value):
    return lax.all_to_all(
        value,
        "expert",
        split_axis=0,
        concat_axis=0,
        tiled=True,
        axis_index_groups=[[0, 1, 2, 3], [4, 5, 6, 7]],
    )


def pairs_of(value, sides):
    far = flip(value, "expert", 4)
    return pl.pallas_call(
        pair_kernel,
        out_shape=out((4, 2, *value.shape), BF16),
        in_specs=[
            pl.BlockSpec(memory_space=pltpu.SMEM),
            *[pl.BlockSpec(memory_space=pltpu.VMEM)] * 2,
        ],
        out_specs=pl.BlockSpec(memory_space=pltpu.VMEM),
        compiler_params=params(),
        cost_estimate=cost(2),
    )(sides, value, far)


def spread(value):
    count = lax.axis_size("expert")
    return exchange(jnp.broadcast_to(value[None], (count, *value.shape)))


def expert_scatter(value):
    return jnp.sum(exchange(value), 0)


def squares_kernel(weights, sums, last, last_other, *refs):
    total_last, both = refs[-2:]
    total_last[...] = last[...] + last_other[...]
    total = jnp.zeros((1, 1), F32)
    for weight, ref in zip(weights, (total_last, *refs[:-2])):
        for piece in decode(ref) if ref.dtype == jnp.int16 else [ref[...]]:
            part = jnp.sum(jnp.sum(piece * piece, -1, keepdims=True), 0, keepdims=True)
            total = total + part * weight
    both[0:1, :] = jnp.broadcast_to(total, (1, 128))
    both[1:2, :] = sums[...]


def sum_all(value):
    while value.ndim > 2:
        value = jnp.sum(value, 0)
    return jnp.sum(jnp.sum(value, 0, keepdims=True), -1, keepdims=True)


TILED = (4, 7, 8)


def tile_spec(index, shape, steps):
    if index == 7:
        return pl.BlockSpec((2, D // steps, shape[2]), lambda i: (0, i, 0))
    if index == 8:
        return pl.BlockSpec((shape[0] // steps, D), lambda i: (i, 0))
    if index == 4 and len(shape) == 3:
        half = steps // 2
        return pl.BlockSpec((1, shape[1], shape[2] // half), lambda i: (i // half, 0, i % half))
    if index == 4:
        return pl.BlockSpec((shape[0], shape[1] // steps), lambda i: (0, i))
    return pl.BlockSpec(shape, lambda i: (0,) * len(shape))


def tile_specs(arrays, steps):
    return [tile_spec(index, array.shape, steps) for index, array in enumerate(arrays)]


def quarter_kernel(sides, gate_up, down, quarter):
    wide = gate_up.shape[2]
    quarter[:, :wide] = gate_up[0].astype(BF16)
    quarter[:, wide:] = down[...].astype(BF16)


def prepare_kernel(count, *refs):
    masters = refs[:count]
    gate_up_low, down_low, totals = refs[count:]
    step = pl.program_id(0)
    gate_up_low[...] = masters[7][...].astype(BF16)
    down_low[...] = masters[8][...].astype(BF16)

    @pl.when(step == 0)
    def _():
        totals[...] = jnp.zeros_like(totals)

    def add(index):
        master = masters[index][...]
        totals[index : index + 1, :] += jnp.broadcast_to(sum_all(master * master), (1, 128))

    for index in TILED:
        add(index)

    @pl.when(step == 0)
    def _():
        for index in range(count):
            if index not in TILED:
                add(index)


def picked_piece(pieces, index, part):
    value = part(pieces[0])
    for other in range(1, len(pieces)):
        value = jnp.where(index == other, part(pieces[other]), value)
    return value


def moments_kernel(fast, count, part_count, small_end, sides, master_squares, *refs):
    square_parts, refs = refs[:part_count], refs[part_count:]
    masters, means, squares = (refs[k * count : (k + 1) * count] for k in range(3))
    results = refs[-3 * count - 2 :]
    pieces = refs[3 * count : -3 * count - 2]
    totals, sums = results[-2:]
    both_sums = ordered_sum(square_parts, sides[3])
    sums[...] = both_sums
    factor = jnp.minimum(1.0, CLIP / jnp.sqrt(both_sums[0:1, 0:1]))
    step = pl.program_id(0)

    @pl.when(step == 0)
    def _():
        totals[:16] = jnp.zeros_like(master_squares)
        totals[16:] = master_squares[...]

    def last_rows(start, stop):
        if not fast:
            return pieces[0][:, start:stop]
        low = sides[0] == 0
        half = pieces[0].shape[1]
        parts = []
        for side in range(2):
            begin, end = max(start, side * half), min(stop, (side + 1) * half)
            if begin < end:
                begin, end = begin - side * half, end - side * half
                mine, other = pieces[0][:, begin:end], pieces[1][:, begin:end]
                parts.append(jnp.where(low == (side == 0), mine, other))
        return jnp.concatenate(parts, 1) if len(parts) > 1 else parts[0]

    def gradient_of(index):
        if index in (0, 3):
            table = last_rows(SMALL_AT, SMALL_AT + SMALL).T
            return table[VECTORS_AT : VECTORS_AT + 5] if index == 0 else table[:HORIZON_AT]
        if index == 6:
            return last_rows(SMALL_AT, SMALL_AT + SMALL)[:, HORIZON_AT:small_end]
        if index == 1:
            return last_rows(0, 3 * D)
        if index == 2:
            return last_rows(3 * D, SMALL_AT)
        if not fast:
            return pieces[{4: 1, 5: 2, 7: 3, 8: 4}[index]][...]
        me = sides[0] * 2 + sides[1]
        shared = pieces[2:6]
        wide = 2 * FFS // 4
        if index == 4:
            return picked_piece(
                shared, jnp.bitwise_xor(step, me), lambda ref: ref[:, :wide]
            )
        if index == 5:
            return jnp.concatenate(
                [
                    picked_piece(shared, jnp.bitwise_xor(piece, me), lambda ref: ref[:, wide:])
                    for piece in range(4)
                ],
                0,
            )
        routed = pieces[6:10]
        split = masters[7].shape[2] // 128
        count_tiles = routed[0].shape[1] // 128 - 1

        def decoded(at, here, first, last):
            powers = picked_piece(routed, at, lambda ref: ref[here, count_tiles * 128 :])
            scale = jnp.exp2(powers.astype(jnp.int32).astype(F32) - 15.0)
            codes = picked_piece(routed, at, lambda ref: ref[here, first * 128 : last * 128])
            codes = codes.astype(jnp.int32).astype(F32)
            return jnp.concatenate(
                [
                    codes[:, (tile - first) * 128 : (tile - first + 1) * 128]
                    * scale[:, tile : tile + 1]
                    for tile in range(first, last)
                ],
                1,
            )

        if index == 7:
            rows = masters[7].shape[1]
            here = pl.ds(pl.multiple_of((step % 2) * rows, 16), rows)
            return jnp.stack(
                [
                    decoded(jnp.bitwise_xor(side * 2 + step // 2, me), here, 0, split)
                    for side in range(2)
                ]
            )
        return decoded(jnp.bitwise_xor(step, me), slice(None), split, count_tiles)

    def update(index):
        gradient = gradient_of(index)
        if index == 4 and gradient.ndim == 3:
            gradient = gradient[0]
        scale = factor.reshape(1, 1, 1) if gradient.ndim == 3 else factor
        mean_next, square_next, direction = lamb_direction(
            masters[index][...], gradient, means[index][...], squares[index][...], scale
        )
        results[index][...] = direction
        results[count + index][...] = mean_next
        results[2 * count + index][...] = square_next
        totals[index : index + 1, :] += jnp.broadcast_to(sum_all(direction * direction), (1, 128))

    for index in TILED:
        update(index)
    for index in range(count):
        if index not in TILED:
            pl.when(step == min(index, 3))(functools.partial(update, index))


def step_kernel(count, part_count, sides, *refs):
    parts, refs = refs[:part_count], refs[part_count:]
    masters, directions = refs[:count], refs[count : 2 * count]
    results = refs[2 * count :]
    all_totals = ordered_sum(parts, sides[3])
    totals, master_totals = all_totals[:count], all_totals[16 : 16 + count]
    diagonal = lax.broadcasted_iota(jnp.int32, (count, 128), 0) == lanes_of((count, 128))
    for row, sums in enumerate((master_totals, totals)):
        flat = jnp.sum(jnp.where(diagonal, jnp.sqrt(sums[:, 0:1]), 0.0), 0, keepdims=True)
        results[-1][row : row + 1, :] = flat[:, :count]
    step = pl.program_id(0)

    def update(index):
        ratio = jnp.sqrt(master_totals[index : index + 1, 0:1]) / jnp.sqrt(
            totals[index : index + 1, 0:1]
        )
        ratio = RATE * ratio
        if len(masters[index].shape) == 3:
            ratio = ratio.reshape(1, 1, 1)
        results[index][...] = masters[index][...] - ratio * directions[index][...]

    for index in TILED:
        update(index)
    for index in range(count):
        if index not in TILED:
            pl.when(step == min(index, 3))(functools.partial(update, index))


def shards(
    points,
    experts,
    lengths,
    domains,
    domain_weights,
    vectors,
    attend_input,
    attend_output,
    router,
    shared_input,
    shared_output,
    horizon,
    expert_input,
    expert_output,
    mean_vectors,
    mean_attend_input,
    mean_attend_output,
    mean_router,
    mean_shared_input,
    mean_shared_output,
    mean_horizon,
    mean_expert_input,
    mean_expert_output,
    square_vectors,
    square_attend_input,
    square_attend_output,
    square_router,
    square_shared_input,
    square_shared_output,
    square_horizon,
    square_expert_input,
    square_expert_output,
):
    expert_count = lax.axis_size("expert")
    group_size = expert_count // EXPERTS
    dp_count = lax.axis_size("dp")
    dp_bits = bits_of("dp")
    amount = points.shape[0]
    local_rows = attend_input.shape[0]
    head_columns = horizon.shape[1]
    hidden_local = expert_output.shape[0]
    small_end = HORIZON_AT + head_columns
    fast = (
        group_size == 1 and dp_count == 4 and local_rows % 16 == 0 and hidden_local == 2 * D
    )
    core = lax.axis_index("dp") & 1
    sides = jnp.stack(
        [
            core, lax.axis_index("dp") >> 1, lax.axis_index("expert") >> 2,
            lax.axis_index("expert") >> 1 if fast else core * 0, lax.axis_index("expert") & 3,
        ]
    ).astype(jnp.int32)
    in_smem = pl.BlockSpec(memory_space=pltpu.SMEM)
    in_vmem = pl.BlockSpec(memory_space=pltpu.VMEM)
    ahead_row = jnp.pad(
        jnp.asarray(ahead_table())[None], ((0, 0), (0, SMALL - head_columns)), constant_values=1 << 20
    )
    packed = pl.pallas_call(
        functools.partial(pack_kernel, small_end),
        out_shape=out((1 if fast else expert_count, local_rows, 2 * D + SMALL), BF16),
        in_specs=[*[in_smem] * 3, *[in_vmem] * 6],
        out_specs=in_vmem,
        compiler_params=params(),
        cost_estimate=cost(2),
    )(sides, lengths, domains, ahead_row, attend_input, attend_output, router.T, horizon, vectors)
    gathered = exchange_near(pairs_of(packed[0], sides)) if fast else exchange(packed)

    def state(group):
        return tuple(a.T if index == 3 else a for index, a in enumerate(group))

    masters = state(
        (
            vectors, attend_input, attend_output, router, shared_input, shared_output, horizon,
            expert_input, expert_output,
        )
    )
    first_moments = state(
        (
            mean_vectors, mean_attend_input, mean_attend_output, mean_router, mean_shared_input,
            mean_shared_output, mean_horizon, mean_expert_input, mean_expert_output,
        )
    )
    second_moments = state(
        (
            square_vectors, square_attend_input, square_attend_output, square_router,
            square_shared_input, square_shared_output, square_horizon, square_expert_input,
            square_expert_output,
        )
    )
    count = len(masters)
    steps = 4
    gate_up_low, down_low, master_squares = pl.pallas_call(
        functools.partial(prepare_kernel, count),
        out_shape=[
            out(expert_input.shape, BF16), out(expert_output.shape, BF16), out((16, 128)),
        ],
        grid=(steps,),
        in_specs=tile_specs(masters, steps),
        out_specs=[
            tile_spec(7, expert_input.shape, steps),
            tile_spec(8, expert_output.shape, steps),
            whole(out((16, 128))),
        ],
        compiler_params=params(),
        cost_estimate=cost(5),
    )(*masters)
    weight_quarter = points
    if fast:
        weight_quarter = pl.pallas_call(
            quarter_kernel,
            out_shape=out((D // 2, hidden_local + D), BF16),
            grid_spec=pltpu.PrefetchScalarGridSpec(
                num_scalar_prefetch=1,
                grid=(1,),
                in_specs=[
                    pl.BlockSpec(
                        (1, D // 2, hidden_local), lambda i, sides: (sides[0], sides[1], 0)
                    ),
                    pl.BlockSpec((D // 2, D), lambda i, sides: (sides[0] * 2 + sides[1], 0)),
                ],
                out_specs=pl.BlockSpec((D // 2, hidden_local + D), lambda i, sides: (0, 0)),
            ),
            compiler_params=params(),
            cost_estimate=cost(2.6),
        )(sides, expert_input, expert_output)
    frequency = jnp.exp(-jnp.log(10000.0) * jnp.arange(HD // 2, dtype=F32) / (HD // 2))
    cosine, sine, known, rows_table = pl.pallas_call(
        tables_kernel,
        out_shape=[out((amount, 128)), out((amount, 128)), out((amount, 128)), out((8, amount))],
        in_specs=[*[in_smem] * 2, *[in_vmem] * 3],
        out_specs=[in_vmem] * 4,
        compiler_params=params(),
        cost_estimate=cost(3),
    )(
        lengths,
        domains,
        jnp.tile(frequency, 128 // (HD // 2))[None],
        points.reshape(1, amount),
        experts.T,
    )
    folds = FFS // D
    shared_piece = jnp.concatenate(
        [
            shared_input,
            shared_output.reshape(folds, local_rows, D).swapaxes(0, 1).reshape(local_rows, -1),
        ],
        1,
    ).astype(BF16)
    for bit in dp_bits:
        shared_piece, unused = halves(shared_piece, 1, (lax.axis_index("dp") & bit) != 0)
    if fast:
        shared_piece = pairs_of(shared_piece, sides)
    gathered = ready(gathered, known, shared_piece, weight_quarter).reshape(D, -1)
    gathered_other = flip(gathered, "dp", 1)
    shared_piece = ready(shared_piece, gathered)
    if fast:
        shared_pieces = exchange_near(shared_piece)
        weight_pieces = [flip(weight_quarter, "expert", 4)]
    else:
        shared_pieces = spread(shared_piece)
    (
        embedded, first, qkv, log_total, mixed, after, second, logits, slots, gains, pack,
        counts_half,
    ) = simple_call(
        functools.partial(front_kernel, fast, local_rows),
        [
            out((amount, D)), out((amount, D), BF16), out((amount, 3 * D), BF16),
            out((amount, 128)), out((amount, D), BF16), out((amount, D)),
            out((amount, D), BF16), out((amount, SMALL)), out((EXPERTS * CAP, D), BF16),
            out((8, D)), out((D, SMALL_AT + SMALL), BF16), out((1, SMALL)),
        ],
        [(sides, in_smem), gathered, gathered_other, cosine, sine, known, rows_table],
        15,
    )

    def to_devices(rows):
        rows = rows.reshape(EXPERTS, CAP, D)
        return exchange(jnp.repeat(rows, group_size, 0)).reshape(-1, D)

    def to_points(rows):
        rows = exchange(rows.reshape(expert_count, CAP, D))
        if group_size > 1:
            kind = rows.dtype
            rows = rows.reshape(EXPERTS, group_size, CAP, D).astype(F32)
            rows = jnp.sum(rows, 1).astype(kind)
        return rows.reshape(-1, D)

    first_bit = dp_bits[-1]
    block = 512
    if fast:
        arrived = exchange_near(
            ready(slots, shared_pieces, weight_pieces[0]).reshape(4, 2, CAP, D)
        )
        weight_pieces.append(flip(ready(weight_pieces[0], slots), "dp", 2))
        weight_pieces += [flip(piece, "dp", 1) for piece in weight_pieces]
        gate_up_far, down_far = simple_call(
            far_weights_kernel,
            [out(expert_input.shape, BF16), out(expert_output.shape, BF16)],
            [(sides, in_smem), ready(weight_pieces[0], gate_up_low), *weight_pieces[1:]],
            3,
        )
        shared_pieces = ready(shared_pieces, weight_pieces[1])
        shared_other = flip(shared_pieces, "dp", 2)
        row_spec = pl.BlockSpec(
            (4, 1, CAP, D), lambda i, sides: (0, jnp.bitwise_xor(i, sides[2]), 0, 0)
        )
        held = [gate_up_low, down_low, gate_up_far, down_far]
        held_specs = [
            pl.BlockSpec(a.shape, lambda *unused, a=a: (0,) * len(a.shape)) for a in held
        ]
        expert_rows = pl.pallas_call(
            pair_expert_kernel,
            out_shape=out((4, 2, CAP + CODE_ROWS, D), jnp.int16),
            grid_spec=pltpu.PrefetchScalarGridSpec(
                num_scalar_prefetch=1,
                grid=(2,),
                in_specs=[row_spec, *held_specs],
                out_specs=pl.BlockSpec(
                    (4, 1, CAP + CODE_ROWS, D),
                    lambda i, sides: (0, jnp.bitwise_xor(i, sides[2]), 0, 0),
                ),
            ),
            compiler_params=params(),
            cost_estimate=cost(10),
        )(sides, arrived, *held)
        returned = exchange_near(expert_rows).reshape(
            EXPERTS, CAP + CODE_ROWS, D
        )
        shared_pieces = ready(shared_pieces, expert_rows)
        shared_quarters = [shared_pieces, shared_other]
        shared_quarters += [flip(piece, "dp", 1) for piece in shared_quarters]
        shin_low, shout_low = simple_call(
            functools.partial(shared_weights_kernel, local_rows),
            [out((D, 2 * FFS), BF16), out((FFS, D), BF16)],
            [(sides, in_smem), *[piece.reshape(D, -1) for piece in shared_quarters]],
            4.3,
        )
    else:
        arrived = to_devices(ready(slots, shared_pieces))
        total_rows = arrived.shape[0]
        row_spec = pl.BlockSpec((block, D), lambda i: (i, 0))
        expert_rows = pl.pallas_call(
            expert_kernel,
            out_shape=out((total_rows, D)),
            grid=(total_rows // block,),
            in_specs=[row_spec, whole(gate_up_low), whole(down_low)],
            out_specs=row_spec,
            compiler_params=params(),
            cost_estimate=cost(10),
        )(arrived, gate_up_low, down_low)
        returned = to_points(expert_rows)
        shared_pack = join(ready(shared_pieces, expert_rows), 2, dp_bits)
        shin_low = shared_pack[:, :, : 2 * FFS].reshape(D, -1)
        shout_low = (
            shared_pack[:, :, 2 * FFS :]
            .reshape(expert_count, local_rows, folds, D)
            .swapaxes(1, 2)
            .reshape(FFS, D)
        )
    chunk = 512
    chunks = FFS // chunk
    shared = pl.pallas_call(
        shared_kernel,
        out_shape=out((amount, D)),
        grid=(chunks,),
        in_specs=[
            whole(second),
            pl.BlockSpec((D, chunk), lambda i: (0, i)),
            pl.BlockSpec((D, chunk), lambda i: (0, i + chunks)),
            pl.BlockSpec((chunk, D), lambda i: (i, 0)),
        ],
        out_specs=pl.BlockSpec((amount, D), lambda i: (0, 0)),
        compiler_params=params(),
        cost_estimate=cost(5.8),
    )(second, shin_low, shin_low, shout_low)
    counts = ready(counts_half, expert_rows)
    for bit in dp_bits[1:]:
        counts = counts + flip(counts, "dp", bit)
    weighting = jnp.pad(domain_weights, (0, SMALL - DOMAINS))[None] / jnp.maximum(counts, 1.0)
    side_pad = ((0, 0), (HORIZON_AT, SMALL - small_end))
    target = jnp.pad(target_columns(points), side_pad)
    ahead_small = jnp.pad(
        jnp.asarray(ahead_table())[None], ((0, 0), side_pad[1]), constant_values=1 << 20
    )
    small_low = columns(pack, SMALL, SMALL_AT // SMALL)
    (
        mixer_slope, shared_slope, slope_slots, logits_slope, small_head, gain_three, local_sums,
    ) = simple_call(
        functools.partial(middle_kernel, fast),
        [
            out((amount, D)), out((amount, D), BF16), out((EXPERTS * CAP, D), BF16),
            out((amount, SMALL), BF16), out((D, SMALL)), out((1, D)), out((1, SMALL)),
        ],
        [
            returned, known, rows_table, after, shared, logits, small_low, gains, target,
            ahead_small, weighting,
        ],
        11.4,
    )
    received = exchange_near(slope_slots.reshape(4, 2, CAP, D)) if fast else to_devices(slope_slots)
    chunk = 2 * D
    chunks = FFS // chunk
    back_in = [
        pl.BlockSpec((amount, D), lambda i, *unused: (0, 0)),
        pl.BlockSpec((amount, D), lambda i, *unused: (0, 0)),
        pl.BlockSpec((D, chunk), lambda i, *unused: (0, i)),
        pl.BlockSpec((D, chunk), lambda i, *unused: (0, i + chunks)),
        pl.BlockSpec((chunk, D), lambda i, *unused: (i, 0)),
    ]
    second_spec = pl.BlockSpec((amount, D), lambda i, *unused: (0, 0))
    back_args = (second, shared_slope, shin_low, shin_low, shout_low)
    if fast:
        in_spec = pl.BlockSpec(
            (1, D, chunk), lambda i, sides: (jnp.bitwise_xor(i, sides[1]), 0, 0)
        )
        give_spec = pl.BlockSpec(
            (1, D, D), lambda i, sides: (jnp.bitwise_xor(i, sides[1]), 0, 0)
        )
        out_spec = pl.BlockSpec((2, D // chunks, D), lambda i, sides: (0, i, 0))
        shared_second_slope, in_keep, in_even, in_odd, out_keep, out_give = pl.pallas_call(
            shared_back_split_kernel,
            out_shape=[
                out((amount, D)), out((2, D, FFS // 2)), *[out((2, D, D))] * 4,
            ],
            grid_spec=pltpu.PrefetchScalarGridSpec(
                num_scalar_prefetch=1,
                grid=(chunks,),
                in_specs=back_in,
                out_specs=[second_spec, in_spec, give_spec, give_spec, out_spec, out_spec],
                scratch_shapes=[pltpu.VMEM((chunk, D), F32)],
            ),
            compiler_params=params(),
            cost_estimate=cost(14),
        )(sides, *back_args)
    else:
        shared_second_slope, grad_shin, grad_shout = pl.pallas_call(
            shared_back_kernel,
            out_shape=[out((amount, D)), out((2, D, FFS)), out((FFS, D))],
            grid=(chunks,),
            in_specs=back_in,
            out_specs=[
                second_spec,
                pl.BlockSpec((2, D, chunk), lambda i: (0, 0, i)),
                pl.BlockSpec((chunk, D), lambda i: (i, 0)),
            ],
            compiler_params=params(),
            cost_estimate=cost(10),
        )(*back_args)
    if fast:
        in_even, in_odd, out_other = (flip(a, "dp", 1) for a in (in_even, in_odd, out_give))
        fold_in = pl.BlockSpec((2, D // 4, FFS // 2), lambda i: (0, i, 0))
        fold_out = pl.BlockSpec((2, D // 4, D), lambda i: (0, i, 0))
        wide = FFS // 2 + D
        fold_to = pl.BlockSpec((D // 4, wide), lambda i: (i, 0))
        code_to = pl.BlockSpec((D // 4, wide + 128), lambda i: (i, 0))
        shared_keep, shared_give = pl.pallas_call(
            fold_kernel,
            out_shape=[out((D, wide)), out((D, wide + 128), jnp.int16)],
            grid=(4,),
            in_specs=[fold_in, *[fold_out] * 4],
            out_specs=[fold_to, code_to],
            compiler_params=params(),
            cost_estimate=cost(5.3),
        )(in_keep, in_even, in_odd, out_keep, out_other)
        received = ready(received, shared_second_slope, shared_give)
        shared_other = flip(shared_give, "dp", 2)
    else:
        received = ready(received, shared_second_slope)
    if fast:
        half_shapes = [out((2, D, hidden_local))] * 2 + [out((2, D, D))] * 2
        row_spec = pl.BlockSpec(
            (2, 1, CAP, D), lambda i, j, sides: (j, jnp.bitwise_xor(i, sides[2]), 0, 0)
        )
        grad_rows, expert_in, expert_in_give, expert_out, expert_out_give = pl.pallas_call(
            expert_back_split_kernel,
            out_shape=[out((4, 2, CAP, D), BF16), *half_shapes],
            grid_spec=pltpu.PrefetchScalarGridSpec(
                num_scalar_prefetch=1,
                grid=(2, 2),
                in_specs=[row_spec, row_spec, *held_specs],
                out_specs=[
                    row_spec,
                    *[
                        pl.BlockSpec((1, *a.shape[1:]), lambda i, j, sides: (i, 0, 0))
                        for a in half_shapes
                    ],
                ],
            ),
            compiler_params=params(),
            cost_estimate=cost(19.5),
        )(sides, arrived, received, *held)
        routed_back = exchange_near(ready(grad_rows, shared_other)).reshape(-1, D)
    else:
        grad_rows, grad_expert_in, grad_expert_out = pl.pallas_call(
            expert_back_kernel,
            out_shape=[
                out((total_rows, D), BF16), out((2, D, hidden_local)), out((hidden_local, D)),
            ],
            grid=(total_rows // block,),
            in_specs=[row_spec, row_spec, whole(gate_up_low), whole(down_low)],
            out_specs=[
                row_spec,
                pl.BlockSpec((2, D, hidden_local), lambda i: (0, 0, 0)),
                pl.BlockSpec((hidden_local, D), lambda i: (0, 0)),
            ],
            compiler_params=params(),
            cost_estimate=cost(10),
        )(arrived, received, gate_up_low, down_low)
        routed_back = to_points(grad_rows)
    if fast:
        (shared_code,) = simple_call(
            functools.partial(add_code_kernel, local_rows),
            [out((D, wide + 128), jnp.int16)],
            [shared_keep, shared_other],
            4.4,
        )
        expert_in_other = flip(expert_in_give, "dp", 1)
        expert_out_other = flip(expert_out_give, "dp", 1)
        half_in = pl.BlockSpec((1, D, hidden_local), lambda i: (i, 0, 0))
        half_out = pl.BlockSpec((1, D, D), lambda i: (i, 0, 0))
        expert_keep, expert_code = pl.pallas_call(
            expert_split_kernel,
            out_shape=[out((2, D // 2, wide)), out((2, D // 2, wide + 128), jnp.int16)],
            grid=(2,),
            in_specs=[in_smem, half_in, half_in, half_out, half_out],
            out_specs=[
                pl.BlockSpec((1, D // 2, wide), lambda i: (i, 0, 0)),
                pl.BlockSpec((1, D // 2, wide + 128), lambda i: (i, 0, 0)),
            ],
            compiler_params=params(),
            cost_estimate=cost(4.6),
        )(sides, expert_in, expert_in_other, expert_out, expert_out_other)
        sums = local_sums + flip(local_sums, "dp", 2)
        routed_plain = routed_back
        routed_back = ready(routed_back, shared_code, expert_code, sums)
    attend_slope, mixed_slope, grad_output, gain_two, small_routed = simple_call(
        functools.partial(attend_back_kernel, fast),
        [
            out((amount, D)), out((amount, D), BF16), out((D, D)), out((1, D)), out((D, SMALL)),
        ],
        [
            routed_back, known, shared_second_slope, logits_slope, small_low, after,
            mixer_slope, gains, mixed, second, columns(pack, D, 3), small_head,
        ],
        6,
    )
    if fast:
        expert_code_other = flip(expert_code, "dp", 2)
        expert_own, expert_far = simple_call(
            expert_far_kernel,
            [out((D // 2, wide)), out((D // 2, wide + 128), jnp.int16)],
            [expert_keep, expert_code_other],
            3.5,
        )
        mixed_slope = ready(mixed_slope, expert_far)
    pack_columns = SMALL_AT + SMALL
    half_columns = SMALL_AT // 2 + SMALL
    last_keep, last_give = simple_call(
        functools.partial(front_back_kernel, fast),
        [
            out((D, half_columns if fast else pack_columns)),
            out((D, half_columns) if fast else (8, 128)),
        ],
        [
            (sides, in_smem), mixed_slope, qkv, log_total, known, rows_table, cosine, sine, first,
            embedded, gains, columns(pack, 3 * D, 0), attend_slope, small_routed, gain_two,
            gain_three, grad_output,
        ],
        18.4,
        [
            pltpu.VMEM((D, 2 * half_columns), F32),
            pltpu.VMEM((amount, D), F32),
            pltpu.VMEM((amount, D), F32),
            pltpu.VMEM((amount, D), F32),
            pltpu.VMEM((amount, 3 * D), BF16),
        ],
    )

    if fast:
        shared_code = ready(shared_code, routed_plain, expert_code)
        shared_code = exchange_near(shared_code.reshape(4, 2, local_rows, wide + 128))
        expert_far_other = flip(expert_far, "expert", 4)
        last_give = ready(last_give, expert_far_other, shared_code)
        shared_own, shared_far = simple_call(
            near_sum_kernel,
            [out((local_rows, wide)), out((local_rows, wide + 128), jnp.int16)],
            [(sides, in_smem), ready(shared_code, last_keep)],
            2.5,
        )
        last_keep = ready(last_keep, shared_far)
        last_codes = simple_call(
            functools.partial(last_code_kernel, local_rows),
            [out((2 * local_rows, half_columns + 128), jnp.int16)] * 4,
            [(sides, in_smem), last_keep, flip(last_give, "dp", 1)],
            3.3,
        )
        (shared_sum,) = simple_call(
            add_kernel, [out((local_rows, wide))], [shared_own, flip(shared_far, "expert", 4)], 1.5
        )
        last_code = last_codes[0]
        last_codes = [last_code] + [
            flip(ready(code, shared_code), "expert", bit)
            for bit, code in enumerate(last_codes)
            if bit
        ]
        last_own, last_far = simple_call(
            functools.partial(last_near_kernel, local_rows),
            [
                out((local_rows, half_columns)),
                out((local_rows, half_columns + 128), jnp.int16),
            ],
            [(sides, in_smem), *last_codes],
            2.5,
        )
        (last_part,) = simple_call(
            last_sum_kernel,
            [out((local_rows, half_columns))],
            [(sides, in_smem), last_own, flip(last_far, "expert", 4)],
            1.5,
        )
        last_other = flip(last_part, "dp", 2)
        (expert_total,) = simple_call(
            expert_total_kernel,
            [out((D // 2, wide + 128), jnp.int16)],
            [ready(expert_own, last_code), expert_far_other],
            2.5,
        )
        expert_cross = flip(expert_total, "dp", 2)
        shared_cross = flip(shared_sum, "dp", 2)
        square_pieces = [
            shared_sum, shared_cross, expert_total, expert_cross,
        ]
        weights = (1.0,) * 5
        square_bits = [1]
        pieces = [
            shared_sum, shared_cross, flip(shared_sum, "dp", 1), flip(shared_cross, "dp", 1),
            expert_total, expert_cross, flip(expert_total, "dp", 1), flip(expert_cross, "dp", 1),
        ]
        piece_specs = [whole(a) for a in pieces]
    else:
        sums = local_sums
        shin_part = scatter_sum(grad_shin, 0, [1])[0].reshape(expert_count, local_rows, FFS)
        shin_part = expert_scatter(scatter_sum(shin_part, 2, dp_bits[1:]))
        shout_part = scatter_sum(grad_shout.reshape(expert_count, -1, D), 1, dp_bits)
        shout_part = expert_scatter(shout_part)
        expert_in_part = scatter_sum(grad_expert_in.reshape(-1, hidden_local), 0, dp_bits)
        expert_out_part = scatter_sum(grad_expert_out, 0, dp_bits)
        last_part = expert_scatter(last_keep.reshape(expert_count, local_rows, -1))
        for bit in dp_bits:
            last_other = flip(last_part, "dp", bit)
            if bit != dp_bits[-1]:
                last_part = last_part + last_other
        square_pieces = [expert_in_part, expert_out_part, shin_part, shout_part]
        weights = (1.0 / dp_count, 1.0, 1.0, 1.0, 1.0)
        square_bits = dp_bits
        pieces = [
            join(join(shin_part, 1, dp_bits[1:])[None], 0, [1]),
            join(shout_part, 0, dp_bits),
            join(expert_in_part, 0, dp_bits).reshape(expert_input.shape),
            join(expert_out_part, 0, dp_bits),
        ]
        piece_specs = [tile_spec(i, a.shape, steps) for i, a in zip((4, 5, 7, 8), pieces)]
    last_part, both_sums = simple_call(
        functools.partial(squares_kernel, weights),
        [out(last_part.shape), out((2, 128))],
        [sums, last_part, last_other, *square_pieces],
        3.5,
    )
    last_pieces = [last_part] + ([flip(last_part, "dp", 1)] if fast else [])
    pieces = last_pieces + pieces
    piece_specs = [whole(a) for a in last_pieces] + piece_specs
    for bit in square_bits:
        both_sums = both_sums + flip(both_sums, "dp", bit)
    square_parts = expert_parts(both_sums)
    part_count = len(square_parts)
    shapes = [out(a.shape) for a in masters]
    state_specs = tile_specs(masters, steps)
    updates = pl.pallas_call(
        functools.partial(moments_kernel, fast, count, part_count, small_end),
        out_shape=[*shapes, *shapes, *shapes, out((32, 128)), out((2, 128))],
        grid=(steps,),
        in_specs=[
            in_smem, whole(master_squares), *[whole(a) for a in square_parts], *state_specs, *state_specs, *state_specs,
            *piece_specs,
        ],
        out_specs=[
            *state_specs, *state_specs, *state_specs, whole(out((32, 128))), whole(out((2, 128))),
        ],
        compiler_params=params(),
        cost_estimate=cost(17),
    )(sides, master_squares, *square_parts, *masters, *first_moments, *second_moments, *pieces)
    both_sums = updates[-1]
    domain_sums = both_sums[1, :DOMAINS]
    grad_norm = jnp.sqrt(both_sums[0, 0:1])
    directions = updates[:count]
    total_parts = expert_parts(updates[-2])
    *next_masters, trust = pl.pallas_call(
        functools.partial(step_kernel, count, part_count),
        out_shape=[*shapes, out((2, count))],
        grid=(steps,),
        in_specs=[in_smem, *[whole(a) for a in total_parts], *state_specs, *state_specs],
        out_specs=[*state_specs, whole(out((2, count)))],
        compiler_params=params(),
        cost_estimate=cost(7),
    )(sides, *total_parts, *masters, *directions)
    results = []
    for index in range(count):
        for group in (next_masters, updates[count : 2 * count], updates[2 * count : 3 * count]):
            results.append(group[index].T if index == 3 else group[index])
    results.append(jnp.stack([domain_sums, counts[0, :DOMAINS]]))
    results.append(grad_norm)
    results.append(trust.T)
    return tuple(results)


def solution(mesh):
    placed = (
        P(("dp", "expert")),
        P(("dp", "expert"), None),
        P(("dp", "expert"), None),
        P(("dp", "expert"), None),
        P(),
        P(None, "expert"),
        P("expert", None),
        P("expert", None),
        P("expert", None),
        P("expert", None),
        P("expert", None),
        P("expert", None),
        P(None, None, "expert"),
        P("expert", None),
        P(None, "expert"),
        P("expert", None),
        P("expert", None),
        P("expert", None),
        P("expert", None),
        P("expert", None),
        P("expert", None),
        P(None, None, "expert"),
        P("expert", None),
        P(None, "expert"),
        P("expert", None),
        P("expert", None),
        P("expert", None),
        P("expert", None),
        P("expert", None),
        P("expert", None),
        P(None, None, "expert"),
        P("expert", None),
    )
    return jax.shard_map(
        shards,
        mesh=mesh,
        in_specs=placed,
        out_specs=(
            P(None, "expert"),
            P(None, "expert"),
            P(None, "expert"),
            P("expert", None),
            P("expert", None),
            P("expert", None),
            P("expert", None),
            P("expert", None),
            P("expert", None),
            P("expert", None),
            P("expert", None),
            P("expert", None),
            P("expert", None),
            P("expert", None),
            P("expert", None),
            P("expert", None),
            P("expert", None),
            P("expert", None),
            P("expert", None),
            P("expert", None),
            P("expert", None),
            P(None, None, "expert"),
            P(None, None, "expert"),
            P(None, None, "expert"),
            P("expert", None),
            P("expert", None),
            P("expert", None),
            P(),
            P(),
            P(),
        ),
        check_vma=False,
    )
```
